32 devices in a mesh: rep: 4 (over x, core), shard: 8 (over z, y).
Axes of the slice: x: 2, y: 2, z: 4, core: 2. Of those that a mesh axis runs over, the one named last changes fastest.
Arguments:
- tokens: bfloat16 [1024, 8, 2048], P('rep', 'shard'), may hold values from -6 to 6
- cotangent: bfloat16 [1024, 8, 2048], P('rep', 'shard'), may hold values from -6 to 6
- seq_lengths: int32 [4, 16], P('rep'), may hold values from 16 to 464, as said below
- seq_order: int32 [4, 16], P('rep'), may hold values from 0 to 15, each once within a row
- ln1_gain: float32 [2048], replicated, may hold values from 0.1 to 1.9
- ln1_bias: float32 [2048], replicated, may hold values from -3 to 3
- ln2_gain: float32 [2048], replicated, may hold values from 0.1 to 1.9
- ln2_bias: float32 [2048], replicated, may hold values from -3 to 3
- w_qkv: bfloat16 [2048, 6144], P('shard'), may hold values from -0.125 to 0.125
- b_qkv: float32 [6144], replicated, may hold values from -3 to 3
- w_dense: bfloat16 [2048, 2048], P('shard'), may hold values from -0.75 to 0.75
- b_dense: float32 [2048], replicated, may hold values from -3 to 3
- w_up: bfloat16 [2048, 8192], P('shard'), may hold values from -0.125 to 0.125
- b_up: float32 [8192], replicated, may hold values from -3 to 3
- w_down: bfloat16 [8192, 2048], P('shard'), may hold values from -0.0625 to 0.0625
- b_down: float32 [2048], replicated, may hold values from -3 to 3
Outputs:
- output: bfloat16 [1024, 8, 2048], P('rep', 'shard')
- input_grad: float32 [1024, 8, 2048], P('rep', 'shard')
- ln1_gain_grad: float32 [2048], replicated
- ln1_bias_grad: float32 [2048], replicated
- ln2_gain_grad: float32 [2048], replicated
- ln2_bias_grad: float32 [2048], replicated
- w_qkv_grad: float32 [2048, 6144], P('shard')
- b_qkv_grad: float32 [6144], replicated
- w_dense_grad: float32 [2048, 2048], P('shard')
- b_dense_grad: float32 [2048], replicated
- w_up_grad: float32 [2048, 8192], P('shard')
- b_up_grad: float32 [8192], replicated
- w_down_grad: float32 [8192, 2048], P('shard')
- b_down_grad: float32 [2048], replicated
The draws below stay inside these ranges and needn't reach their ends.
Inputs may be any that keep to these rules, and one draw needn't show every extreme that they name: `seq_lengths`: lengths are multiples of 8; the two sequences dealt to one device hold at most 480 tokens together, exactly 480 on some device of each group; a group's lengths sum to 2048. `seq_order`: each row holds every sequence number of its group once.
All inputs are finite; a program needn't handle non-finite values.
Results may differ from the reference program's by a relative error of at most 0.015.
Values may be sent and summed in bfloat16 or wider, within the bound.
No kernel may reach another device: no remote copies, remote signals or barrier semaphores. Data moves between devices by JAX's collectives and lax.ppermute only.
A program may use at most 640 MiB of HBM per device.

```python
import math
import jax
import jax.numpy as jnp
from jax import lax

D = 2048
HEADS = 8
HEAD = 256
FF = 8192
ROT = 64
TOK_DEV = 256
TOKENS = 2048
ROWS = 1024
NSEQ = 16
CAP = 480
N_REP = 4
N_SHARD = 8


def draw_seq_lengths(key, part):
    key = jax.random.fold_in(key, 7)
    unit_count = TOK_DEV // N_SHARD
    pair_count = N_SHARD // 2
    most_units = 2 * unit_count - 4
    key_one, key_two, key_three = jax.random.split(key, 3)
    first_total = jax.random.randint(key_one, (N_REP, pair_count), 4, most_units + 1)
    chosen_pair = jax.random.randint(key_two, (N_REP, 1), 0, pair_count)
    pair_range = jnp.arange(pair_count, dtype=jnp.int32)[None, :]
    first_total = jnp.where(pair_range == chosen_pair, most_units, first_total)
    device_totals = jnp.stack([first_total, 2 * unit_count - first_total], axis=-1).reshape(N_REP, N_SHARD)
    first_units = jax.random.randint(key_three, (N_REP, N_SHARD), 2, device_totals - 1)
    device_range = jnp.arange(N_SHARD, dtype=jnp.int32)[None, :]
    first_units = jnp.where(device_range == 2 * chosen_pair, 2, first_units)
    seq_units = jnp.stack([first_units, device_totals - first_units], axis=-1).reshape(N_REP, 2 * N_SHARD)
    return (seq_units * N_SHARD).astype(jnp.int32)


def levels(stream_key, extent, cuts, least, largest):
    level = 1.0
    for dim, shards_of in cuts:
        steps = jax.random.uniform(jax.random.fold_in(jax.random.fold_in(stream_key, 6), dim), (shards_of,), jnp.float32, least / len(cuts), largest / len(cuts))
        level = level * jnp.repeat(jnp.exp(steps), extent[dim] // shards_of).reshape((-1,) + (1,) * (len(extent) - 1 - dim))
    return level


def bell_draw(stream_key, dims, spread, reach, shards=(), held_as=jnp.bfloat16):
    entries = spread * jax.random.normal(stream_key, dims, jnp.float32)
    if shards:
        entries = entries * levels(stream_key, dims, shards, -0.22, 0.18)
    return jnp.clip(entries, -reach, reach).astype(held_as)


def setup_inputs(seed: int = 0) -> dict:
    seeds = jax.random.split(jax.random.key(seed), 17)
    return {
        "tokens": bell_draw(seeds[0], (ROWS, N_SHARD, D), 1.0, 6.0, ((0, 4), (1, 8))),
        "cotangent": bell_draw(seeds[1], (ROWS, N_SHARD, D), 1.0, 6.0, ((0, 4), (1, 8))),
        "seq_lengths": draw_seq_lengths(jax.random.fold_in(seeds[16], 71), 0),
        "seq_order": jax.vmap(lambda own: jax.random.permutation(own, NSEQ))(jax.random.split(seeds[3], N_REP)).reshape((N_REP, NSEQ)).astype(jnp.int32),
        "ln1_gain": jnp.clip(1.0 + 0.18 * jax.random.normal(seeds[4], (D,), jnp.float32), 0.1, 1.9),
        "ln1_bias": bell_draw(seeds[5], (D,), 0.5, 3.0, (), jnp.float32),
        "ln2_gain": jnp.clip(1.0 + 0.18 * jax.random.normal(seeds[6], (D,), jnp.float32), 0.1, 1.9),
        "ln2_bias": bell_draw(seeds[7], (D,), 0.5, 3.0, (), jnp.float32),
        "w_qkv": bell_draw(seeds[8], (D, 3 * D), D ** -0.5, 0.125, ((0, 8),)),
        "b_qkv": bell_draw(seeds[9], (3 * D,), 0.5, 3.0, (), jnp.float32),
        "w_dense": bell_draw(seeds[10], (D, D), (D // 32) ** -0.5, 0.75, ((0, 8),)),
        "b_dense": bell_draw(seeds[11], (D,), 0.5, 3.0, (), jnp.float32),
        "w_up": bell_draw(seeds[12], (D, FF), D ** -0.5, 0.125, ((0, 8),)),
        "b_up": bell_draw(seeds[13], (FF,), 0.5, 3.0, (), jnp.float32),
        "w_down": bell_draw(seeds[14], (FF, D), FF ** -0.5, 0.0625, ((0, 8),)),
        "b_down": bell_draw(seeds[15], (D,), 0.5, 3.0, (), jnp.float32),
    }


EPSILON = 1e-05

@jax.custom_vjp
def low(v):
    return lax.optimization_barrier(v.astype(jnp.bfloat16)).astype(jnp.float32)

@jax.custom_vjp
def low_back(v):
    return v

def low_keep(v):
    return (low(v), None)

def low_pass(kept, grad):
    return (grad,)

def back_keep(v):
    return (v, None)

def back_low(kept, grad):
    return (low(grad),)
low.defvjp(low_keep, low_pass)
low_back.defvjp(back_keep, back_low)

def matmul(left, right):
    return jnp.dot(left, right, precision=lax.Precision.HIGHEST)

def layer_norm(vector, gain_vec, shift_vec):
    mean_val = lax.optimization_barrier(jnp.mean(vector, axis=-1, keepdims=True))
    centered = vector - mean_val
    variance = lax.optimization_barrier(jnp.mean(centered * centered, axis=-1, keepdims=True))
    return centered * lax.rsqrt(variance + EPSILON) * gain_vec + shift_vec

def rotary_tables(positions):
    half_rot = ROT // 2
    freq_index = jnp.arange(half_rot, dtype=jnp.float32)
    inverse_freq = jnp.exp(freq_index * (-2.0 * math.log(10000.0) / ROT))
    angles = positions[:, None] * inverse_freq[None, :]
    return (jnp.cos(angles), jnp.sin(angles))

def rotate(heads_in, cosine_table, sine_table):
    half_rot = ROT // 2
    first_half = heads_in[..., :half_rot]
    second_half = heads_in[..., half_rot:ROT]
    cos_wide = cosine_table[:, None, :]
    sin_wide = sine_table[:, None, :]
    return jnp.concatenate([first_half * cos_wide - second_half * sin_wide, second_half * cos_wide + first_half * sin_wide, heads_in[..., ROT:]], axis=-1)

def stream_positions(lengths, seq_perm):
    seq_range = jnp.arange(lengths.shape[0], dtype=jnp.int32)
    ranking = lax.optimization_barrier(jnp.sum(jnp.where(seq_perm[:, None] == seq_range[None, :], seq_range[:, None], 0), axis=0))
    offsets = lax.optimization_barrier(jnp.sum(jnp.where(ranking[None, :] < ranking[:, None], lengths[None, :], 0), axis=1))
    token_range = jnp.arange(TOKENS, dtype=jnp.int32)
    member = (token_range[:, None] >= offsets[None, :]) & (token_range[:, None] < (offsets + lengths)[None, :])
    seq_ids = lax.optimization_barrier(jnp.sum(jnp.where(member, seq_range[None, :], 0), axis=1)).astype(jnp.int32)
    positions = (token_range - lax.optimization_barrier(jnp.sum(jnp.where(member, offsets[None, :], 0), axis=1))).astype(jnp.int32)
    return (seq_ids, positions)

def attention(queries, key_heads, value_heads, seq_ids, positions):
    window = CAP
    block_rows = math.gcd(TOKENS, 512)
    pad_heads = jnp.zeros((window, HEADS, HEAD), queries.dtype)
    padded_keys = jnp.concatenate([pad_heads, key_heads], axis=0)
    padded_values = jnp.concatenate([pad_heads, value_heads], axis=0)
    padded_ids = jnp.concatenate([jnp.full((window,), -1, jnp.int32), seq_ids], axis=0)
    padded_pos = jnp.concatenate([jnp.zeros((window,), jnp.int32), positions], axis=0)
    score_scale = HEAD ** (-0.5)

    def one_block(block_index):
        row_start = (block_index * block_rows).astype(jnp.int32)
        query_blk = lax.dynamic_slice_in_dim(queries, row_start, block_rows, 0)
        key_blk = lax.dynamic_slice_in_dim(padded_keys, row_start, block_rows + window, 0)
        value_blk = lax.dynamic_slice_in_dim(padded_values, row_start, block_rows + window, 0)
        query_ids = lax.dynamic_slice_in_dim(seq_ids, row_start, block_rows, 0)
        key_ids = lax.dynamic_slice_in_dim(padded_ids, row_start, block_rows + window, 0)
        query_pos = lax.dynamic_slice_in_dim(positions, row_start, block_rows, 0)
        key_pos = lax.dynamic_slice_in_dim(padded_pos, row_start, block_rows + window, 0)
        scores = low_back(jnp.einsum('qhe,khe->hqk', query_blk, key_blk, precision=lax.Precision.HIGHEST) * score_scale)
        allowed = (query_ids[:, None] == key_ids[None, :]) & (key_pos[None, :] <= query_pos[:, None])
        scores = jnp.where(allowed[None], scores, -1e+30)
        attn_probs = low(jax.nn.softmax(scores, axis=-1))
        return jnp.einsum('hqk,khe->qhe', attn_probs, value_blk, precision=lax.Precision.HIGHEST)
    blocks_out = lax.map(jax.checkpoint(one_block), jnp.arange(TOKENS // block_rows, dtype=jnp.int32))
    return blocks_out.reshape(TOKENS, HEADS * HEAD)

def layer_forward(stream, params, seq_ids, positions):
    ln1_gain, ln1_bias, ln2_gain, ln2_bias, w_qkv, b_qkv, w_dense, b_dense, w_up, b_up, w_down, b_down = params
    normed_one = low(layer_norm(stream, ln1_gain, ln1_bias))
    normed_two = low(layer_norm(stream, ln2_gain, ln2_bias))
    qkv = low(low_back(matmul(normed_one, w_qkv) + b_qkv))
    query_heads = qkv[:, :D].reshape(TOKENS, HEADS, HEAD)
    key_heads = qkv[:, D:2 * D].reshape(TOKENS, HEADS, HEAD)
    value_heads = qkv[:, 2 * D:].reshape(TOKENS, HEADS, HEAD)
    cosine_table, sine_table = rotary_tables(positions.astype(jnp.float32))
    rotated_queries = low(rotate(query_heads, cosine_table, sine_table))
    rotated_keys = low(rotate(key_heads, cosine_table, sine_table))
    attended = low(low_back(attention(rotated_queries, rotated_keys, value_heads, seq_ids, positions)))
    pre_up = low_back(matmul(normed_two, w_up) + b_up)
    activated = low(jax.nn.gelu(pre_up, approximate=False))
    return stream + (matmul(attended, w_dense) + b_dense) + (matmul(activated, w_down) + b_down)

def reference(tokens, cotangent, seq_lengths, seq_order, ln1_gain, ln1_bias, ln2_gain, ln2_bias, w_qkv, b_qkv, w_dense, b_dense, w_up, b_up, w_down, b_down):
    params = tuple((param.astype(jnp.float32) for param in (ln1_gain, ln1_bias, ln2_gain, ln2_bias, w_qkv, b_qkv, w_dense, b_dense, w_up, b_up, w_down, b_down)))
    streams = tokens.astype(jnp.float32).reshape(N_REP, TOKENS, D)
    grad_streams = cotangent.astype(jnp.float32).reshape(N_REP, TOKENS, D)
    zero_grads = tuple((jnp.zeros_like(param) for param in params))

    def per_group(carried, group_items):
        stream, grad_stream, lengths, seq_perm = group_items
        seq_ids, positions = stream_positions(lengths, seq_perm)

        def forward(values_in, weights_in):
            return layer_forward(values_in, weights_in, seq_ids, positions)
        result, pull_back = jax.vjp(forward, stream, params)
        grad_input, grad_params = pull_back(grad_stream)
        summed = tuple((running + extra for running, extra in zip(carried, grad_params)))
        return (summed, (result.astype(jnp.bfloat16), grad_input))
    totals, (outputs, input_grads) = lax.scan(per_group, zero_grads, (streams, grad_streams, seq_lengths, seq_order))
    return (outputs.reshape(ROWS, N_SHARD, D), input_grads.reshape(ROWS, N_SHARD, D), totals[0], totals[1], totals[2], totals[3], totals[4], totals[5], totals[6], totals[7], totals[8], totals[9], totals[10], totals[11])
```

```python
import functools
import math

import jax
import jax.numpy as jnp
from jax import lax
from jax.experimental import pallas as pl
from jax.experimental.pallas import tpu as pltpu
from jax.sharding import PartitionSpec as P

HEADS = 8
HEAD = 256
ROT = 64


EPSILON = 1e-05
MASKED = -1e30


def layer_norm(vector, gain_vec, shift_vec):
    mean_val = jnp.mean(vector, axis=-1, keepdims=True)
    centered = vector - mean_val
    variance = jnp.mean(centered * centered, axis=-1, keepdims=True)
    return centered * lax.rsqrt(variance + EPSILON) * gain_vec + shift_vec


def gelu_exact(vector):
    return jax.nn.gelu(vector, approximate=False)


def rotary_tables(positions):
    half_rot = ROT // 2
    freq_index = jnp.arange(half_rot, dtype=jnp.float32)
    inverse_freq = jnp.exp(freq_index * (-2.0 * math.log(10000.0) / ROT))
    angles = positions[:, None] * inverse_freq[None, :]
    return (jnp.cos(angles), jnp.sin(angles))


def rotate(heads_in, cosine_table, sine_table):
    half_rot = ROT // 2
    first_half = heads_in[..., :half_rot]
    second_half = heads_in[..., half_rot:ROT]
    cos_wide = cosine_table[:, None, :]
    sin_wide = sine_table[:, None, :]
    return jnp.concatenate(
        [
            first_half * cos_wide - second_half * sin_wide,
            second_half * cos_wide + first_half * sin_wide,
            heads_in[..., ROT:],
        ],
        axis=-1,
    )


def stream_rows(lengths, seq_perm, shard_count):
    seq_range = jnp.arange(lengths.shape[0], dtype=jnp.int32)
    ranking = jnp.sum(
        jnp.where(seq_perm[:, None] == seq_range[None, :], seq_range[:, None], 0), axis=0
    )
    offsets = jnp.sum(jnp.where(ranking[None, :] < ranking[:, None], lengths[None, :], 0), axis=1)
    return (offsets // shard_count, lengths // shard_count)


def row_product(left, right):
    return jnp.dot(left.T, right, preferred_element_type=jnp.float32)


def block_mask(seq_flag, positions, live):
    return (
        live[:, None]
        & live[None, :]
        & (seq_flag[:, None] == seq_flag[None, :])
        & (positions[None, :] <= positions[:, None])
    )


def shards(
    tokens,
    cotangent,
    seq_lengths,
    seq_order,
    ln1_gain,
    ln1_bias,
    ln2_gain,
    ln2_bias,
    w_qkv,
    b_qkv,
    w_dense,
    b_dense,
    w_up,
    b_up,
    w_down,
    b_down,
):
    shard_count = lax.axis_size("shard")
    my_index = lax.axis_index("shard")
    inputs = tokens[:, 0, :].astype(jnp.float32)
    grad_out = cotangent[:, 0, :]
    local_rows, width = inputs.shape
    slot_rows = 2 * (local_rows // shard_count) - 4
    buffer_rows = slot_rows * shard_count
    row_offsets, row_counts = stream_rows(seq_lengths[0], seq_order[0], shard_count)
    first_count = row_counts[0::2]
    second_count = row_counts[1::2]
    first_start = row_offsets[0::2]
    second_start = row_offsets[1::2]
    slot_range = jnp.arange(slot_rows, dtype=jnp.int32)[None, :]
    in_first = slot_range < first_count[:, None]
    slot_live = slot_range < (first_count + second_count)[:, None]
    source_rows = jnp.where(
        in_first,
        first_start[:, None] + slot_range,
        second_start[:, None] + slot_range - first_count[:, None],
    )
    source_rows = jnp.where(slot_live, source_rows, 0)
    seq_range = jnp.arange(row_counts.shape[0], dtype=jnp.int32)
    parity = seq_range % 2
    slot_base = seq_range // 2 * slot_rows + parity * row_counts[seq_range - parity] - row_offsets
    token_range = jnp.arange(local_rows, dtype=jnp.int32)[:, None]
    member = (token_range >= row_offsets[None, :]) & (
        token_range < (row_offsets + row_counts)[None, :]
    )
    return_rows = token_range[:, 0] + jnp.sum(jnp.where(member, slot_base[None, :], 0), axis=1)
    own_first = first_count[my_index]
    own_second = second_count[my_index]
    buffer_range = jnp.arange(buffer_rows, dtype=jnp.int32)
    slot_index = buffer_range % slot_rows
    source_index = buffer_range // slot_rows
    seq_flag = (slot_index >= own_first).astype(jnp.int32)
    positions = (slot_index - seq_flag * own_first) * shard_count + source_index
    live = slot_index < own_first + own_second
    attn_full, dense_full = (
        lax.all_gather(w_qkv, "shard", axis=0, tiled=True),
        lax.all_gather(w_dense, "shard", axis=0, tiled=True),
    )
    up_full, down_full = (
        lax.all_gather(w_up, "shard", axis=0, tiled=True),
        lax.all_gather(w_down, "shard", axis=0, tiled=True),
    )
    normed_one_wide, pull_one = jax.vjp(layer_norm, inputs, ln1_gain, ln1_bias)
    normed_two_wide, pull_two = jax.vjp(layer_norm, inputs, ln2_gain, ln2_bias)
    normed_one = normed_one_wide.astype(jnp.bfloat16)
    normed_two = normed_two_wide.astype(jnp.bfloat16)
    qkv = (jnp.dot(normed_one, attn_full, preferred_element_type=jnp.float32) + b_qkv).astype(
        jnp.bfloat16
    )
    arrived = lax.all_to_all(
        jnp.take(qkv, source_rows, axis=0), "shard", split_axis=0, concat_axis=0, tiled=True
    )
    arrived = arrived.reshape(buffer_rows, 3 * width)
    heads_shape = (buffer_rows, HEADS, HEAD)
    cosine_table, sine_table = rotary_tables(positions.astype(jnp.float32))

    def rotate_here(heads_in):
        return rotate(heads_in, cosine_table, sine_table)

    query_wide, pull_query = jax.vjp(
        rotate_here, arrived[:, :width].astype(jnp.float32).reshape(heads_shape)
    )
    key_wide, pull_key = jax.vjp(
        rotate_here, arrived[:, width : 2 * width].astype(jnp.float32).reshape(heads_shape)
    )
    rotated_queries = query_wide.astype(jnp.bfloat16)
    rotated_keys = key_wide.astype(jnp.bfloat16)
    value_heads = arrived[:, 2 * width :].reshape(heads_shape)
    sources_per = shard_count
    while sources_per > 1 and sources_per * slot_rows > 1024:
        sources_per = sources_per // 2
    block_rows = sources_per * slot_rows
    block_total = buffer_rows // block_rows
    score_scale = HEAD ** (-0.5)

    def forward_block(block_index):
        allowed = block_mask(seq_flag, positions, live)
        scores = (
            jnp.einsum(
                "qhe,khe->hqk", rotated_queries, rotated_keys, preferred_element_type=jnp.float32
            )
            * score_scale
        )
        scores = jnp.where(allowed[None], scores, MASKED)
        row_max = jnp.max(scores, axis=-1, keepdims=True)
        exp_scores = jnp.exp(scores - row_max)
        exp_total = jnp.sum(exp_scores, axis=-1, keepdims=True)
        attn_probs = jnp.where(allowed[None], exp_scores / exp_total, 0.0)
        attended_blk = jnp.einsum(
            "hqk,khe->qhe",
            attn_probs.astype(jnp.bfloat16),
            value_heads,
            preferred_element_type=jnp.float32,
        )
        return (attended_blk.astype(jnp.bfloat16), row_max[..., 0] + jnp.log(exp_total[..., 0]))

    attended_blocks, log_totals = lax.map(forward_block, jnp.arange(block_total, dtype=jnp.int32))
    attended_slots = attended_blocks.reshape(shard_count, slot_rows, width)
    attn_back = lax.all_to_all(
        attended_slots, "shard", split_axis=0, concat_axis=0, tiled=True
    ).reshape(buffer_rows, width)
    attn_in = jnp.take(attn_back, return_rows, axis=0)
    attn_out = jnp.dot(attn_in, dense_full, preferred_element_type=jnp.float32) + b_dense
    pre_up = jnp.dot(normed_two, up_full, preferred_element_type=jnp.float32) + b_up
    activated_wide, pull_gelu = jax.vjp(gelu_exact, pre_up)
    activated = activated_wide.astype(jnp.bfloat16)
    mlp_out = jnp.dot(activated, down_full, preferred_element_type=jnp.float32) + b_down
    output = (inputs + attn_out + mlp_out).astype(jnp.bfloat16)
    attn_second, dense_second = (
        lax.all_gather(w_qkv, "shard", axis=0, tiled=True),
        lax.all_gather(w_dense, "shard", axis=0, tiled=True),
    )
    up_second, down_second = (
        lax.all_gather(w_up, "shard", axis=0, tiled=True),
        lax.all_gather(w_down, "shard", axis=0, tiled=True),
    )
    grad_attended = jnp.dot(grad_out, dense_second.T, preferred_element_type=jnp.float32).astype(
        jnp.bfloat16
    )
    grad_slots = jnp.where(
        slot_live[:, :, None],
        jnp.take(grad_attended, source_rows, axis=0),
        jnp.zeros((), jnp.bfloat16),
    )
    grad_heads = lax.all_to_all(
        grad_slots, "shard", split_axis=0, concat_axis=0, tiled=True
    ).reshape(heads_shape)

    def backward_block(carried, block_index):
        grad_keys, grad_values = carried
        allowed = block_mask(seq_flag, positions, live)
        scores = (
            jnp.einsum(
                "qhe,khe->hqk", rotated_queries, rotated_keys, preferred_element_type=jnp.float32
            )
            * score_scale
        )
        attn_probs = jnp.where(
            allowed[None], jnp.exp(scores - log_totals[block_index][..., None]), 0.0
        )
        grad_probs = jnp.einsum(
            "qhe,khe->hqk", grad_heads, value_heads, preferred_element_type=jnp.float32
        )
        row_delta = jnp.sum(attn_probs * grad_probs, axis=-1, keepdims=True)
        grad_scores = (attn_probs * (grad_probs - row_delta)).astype(jnp.bfloat16)
        grad_query = (
            jnp.einsum(
                "hqk,khe->qhe", grad_scores, rotated_keys, preferred_element_type=jnp.float32
            )
            * score_scale
        )
        grad_keys = (
            grad_keys
            + jnp.einsum(
                "hqk,qhe->khe", grad_scores, rotated_queries, preferred_element_type=jnp.float32
            )
            * score_scale
        )
        grad_values = grad_values + jnp.einsum(
            "hqk,qhe->khe",
            attn_probs.astype(jnp.bfloat16),
            grad_heads,
            preferred_element_type=jnp.float32,
        )
        return ((grad_keys, grad_values), grad_query)

    zero_heads = jnp.zeros(heads_shape, jnp.float32)
    (grad_keys, grad_values), grad_query_blocks = lax.scan(
        backward_block, (zero_heads, zero_heads), jnp.arange(block_total, dtype=jnp.int32)
    )
    grad_q_pre = pull_query(grad_query_blocks.reshape(heads_shape))[0]
    grad_k_pre = pull_key(grad_keys)[0]
    grad_qkv_slots = jnp.concatenate(
        [
            grad_q_pre.reshape(buffer_rows, width),
            grad_k_pre.reshape(buffer_rows, width),
            grad_values.reshape(buffer_rows, width),
        ],
        axis=1,
    ).astype(jnp.bfloat16)
    grad_qkv_slots = grad_qkv_slots.reshape(shard_count, slot_rows, 3 * width)
    grad_qkv_back = lax.all_to_all(grad_qkv_slots, "shard", split_axis=0, concat_axis=0, tiled=True)
    grad_qkv = jnp.take(grad_qkv_back.reshape(buffer_rows, 3 * width), return_rows, axis=0)
    grad_activated = jnp.dot(grad_out, down_second.T, preferred_element_type=jnp.float32)
    grad_pre = pull_gelu(grad_activated)[0].astype(jnp.bfloat16)
    grad_normed_one = jnp.dot(grad_qkv, attn_second.T, preferred_element_type=jnp.float32)
    grad_normed_two = jnp.dot(grad_pre, up_second.T, preferred_element_type=jnp.float32)
    grad_in_one, grad_gain_one, grad_bias_one = pull_one(grad_normed_one)
    grad_in_two, grad_gain_two, grad_bias_two = pull_two(grad_normed_two)
    input_grad = grad_out.astype(jnp.float32) + grad_in_one + grad_in_two
    qkv_rows = lax.psum_scatter(
        row_product(normed_one, grad_qkv).astype(jnp.bfloat16),
        "shard",
        scatter_dimension=0,
        tiled=True,
    ).astype(jnp.float32)
    dense_rows = lax.psum_scatter(
        row_product(attn_in, grad_out).astype(jnp.bfloat16),
        "shard",
        scatter_dimension=0,
        tiled=True,
    ).astype(jnp.float32)
    up_rows = lax.psum_scatter(
        row_product(normed_two, grad_pre).astype(jnp.bfloat16),
        "shard",
        scatter_dimension=0,
        tiled=True,
    ).astype(jnp.float32)
    down_rows = lax.psum_scatter(
        row_product(activated, grad_out).astype(jnp.bfloat16),
        "shard",
        scatter_dimension=0,
        tiled=True,
    ).astype(jnp.float32)
    qkv_rows, dense_rows, up_rows, down_rows = (
        lax.psum(qkv_rows.astype(jnp.bfloat16), "rep").astype(jnp.float32),
        lax.psum(dense_rows.astype(jnp.bfloat16), "rep").astype(jnp.float32),
        lax.psum(up_rows.astype(jnp.bfloat16), "rep").astype(jnp.float32),
        lax.psum(down_rows.astype(jnp.bfloat16), "rep").astype(jnp.float32),
    )
    out_column_sum = jnp.sum(grad_out, axis=0, dtype=jnp.float32)
    small_totals = lax.psum(
        (
            grad_gain_one,
            grad_bias_one,
            grad_gain_two,
            grad_bias_two,
            jnp.sum(grad_qkv, axis=0, dtype=jnp.float32),
            out_column_sum,
            jnp.sum(grad_pre, axis=0, dtype=jnp.float32),
        ),
        ("rep", "shard"),
    )
    return (
        output[:, None, :],
        input_grad[:, None, :],
        small_totals[0],
        small_totals[1],
        small_totals[2],
        small_totals[3],
        qkv_rows,
        small_totals[4],
        dense_rows,
        small_totals[5],
        up_rows,
        small_totals[6],
        down_rows,
        small_totals[5],
    )


TILE_ROWS = 32
F32 = jnp.float32
BF16 = jnp.bfloat16


def flip(value, axis, bit):
    size = lax.axis_size(axis)
    return lax.ppermute(value, axis, [(i, i ^ bit) for i in range(size)])


def send(value, pairs):
    return lax.ppermute(value, "shard", [(2 * a + y, 2 * b + y) for a, b in pairs for y in (0, 1)])


MIDDLE = ((1, 2), (2, 1))
OUTWARD = ((1, 0), (2, 3))
INWARD = ((0, 1), (3, 2))


def plus(*terms):
    total = terms[0].astype(F32)
    for term in terms[1:]:
        total = total + term.astype(F32)
    return total


def gather_blocks(own, is_middle):
    near = flip(own, "shard", 2)
    across = send(own, MIDDLE)
    across_near = send(near, MIDDLE)
    two = jnp.where(is_middle, across_near, send(across, OUTWARD))
    three = jnp.where(is_middle, across, send(across_near, OUTWARD))
    mine = [own, near, two, three]
    return mine + [flip(block, "shard", 1) for block in mine]


def scatter_sum(blocks):
    three = plus(blocks[3], flip(blocks[7], "shard", 1)).astype(BF16)
    from_corner = send(three, INWARD)
    two = plus(blocks[2], flip(blocks[6], "shard", 1), from_corner).astype(BF16)
    across_near = send(two, MIDDLE)
    across = send(two, INWARD)
    one = plus(blocks[1], flip(blocks[5], "shard", 1), across_near).astype(BF16)
    three = plus(three, across).astype(BF16)
    return plus(
        blocks[0], flip(blocks[4], "shard", 1), flip(one, "shard", 2), send(three, MIDDLE)
    )


def turn(heads_in, cosine, sine):
    left = heads_in[:, :128]
    lane = lax.broadcasted_iota(jnp.int32, left.shape, 1)
    half = ROT // 2
    partner = jnp.where(lane < half, pltpu.roll(left, 128 - half, 1), pltpu.roll(left, half, 1))
    return jnp.concatenate([left * cosine + partner * sine, heads_in[:, 128:]], axis=1)


def token_labels(my_index, shape, dim):
    inner = lax.broadcasted_iota(jnp.int32, shape, dim)
    block = inner // TILE_ROWS
    apart = (block % 4) * 2 + block // 4
    return (inner % TILE_ROWS) * HEADS + jnp.bitwise_xor(apart, my_index)


def tile_weights(tile, seq_ref, query, key_tiles, count):
    tile_tokens = TILE_ROWS * HEADS
    my_index = seq_ref[count]
    query_label = token_labels(my_index, (tile_tokens, 1), 0) + tile * tile_tokens
    key_label = token_labels(my_index, (1, tile_tokens), 1)
    scores = []
    for place, key in key_tiles:
        label = key_label + place * tile_tokens
        last = jnp.full(label.shape, 1 << 30, jnp.int32)
        for k in range(count):
            last = jnp.minimum(last, jnp.where(label < seq_ref[k], seq_ref[k], 1 << 30))
        allowed = query_label < last
        if place == tile:
            allowed = allowed & (label <= query_label)
        product = lax.dot_general(query, key, (((1,), (1,)), ((), ())), preferred_element_type=F32)
        scores.append(jnp.where(allowed, product * HEAD ** (-0.5), MASKED))
    scores = jnp.concatenate(scores, axis=1)
    exp_scores = jnp.exp(scores - jnp.max(scores, axis=1, keepdims=True))
    return exp_scores * (1.0 / jnp.sum(exp_scores, axis=1, keepdims=True))


def attend_kernel(seq_ref, qkv_ref, cos_ref, sin_ref, out_ref, query_ref, key_ref):
    tiles = query_ref.shape[0]
    tile_tokens = TILE_ROWS * HEADS

    def part(tile, lane):
        rows = qkv_ref[:, tile * TILE_ROWS : (tile + 1) * TILE_ROWS, lane : lane + HEAD]
        return rows.reshape(tile_tokens, HEAD)

    for tile in range(tiles):
        cosine, sine = cos_ref[tile], sin_ref[tile]
        query = turn(part(tile, 0).astype(F32), cosine, sine).astype(BF16)
        query_ref[tile] = query
        key_ref[tile] = turn(part(tile, HEAD).astype(F32), cosine, sine).astype(BF16)
        near = list(range(max(tile - 2, 0), tile + 1))
        probs = tile_weights(
            tile, seq_ref, query, [(k, key_ref[k]) for k in near], seq_ref.shape[0] - 1
        ).astype(BF16)
        total = jnp.zeros((tile_tokens, HEAD), F32)
        for at, k in enumerate(near):
            total = total + jnp.dot(
                probs[:, at * tile_tokens : (at + 1) * tile_tokens],
                part(k, 2 * HEAD),
                preferred_element_type=F32,
            )
        out_ref[:, tile * TILE_ROWS : (tile + 1) * TILE_ROWS, :] = total.astype(BF16).reshape(
            HEADS, TILE_ROWS, HEAD
        )


def attend_back_kernel(
    seq_ref, qkv_ref, grad_ref, cos_ref, sin_ref, query_ref, key_ref, out_ref, sum_ref, gk_ref, gv_ref
):
    tiles = query_ref.shape[0]
    tile_tokens = TILE_ROWS * HEADS
    scale = HEAD ** (-0.5)
    over_rows = (((0,), (0,)), ((), ()))
    over_lanes = (((1,), (1,)), ((), ()))

    def rows_of(tile):
        return slice(tile * TILE_ROWS, (tile + 1) * TILE_ROWS)

    def put(tile, lane, value):
        low = value.astype(BF16)
        out_ref[:, rows_of(tile), lane : lane + HEAD] = low.reshape(HEADS, TILE_ROWS, HEAD)
        columns = jnp.sum(low.astype(F32), axis=0, keepdims=True)
        if tile == 0:
            sum_ref[:, lane : lane + HEAD] = columns
        else:
            sum_ref[:, lane : lane + HEAD] += columns

    def finish(tile):
        put(tile, HEAD, turn(gk_ref[tile] * scale, cos_ref[tile], -sin_ref[tile]))
        put(tile, 2 * HEAD, gv_ref[tile])

    for tile in range(tiles):
        query = query_ref[tile]
        near = list(range(max(tile - 2, 0), tile + 1))
        grad = grad_ref[:, rows_of(tile), :].reshape(tile_tokens, HEAD)
        probs = tile_weights(
            tile, seq_ref, query, [(k, key_ref[k]) for k in near], seq_ref.shape[0] - 1
        )
        grad_probs = jnp.concatenate(
            [
                lax.dot_general(
                    grad,
                    qkv_ref[:, rows_of(k), 2 * HEAD :].reshape(tile_tokens, HEAD),
                    over_lanes,
                    preferred_element_type=F32,
                )
                for k in near
            ],
            axis=1,
        )
        delta = jnp.sum(probs * grad_probs, axis=1, keepdims=True)
        grad_scores = (probs * (grad_probs - delta)).astype(BF16)
        probs = probs.astype(BF16)
        grad_query = jnp.zeros((tile_tokens, HEAD), F32)
        for at, k in enumerate(near):
            span = slice(at * tile_tokens, (at + 1) * tile_tokens)
            grad_query = grad_query + jnp.dot(
                grad_scores[:, span], key_ref[k], preferred_element_type=F32
            )
            to_key = lax.dot_general(
                grad_scores[:, span], query, over_rows, preferred_element_type=F32
            )
            to_value = lax.dot_general(probs[:, span], grad, over_rows, preferred_element_type=F32)
            if k == tile:
                gk_ref[k] = to_key
                gv_ref[k] = to_value
            else:
                gk_ref[k] += to_key
                gv_ref[k] += to_value
        put(tile, 0, turn(grad_query * scale, cos_ref[tile], -sin_ref[tile]))
        if tile >= 2:
            finish(tile - 2)
    for tile in range(max(tiles - 2, 0), tiles):
        finish(tile)


VMEM_SPEC = pl.BlockSpec(memory_space=pltpu.VMEM)
SMEM_SPEC = pl.BlockSpec(memory_space=pltpu.SMEM)


def attend(seq_scalars, qkv, cosine, sine):
    blocks, rows, _ = qkv.shape
    tiled = (rows // TILE_ROWS, blocks * TILE_ROWS, HEAD)
    return pl.pallas_call(
        attend_kernel,
        out_shape=(
            jax.ShapeDtypeStruct((blocks, rows, HEAD), BF16),
            jax.ShapeDtypeStruct(tiled, BF16),
            jax.ShapeDtypeStruct(tiled, BF16),
        ),
        in_specs=[SMEM_SPEC, VMEM_SPEC, VMEM_SPEC, VMEM_SPEC],
        out_specs=(VMEM_SPEC, VMEM_SPEC, VMEM_SPEC),
        compiler_params=pltpu.CompilerParams(vmem_limit_bytes=48 << 20),
        cost_estimate=pl.CostEstimate(
            flops=4 * blocks * rows * 768 * HEAD, bytes_accessed=10 << 20, transcendentals=0
        ),
    )(seq_scalars, qkv, cosine, sine)


def attend_back(seq_scalars, qkv, grad, cosine, sine, query, key):
    blocks, rows, wide = qkv.shape
    return pl.pallas_call(
        attend_back_kernel,
        out_shape=(
            jax.ShapeDtypeStruct((blocks, rows, wide), BF16),
            jax.ShapeDtypeStruct((1, wide), F32),
        ),
        in_specs=[SMEM_SPEC] + [VMEM_SPEC] * 6,
        out_specs=(VMEM_SPEC, VMEM_SPEC),
        scratch_shapes=[pltpu.VMEM(query.shape, F32), pltpu.VMEM(query.shape, F32)],
        compiler_params=pltpu.CompilerParams(vmem_limit_bytes=48 << 20),
        cost_estimate=pl.CostEstimate(
            flops=10 * blocks * rows * 768 * HEAD, bytes_accessed=12 << 20, transcendentals=0
        ),
    )(seq_scalars, qkv, grad, cosine, sine, query, key)


def place_weights_kernel(order_ref, part_ref, gain_ref, shift_ref, raw_ref, scaled_ref, sum_ref, *, hidden):
    raw = part_ref[0]
    raw_ref[...] = raw
    weight = raw.astype(F32)
    lane = lax.broadcasted_iota(jnp.int32, weight.shape, 1)
    gain = jnp.where(lane < hidden, gain_ref[:, 1:2], gain_ref[:, 0:1])
    shift = jnp.where(lane < hidden, shift_ref[:, 1:2], shift_ref[:, 0:1])
    scaled_ref[...] = (weight * gain).astype(BF16)
    share = jnp.sum(weight * shift, axis=0, keepdims=True)

    @pl.when(pl.program_id(0) == 0)
    def _():
        sum_ref[...] = share

    @pl.when(pl.program_id(0) > 0)
    def _():
        sum_ref[...] += share


def place_weights(order, parts, gains, shifts, hidden):
    count, rows, wide = parts.shape
    whole = jax.ShapeDtypeStruct((count * rows, wide), BF16)
    by_row = pl.BlockSpec((rows, wide), lambda i, order_ref: (i, 0))
    pair = pl.BlockSpec((rows, 2), lambda i, order_ref: (i, 0))
    return pl.pallas_call(
        functools.partial(place_weights_kernel, hidden=hidden),
        out_shape=(whole, whole, jax.ShapeDtypeStruct((1, wide), F32)),
        grid_spec=pltpu.PrefetchScalarGridSpec(
            num_scalar_prefetch=1,
            grid=(count,),
            in_specs=[
                pl.BlockSpec((1, rows, wide), lambda i, order_ref: (order_ref[i], 0, 0)),
                pair,
                pair,
            ],
            out_specs=(by_row, by_row, pl.BlockSpec((1, wide), lambda i, order_ref: (0, 0))),
        ),
        cost_estimate=pl.CostEstimate(
            flops=4 * count * rows * wide, bytes_accessed=6 * count * rows * wide, transcendentals=0
        ),
    )(order, parts, gains, shifts)


def place_grads_kernel(order_ref, part_ref, up_ref, qkv_ref, *, hidden):
    values = part_ref[0].astype(F32)
    up_ref[...] = values[:, :hidden]
    third = qkv_ref.shape[1] // 3
    for k in range(3):
        start = pl.multiple_of(k * third + pl.program_id(1) * HEAD, HEAD)
        qkv_ref[:, pl.ds(start, HEAD)] = values[:, hidden + k * HEAD : hidden + (k + 1) * HEAD]


def place_grads(order, parts, hidden):
    count, rows, wide = parts.shape
    depth = count // HEADS * rows
    return pl.pallas_call(
        functools.partial(place_grads_kernel, hidden=hidden),
        out_shape=(
            jax.ShapeDtypeStruct((depth, HEADS * hidden), F32),
            jax.ShapeDtypeStruct((depth, 3 * HEADS * HEAD), F32),
        ),
        grid_spec=pltpu.PrefetchScalarGridSpec(
            num_scalar_prefetch=1,
            grid=(count // HEADS, HEADS),
            in_specs=[
                pl.BlockSpec(
                    (1, rows, wide), lambda q, s, order_ref: (order_ref[s * 4 + q], 0, 0)
                )
            ],
            out_specs=(
                pl.BlockSpec((rows, hidden), lambda q, s, order_ref: (q, s)),
                pl.BlockSpec((rows, 3 * HEADS * HEAD), lambda q, s, order_ref: (q, 0)),
            ),
        ),
        cost_estimate=pl.CostEstimate(
            flops=0, bytes_accessed=6 * count * rows * wide, transcendentals=0
        ),
    )(order, parts)


def dot32(left, right, left_dim=1, right_dim=0):
    return lax.dot_general(
        left, right, (((left_dim,), (right_dim,)), ((), ())), preferred_element_type=F32
    )


def split_shards(
    tokens,
    cotangent,
    seq_lengths,
    seq_order,
    ln1_gain,
    ln1_bias,
    ln2_gain,
    ln2_bias,
    w_qkv,
    b_qkv,
    w_dense,
    b_dense,
    w_up,
    b_up,
    w_down,
    b_down,
):
    me = lax.axis_index("shard")
    rep = lax.axis_index("rep")
    place = me // 2
    is_middle = (place == 1) | (place == 2)
    own = tokens[:, 0, :]
    own_grad = cotangent[:, 0, :]
    rows, width = own.shape
    group_tokens = rows * HEADS
    depth = w_up.shape[0]
    hidden = w_down.shape[0]
    wide = hidden + 3 * HEAD
    quarter = depth // 4

    up_rows = lax.dynamic_slice_in_dim(w_up, rep * quarter, quarter, 0)
    qkv_rows = lax.dynamic_slice_in_dim(w_qkv, rep * quarter, quarter, 0)

    def columns_for(target):
        pieces = [lax.dynamic_slice_in_dim(up_rows, target * hidden, hidden, 1)]
        for k in range(3):
            pieces.append(
                lax.dynamic_slice_in_dim(qkv_rows, k * width + target * HEAD, HEAD, 1)
            )
        return jnp.concatenate(pieces, axis=1)

    keep = [columns_for(me ^ (2 * z)) for z in range(4)]
    moved = flip(jnp.stack([columns_for(me ^ (2 * z + 1)) for z in range(4)]), "shard", 1)
    pairs = [jnp.stack([keep[z], moved[z]]) for z in range(4)]
    for z in range(1, 4):
        pairs[z] = flip(pairs[z], "shard", 2 * z)
    part = jnp.stack(pairs)
    part = jnp.stack([part, flip(part, "rep", 2)])
    part = jnp.stack([part, flip(part, "rep", 1)], axis=1)
    from_shard = jnp.arange(HEADS, dtype=jnp.int32)[:, None] ^ me
    from_rep = jnp.arange(4, dtype=jnp.int32)[None, :] ^ rep
    order = (from_rep * HEADS + from_shard).reshape(-1)
    gains = jnp.stack([ln1_gain, ln2_gain], axis=1)
    shifts = jnp.stack([ln1_bias, ln2_bias], axis=1)
    w_in, w_scaled, shifted = place_weights(
        order, part.reshape(4 * HEADS, quarter, wide), gains, shifts, hidden
    )
    is_hidden = jnp.arange(wide, dtype=jnp.int32)[None, :] < hidden
    gain = jnp.where(is_hidden, ln2_gain[:, None], ln1_gain[:, None])
    shift = jnp.where(is_hidden, ln2_bias[:, None], ln1_bias[:, None])
    b_in = jnp.concatenate(
        [lax.dynamic_slice_in_dim(b_up, me * hidden, hidden, 0)]
        + [lax.dynamic_slice_in_dim(b_qkv, k * width + me * HEAD, HEAD, 0) for k in range(3)]
    )
    b_in = b_in + shifted[0]
    w_out = jnp.concatenate([w_down, w_dense], axis=0)

    row_offsets, row_counts = stream_rows(seq_lengths[0], seq_order[0], HEADS)
    ends = (row_offsets + row_counts) * HEADS
    seq_scalars = jnp.concatenate([ends, me[None]]).astype(jnp.int32)
    row_range = jnp.arange(rows, dtype=jnp.int32)
    member = (row_range[:, None] >= row_offsets[None, :]) & (
        row_range[:, None] < (row_offsets + row_counts)[None, :]
    )
    in_seq = row_range - jnp.sum(jnp.where(member, row_offsets[None, :], 0), axis=1)
    block_range = jnp.arange(HEADS, dtype=jnp.int32)
    apart = (block_range % 4) * 2 + block_range // 4
    positions = (
        in_seq.reshape(rows // TILE_ROWS, 1, TILE_ROWS) * HEADS + (apart ^ me)[None, :, None]
    )
    cosine, sine = rotary_tables(positions.reshape(-1).astype(F32))
    rest = 128 - ROT
    cosine = jnp.concatenate([cosine, cosine, jnp.ones((group_tokens, rest), F32)], axis=1)
    sine = jnp.concatenate([-sine, sine, jnp.zeros((group_tokens, rest), F32)], axis=1)
    tiled = (rows // TILE_ROWS, TILE_ROWS * HEADS, 128)
    cosine = cosine.reshape(tiled)
    sine = sine.reshape(tiled)

    stream = jnp.concatenate(gather_blocks(own, is_middle), axis=0)
    grad_out = jnp.concatenate(gather_blocks(own_grad, is_middle), axis=0)

    def normalize(values):
        values = values.astype(F32)
        centered = values - jnp.mean(values, axis=-1, keepdims=True)
        rstd = lax.rsqrt(jnp.mean(centered * centered, axis=-1, keepdims=True) + EPSILON)
        return centered * rstd, rstd

    normed = normalize(stream)[0].astype(BF16)
    qkv = (dot32(normed, w_scaled[:, hidden:]) + b_in[hidden:]).astype(BF16)
    qkv = qkv.reshape(HEADS, rows, 3 * HEAD)
    attended, query, key = attend(seq_scalars, qkv, cosine, sine)
    pre_up = dot32(normed, w_scaled[:, :hidden]) + b_in[:hidden]
    normal = 0.5 * (1.0 + lax.erf(pre_up * (0.5**0.5)))
    slope = normal + pre_up * jnp.exp(-0.5 * pre_up * pre_up) * ((2.0 * math.pi) ** -0.5)
    slope = slope.astype(BF16)
    activated = (pre_up * normal).astype(BF16)
    mixed = jnp.concatenate([activated, attended.reshape(group_tokens, HEAD)], axis=1)
    out_part = dot32(mixed, w_out).astype(BF16).reshape(HEADS, rows, width)
    out_sum = scatter_sum([out_part[k] for k in range(HEADS)])
    output = (own.astype(F32) + out_sum + (b_dense + b_down)).astype(BF16)

    grad_mixed = dot32(grad_out, w_out, 1, 1)
    grad_attended = grad_mixed[:, hidden:].astype(BF16).reshape(HEADS, rows, HEAD)
    grad_pre = (grad_mixed[:, :hidden] * slope.astype(F32)).astype(BF16)
    grad_qkv, qkv_columns = attend_back(
        seq_scalars, qkv, grad_attended, cosine, sine, query, key
    )
    grad_in = jnp.concatenate([grad_pre, grad_qkv.reshape(group_tokens, 3 * HEAD)], axis=1)
    columns = jnp.concatenate([jnp.sum(grad_pre, axis=0, dtype=F32), qkv_columns[0]])

    gy_part = dot32(grad_in, w_scaled, 1, 1).astype(BF16).reshape(HEADS, rows, width)
    gy = scatter_sum([gy_part[k] for k in range(HEADS)])
    own_normed, own_rstd = normalize(own)
    input_grad = own_grad.astype(F32) + own_rstd * (
        gy
        - jnp.mean(gy, axis=-1, keepdims=True)
        - own_normed * jnp.mean(gy * own_normed, axis=-1, keepdims=True)
    )

    out_grads = dot32(mixed, grad_out, 0, 0).astype(BF16)
    half_rows = out_grads.shape[0] // 2
    my_core = rep % 2
    my_side = rep // 2
    halves = out_grads.reshape(2, half_rows, width)
    half = plus(
        lax.dynamic_index_in_dim(halves, my_core, 0, False),
        flip(lax.dynamic_index_in_dim(halves, 1 - my_core, 0, False), "rep", 1),
    ).astype(BF16)
    half = plus(half, flip(half, "rep", 2)).astype(BF16)
    other = flip(half, "rep", 1)
    first = jnp.where(my_core == 0, half, other)
    second = jnp.where(my_core == 0, other, half)
    out_grads = jnp.concatenate([first, second], axis=0).astype(F32)

    moments = dot32(normed, grad_in, 0, 0)
    w_wide = w_in.astype(F32)
    gain_terms = moments * w_wide
    bias_terms = w_wide * columns[None, :]
    in_grads = (moments * gain + shift * columns[None, :]).astype(BF16)
    in_grads = in_grads.reshape(HEADS, 2, 2, quarter, wide)
    summed = plus(
        lax.dynamic_index_in_dim(in_grads, my_core, 2, False),
        flip(lax.dynamic_index_in_dim(in_grads, 1 - my_core, 2, False), "rep", 1),
    ).astype(BF16)
    summed = plus(
        lax.dynamic_index_in_dim(summed, my_side, 1, False),
        flip(lax.dynamic_index_in_dim(summed, 1 - my_side, 1, False), "rep", 2),
    ).astype(BF16)
    summed = summed.reshape(4, 2, quarter, wide)
    my_row = me % 2
    keep_half = lax.dynamic_index_in_dim(summed, my_row, 1, False)
    got_half = flip(lax.dynamic_index_in_dim(summed, 1 - my_row, 1, False), "shard", 1)
    both = jnp.stack([keep_half, got_half], axis=1)
    came = []
    for z in range(4):
        piece = lax.dynamic_index_in_dim(both, place ^ z, 0, False)
        came.append(piece if z == 0 else flip(piece, "shard", 2 * z))
    came = jnp.stack(came)
    came = jnp.stack([came, flip(came, "rep", 2)])
    came = jnp.stack([came, flip(came, "rep", 1)], axis=1)
    up_grad, qkv_grad = place_grads(order, came.reshape(4 * HEADS, quarter, wide), hidden)

    small = jnp.concatenate(
        [
            jnp.sum(gain_terms[:, hidden:], axis=1),
            jnp.sum(bias_terms[:, hidden:], axis=1),
            jnp.sum(gain_terms[:, :hidden], axis=1),
            jnp.sum(bias_terms[:, :hidden], axis=1),
            jnp.sum(own_grad, axis=0, dtype=F32),
            jnp.where(block_range[:, None] == me, columns[None, :], 0.0).reshape(-1),
        ]
    )
    for axis, bit in (("rep", 1), ("shard", 1), ("shard", 2), ("shard", 4), ("rep", 2)):
        small = small + flip(small, axis, bit)
    vectors = small[: 5 * width].reshape(5, width)
    slots = small[5 * width :].reshape(HEADS, wide)
    b_up_grad = slots[:, :hidden].reshape(-1)
    b_qkv_grad = slots[:, hidden:].reshape(HEADS, 3, HEAD).transpose(1, 0, 2).reshape(-1)
    return (
        output[:, None, :],
        input_grad[:, None, :],
        vectors[0],
        vectors[1],
        vectors[2],
        vectors[3],
        qkv_grad,
        b_qkv_grad,
        out_grads[hidden:],
        vectors[4],
        up_grad,
        b_up_grad,
        out_grads[:hidden],
        vectors[4],
    )


def solution(mesh):
    in_specs = (
        P("rep", "shard", None),
        P("rep", "shard", None),
        P("rep", None),
        P("rep", None),
        P(),
        P(),
        P(),
        P(),
        P("shard", None),
        P(),
        P("shard", None),
        P(),
        P("shard", None),
        P(),
        P("shard", None),
        P(),
    )
    out_specs = (
        P("rep", "shard", None),
        P("rep", "shard", None),
        P(),
        P(),
        P(),
        P(),
        P("shard", None),
        P(),
        P("shard", None),
        P(),
        P("shard", None),
        P(),
        P("shard", None),
        P(),
    )
    body = split_shards if mesh.shape["shard"] == HEADS else shards
    return jax.shard_map(
        body, mesh=mesh, in_specs=in_specs, out_specs=out_specs, check_vma=False
    )
```

```python
import functools
import math

import jax
import jax.numpy as jnp
from jax import lax
from jax.experimental import pallas as pl
from jax.experimental.pallas import tpu as pltpu
from jax.sharding import PartitionSpec as P

HEADS = 8
HEAD = 256
ROT = 64


EPSILON = 1e-05
MASKED = -1e30


def layer_norm(vector, gain_vec, shift_vec):
    mean_val = jnp.mean(vector, axis=-1, keepdims=True)
    centered = vector - mean_val
    variance = jnp.mean(centered * centered, axis=-1, keepdims=True)
    return centered * lax.rsqrt(variance + EPSILON) * gain_vec + shift_vec


def gelu_exact(vector):
    return jax.nn.gelu(vector, approximate=False)


def rotary_tables(positions):
    half_rot = ROT // 2
    freq_index = jnp.arange(half_rot, dtype=jnp.float32)
    inverse_freq = jnp.exp(freq_index * (-2.0 * math.log(10000.0) / ROT))
    angles = positions[:, None] * inverse_freq[None, :]
    return (jnp.cos(angles), jnp.sin(angles))


def rotate(heads_in, cosine_table, sine_table):
    half_rot = ROT // 2
    first_half = heads_in[..., :half_rot]
    second_half = heads_in[..., half_rot:ROT]
    cos_wide = cosine_table[:, None, :]
    sin_wide = sine_table[:, None, :]
    return jnp.concatenate(
        [
            first_half * cos_wide - second_half * sin_wide,
            second_half * cos_wide + first_half * sin_wide,
            heads_in[..., ROT:],
        ],
        axis=-1,
    )


def stream_rows(lengths, seq_perm, shard_count):
    seq_range = jnp.arange(lengths.shape[0], dtype=jnp.int32)
    ranking = jnp.sum(
        jnp.where(seq_perm[:, None] == seq_range[None, :], seq_range[:, None], 0), axis=0
    )
    offsets = jnp.sum(jnp.where(ranking[None, :] < ranking[:, None], lengths[None, :], 0), axis=1)
    return (offsets // shard_count, lengths // shard_count)


def row_product(left, right):
    return jnp.dot(left.T, right, preferred_element_type=jnp.float32)


def block_mask(seq_flag, positions, live):
    return (
        live[:, None]
        & live[None, :]
        & (seq_flag[:, None] == seq_flag[None, :])
        & (positions[None, :] <= positions[:, None])
    )


def shards(
    tokens,
    cotangent,
    seq_lengths,
    seq_order,
    ln1_gain,
    ln1_bias,
    ln2_gain,
    ln2_bias,
    w_qkv,
    b_qkv,
    w_dense,
    b_dense,
    w_up,
    b_up,
    w_down,
    b_down,
):
    shard_count = lax.axis_size("shard")
    my_index = lax.axis_index("shard")
    inputs = tokens[:, 0, :].astype(jnp.float32)
    grad_out = cotangent[:, 0, :]
    local_rows, width = inputs.shape
    slot_rows = 2 * (local_rows // shard_count) - 4
    buffer_rows = slot_rows * shard_count
    row_offsets, row_counts = stream_rows(seq_lengths[0], seq_order[0], shard_count)
    first_count = row_counts[0::2]
    second_count = row_counts[1::2]
    first_start = row_offsets[0::2]
    second_start = row_offsets[1::2]
    slot_range = jnp.arange(slot_rows, dtype=jnp.int32)[None, :]
    in_first = slot_range < first_count[:, None]
    slot_live = slot_range < (first_count + second_count)[:, None]
    source_rows = jnp.where(
        in_first,
        first_start[:, None] + slot_range,
        second_start[:, None] + slot_range - first_count[:, None],
    )
    source_rows = jnp.where(slot_live, source_rows, 0)
    seq_range = jnp.arange(row_counts.shape[0], dtype=jnp.int32)
    parity = seq_range % 2
    slot_base = seq_range // 2 * slot_rows + parity * row_counts[seq_range - parity] - row_offsets
    token_range = jnp.arange(local_rows, dtype=jnp.int32)[:, None]
    member = (token_range >= row_offsets[None, :]) & (
        token_range < (row_offsets + row_counts)[None, :]
    )
    return_rows = token_range[:, 0] + jnp.sum(jnp.where(member, slot_base[None, :], 0), axis=1)
    own_first = first_count[my_index]
    own_second = second_count[my_index]
    buffer_range = jnp.arange(buffer_rows, dtype=jnp.int32)
    slot_index = buffer_range % slot_rows
    source_index = buffer_range // slot_rows
    seq_flag = (slot_index >= own_first).astype(jnp.int32)
    positions = (slot_index - seq_flag * own_first) * shard_count + source_index
    live = slot_index < own_first + own_second
    attn_full, dense_full = (
        lax.all_gather(w_qkv, "shard", axis=0, tiled=True),
        lax.all_gather(w_dense, "shard", axis=0, tiled=True),
    )
    up_full, down_full = (
        lax.all_gather(w_up, "shard", axis=0, tiled=True),
        lax.all_gather(w_down, "shard", axis=0, tiled=True),
    )
    normed_one_wide, pull_one = jax.vjp(layer_norm, inputs, ln1_gain, ln1_bias)
    normed_two_wide, pull_two = jax.vjp(layer_norm, inputs, ln2_gain, ln2_bias)
    normed_one = normed_one_wide.astype(jnp.bfloat16)
    normed_two = normed_two_wide.astype(jnp.bfloat16)
    qkv = (jnp.dot(normed_one, attn_full, preferred_element_type=jnp.float32) + b_qkv).astype(
        jnp.bfloat16
    )
    arrived = lax.all_to_all(
        jnp.take(qkv, source_rows, axis=0), "shard", split_axis=0, concat_axis=0, tiled=True
    )
    arrived = arrived.reshape(buffer_rows, 3 * width)
    heads_shape = (buffer_rows, HEADS, HEAD)
    cosine_table, sine_table = rotary_tables(positions.astype(jnp.float32))

    def rotate_here(heads_in):
        return rotate(heads_in, cosine_table, sine_table)

    query_wide, pull_query = jax.vjp(
        rotate_here, arrived[:, :width].astype(jnp.float32).reshape(heads_shape)
    )
    key_wide, pull_key = jax.vjp(
        rotate_here, arrived[:, width : 2 * width].astype(jnp.float32).reshape(heads_shape)
    )
    rotated_queries = query_wide.astype(jnp.bfloat16)
    rotated_keys = key_wide.astype(jnp.bfloat16)
    value_heads = arrived[:, 2 * width :].reshape(heads_shape)
    sources_per = shard_count
    while sources_per > 1 and sources_per * slot_rows > 1024:
        sources_per = sources_per // 2
    block_rows = sources_per * slot_rows
    block_total = buffer_rows // block_rows
    score_scale = HEAD ** (-0.5)

    def forward_block(block_index):
        allowed = block_mask(seq_flag, positions, live)
        scores = (
            jnp.einsum(
                "qhe,khe->hqk", rotated_queries, rotated_keys, preferred_element_type=jnp.float32
            )
            * score_scale
        )
        scores = jnp.where(allowed[None], scores, MASKED)
        row_max = jnp.max(scores, axis=-1, keepdims=True)
        exp_scores = jnp.exp(scores - row_max)
        exp_total = jnp.sum(exp_scores, axis=-1, keepdims=True)
        attn_probs = jnp.where(allowed[None], exp_scores / exp_total, 0.0)
        attended_blk = jnp.einsum(
            "hqk,khe->qhe",
            attn_probs.astype(jnp.bfloat16),
            value_heads,
            preferred_element_type=jnp.float32,
        )
        return (attended_blk.astype(jnp.bfloat16), row_max[..., 0] + jnp.log(exp_total[..., 0]))

    attended_blocks, log_totals = lax.map(forward_block, jnp.arange(block_total, dtype=jnp.int32))
    attended_slots = attended_blocks.reshape(shard_count, slot_rows, width)
    attn_back = lax.all_to_all(
        attended_slots, "shard", split_axis=0, concat_axis=0, tiled=True
    ).reshape(buffer_rows, width)
    attn_in = jnp.take(attn_back, return_rows, axis=0)
    attn_out = jnp.dot(attn_in, dense_full, preferred_element_type=jnp.float32) + b_dense
    pre_up = jnp.dot(normed_two, up_full, preferred_element_type=jnp.float32) + b_up
    activated_wide, pull_gelu = jax.vjp(gelu_exact, pre_up)
    activated = activated_wide.astype(jnp.bfloat16)
    mlp_out = jnp.dot(activated, down_full, preferred_element_type=jnp.float32) + b_down
    output = (inputs + attn_out + mlp_out).astype(jnp.bfloat16)
    attn_second, dense_second = (
        lax.all_gather(w_qkv, "shard", axis=0, tiled=True),
        lax.all_gather(w_dense, "shard", axis=0, tiled=True),
    )
    up_second, down_second = (
        lax.all_gather(w_up, "shard", axis=0, tiled=True),
        lax.all_gather(w_down, "shard", axis=0, tiled=True),
    )
    grad_attended = jnp.dot(grad_out, dense_second.T, preferred_element_type=jnp.float32).astype(
        jnp.bfloat16
    )
    grad_slots = jnp.where(
        slot_live[:, :, None],
        jnp.take(grad_attended, source_rows, axis=0),
        jnp.zeros((), jnp.bfloat16),
    )
    grad_heads = lax.all_to_all(
        grad_slots, "shard", split_axis=0, concat_axis=0, tiled=True
    ).reshape(heads_shape)

    def backward_block(carried, block_index):
        grad_keys, grad_values = carried
        allowed = block_mask(seq_flag, positions, live)
        scores = (
            jnp.einsum(
                "qhe,khe->hqk", rotated_queries, rotated_keys, preferred_element_type=jnp.float32
            )
            * score_scale
        )
        attn_probs = jnp.where(
            allowed[None], jnp.exp(scores - log_totals[block_index][..., None]), 0.0
        )
        grad_probs = jnp.einsum(
            "qhe,khe->hqk", grad_heads, value_heads, preferred_element_type=jnp.float32
        )
        row_delta = jnp.sum(attn_probs * grad_probs, axis=-1, keepdims=True)
        grad_scores = (attn_probs * (grad_probs - row_delta)).astype(jnp.bfloat16)
        grad_query = (
            jnp.einsum(
                "hqk,khe->qhe", grad_scores, rotated_keys, preferred_element_type=jnp.float32
            )
            * score_scale
        )
        grad_keys = (
            grad_keys
            + jnp.einsum(
                "hqk,qhe->khe", grad_scores, rotated_queries, preferred_element_type=jnp.float32
            )
            * score_scale
        )
        grad_values = grad_values + jnp.einsum(
            "hqk,qhe->khe",
            attn_probs.astype(jnp.bfloat16),
            grad_heads,
            preferred_element_type=jnp.float32,
        )
        return ((grad_keys, grad_values), grad_query)

    zero_heads = jnp.zeros(heads_shape, jnp.float32)
    (grad_keys, grad_values), grad_query_blocks = lax.scan(
        backward_block, (zero_heads, zero_heads), jnp.arange(block_total, dtype=jnp.int32)
    )
    grad_q_pre = pull_query(grad_query_blocks.reshape(heads_shape))[0]
    grad_k_pre = pull_key(grad_keys)[0]
    grad_qkv_slots = jnp.concatenate(
        [
            grad_q_pre.reshape(buffer_rows, width),
            grad_k_pre.reshape(buffer_rows, width),
            grad_values.reshape(buffer_rows, width),
        ],
        axis=1,
    ).astype(jnp.bfloat16)
    grad_qkv_slots = grad_qkv_slots.reshape(shard_count, slot_rows, 3 * width)
    grad_qkv_back = lax.all_to_all(grad_qkv_slots, "shard", split_axis=0, concat_axis=0, tiled=True)
    grad_qkv = jnp.take(grad_qkv_back.reshape(buffer_rows, 3 * width), return_rows, axis=0)
    grad_activated = jnp.dot(grad_out, down_second.T, preferred_element_type=jnp.float32)
    grad_pre = pull_gelu(grad_activated)[0].astype(jnp.bfloat16)
    grad_normed_one = jnp.dot(grad_qkv, attn_second.T, preferred_element_type=jnp.float32)
    grad_normed_two = jnp.dot(grad_pre, up_second.T, preferred_element_type=jnp.float32)
    grad_in_one, grad_gain_one, grad_bias_one = pull_one(grad_normed_one)
    grad_in_two, grad_gain_two, grad_bias_two = pull_two(grad_normed_two)
    input_grad = grad_out.astype(jnp.float32) + grad_in_one + grad_in_two
    qkv_rows = lax.psum_scatter(
        row_product(normed_one, grad_qkv).astype(jnp.bfloat16),
        "shard",
        scatter_dimension=0,
        tiled=True,
    ).astype(jnp.float32)
    dense_rows = lax.psum_scatter(
        row_product(attn_in, grad_out).astype(jnp.bfloat16),
        "shard",
        scatter_dimension=0,
        tiled=True,
    ).astype(jnp.float32)
    up_rows = lax.psum_scatter(
        row_product(normed_two, grad_pre).astype(jnp.bfloat16),
        "shard",
        scatter_dimension=0,
        tiled=True,
    ).astype(jnp.float32)
    down_rows = lax.psum_scatter(
        row_product(activated, grad_out).astype(jnp.bfloat16),
        "shard",
        scatter_dimension=0,
        tiled=True,
    ).astype(jnp.float32)
    qkv_rows, dense_rows, up_rows, down_rows = (
        lax.psum(qkv_rows.astype(jnp.bfloat16), "rep").astype(jnp.float32),
        lax.psum(dense_rows.astype(jnp.bfloat16), "rep").astype(jnp.float32),
        lax.psum(up_rows.astype(jnp.bfloat16), "rep").astype(jnp.float32),
        lax.psum(down_rows.astype(jnp.bfloat16), "rep").astype(jnp.float32),
    )
    out_column_sum = jnp.sum(grad_out, axis=0, dtype=jnp.float32)
    small_totals = lax.psum(
        (
            grad_gain_one,
            grad_bias_one,
            grad_gain_two,
            grad_bias_two,
            jnp.sum(grad_qkv, axis=0, dtype=jnp.float32),
            out_column_sum,
            jnp.sum(grad_pre, axis=0, dtype=jnp.float32),
        ),
        ("rep", "shard"),
    )
    return (
        output[:, None, :],
        input_grad[:, None, :],
        small_totals[0],
        small_totals[1],
        small_totals[2],
        small_totals[3],
        qkv_rows,
        small_totals[4],
        dense_rows,
        small_totals[5],
        up_rows,
        small_totals[6],
        down_rows,
        small_totals[5],
    )


TILE_ROWS = 32
BIG_VMEM = 56 << 20
SMALL_COST = pl.CostEstimate(flops=1 << 20, bytes_accessed=1 << 20, transcendentals=0)
F32 = jnp.float32
BF16 = jnp.bfloat16


def flip(value, axis, bit):
    size = lax.axis_size(axis)
    return lax.ppermute(value, axis, [(i, i ^ bit) for i in range(size)])


def send(value, pairs):
    return lax.ppermute(value, "shard", [(2 * a + y, 2 * b + y) for a, b in pairs for y in (0, 1)])


MIDDLE = ((1, 2), (2, 1))
OUTWARD = ((1, 0), (2, 3))
INWARD = ((0, 1), (3, 2))


def plus(*terms):
    total = terms[0].astype(F32)
    for term in terms[1:]:
        total = total + term.astype(F32)
    return total


def hold(values, gates):
    return lax.optimization_barrier(tuple(values) + tuple(gates))[: len(values)]


def turn(heads_in, cosine, sine):
    left = heads_in[:, :128]
    lane = lax.broadcasted_iota(jnp.int32, left.shape, 1)
    half = ROT // 2
    partner = jnp.where(lane < half, pltpu.roll(left, 128 - half, 1), pltpu.roll(left, half, 1))
    return jnp.concatenate([left * cosine + partner * sine, heads_in[:, 128:]], axis=1)


def token_labels(my_index, shape, dim):
    inner = lax.broadcasted_iota(jnp.int32, shape, dim)
    block = inner // TILE_ROWS
    apart = (block % 4) * 2 + block // 4
    return (inner % TILE_ROWS) * HEADS + jnp.bitwise_xor(apart, my_index)


def tile_weights(tile, seq_ref, query, key_tiles, count):
    tile_tokens = TILE_ROWS * HEADS
    my_index = seq_ref[count]
    query_label = token_labels(my_index, (tile_tokens, 1), 0) + tile * tile_tokens
    key_label = token_labels(my_index, (1, tile_tokens), 1)
    scores = []
    for place, key in key_tiles:
        label = key_label + place * tile_tokens
        last = jnp.full(label.shape, 1 << 30, jnp.int32)
        for k in range(count):
            last = jnp.minimum(last, jnp.where(label < seq_ref[k], seq_ref[k], 1 << 30))
        allowed = query_label < last
        if place == tile:
            allowed = allowed & (label <= query_label)
        product = lax.dot_general(query, key, (((1,), (1,)), ((), ())), preferred_element_type=F32)
        scores.append(jnp.where(allowed, product * HEAD ** (-0.5), MASKED))
    scores = jnp.concatenate(scores, axis=1)
    exp_scores = jnp.exp(scores - jnp.max(scores, axis=1, keepdims=True))
    return exp_scores * (1.0 / jnp.sum(exp_scores, axis=1, keepdims=True))


def attend_kernel(seq_ref, qkv_ref, cos_ref, sin_ref, out_ref, query_ref, key_ref):
    tiles = query_ref.shape[0]
    tile_tokens = TILE_ROWS * HEADS

    def part(tile, lane):
        rows = qkv_ref[:, tile * TILE_ROWS : (tile + 1) * TILE_ROWS, lane : lane + HEAD]
        return rows.reshape(tile_tokens, HEAD)

    for tile in range(tiles):
        cosine, sine = cos_ref[tile], sin_ref[tile]
        query = turn(part(tile, 0).astype(F32), cosine, sine).astype(BF16)
        query_ref[tile] = query
        key_ref[tile] = turn(part(tile, HEAD).astype(F32), cosine, sine).astype(BF16)
        near = list(range(max(tile - 2, 0), tile + 1))
        probs = tile_weights(
            tile, seq_ref, query, [(k, key_ref[k]) for k in near], seq_ref.shape[0] - 1
        ).astype(BF16)
        total = jnp.zeros((tile_tokens, HEAD), F32)
        for at, k in enumerate(near):
            total = total + jnp.dot(
                probs[:, at * tile_tokens : (at + 1) * tile_tokens],
                part(k, 2 * HEAD),
                preferred_element_type=F32,
            )
        out_ref[:, tile * TILE_ROWS : (tile + 1) * TILE_ROWS, :] = total.astype(BF16).reshape(
            HEADS, TILE_ROWS, HEAD
        )


def attend_back_kernel(
    seq_ref, qkv_ref, grad_ref, cos_ref, sin_ref, query_ref, key_ref, out_ref, sum_ref, gk_ref, gv_ref
):
    tiles = query_ref.shape[0]
    tile_tokens = TILE_ROWS * HEADS
    scale = HEAD ** (-0.5)
    over_rows = (((0,), (0,)), ((), ()))
    over_lanes = (((1,), (1,)), ((), ()))

    def rows_of(tile):
        return slice(tile * TILE_ROWS, (tile + 1) * TILE_ROWS)

    def put(tile, lane, value):
        low = value.astype(BF16)
        out_ref[:, rows_of(tile), lane : lane + HEAD] = low.reshape(HEADS, TILE_ROWS, HEAD)
        columns = jnp.sum(low.astype(F32), axis=0, keepdims=True)
        if tile == 0:
            sum_ref[:, lane : lane + HEAD] = columns
        else:
            sum_ref[:, lane : lane + HEAD] += columns

    def finish(tile):
        put(tile, HEAD, turn(gk_ref[tile] * scale, cos_ref[tile], -sin_ref[tile]))
        put(tile, 2 * HEAD, gv_ref[tile])

    for tile in range(tiles):
        query = query_ref[tile]
        near = list(range(max(tile - 2, 0), tile + 1))
        grad = grad_ref[:, rows_of(tile), :].reshape(tile_tokens, HEAD)
        probs = tile_weights(
            tile, seq_ref, query, [(k, key_ref[k]) for k in near], seq_ref.shape[0] - 1
        )
        grad_probs = jnp.concatenate(
            [
                lax.dot_general(
                    grad,
                    qkv_ref[:, rows_of(k), 2 * HEAD :].reshape(tile_tokens, HEAD),
                    over_lanes,
                    preferred_element_type=F32,
                )
                for k in near
            ],
            axis=1,
        )
        delta = jnp.sum(probs * grad_probs, axis=1, keepdims=True)
        grad_scores = (probs * (grad_probs - delta)).astype(BF16)
        probs = probs.astype(BF16)
        grad_query = jnp.zeros((tile_tokens, HEAD), F32)
        for at, k in enumerate(near):
            span = slice(at * tile_tokens, (at + 1) * tile_tokens)
            grad_query = grad_query + jnp.dot(
                grad_scores[:, span], key_ref[k], preferred_element_type=F32
            )
            to_key = lax.dot_general(
                grad_scores[:, span], query, over_rows, preferred_element_type=F32
            )
            to_value = lax.dot_general(probs[:, span], grad, over_rows, preferred_element_type=F32)
            if k == tile:
                gk_ref[k] = to_key
                gv_ref[k] = to_value
            else:
                gk_ref[k] += to_key
                gv_ref[k] += to_value
        put(tile, 0, turn(grad_query * scale, cos_ref[tile], -sin_ref[tile]))
        if tile >= 2:
            finish(tile - 2)
    for tile in range(max(tiles - 2, 0), tiles):
        finish(tile)


VMEM_SPEC = pl.BlockSpec(memory_space=pltpu.VMEM)
SMEM_SPEC = pl.BlockSpec(memory_space=pltpu.SMEM)


def attend(seq_scalars, qkv, cosine, sine):
    blocks, rows, _ = qkv.shape
    tiled = (rows // TILE_ROWS, blocks * TILE_ROWS, HEAD)
    return pl.pallas_call(
        attend_kernel,
        out_shape=(
            jax.ShapeDtypeStruct((blocks, rows, HEAD), BF16),
            jax.ShapeDtypeStruct(tiled, BF16),
            jax.ShapeDtypeStruct(tiled, BF16),
        ),
        in_specs=[SMEM_SPEC, VMEM_SPEC, VMEM_SPEC, VMEM_SPEC],
        out_specs=(VMEM_SPEC, VMEM_SPEC, VMEM_SPEC),
        compiler_params=pltpu.CompilerParams(vmem_limit_bytes=48 << 20),
        cost_estimate=SMALL_COST,
    )(seq_scalars, qkv, cosine, sine)


def attend_back(seq_scalars, qkv, grad, cosine, sine, query, key):
    blocks, rows, wide = qkv.shape
    return pl.pallas_call(
        attend_back_kernel,
        out_shape=(
            jax.ShapeDtypeStruct((blocks, rows, wide), BF16),
            jax.ShapeDtypeStruct((1, wide), F32),
        ),
        in_specs=[SMEM_SPEC] + [VMEM_SPEC] * 6,
        out_specs=(VMEM_SPEC, VMEM_SPEC),
        scratch_shapes=[pltpu.VMEM(query.shape, F32), pltpu.VMEM(query.shape, F32)],
        compiler_params=pltpu.CompilerParams(vmem_limit_bytes=48 << 20),
        cost_estimate=SMALL_COST,
    )(seq_scalars, qkv, grad, cosine, sine, query, key)


def place_weights_kernel(
    at_ref, p0_ref, p1_ref, p2_ref, p3_ref, gain_ref, shift_ref, *out_refs, hidden
):
    raw_refs, scaled_refs, sum_ref = out_refs[:2], out_refs[2:4], out_refs[4]
    quarter, wide = p0_ref.shape[1:]

    @pl.when(pl.program_id(0) == 0)
    def _():
        sum_ref[...] = jnp.zeros_like(sum_ref)

    for k, part_ref in enumerate((p0_ref, p1_ref, p2_ref, p3_ref)):
        rows = pl.ds(pl.multiple_of((at_ref[1] ^ k) * quarter, quarter), quarter)
        for norm, columns in ((1, slice(0, hidden)), (0, slice(hidden, wide))):
            raw = part_ref[0, :, columns]
            raw_refs[1 - norm][rows, :] = raw
            weight = raw.astype(F32)
            gain, shift = gain_ref[rows, norm : norm + 1], shift_ref[rows, norm : norm + 1]
            scaled_refs[1 - norm][rows, :] = (weight * gain).astype(BF16)
            sum_ref[:, columns] += jnp.sum(weight * shift, axis=0, keepdims=True)


def place_weights(me, rep, parts, gains, shifts, hidden):
    count, rows, wide = parts[0].shape
    widths = (hidden, wide - hidden) * 2
    pair = pl.BlockSpec((4 * rows, 2), lambda i, at_ref: (i ^ at_ref[0], 0))
    part = pl.BlockSpec((1, rows, wide), lambda i, at_ref: (i, 0, 0))
    return pl.pallas_call(
        functools.partial(place_weights_kernel, hidden=hidden),
        out_shape=tuple(jax.ShapeDtypeStruct((count * 4 * rows, n), BF16) for n in widths)
        + (jax.ShapeDtypeStruct((1, wide), F32),),
        grid_spec=pltpu.PrefetchScalarGridSpec(
            num_scalar_prefetch=1,
            grid=(count,),
            in_specs=[part] * 4 + [pair, pair],
            out_specs=tuple(
                pl.BlockSpec((4 * rows, n), lambda i, at_ref: (i ^ at_ref[0], 0)) for n in widths
            )
            + (pl.BlockSpec((1, wide), lambda i, at_ref: (0, 0)),),
        ),
        compiler_params=pltpu.CompilerParams(vmem_limit_bytes=32 << 20),
        cost_estimate=SMALL_COST,
    )(jnp.stack([me, rep]).astype(jnp.int32), *parts, gains, shifts)


def place_grads_kernel(at_ref, p0_ref, p1_ref, p2_ref, p3_ref, out_ref, *, pieces):
    quarter, wide = p0_ref.shape[1:]
    source = pl.program_id(0) ^ at_ref[0]
    size = wide // pieces
    for k, part_ref in enumerate((p0_ref, p1_ref, p2_ref, p3_ref)):
        rows = pl.ds(pl.multiple_of((at_ref[1] ^ k) * quarter, quarter), quarter)
        values = part_ref[0].astype(F32)
        if pieces == 1:
            out_ref[rows, :] = values
        else:
            for j in range(pieces):
                start = pl.multiple_of((j * HEADS + source) * size, size)
                out_ref[rows, pl.ds(start, size)] = values[:, j * size : (j + 1) * size]


def place_grads(me, rep, parts, pieces):
    count, rows, wide = parts[0].shape
    part = pl.BlockSpec((1, rows, wide), lambda i, at_ref: (i, 0, 0))
    if pieces == 1:
        out = pl.BlockSpec((4 * rows, wide), lambda i, at_ref: (0, i ^ at_ref[0]))
    else:
        out = pl.BlockSpec((4 * rows, count * wide), lambda i, at_ref: (0, 0))
    return pl.pallas_call(
        functools.partial(place_grads_kernel, pieces=pieces),
        out_shape=jax.ShapeDtypeStruct((4 * rows, count * wide), F32),
        grid_spec=pltpu.PrefetchScalarGridSpec(
            num_scalar_prefetch=1, grid=(count,), in_specs=[part] * 4, out_specs=out
        ),
        compiler_params=pltpu.CompilerParams(vmem_limit_bytes=40 << 20),
        cost_estimate=SMALL_COST,
    )(jnp.stack([me, rep]).astype(jnp.int32), *parts)


def place_halves_kernel(core_ref, mine_ref, other_ref, down_ref, dense_ref, *, cut):
    step = pl.program_id(0)
    first = (step < pl.num_programs(0) // 2) == (core_ref[0] == 0)
    values = jnp.where(first, mine_ref[...], other_ref[...]).astype(F32)
    in_down = step < cut

    @pl.when(in_down)
    def _():
        down_ref[...] = values

    @pl.when(jnp.logical_not(in_down))
    def _():
        dense_ref[...] = values


def place_halves(core, mine, other, hidden):
    rows, width = mine.shape
    tile = 128
    half, cut = rows // tile, hidden // tile
    part = pl.BlockSpec((tile, width), lambda i, core_ref: (i % half, 0))
    return pl.pallas_call(
        functools.partial(place_halves_kernel, cut=cut),
        out_shape=(
            jax.ShapeDtypeStruct((hidden, width), F32),
            jax.ShapeDtypeStruct((2 * rows - hidden, width), F32),
        ),
        grid_spec=pltpu.PrefetchScalarGridSpec(
            num_scalar_prefetch=1,
            grid=(2 * half,),
            in_specs=[part, part],
            out_specs=(
                pl.BlockSpec((tile, width), lambda i, core_ref: (jnp.minimum(i, cut - 1), 0)),
                pl.BlockSpec((tile, width), lambda i, core_ref: (jnp.maximum(i - cut, 0), 0)),
            ),
        ),
        compiler_params=pltpu.CompilerParams(vmem_limit_bytes=32 << 20),
        cost_estimate=SMALL_COST,
    )(core[None].astype(jnp.int32), mine, other)


def normalize(values):
    values = values.astype(F32)
    centered = values - jnp.mean(values, axis=-1, keepdims=True)
    rstd = lax.rsqrt(jnp.mean(centered * centered, axis=-1, keepdims=True) + EPSILON)
    return centered * rstd, rstd


def norm_kernel(*refs, count, steps):
    blocks, out_ref = refs[:count], refs[-1]
    for k in range(count):

        @pl.when(pl.program_id(0) // steps == k)
        def _(block_ref=blocks[k]):
            out_ref[...] = normalize(block_ref[...])[0].astype(BF16)


def norm_blocks(blocks, places, buffer):
    rows, width = blocks[0].shape
    steps = 2
    tile = rows // steps
    count = len(blocks)

    def spec(k):
        return pl.BlockSpec((tile, width), lambda i: (jnp.clip(i - steps * k, 0, steps - 1), 0))

    def put(i):
        place = places[0]
        for k in range(1, count):
            place = jnp.where(i // steps >= k, places[k], place)
        return place * steps + i % steps, 0

    extra = [] if buffer is None else [buffer]
    return pl.pallas_call(
        functools.partial(norm_kernel, count=count, steps=steps),
        out_shape=jax.ShapeDtypeStruct((HEADS * rows, width), BF16),
        grid=(count * steps,),
        in_specs=[spec(k) for k in range(count)] + [pl.BlockSpec(memory_space=pl.ANY)] * len(extra),
        out_specs=pl.BlockSpec((tile, width), put),
        input_output_aliases={count: 0} if extra else {},
        cost_estimate=SMALL_COST,
    )(*blocks, *extra)


def dot32(left, right, left_dim=1, right_dim=0):
    return lax.dot_general(
        left, right, (((left_dim,), (right_dim,)), ((), ())), preferred_element_type=F32
    )


def tokens_spec(tile, width, first):
    return pl.BlockSpec((tile, width), lambda i: (first + i, 0))


def whole_spec(shape):
    return pl.BlockSpec(shape, lambda i: (0, 0), pipeline_mode=pl.Buffered(1))


def block_specs(count, tile, width):
    return [pl.BlockSpec((tile, width), lambda i: (0, 0)) for _ in range(count)]


def project_kernel(normed_ref, up_ref, qkv_w_ref, shift_ref, act_ref, slope_ref, qkv_ref):
    hidden = act_ref.shape[1]
    lanes = 256
    for start in range(0, hidden, lanes):
        columns = slice(start, start + lanes)
        value = dot32(normed_ref[...], up_ref[:, columns]) + shift_ref[:, columns]
        normal = 0.5 + 0.5 * lax.erf(value * (0.5**0.5))
        bell = jnp.exp(value * value * -0.5) * ((2.0 * math.pi) ** -0.5)
        act_ref[:, columns] = (value * normal).astype(BF16)
        slope_ref[:, columns] = (normal + value * bell).astype(BF16)
    for start in range(0, qkv_ref.shape[1], lanes):
        columns = slice(start, start + lanes)
        value = dot32(normed_ref[...], qkv_w_ref[:, columns])
        value = value + shift_ref[:, hidden + start : hidden + start + lanes]
        qkv_ref[:, columns] = value.astype(BF16)


def project(normed, w_up, w_qkv, shift):
    count, width = normed.shape
    hidden, rest = w_up.shape[1], w_qkv.shape[1]
    tile = 512
    return pl.pallas_call(
        project_kernel,
        out_shape=(
            jax.ShapeDtypeStruct((count, hidden), BF16),
            jax.ShapeDtypeStruct((count, hidden), BF16),
            jax.ShapeDtypeStruct((count, rest), BF16),
        ),
        grid=(count // tile,),
        in_specs=[
            tokens_spec(tile, width, 0),
            whole_spec(w_up.shape),
            whole_spec(w_qkv.shape),
            whole_spec(shift.shape),
        ],
        out_specs=(
            tokens_spec(tile, hidden, 0),
            tokens_spec(tile, hidden, 0),
            tokens_spec(tile, rest, 0),
        ),
        compiler_params=pltpu.CompilerParams(vmem_limit_bytes=BIG_VMEM),
        cost_estimate=SMALL_COST,
    )(normed, w_up, w_qkv, shift)


def combine_kernel(one_ref, two_ref, w_one_ref, w_two_ref, *out_refs, right_dim):
    lanes = 512
    width = w_one_ref.shape[1 - right_dim]
    for k, out_ref in enumerate(out_refs):

        @pl.when(pl.program_id(0) == k)
        def _(out_ref=out_ref):
            for start in range(0, width, lanes):
                columns = slice(start, start + lanes)
                if right_dim:
                    w_one, w_two = w_one_ref[columns, :], w_two_ref[columns, :]
                else:
                    w_one, w_two = w_one_ref[:, columns], w_two_ref[:, columns]
                value = dot32(one_ref[...], w_one, 1, right_dim)
                value = value + dot32(two_ref[...], w_two, 1, right_dim)
                out_ref[:, columns] = value.astype(BF16)


def combine(one, two, w_one, w_two, rows, first, right_dim):
    width = w_one.shape[1 - right_dim]
    return pl.pallas_call(
        functools.partial(combine_kernel, right_dim=right_dim),
        out_shape=tuple(jax.ShapeDtypeStruct((rows, width), BF16) for _ in range(4)),
        grid=(4,),
        in_specs=[
            tokens_spec(rows, one.shape[1], first),
            tokens_spec(rows, two.shape[1], first),
            whole_spec(w_one.shape),
            whole_spec(w_two.shape),
        ],
        out_specs=tuple(block_specs(4, rows, width)),
        compiler_params=pltpu.CompilerParams(vmem_limit_bytes=BIG_VMEM),
        cost_estimate=SMALL_COST,
    )(one, two, w_one, w_two)


def pull_kernel(*refs, extra):
    blocks, (w_one_ref, w_two_ref, slope_ref) = refs[:4], refs[4:7]
    pre_ref, att_ref, sum_ref = refs[7 + extra :]
    hidden = w_one_ref.shape[0]
    lanes = 256

    @pl.when(pl.program_id(0) == 0)
    def _():
        sum_ref[...] = jnp.zeros_like(sum_ref)

    for k, block_ref in enumerate(blocks):

        @pl.when(pl.program_id(0) == k)
        def _(block_ref=block_ref):
            for start in range(0, hidden, lanes):
                columns = slice(start, start + lanes)
                value = dot32(block_ref[...], w_one_ref[columns, :], 1, 1)
                value = (value * slope_ref[:, columns].astype(F32)).astype(BF16)
                pre_ref[:, columns] = value
                sum_ref[:, columns] += jnp.sum(value.astype(F32), axis=0, keepdims=True)
            att_ref[...] = dot32(block_ref[...], w_two_ref[...], 1, 1).astype(BF16)


def pull(blocks, w_down, w_dense, slope, half, buffers):
    rows, width = blocks[0].shape
    hidden, head = w_down.shape[0], w_dense.shape[0]
    count = HEADS * rows
    return pl.pallas_call(
        functools.partial(pull_kernel, extra=len(buffers)),
        out_shape=(
            jax.ShapeDtypeStruct((count, hidden), BF16),
            jax.ShapeDtypeStruct((count, head), BF16),
            jax.ShapeDtypeStruct((1, hidden), F32),
        ),
        grid=(4,),
        in_specs=block_specs(4, rows, width)
        + [whole_spec(w_down.shape), whole_spec(w_dense.shape), tokens_spec(rows, hidden, 4 * half)]
        + [pl.BlockSpec(memory_space=pl.ANY)] * len(buffers),
        out_specs=(
            tokens_spec(rows, hidden, 4 * half),
            tokens_spec(rows, head, 4 * half),
            pl.BlockSpec((1, hidden), lambda i: (0, 0)),
        ),
        input_output_aliases={7 + k: k for k in range(len(buffers))},
        compiler_params=pltpu.CompilerParams(vmem_limit_bytes=BIG_VMEM),
        cost_estimate=SMALL_COST,
    )(*blocks, w_down, w_dense, slope, *buffers)


def moments_kernel(normed_ref, right_ref, weight_ref, gain_ref, shift_ref, columns_ref, out_ref, sums_ref):
    lanes = 256
    turned = normed_ref[...].T
    gain, shift = gain_ref[...], shift_ref[...]
    gain_terms, bias_terms = None, None
    for start in range(0, out_ref.shape[1], lanes):
        columns = slice(start, start + lanes)
        moment = dot32(turned, right_ref[:, columns])
        weight = weight_ref[:, columns].astype(F32)
        total = columns_ref[:, columns]
        out_ref[:, columns] = (moment * gain + shift * total).astype(BF16)
        one, two = moment * weight, weight * total
        gain_terms = one if gain_terms is None else gain_terms + one
        bias_terms = two if bias_terms is None else bias_terms + two
    sums_ref[:, 0:1] = jnp.sum(gain_terms, axis=1, keepdims=True)
    sums_ref[:, 1:2] = jnp.sum(bias_terms, axis=1, keepdims=True)


def moments_of(normed, right, weight, gain, shift, columns):
    count, width = normed.shape
    wide = weight.shape[1]
    tile = 256
    return pl.pallas_call(
        moments_kernel,
        out_shape=(
            jax.ShapeDtypeStruct((width, wide), BF16),
            jax.ShapeDtypeStruct((width, 2), F32),
        ),
        grid=(width // tile,),
        in_specs=[
            pl.BlockSpec((count, tile), lambda i: (0, i)),
            whole_spec(right.shape),
            tokens_spec(tile, wide, 0),
            tokens_spec(tile, 1, 0),
            tokens_spec(tile, 1, 0),
            whole_spec(columns.shape),
        ],
        out_specs=(tokens_spec(tile, wide, 0), tokens_spec(tile, 2, 0)),
        compiler_params=pltpu.CompilerParams(vmem_limit_bytes=BIG_VMEM),
        cost_estimate=SMALL_COST,
    )(normed, right, weight, gain[:, None], shift[:, None], columns)


def outer_kernel(act_ref, att_ref, *refs):
    blocks, out_ref = refs[:HEADS], refs[HEADS]
    rows = blocks[0].shape[0]
    lanes = 512
    last = pl.num_programs(0) - 1

    def fill(left_ref):
        turned = left_ref[...].T
        for start in range(0, out_ref.shape[1], lanes):
            columns = slice(start, start + lanes)
            total = None
            for k, block_ref in enumerate(blocks):
                term = dot32(turned[:, k * rows : (k + 1) * rows], block_ref[:, columns])
                total = term if total is None else total + term
            out_ref[:, columns] = total.astype(BF16)

    @pl.when(pl.program_id(0) < last)
    def _():
        fill(act_ref)

    @pl.when(pl.program_id(0) == last)
    def _():
        fill(att_ref)


def outer(activated, attended, blocks):
    count, hidden = activated.shape
    rows, width = blocks[0].shape
    tile = attended.shape[1]
    steps = hidden // tile
    return pl.pallas_call(
        outer_kernel,
        out_shape=jax.ShapeDtypeStruct((hidden + tile, width), BF16),
        grid=(steps + 1,),
        in_specs=[
            pl.BlockSpec((count, tile), lambda i: (0, jnp.minimum(i, steps - 1))),
            whole_spec(attended.shape),
        ]
        + [whole_spec((rows, width)) for _ in blocks],
        out_specs=tokens_spec(tile, width, 0),
        compiler_params=pltpu.CompilerParams(vmem_limit_bytes=BIG_VMEM),
        cost_estimate=SMALL_COST,
    )(activated, attended, *blocks)


def split_shards(
    tokens,
    cotangent,
    seq_lengths,
    seq_order,
    ln1_gain,
    ln1_bias,
    ln2_gain,
    ln2_bias,
    w_qkv,
    b_qkv,
    w_dense,
    b_dense,
    w_up,
    b_up,
    w_down,
    b_down,
):
    me = lax.axis_index("shard")
    rep = lax.axis_index("rep")
    place = me // 2
    is_middle = (place == 1) | (place == 2)
    own = tokens[:, 0, :]
    own_grad = cotangent[:, 0, :]
    rows, width = own.shape
    group_tokens = rows * HEADS
    depth = w_up.shape[0]
    hidden = w_down.shape[0]
    wide = hidden + 3 * HEAD
    quarter = depth // 4

    up_rows = lax.dynamic_slice_in_dim(w_up, rep * quarter, quarter, 0)
    qkv_rows = lax.dynamic_slice_in_dim(w_qkv, rep * quarter, quarter, 0)

    def columns_for(target):
        pieces = [lax.dynamic_slice_in_dim(up_rows, target * hidden, hidden, 1)]
        for k in range(3):
            pieces.append(
                lax.dynamic_slice_in_dim(qkv_rows, k * width + target * HEAD, HEAD, 1)
            )
        return jnp.concatenate(pieces, axis=1)

    odd = jnp.stack([columns_for(me ^ (2 * z + 1)) for z in range(4)])
    odd_came = flip(odd, "shard", 1)
    x_near = flip(own, "shard", 2)
    x_across = send(own, MIDDLE)
    keep = [columns_for(me ^ (2 * z)) for z in range(4)]
    row_offsets, row_counts = stream_rows(seq_lengths[0], seq_order[0], HEADS)
    ends = (row_offsets + row_counts) * HEADS
    seq_scalars = jnp.concatenate([ends, me[None]]).astype(jnp.int32)
    row_range = jnp.arange(rows, dtype=jnp.int32)
    member = (row_range[:, None] >= row_offsets[None, :]) & (
        row_range[:, None] < (row_offsets + row_counts)[None, :]
    )
    in_seq = row_range - jnp.sum(jnp.where(member, row_offsets[None, :], 0), axis=1)
    block_range = jnp.arange(HEADS, dtype=jnp.int32)
    apart = (block_range % 4) * 2 + block_range // 4
    positions = (
        in_seq.reshape(rows // TILE_ROWS, 1, TILE_ROWS) * HEADS + (apart ^ me)[None, :, None]
    )
    cosine, sine = rotary_tables(positions.reshape(-1).astype(F32))
    rest = 128 - ROT
    cosine = jnp.concatenate([cosine, cosine, jnp.ones((group_tokens, rest), F32)], axis=1)
    sine = jnp.concatenate([-sine, sine, jnp.zeros((group_tokens, rest), F32)], axis=1)
    tiled = (rows // TILE_ROWS, TILE_ROWS * HEADS, 128)
    cosine = cosine.reshape(tiled)
    sine = sine.reshape(tiled)


    own, own_grad, x_near, x_across, odd_came, *keep = hold(
        (own, own_grad, x_near, x_across, odd_came, *keep), (cosine, sine)
    )
    pairs = [jnp.stack([keep[z], odd_came[z]]) for z in range(4)]
    got = [flip(pairs[z], "shard", 2 * z) for z in range(1, 4)]
    x_own_y = flip(own, "shard", 1)
    x_near_y = flip(x_near, "shard", 1)
    beside = [flip(pairs[0], "rep", 2)]
    x_near, x_across, own_grad, x_near_y, *got = hold(
        (x_near, x_across, own_grad, x_near_y, *got), (x_own_y, beside[0])
    )
    x_across_near = send(x_near, MIDDLE)
    x_two = send(x_across, OUTWARD)
    g_own_y = flip(own_grad, "shard", 1)
    beside = beside + [flip(jnp.stack(got), "rep", 2)]
    part = jnp.stack([pairs[0]] + got).reshape(HEADS, quarter, wide)
    x_across_near, x_two, own_grad, *beside = hold(
        (x_across_near, x_two, own_grad, *beside), (part, g_own_y)
    )
    two = jnp.where(is_middle, x_across_near, x_two)
    x_three = send(x_across_near, OUTWARD)
    g_across = send(own_grad, MIDDLE)
    x_two_y = flip(two, "shard", 1)
    beside = jnp.concatenate([beside[0][None], beside[1]]).reshape(HEADS, quarter, wide)
    part_c = flip(part, "rep", 1)
    beside_c = flip(beside, "rep", 1)
    normed = norm_blocks([own, x_near, x_own_y, x_near_y, two], (0, 1, 4, 5, 2), None)
    x_three, own_grad, g_across, beside_c, part_c, x_two_y = hold(
        (x_three, own_grad, g_across, beside_c, part_c, x_two_y), (normed,)
    )
    three = jnp.where(is_middle, x_across, x_three)
    g_near = flip(own_grad, "shard", 2)
    x_three_y = flip(three, "shard", 1)
    parts = (part, part_c, beside, beside_c)
    gains = jnp.stack([ln1_gain, ln2_gain], axis=1)
    shifts = jnp.stack([ln1_bias, ln2_bias], axis=1)
    up_raw, qkv_raw, up_scaled, qkv_scaled, shifted = place_weights(
        me, rep, parts, gains, shifts, hidden
    )
    b_in = jnp.concatenate(
        [lax.dynamic_slice_in_dim(b_up, me * hidden, hidden, 0)]
        + [lax.dynamic_slice_in_dim(b_qkv, k * width + me * HEAD, HEAD, 0) for k in range(3)]
    )
    b_in = b_in[None, :] + shifted
    normed = norm_blocks([three, x_two_y], (3, 6), normed)
    g_near, x_three_y, normed = hold((g_near, x_three_y, normed), (b_in,))
    g_across_near = send(g_near, MIDDLE)
    g_two = send(g_across, OUTWARD)
    g_near_y = flip(g_near, "shard", 1)
    normed = norm_blocks([x_three_y], (7,), normed)
    activated, slope, qkv = project(normed, up_scaled, qkv_scaled, b_in)
    g_across_near, g_two, qkv, g_near_y = hold((g_across_near, g_two, qkv, g_near_y), (activated,))
    g_two = jnp.where(is_middle, g_across_near, g_two)
    g_three = send(g_across_near, OUTWARD)
    g_two_y = flip(g_two, "shard", 1)
    qkv = qkv.reshape(HEADS, rows, 3 * HEAD)
    attended, query, key = attend(seq_scalars, qkv, cosine, sine)
    attended = attended.reshape(group_tokens, HEAD)
    far = combine(activated, attended, w_down, w_dense, rows, 4, 0)
    g_three, g_two_y, *far = hold((g_three, g_two_y, *far), ())
    g_three = jnp.where(is_middle, g_across, g_three)
    g_three_y = flip(g_three, "shard", 1)
    close = combine(activated, attended, w_down, w_dense, rows, 0, 0)
    grad_pre, grad_attended, pre_sums = pull(
        [own_grad, g_near, g_two, g_three], w_down, w_dense, slope, 0, []
    )
    g_three_y, grad_pre, *far = hold((g_three_y, grad_pre, *far), close)
    came_three = flip(far[3], "shard", 1)
    grad_pre, grad_attended, more_sums = pull(
        [g_own_y, g_near_y, g_two_y, g_three_y],
        w_down,
        w_dense,
        slope,
        1,
        [grad_pre, grad_attended],
    )
    pre_sums = pre_sums + more_sums
    my_core = rep % 2
    my_side = rep // 2
    my_row = me % 2

    def split(values, index):
        return (
            lax.dynamic_index_in_dim(values, index, 1, False),
            lax.dynamic_index_in_dim(values, 1 - index, 1, False),
        )

    def by_core(grads):
        return split(grads.reshape(2 * HEADS, 2, quarter, grads.shape[1]), my_core)

    def by_side(summed):
        return split(summed.reshape(HEADS, 2, quarter, summed.shape[-1]), my_side)

    def by_row(summed):
        return split(summed.reshape(4, 2, quarter, summed.shape[-1]), my_row)

    def joined(mine, came):
        return plus(mine, came).astype(BF16)

    def by_place(mine, came):
        both = jnp.stack([mine, came], axis=1)
        return [lax.dynamic_index_in_dim(both, place ^ z, 0, False) for z in range(4)]

    def far_places(pieces):
        return flip(jnp.stack(pieces[2:]), "shard", 4)

    def near_place(pieces, far):
        return flip(jnp.stack([pieces[1], far[1]]), "shard", 2)

    def sources(pieces, far, near):
        both = jnp.stack([pieces[0], near[0], far[0], near[1]])
        return both.reshape(HEADS, quarter, both.shape[-1])

    up_grads, up_sums = moments_of(normed, grad_pre, up_raw, ln2_gain, ln2_bias, pre_sums)
    up_keep, up_give = by_core(up_grads)
    came_three, grad_attended, up_give, *far = hold((came_three, grad_attended, up_give, *far), ())
    came_two = flip(far[2], "shard", 1)
    three = plus(close[3], came_three).astype(BF16)
    from_corner = send(three, INWARD)
    up_came = flip(up_give, "rep", 1)
    grad_qkv, qkv_sums = attend_back(
        seq_scalars,
        qkv,
        grad_attended.reshape(HEADS, rows, HEAD),
        cosine,
        sine,
        query,
        key,
    )
    grad_qkv = grad_qkv.reshape(group_tokens, 3 * HEAD)
    qkv_grads, qkv_row_sums = moments_of(normed, grad_qkv, qkv_raw, ln1_gain, ln1_bias, qkv_sums)
    qkv_keep, qkv_give = by_core(qkv_grads)
    came_two, from_corner, up_came, qkv_give, grad_qkv, *far = hold(
        (came_two, from_corner, up_came, qkv_give, grad_qkv, *far), ()
    )
    up_keep, up_give = by_side(joined(up_keep, up_came))
    up_came = flip(up_give, "rep", 2)
    came_one = flip(far[1], "shard", 1)
    two = plus(close[2], came_two, from_corner).astype(BF16)
    across_near = send(two, MIDDLE)
    across = send(two, INWARD)
    qkv_came = flip(qkv_give, "rep", 1)
    gy_far = combine(grad_pre, grad_qkv, up_scaled, qkv_scaled, rows, 4, 1)
    gy_close = combine(grad_pre, grad_qkv, up_scaled, qkv_scaled, rows, 0, 1)
    up_came, came_one, across_near, across, qkv_came, own_grad, *both = hold(
        (up_came, came_one, across_near, across, qkv_came, own_grad, *far, *gy_far, *gy_close), ()
    )
    far, gy_far, gy_close = both[:4], both[4:8], both[8:]
    up_keep, up_give = by_row(joined(up_keep, up_came))
    came_own = flip(far[0], "shard", 1)
    up_came = flip(up_give, "shard", 1)
    one = plus(close[1], came_one, across_near).astype(BF16)
    three = plus(three, across).astype(BF16)
    one_near = flip(one, "shard", 2)
    three_across = send(three, MIDDLE)
    qkv_keep, qkv_give = by_side(joined(qkv_keep, qkv_came))
    qkv_came = flip(qkv_give, "rep", 2)
    out_grads = outer(
        activated,
        attended,
        [own_grad, g_near, g_two, g_three, g_own_y, g_near_y, g_two_y, g_three_y],
    )
    half_rows = out_grads.shape[0] // 2
    half_keep, half_give = split(out_grads.reshape(1, 2, half_rows, width), my_core)
    small = jnp.concatenate(
        [
            qkv_row_sums.T.reshape(-1),
            up_sums.T.reshape(-1),
            jnp.sum(own_grad, axis=0, dtype=F32),
            jnp.where(
                block_range[:, None] == me, jnp.concatenate([pre_sums, qkv_sums], axis=1), 0.0
            ).reshape(-1),
        ]
    )
    came_own, one_near, three_across, up_came, qkv_came, half_give, small, *gy_far = hold(
        (came_own, one_near, three_across, up_came, qkv_came, half_give, small, *gy_far), ()
    )
    came_three = flip(gy_far[3], "shard", 1)
    qkv_keep, qkv_give = by_row(joined(qkv_keep, qkv_came))
    qkv_came = flip(qkv_give, "shard", 1)
    up_pieces = by_place(up_keep, up_came)
    up_far = far_places(up_pieces)
    half_came = flip(half_give, "rep", 1)
    small = small + flip(small, "rep", 1)
    out_sum = plus(close[0], came_own, one_near, three_across)
    output = (own.astype(F32) + out_sum + (b_dense + b_down)).astype(BF16)
    came_three, qkv_came, up_far, half_came, small, *gy_far = hold(
        (came_three, qkv_came, up_far, half_came, small, *gy_far), (output,)
    )
    came_two = flip(gy_far[2], "shard", 1)
    three = plus(gy_close[3], came_three).astype(BF16)
    from_corner = send(three, INWARD)
    up_near = near_place(up_pieces, up_far)
    qkv_pieces = by_place(qkv_keep, qkv_came)
    qkv_far = far_places(qkv_pieces)
    half = joined(half_keep, half_came).reshape(half_rows, width)
    half_far = flip(half, "rep", 2)
    came_two, from_corner, up_near, qkv_far, *gy_far = hold(
        (came_two, from_corner, up_near, qkv_far, *gy_far), ()
    )
    came_one = flip(gy_far[1], "shard", 1)
    two = plus(gy_close[2], came_two, from_corner).astype(BF16)
    across_near = send(two, MIDDLE)
    across = send(two, INWARD)
    qkv_near = near_place(qkv_pieces, qkv_far)
    up_part = sources(up_pieces, up_far, up_near)
    came_one, across_near, across, qkv_near, up_part, half_far, *gy_far = hold(
        (came_one, across_near, across, qkv_near, up_part, half_far, *gy_far), ()
    )
    came_own = flip(gy_far[0], "shard", 1)
    one = plus(gy_close[1], came_one, across_near).astype(BF16)
    three = plus(three, across).astype(BF16)
    one_near = flip(one, "shard", 2)
    three_across = send(three, MIDDLE)
    up_beside = flip(up_part, "rep", 2)
    up_c = flip(up_part, "rep", 1)
    half = joined(half, half_far)
    qkv_part = sources(qkv_pieces, qkv_far, qkv_near)
    came_own, one_near, three_across, up_beside, half, qkv_part, small = hold(
        (came_own, one_near, three_across, up_beside, half, qkv_part, small), (up_c,)
    )
    qkv_beside = flip(qkv_part, "rep", 2)
    qkv_c = flip(qkv_part, "rep", 1)
    up_beside_c = flip(up_beside, "rep", 1)
    other = flip(half, "rep", 1)
    small = small + flip(small, "rep", 2)
    gy = plus(gy_close[0], came_own, one_near, three_across)
    own_normed, own_rstd = normalize(own)
    input_grad = own_grad.astype(F32) + own_rstd * (
        gy
        - jnp.mean(gy, axis=-1, keepdims=True)
        - own_normed * jnp.mean(gy * own_normed, axis=-1, keepdims=True)
    )
    qkv_beside, up_beside_c, other, small = hold(
        (qkv_beside, up_beside_c, other, small), (input_grad, qkv_c)
    )
    qkv_beside_c = flip(qkv_beside, "rep", 1)
    for bit in (1, 2, 4):
        small = small + flip(small, "shard", bit)
    up_grad = place_grads(me, rep, (up_part, up_c, up_beside, up_beside_c), 1)
    down_grad, dense_grad = place_halves(my_core, half, other, hidden)
    qkv_grad = place_grads(me, rep, (qkv_part, qkv_c, qkv_beside, qkv_beside_c), 3)
    vectors = small[: 5 * width].reshape(5, width)
    slots = small[5 * width :].reshape(HEADS, wide)
    b_up_grad = slots[:, :hidden].reshape(-1)
    b_qkv_grad = slots[:, hidden:].reshape(HEADS, 3, HEAD).transpose(1, 0, 2).reshape(-1)
    return (
        output[:, None, :],
        input_grad[:, None, :],
        vectors[0],
        vectors[1],
        vectors[2],
        vectors[3],
        qkv_grad,
        b_qkv_grad,
        dense_grad,
        vectors[4],
        up_grad,
        b_up_grad,
        down_grad,
        vectors[4],
    )


def solution(mesh):
    in_specs = (
        P("rep", "shard", None),
        P("rep", "shard", None),
        P("rep", None),
        P("rep", None),
        P(),
        P(),
        P(),
        P(),
        P("shard", None),
        P(),
        P("shard", None),
        P(),
        P("shard", None),
        P(),
        P("shard", None),
        P(),
    )
    out_specs = (
        P("rep", "shard", None),
        P("rep", "shard", None),
        P(),
        P(),
        P(),
        P(),
        P("shard", None),
        P(),
        P("shard", None),
        P(),
        P("shard", None),
        P(),
        P("shard", None),
        P(),
    )
    body = split_shards if mesh.shape["shard"] == HEADS else shards
    return jax.shard_map(
        body, mesh=mesh, in_specs=in_specs, out_specs=out_specs, check_vma=False
    )
```

```python
import functools
import math

import jax
import jax.numpy as jnp
from jax import lax
from jax.experimental import pallas as pl
from jax.experimental.pallas import tpu as pltpu
from jax.sharding import PartitionSpec as P

HEADS = 8
HEAD = 256
ROT = 64


EPSILON = 1e-05
MASKED = -1e30


def layer_norm(vector, gain_vec, shift_vec):
    mean_val = jnp.mean(vector, axis=-1, keepdims=True)
    centered = vector - mean_val
    variance = jnp.mean(centered * centered, axis=-1, keepdims=True)
    return centered * lax.rsqrt(variance + EPSILON) * gain_vec + shift_vec


def gelu_exact(vector):
    return jax.nn.gelu(vector, approximate=False)


def rotary_tables(positions):
    half_rot = ROT // 2
    freq_index = jnp.arange(half_rot, dtype=jnp.float32)
    inverse_freq = jnp.exp(freq_index * (-2.0 * math.log(10000.0) / ROT))
    angles = positions[:, None] * inverse_freq[None, :]
    return (jnp.cos(angles), jnp.sin(angles))


def rotate(heads_in, cosine_table, sine_table):
    half_rot = ROT // 2
    first_half = heads_in[..., :half_rot]
    second_half = heads_in[..., half_rot:ROT]
    cos_wide = cosine_table[:, None, :]
    sin_wide = sine_table[:, None, :]
    return jnp.concatenate(
        [
            first_half * cos_wide - second_half * sin_wide,
            second_half * cos_wide + first_half * sin_wide,
            heads_in[..., ROT:],
        ],
        axis=-1,
    )


def stream_rows(lengths, seq_perm, shard_count):
    seq_range = jnp.arange(lengths.shape[0], dtype=jnp.int32)
    ranking = jnp.sum(
        jnp.where(seq_perm[:, None] == seq_range[None, :], seq_range[:, None], 0), axis=0
    )
    offsets = jnp.sum(jnp.where(ranking[None, :] < ranking[:, None], lengths[None, :], 0), axis=1)
    return (offsets // shard_count, lengths // shard_count)


def row_product(left, right):
    return jnp.dot(left.T, right, preferred_element_type=jnp.float32)


def block_mask(seq_flag, positions, live):
    return (
        live[:, None]
        & live[None, :]
        & (seq_flag[:, None] == seq_flag[None, :])
        & (positions[None, :] <= positions[:, None])
    )


def shards(
    tokens,
    cotangent,
    seq_lengths,
    seq_order,
    ln1_gain,
    ln1_bias,
    ln2_gain,
    ln2_bias,
    w_qkv,
    b_qkv,
    w_dense,
    b_dense,
    w_up,
    b_up,
    w_down,
    b_down,
):
    shard_count = lax.axis_size("shard")
    my_index = lax.axis_index("shard")
    inputs = tokens[:, 0, :].astype(jnp.float32)
    grad_out = cotangent[:, 0, :]
    local_rows, width = inputs.shape
    slot_rows = 2 * (local_rows // shard_count) - 4
    buffer_rows = slot_rows * shard_count
    row_offsets, row_counts = stream_rows(seq_lengths[0], seq_order[0], shard_count)
    first_count = row_counts[0::2]
    second_count = row_counts[1::2]
    first_start = row_offsets[0::2]
    second_start = row_offsets[1::2]
    slot_range = jnp.arange(slot_rows, dtype=jnp.int32)[None, :]
    in_first = slot_range < first_count[:, None]
    slot_live = slot_range < (first_count + second_count)[:, None]
    source_rows = jnp.where(
        in_first,
        first_start[:, None] + slot_range,
        second_start[:, None] + slot_range - first_count[:, None],
    )
    source_rows = jnp.where(slot_live, source_rows, 0)
    seq_range = jnp.arange(row_counts.shape[0], dtype=jnp.int32)
    parity = seq_range % 2
    slot_base = seq_range // 2 * slot_rows + parity * row_counts[seq_range - parity] - row_offsets
    token_range = jnp.arange(local_rows, dtype=jnp.int32)[:, None]
    member = (token_range >= row_offsets[None, :]) & (
        token_range < (row_offsets + row_counts)[None, :]
    )
    return_rows = token_range[:, 0] + jnp.sum(jnp.where(member, slot_base[None, :], 0), axis=1)
    own_first = first_count[my_index]
    own_second = second_count[my_index]
    buffer_range = jnp.arange(buffer_rows, dtype=jnp.int32)
    slot_index = buffer_range % slot_rows
    source_index = buffer_range // slot_rows
    seq_flag = (slot_index >= own_first).astype(jnp.int32)
    positions = (slot_index - seq_flag * own_first) * shard_count + source_index
    live = slot_index < own_first + own_second
    attn_full, dense_full = (
        lax.all_gather(w_qkv, "shard", axis=0, tiled=True),
        lax.all_gather(w_dense, "shard", axis=0, tiled=True),
    )
    up_full, down_full = (
        lax.all_gather(w_up, "shard", axis=0, tiled=True),
        lax.all_gather(w_down, "shard", axis=0, tiled=True),
    )
    normed_one_wide, pull_one = jax.vjp(layer_norm, inputs, ln1_gain, ln1_bias)
    normed_two_wide, pull_two = jax.vjp(layer_norm, inputs, ln2_gain, ln2_bias)
    normed_one = normed_one_wide.astype(jnp.bfloat16)
    normed_two = normed_two_wide.astype(jnp.bfloat16)
    qkv = (jnp.dot(normed_one, attn_full, preferred_element_type=jnp.float32) + b_qkv).astype(
        jnp.bfloat16
    )
    arrived = lax.all_to_all(
        jnp.take(qkv, source_rows, axis=0), "shard", split_axis=0, concat_axis=0, tiled=True
    )
    arrived = arrived.reshape(buffer_rows, 3 * width)
    heads_shape = (buffer_rows, HEADS, HEAD)
    cosine_table, sine_table = rotary_tables(positions.astype(jnp.float32))

    def rotate_here(heads_in):
        return rotate(heads_in, cosine_table, sine_table)

    query_wide, pull_query = jax.vjp(
        rotate_here, arrived[:, :width].astype(jnp.float32).reshape(heads_shape)
    )
    key_wide, pull_key = jax.vjp(
        rotate_here, arrived[:, width : 2 * width].astype(jnp.float32).reshape(heads_shape)
    )
    rotated_queries = query_wide.astype(jnp.bfloat16)
    rotated_keys = key_wide.astype(jnp.bfloat16)
    value_heads = arrived[:, 2 * width :].reshape(heads_shape)
    sources_per = shard_count
    while sources_per > 1 and sources_per * slot_rows > 1024:
        sources_per = sources_per // 2
    block_rows = sources_per * slot_rows
    block_total = buffer_rows // block_rows
    score_scale = HEAD ** (-0.5)

    def forward_block(block_index):
        allowed = block_mask(seq_flag, positions, live)
        scores = (
            jnp.einsum(
                "qhe,khe->hqk", rotated_queries, rotated_keys, preferred_element_type=jnp.float32
            )
            * score_scale
        )
        scores = jnp.where(allowed[None], scores, MASKED)
        row_max = jnp.max(scores, axis=-1, keepdims=True)
        exp_scores = jnp.exp(scores - row_max)
        exp_total = jnp.sum(exp_scores, axis=-1, keepdims=True)
        attn_probs = jnp.where(allowed[None], exp_scores / exp_total, 0.0)
        attended_blk = jnp.einsum(
            "hqk,khe->qhe",
            attn_probs.astype(jnp.bfloat16),
            value_heads,
            preferred_element_type=jnp.float32,
        )
        return (attended_blk.astype(jnp.bfloat16), row_max[..., 0] + jnp.log(exp_total[..., 0]))

    attended_blocks, log_totals = lax.map(forward_block, jnp.arange(block_total, dtype=jnp.int32))
    attended_slots = attended_blocks.reshape(shard_count, slot_rows, width)
    attn_back = lax.all_to_all(
        attended_slots, "shard", split_axis=0, concat_axis=0, tiled=True
    ).reshape(buffer_rows, width)
    attn_in = jnp.take(attn_back, return_rows, axis=0)
    attn_out = jnp.dot(attn_in, dense_full, preferred_element_type=jnp.float32) + b_dense
    pre_up = jnp.dot(normed_two, up_full, preferred_element_type=jnp.float32) + b_up
    activated_wide, pull_gelu = jax.vjp(gelu_exact, pre_up)
    activated = activated_wide.astype(jnp.bfloat16)
    mlp_out = jnp.dot(activated, down_full, preferred_element_type=jnp.float32) + b_down
    output = (inputs + attn_out + mlp_out).astype(jnp.bfloat16)
    attn_second, dense_second = (
        lax.all_gather(w_qkv, "shard", axis=0, tiled=True),
        lax.all_gather(w_dense, "shard", axis=0, tiled=True),
    )
    up_second, down_second = (
        lax.all_gather(w_up, "shard", axis=0, tiled=True),
        lax.all_gather(w_down, "shard", axis=0, tiled=True),
    )
    grad_attended = jnp.dot(grad_out, dense_second.T, preferred_element_type=jnp.float32).astype(
        jnp.bfloat16
    )
    grad_slots = jnp.where(
        slot_live[:, :, None],
        jnp.take(grad_attended, source_rows, axis=0),
        jnp.zeros((), jnp.bfloat16),
    )
    grad_heads = lax.all_to_all(
        grad_slots, "shard", split_axis=0, concat_axis=0, tiled=True
    ).reshape(heads_shape)

    def backward_block(carried, block_index):
        grad_keys, grad_values = carried
        allowed = block_mask(seq_flag, positions, live)
        scores = (
            jnp.einsum(
                "qhe,khe->hqk", rotated_queries, rotated_keys, preferred_element_type=jnp.float32
            )
            * score_scale
        )
        attn_probs = jnp.where(
            allowed[None], jnp.exp(scores - log_totals[block_index][..., None]), 0.0
        )
        grad_probs = jnp.einsum(
            "qhe,khe->hqk", grad_heads, value_heads, preferred_element_type=jnp.float32
        )
        row_delta = jnp.sum(attn_probs * grad_probs, axis=-1, keepdims=True)
        grad_scores = (attn_probs * (grad_probs - row_delta)).astype(jnp.bfloat16)
        grad_query = (
            jnp.einsum(
                "hqk,khe->qhe", grad_scores, rotated_keys, preferred_element_type=jnp.float32
            )
            * score_scale
        )
        grad_keys = (
            grad_keys
            + jnp.einsum(
                "hqk,qhe->khe", grad_scores, rotated_queries, preferred_element_type=jnp.float32
            )
            * score_scale
        )
        grad_values = grad_values + jnp.einsum(
            "hqk,qhe->khe",
            attn_probs.astype(jnp.bfloat16),
            grad_heads,
            preferred_element_type=jnp.float32,
        )
        return ((grad_keys, grad_values), grad_query)

    zero_heads = jnp.zeros(heads_shape, jnp.float32)
    (grad_keys, grad_values), grad_query_blocks = lax.scan(
        backward_block, (zero_heads, zero_heads), jnp.arange(block_total, dtype=jnp.int32)
    )
    grad_q_pre = pull_query(grad_query_blocks.reshape(heads_shape))[0]
    grad_k_pre = pull_key(grad_keys)[0]
    grad_qkv_slots = jnp.concatenate(
        [
            grad_q_pre.reshape(buffer_rows, width),
            grad_k_pre.reshape(buffer_rows, width),
            grad_values.reshape(buffer_rows, width),
        ],
        axis=1,
    ).astype(jnp.bfloat16)
    grad_qkv_slots = grad_qkv_slots.reshape(shard_count, slot_rows, 3 * width)
    grad_qkv_back = lax.all_to_all(grad_qkv_slots, "shard", split_axis=0, concat_axis=0, tiled=True)
    grad_qkv = jnp.take(grad_qkv_back.reshape(buffer_rows, 3 * width), return_rows, axis=0)
    grad_activated = jnp.dot(grad_out, down_second.T, preferred_element_type=jnp.float32)
    grad_pre = pull_gelu(grad_activated)[0].astype(jnp.bfloat16)
    grad_normed_one = jnp.dot(grad_qkv, attn_second.T, preferred_element_type=jnp.float32)
    grad_normed_two = jnp.dot(grad_pre, up_second.T, preferred_element_type=jnp.float32)
    grad_in_one, grad_gain_one, grad_bias_one = pull_one(grad_normed_one)
    grad_in_two, grad_gain_two, grad_bias_two = pull_two(grad_normed_two)
    input_grad = grad_out.astype(jnp.float32) + grad_in_one + grad_in_two
    qkv_rows = lax.psum_scatter(
        row_product(normed_one, grad_qkv).astype(jnp.bfloat16),
        "shard",
        scatter_dimension=0,
        tiled=True,
    ).astype(jnp.float32)
    dense_rows = lax.psum_scatter(
        row_product(attn_in, grad_out).astype(jnp.bfloat16),
        "shard",
        scatter_dimension=0,
        tiled=True,
    ).astype(jnp.float32)
    up_rows = lax.psum_scatter(
        row_product(normed_two, grad_pre).astype(jnp.bfloat16),
        "shard",
        scatter_dimension=0,
        tiled=True,
    ).astype(jnp.float32)
    down_rows = lax.psum_scatter(
        row_product(activated, grad_out).astype(jnp.bfloat16),
        "shard",
        scatter_dimension=0,
        tiled=True,
    ).astype(jnp.float32)
    qkv_rows, dense_rows, up_rows, down_rows = (
        lax.psum(qkv_rows.astype(jnp.bfloat16), "rep").astype(jnp.float32),
        lax.psum(dense_rows.astype(jnp.bfloat16), "rep").astype(jnp.float32),
        lax.psum(up_rows.astype(jnp.bfloat16), "rep").astype(jnp.float32),
        lax.psum(down_rows.astype(jnp.bfloat16), "rep").astype(jnp.float32),
    )
    out_column_sum = jnp.sum(grad_out, axis=0, dtype=jnp.float32)
    small_totals = lax.psum(
        (
            grad_gain_one,
            grad_bias_one,
            grad_gain_two,
            grad_bias_two,
            jnp.sum(grad_qkv, axis=0, dtype=jnp.float32),
            out_column_sum,
            jnp.sum(grad_pre, axis=0, dtype=jnp.float32),
        ),
        ("rep", "shard"),
    )
    return (
        output[:, None, :],
        input_grad[:, None, :],
        small_totals[0],
        small_totals[1],
        small_totals[2],
        small_totals[3],
        qkv_rows,
        small_totals[4],
        dense_rows,
        small_totals[5],
        up_rows,
        small_totals[6],
        down_rows,
        small_totals[5],
    )


TILE_ROWS = 32
BIG_VMEM = 56 << 20
SMALL_COST = pl.CostEstimate(flops=1 << 20, bytes_accessed=1 << 20, transcendentals=0)
F32 = jnp.float32
BF16 = jnp.bfloat16


def flip(value, axis, bit):
    size = lax.axis_size(axis)
    return lax.ppermute(value, axis, [(i, i ^ bit) for i in range(size)])


def send(value, pairs):
    return lax.ppermute(value, "shard", [(2 * a + y, 2 * b + y) for a, b in pairs for y in (0, 1)])


MIDDLE = ((1, 2), (2, 1))
OUTWARD = ((1, 0), (2, 3))
INWARD = ((0, 1), (3, 2))


def plus(*terms):
    total = terms[0].astype(F32)
    for term in terms[1:]:
        total = total + term.astype(F32)
    return total


def hold(values, gates):
    return lax.optimization_barrier(tuple(values) + tuple(gates))[: len(values)]


def turn(heads_in, cosine, sine):
    left = heads_in[:, :128]
    lane = lax.broadcasted_iota(jnp.int32, left.shape, 1)
    half = ROT // 2
    partner = jnp.where(lane < half, pltpu.roll(left, 128 - half, 1), pltpu.roll(left, half, 1))
    return jnp.concatenate([left * cosine + partner * sine, heads_in[:, 128:]], axis=1)


def token_labels(my_index, shape, dim):
    inner = lax.broadcasted_iota(jnp.int32, shape, dim)
    block = inner // TILE_ROWS
    apart = block // 4 * 4 + block % 2 * 2 + block // 2 % 2
    return (inner % TILE_ROWS) * HEADS + jnp.bitwise_xor(apart, my_index)


def tile_weights(tile, seq_ref, query, key_tiles, count):
    tile_tokens = TILE_ROWS * HEADS
    my_index = seq_ref[count]
    query_label = token_labels(my_index, (tile_tokens, 1), 0) + tile * tile_tokens
    key_label = token_labels(my_index, (1, tile_tokens), 1)
    scores = []
    for place, key in key_tiles:
        label = key_label + place * tile_tokens
        last = jnp.full(label.shape, 1 << 30, jnp.int32)
        for k in range(count):
            last = jnp.minimum(last, jnp.where(label < seq_ref[k], seq_ref[k], 1 << 30))
        allowed = query_label < last
        if place == tile:
            allowed = allowed & (label <= query_label)
        product = lax.dot_general(query, key, (((1,), (1,)), ((), ())), preferred_element_type=F32)
        scores.append(jnp.where(allowed, product * HEAD ** (-0.5), MASKED))
    scores = jnp.concatenate(scores, axis=1)
    exp_scores = jnp.exp(scores - jnp.max(scores, axis=1, keepdims=True))
    return exp_scores * (1.0 / jnp.sum(exp_scores, axis=1, keepdims=True))


def attend_kernel(seq_ref, qkv_ref, cos_ref, sin_ref, out_ref, query_ref, key_ref):
    tiles = query_ref.shape[0]
    tile_tokens = TILE_ROWS * HEADS

    def part(tile, lane):
        rows = qkv_ref[:, tile * TILE_ROWS : (tile + 1) * TILE_ROWS, lane : lane + HEAD]
        return rows.reshape(tile_tokens, HEAD)

    for tile in range(tiles):
        cosine, sine = cos_ref[tile], sin_ref[tile]
        query = turn(part(tile, 0).astype(F32), cosine, sine).astype(BF16)
        query_ref[tile] = query
        key_ref[tile] = turn(part(tile, HEAD).astype(F32), cosine, sine).astype(BF16)
        near = list(range(max(tile - 2, 0), tile + 1))
        probs = tile_weights(
            tile, seq_ref, query, [(k, key_ref[k]) for k in near], seq_ref.shape[0] - 1
        ).astype(BF16)
        total = jnp.zeros((tile_tokens, HEAD), F32)
        for at, k in enumerate(near):
            total = total + jnp.dot(
                probs[:, at * tile_tokens : (at + 1) * tile_tokens],
                part(k, 2 * HEAD),
                preferred_element_type=F32,
            )
        out_ref[:, tile * TILE_ROWS : (tile + 1) * TILE_ROWS, :] = total.astype(BF16).reshape(
            HEADS, TILE_ROWS, HEAD
        )


def attend_back_kernel(
    seq_ref, qkv_ref, grad_ref, cos_ref, sin_ref, query_ref, key_ref, out_ref, sum_ref, gk_ref, gv_ref
):
    tiles = query_ref.shape[0]
    tile_tokens = TILE_ROWS * HEADS
    scale = HEAD ** (-0.5)
    over_rows = (((0,), (0,)), ((), ()))
    over_lanes = (((1,), (1,)), ((), ()))

    def rows_of(tile):
        return slice(tile * TILE_ROWS, (tile + 1) * TILE_ROWS)

    def put(tile, lane, value):
        low = value.astype(BF16)
        out_ref[:, rows_of(tile), lane : lane + HEAD] = low.reshape(HEADS, TILE_ROWS, HEAD)
        columns = jnp.sum(low.astype(F32), axis=0, keepdims=True)
        if tile == 0:
            sum_ref[:, lane : lane + HEAD] = columns
        else:
            sum_ref[:, lane : lane + HEAD] += columns

    def finish(tile):
        put(tile, HEAD, turn(gk_ref[tile] * scale, cos_ref[tile], -sin_ref[tile]))
        put(tile, 2 * HEAD, gv_ref[tile])

    for tile in range(tiles):
        query = query_ref[tile]
        near = list(range(max(tile - 2, 0), tile + 1))
        grad = grad_ref[:, rows_of(tile), :].reshape(tile_tokens, HEAD)
        probs = tile_weights(
            tile, seq_ref, query, [(k, key_ref[k]) for k in near], seq_ref.shape[0] - 1
        )
        grad_probs = jnp.concatenate(
            [
                lax.dot_general(
                    grad,
                    qkv_ref[:, rows_of(k), 2 * HEAD :].reshape(tile_tokens, HEAD),
                    over_lanes,
                    preferred_element_type=F32,
                )
                for k in near
            ],
            axis=1,
        )
        delta = jnp.sum(probs * grad_probs, axis=1, keepdims=True)
        grad_scores = (probs * (grad_probs - delta)).astype(BF16)
        probs = probs.astype(BF16)
        grad_query = jnp.zeros((tile_tokens, HEAD), F32)
        for at, k in enumerate(near):
            span = slice(at * tile_tokens, (at + 1) * tile_tokens)
            grad_query = grad_query + jnp.dot(
                grad_scores[:, span], key_ref[k], preferred_element_type=F32
            )
            to_key = lax.dot_general(
                grad_scores[:, span], query, over_rows, preferred_element_type=F32
            )
            to_value = lax.dot_general(probs[:, span], grad, over_rows, preferred_element_type=F32)
            if k == tile:
                gk_ref[k] = to_key
                gv_ref[k] = to_value
            else:
                gk_ref[k] += to_key
                gv_ref[k] += to_value
        put(tile, 0, turn(grad_query * scale, cos_ref[tile], -sin_ref[tile]))
        if tile >= 2:
            finish(tile - 2)
    for tile in range(max(tiles - 2, 0), tiles):
        finish(tile)


VMEM_SPEC = pl.BlockSpec(memory_space=pltpu.VMEM)
SMEM_SPEC = pl.BlockSpec(memory_space=pltpu.SMEM)


def attend(seq_scalars, qkv, cosine, sine):
    blocks, rows, _ = qkv.shape
    tiled = (rows // TILE_ROWS, blocks * TILE_ROWS, HEAD)
    return pl.pallas_call(
        attend_kernel,
        out_shape=(
            jax.ShapeDtypeStruct((blocks, rows, HEAD), BF16),
            jax.ShapeDtypeStruct(tiled, BF16),
            jax.ShapeDtypeStruct(tiled, BF16),
        ),
        in_specs=[SMEM_SPEC, VMEM_SPEC, VMEM_SPEC, VMEM_SPEC],
        out_specs=(VMEM_SPEC, VMEM_SPEC, VMEM_SPEC),
        compiler_params=pltpu.CompilerParams(vmem_limit_bytes=48 << 20),
        cost_estimate=SMALL_COST,
    )(seq_scalars, qkv, cosine, sine)


def attend_back(seq_scalars, qkv, grad, cosine, sine, query, key):
    blocks, rows, wide = qkv.shape
    return pl.pallas_call(
        attend_back_kernel,
        out_shape=(
            jax.ShapeDtypeStruct((blocks, rows, wide), BF16),
            jax.ShapeDtypeStruct((1, wide), F32),
        ),
        in_specs=[SMEM_SPEC] + [VMEM_SPEC] * 6,
        out_specs=(VMEM_SPEC, VMEM_SPEC),
        scratch_shapes=[pltpu.VMEM(query.shape, F32), pltpu.VMEM(query.shape, F32)],
        compiler_params=pltpu.CompilerParams(vmem_limit_bytes=48 << 20),
        cost_estimate=SMALL_COST,
    )(seq_scalars, qkv, grad, cosine, sine, query, key)


def place_weights_kernel(
    at_ref, p0_ref, p1_ref, p2_ref, p3_ref, gain_ref, shift_ref, *out_refs, hidden
):
    raw_refs, scaled_refs, sum_ref = out_refs[:2], out_refs[2:4], out_refs[4]
    quarter, wide = p0_ref.shape[1:]

    @pl.when(pl.program_id(0) == 0)
    def _():
        sum_ref[...] = jnp.zeros_like(sum_ref)

    for k, part_ref in enumerate((p0_ref, p1_ref, p2_ref, p3_ref)):
        rows = pl.ds(pl.multiple_of((at_ref[1] ^ k) * quarter, quarter), quarter)
        for norm, columns in ((1, slice(0, hidden)), (0, slice(hidden, wide))):
            raw = part_ref[0, :, columns]
            raw_refs[1 - norm][rows, :] = raw
            weight = raw.astype(F32)
            gain, shift = gain_ref[rows, norm : norm + 1], shift_ref[rows, norm : norm + 1]
            scaled_refs[1 - norm][rows, :] = (weight * gain).astype(BF16)
            sum_ref[:, columns] += jnp.sum(weight * shift, axis=0, keepdims=True)


def place_weights(me, rep, parts, gains, shifts, hidden):
    count, rows, wide = parts[0].shape
    widths = (hidden, wide - hidden) * 2
    pair = pl.BlockSpec((4 * rows, 2), lambda i, at_ref: (i ^ at_ref[0], 0))
    part = pl.BlockSpec((1, rows, wide), lambda i, at_ref: (i, 0, 0))
    return pl.pallas_call(
        functools.partial(place_weights_kernel, hidden=hidden),
        out_shape=tuple(jax.ShapeDtypeStruct((count * 4 * rows, n), BF16) for n in widths)
        + (jax.ShapeDtypeStruct((1, wide), F32),),
        grid_spec=pltpu.PrefetchScalarGridSpec(
            num_scalar_prefetch=1,
            grid=(count,),
            in_specs=[part] * 4 + [pair, pair],
            out_specs=tuple(
                pl.BlockSpec((4 * rows, n), lambda i, at_ref: (i ^ at_ref[0], 0)) for n in widths
            )
            + (pl.BlockSpec((1, wide), lambda i, at_ref: (0, 0)),),
        ),
        compiler_params=pltpu.CompilerParams(vmem_limit_bytes=32 << 20),
        cost_estimate=SMALL_COST,
    )(jnp.stack([me, rep]).astype(jnp.int32), *parts, gains, shifts)


def place_grads_kernel(at_ref, p0_ref, p1_ref, p2_ref, p3_ref, out_ref, *, pieces):
    quarter, wide = p0_ref.shape[1:]
    source = pl.program_id(0) ^ at_ref[0]
    size = wide // pieces
    for k, part_ref in enumerate((p0_ref, p1_ref, p2_ref, p3_ref)):
        rows = pl.ds(pl.multiple_of((at_ref[1] ^ k) * quarter, quarter), quarter)
        values = part_ref[0].astype(F32)
        if pieces == 1:
            out_ref[rows, :] = values
        else:
            for j in range(pieces):
                start = pl.multiple_of((j * HEADS + source) * size, size)
                out_ref[rows, pl.ds(start, size)] = values[:, j * size : (j + 1) * size]


def place_grads(me, rep, parts, pieces):
    count, rows, wide = parts[0].shape
    part = pl.BlockSpec((1, rows, wide), lambda i, at_ref: (i, 0, 0))
    if pieces == 1:
        out = pl.BlockSpec((4 * rows, wide), lambda i, at_ref: (0, i ^ at_ref[0]))
    else:
        out = pl.BlockSpec((4 * rows, count * wide), lambda i, at_ref: (0, 0))
    return pl.pallas_call(
        functools.partial(place_grads_kernel, pieces=pieces),
        out_shape=jax.ShapeDtypeStruct((4 * rows, count * wide), F32),
        grid_spec=pltpu.PrefetchScalarGridSpec(
            num_scalar_prefetch=1, grid=(count,), in_specs=[part] * 4, out_specs=out
        ),
        compiler_params=pltpu.CompilerParams(vmem_limit_bytes=40 << 20),
        cost_estimate=SMALL_COST,
    )(jnp.stack([me, rep]).astype(jnp.int32), *parts)


def place_halves_kernel(core_ref, mine_ref, other_ref, down_ref, dense_ref, *, cut):
    half = mine_ref.shape[1]

    def fill(out_ref):
        for part_ref, core in ((mine_ref, core_ref[0]), (other_ref, 1 - core_ref[0])):
            start = pl.multiple_of(core * half, half)
            out_ref[:, pl.ds(start, half)] = part_ref[...].astype(F32)

    @pl.when(pl.program_id(0) < cut)
    def _():
        fill(down_ref)

    @pl.when(pl.program_id(0) >= cut)
    def _():
        fill(dense_ref)


def place_halves(core, mine, other, hidden):
    rows, half = mine.shape
    tile = 256
    cut = hidden // tile
    part = pl.BlockSpec((tile, half), lambda i, core_ref: (i, 0))
    return pl.pallas_call(
        functools.partial(place_halves_kernel, cut=cut),
        out_shape=(
            jax.ShapeDtypeStruct((hidden, 2 * half), F32),
            jax.ShapeDtypeStruct((rows - hidden, 2 * half), F32),
        ),
        grid_spec=pltpu.PrefetchScalarGridSpec(
            num_scalar_prefetch=1,
            grid=(rows // tile,),
            in_specs=[part, part],
            out_specs=(
                pl.BlockSpec((tile, 2 * half), lambda i, core_ref: (jnp.minimum(i, cut - 1), 0)),
                pl.BlockSpec((tile, 2 * half), lambda i, core_ref: (jnp.maximum(i - cut, 0), 0)),
            ),
        ),
        compiler_params=pltpu.CompilerParams(vmem_limit_bytes=32 << 20),
        cost_estimate=SMALL_COST,
    )(core[None].astype(jnp.int32), mine, other)


def normalize(values):
    values = values.astype(F32)
    centered = values - jnp.mean(values, axis=-1, keepdims=True)
    rstd = lax.rsqrt(jnp.mean(centered * centered, axis=-1, keepdims=True) + EPSILON)
    return centered * rstd, rstd


def norm_kernel(*refs, count, steps):
    blocks, out_ref = refs[:count], refs[-1]
    for k in range(count):

        @pl.when(pl.program_id(0) // steps == k)
        def _(block_ref=blocks[k]):
            out_ref[...] = normalize(block_ref[...])[0].astype(BF16)


def norm_blocks(blocks, places, buffer):
    rows, width = blocks[0].shape
    steps = 2
    tile = rows // steps
    count = len(blocks)

    def spec(k):
        return pl.BlockSpec((tile, width), lambda i: (jnp.clip(i - steps * k, 0, steps - 1), 0))

    def put(i):
        place = places[0]
        for k in range(1, count):
            place = jnp.where(i // steps >= k, places[k], place)
        return place * steps + i % steps, 0

    extra = [] if buffer is None else [buffer]
    return pl.pallas_call(
        functools.partial(norm_kernel, count=count, steps=steps),
        out_shape=jax.ShapeDtypeStruct((HEADS * rows, width), BF16),
        grid=(count * steps,),
        in_specs=[spec(k) for k in range(count)] + [pl.BlockSpec(memory_space=pl.ANY)] * len(extra),
        out_specs=pl.BlockSpec((tile, width), put),
        input_output_aliases={count: 0} if extra else {},
        cost_estimate=SMALL_COST,
    )(*blocks, *extra)


def dot32(left, right, left_dim=1, right_dim=0):
    return lax.dot_general(
        left, right, (((left_dim,), (right_dim,)), ((), ())), preferred_element_type=F32
    )


def tokens_spec(tile, width, first):
    return pl.BlockSpec((tile, width), lambda i: (first + i, 0))


def whole_spec(shape):
    return pl.BlockSpec(shape, lambda i: (0, 0), pipeline_mode=pl.Buffered(1))


def block_specs(count, tile, width):
    return [pl.BlockSpec((tile, width), lambda i: (0, 0)) for _ in range(count)]


def project_kernel(normed_ref, up_ref, qkv_w_ref, shift_ref, *refs):
    act_ref, slope_ref, qkv_ref = refs[-3:]
    hidden = act_ref.shape[1]
    lanes = 256
    for start in range(0, hidden, lanes):
        columns = slice(start, start + lanes)
        value = dot32(normed_ref[...], up_ref[:, columns]) + shift_ref[:, columns]
        normal = 0.5 + 0.5 * lax.erf(value * (0.5**0.5))
        bell = jnp.exp(value * value * -0.5) * ((2.0 * math.pi) ** -0.5)
        act_ref[:, columns] = (value * normal).astype(BF16)
        slope_ref[:, columns] = (normal + value * bell).astype(BF16)
    for start in range(0, qkv_ref.shape[1], lanes):
        columns = slice(start, start + lanes)
        value = dot32(normed_ref[...], qkv_w_ref[:, columns])
        value = value + shift_ref[:, hidden + start : hidden + start + lanes]
        qkv_ref[:, columns] = value.astype(BF16)


def project(normed, w_up, w_qkv, shift, first, last, buffers):
    count, width = normed.shape
    tile = 2 * count // HEADS
    widths = (w_up.shape[1], w_up.shape[1], w_qkv.shape[1])
    return pl.pallas_call(
        project_kernel,
        out_shape=tuple(jax.ShapeDtypeStruct((count, n), BF16) for n in widths),
        grid=(last - first,),
        in_specs=[
            tokens_spec(tile, width, first),
            whole_spec(w_up.shape),
            whole_spec(w_qkv.shape),
            whole_spec(shift.shape),
        ]
        + [pl.BlockSpec(memory_space=pl.ANY)] * len(buffers),
        out_specs=tuple(tokens_spec(tile, n, first) for n in widths),
        input_output_aliases={4 + k: k for k in range(len(buffers))},
        compiler_params=pltpu.CompilerParams(vmem_limit_bytes=BIG_VMEM),
        cost_estimate=SMALL_COST,
    )(normed, w_up, w_qkv, shift, *buffers)


def combine_kernel(one_a_ref, one_b_ref, two_a_ref, two_b_ref, w_one_ref, w_two_ref, *out_refs, right_dim):
    rows = out_refs[0].shape[0]
    for pair, (one_ref, two_ref) in enumerate(((one_a_ref, two_a_ref), (one_b_ref, two_b_ref))):
        value = dot32(one_ref[...], w_one_ref[...], 1, right_dim)
        value = value + dot32(two_ref[...], w_two_ref[...], 1, right_dim)
        out_refs[2 * pair][...] = value[:rows].astype(BF16)
        out_refs[2 * pair + 1][...] = value[rows:].astype(BF16)


def combine(one, two, w_one, w_two, rows, side, right_dim):
    width = w_one.shape[1 - right_dim]
    lanes = 256

    def weight_spec(weight):
        if right_dim:
            return pl.BlockSpec((lanes, weight.shape[1]), lambda i: (i, 0))
        return pl.BlockSpec((weight.shape[0], lanes), lambda i: (0, i))

    def left_spec(left, pair):
        return pl.BlockSpec(
            (2 * rows, left.shape[1]),
            lambda i: (2 * pair + side, 0),
            pipeline_mode=pl.Buffered(1),
        )

    return pl.pallas_call(
        functools.partial(combine_kernel, right_dim=right_dim),
        out_shape=tuple(jax.ShapeDtypeStruct((rows, width), BF16) for _ in range(4)),
        grid=(width // lanes,),
        in_specs=[left_spec(left, pair) for left in (one, two) for pair in (0, 1)]
        + [weight_spec(w_one), weight_spec(w_two)],
        out_specs=tuple(pl.BlockSpec((rows, lanes), lambda i: (0, i)) for _ in range(4)),
        compiler_params=pltpu.CompilerParams(vmem_limit_bytes=BIG_VMEM),
        cost_estimate=SMALL_COST,
    )(one, one, two, two, w_one, w_two)


def pull_kernel(*refs, count):
    blocks, (w_one_ref, w_two_ref, slope_ref) = refs[:count], refs[count : count + 3]
    pre_ref, att_ref, sum_ref, left_ref, sems = refs[-5:]
    rows = blocks[0].shape[0]
    last = pl.num_programs(0) - 1

    @pl.when(pl.program_id(0) == 0)
    def _():
        copies = [
            pltpu.make_async_copy(block, left_ref.at[pl.ds(k * rows, rows)], sems.at[k])
            for k, block in enumerate(blocks)
        ]
        for copy in copies:
            copy.start()
        for copy in copies:
            copy.wait()

    @pl.when(pl.program_id(0) < last)
    def _():
        value = dot32(left_ref[...], w_one_ref[...], 1, 1)
        value = (value * slope_ref[...].astype(F32)).astype(BF16)
        pre_ref[...] = value
        sum_ref[...] = jnp.sum(value.astype(F32), axis=0, keepdims=True)

    @pl.when(pl.program_id(0) == last)
    def _():
        att_ref[...] = dot32(left_ref[...], w_two_ref[...], 1, 1).astype(BF16)


def pull(blocks, w_down, w_dense, slope, part, buffers):
    rows, width = blocks[0].shape
    hidden, head = w_down.shape[0], w_dense.shape[0]
    tokens = HEADS * rows
    count = len(blocks)
    lanes = 256
    steps = hidden // lanes

    def at(i):
        return jnp.minimum(i, steps - 1)

    anywhere = pl.BlockSpec(memory_space=pl.ANY)
    return pl.pallas_call(
        functools.partial(pull_kernel, count=count),
        out_shape=(
            jax.ShapeDtypeStruct((tokens, hidden), BF16),
            jax.ShapeDtypeStruct((tokens, head), BF16),
            jax.ShapeDtypeStruct((1, hidden), F32),
        ),
        grid=(steps + 1,),
        in_specs=[anywhere] * count
        + [
            pl.BlockSpec((lanes, width), lambda i: (at(i), 0)),
            whole_spec(w_dense.shape),
            pl.BlockSpec((count * rows, lanes), lambda i: (part, at(i))),
        ]
        + [anywhere] * len(buffers),
        out_specs=(
            pl.BlockSpec((count * rows, lanes), lambda i: (part, at(i))),
            pl.BlockSpec((count * rows, head), lambda i: (part, 0)),
            pl.BlockSpec((1, lanes), lambda i: (0, at(i))),
        ),
        scratch_shapes=[pltpu.VMEM((count * rows, width), BF16), pltpu.SemaphoreType.DMA((count,))],
        input_output_aliases={count + 3 + k: k for k in range(len(buffers))},
        compiler_params=pltpu.CompilerParams(vmem_limit_bytes=BIG_VMEM),
        cost_estimate=SMALL_COST,
    )(*blocks, w_down, w_dense, slope, *buffers)


def moments_kernel(
    core_ref,
    normed_ref,
    right_ref,
    weight_ref,
    gain_ref,
    shift_ref,
    columns_ref,
    keep_ref,
    give_ref,
    sums_ref,
    low_ref,
    *,
    quarter,
):
    lanes = 256
    turned = normed_ref[...].T
    gain, shift = gain_ref[...], shift_ref[...]
    gain_terms, bias_terms = None, None
    for start in range(0, low_ref.shape[1], lanes):
        columns = slice(start, start + lanes)
        moment = dot32(turned, right_ref[:, columns])
        weight = weight_ref[:, columns].astype(F32)
        total = columns_ref[:, columns]
        low_ref[:, columns] = (moment * gain + shift * total).astype(BF16)
        one, two = moment * weight, weight * total
        gain_terms = one if gain_terms is None else gain_terms + one
        bias_terms = two if bias_terms is None else bias_terms + two
    sums_ref[:, 0:1] = jnp.sum(gain_terms, axis=1, keepdims=True)
    sums_ref[:, 1:2] = jnp.sum(bias_terms, axis=1, keepdims=True)
    for core in (0, 1):

        @pl.when(core_ref[0] == core)
        def _(core=core):
            for k in range(low_ref.shape[0] // quarter):
                target = keep_ref if k % 2 == core else give_ref
                target[k // 2 * quarter : (k // 2 + 1) * quarter, :] = low_ref[
                    k * quarter : (k + 1) * quarter, :
                ]


def moments_of(core, normed, right, weight, gain, shift, columns, quarter):
    count, width = normed.shape
    wide = weight.shape[1]
    tile = 8 * quarter
    return pl.pallas_call(
        functools.partial(moments_kernel, quarter=quarter),
        out_shape=(
            jax.ShapeDtypeStruct((width // 2, wide), BF16),
            jax.ShapeDtypeStruct((width // 2, wide), BF16),
            jax.ShapeDtypeStruct((width, 2), F32),
        ),
        grid=(width // tile,),
        in_specs=[
            SMEM_SPEC,
            pl.BlockSpec((count, tile), lambda i: (0, i)),
            whole_spec(right.shape),
            tokens_spec(tile, wide, 0),
            tokens_spec(tile, 1, 0),
            tokens_spec(tile, 1, 0),
            whole_spec(columns.shape),
        ],
        out_specs=(
            tokens_spec(tile // 2, wide, 0),
            tokens_spec(tile // 2, wide, 0),
            tokens_spec(tile, 2, 0),
        ),
        scratch_shapes=[pltpu.VMEM((tile, wide), BF16)],
        compiler_params=pltpu.CompilerParams(vmem_limit_bytes=BIG_VMEM),
        cost_estimate=SMALL_COST,
    )(core[None].astype(jnp.int32), normed, right, weight, gain, shift, columns)


def outer_kernel(core_ref, act_ref, att_ref, *refs):
    blocks, out_refs = refs[:HEADS], refs[HEADS:]
    rows = blocks[0].shape[0]
    lanes = 512
    last = pl.num_programs(1) - 1

    def fill(left_ref, out_ref):
        turned = left_ref[...].T
        for start in range(0, out_ref.shape[1], lanes):
            columns = slice(start, start + lanes)
            total = None
            for k, block_ref in enumerate(blocks):
                term = dot32(turned[:, k * rows : (k + 1) * rows], block_ref[:, columns])
                total = term if total is None else total + term
            out_ref[:, columns] = total.astype(BF16)

    for side in (0, 1):
        for left_ref, chosen in (
            (act_ref, pl.program_id(1) < last),
            (att_ref, pl.program_id(1) == last),
        ):

            @pl.when((pl.program_id(0) == side) & chosen)
            def _(left_ref=left_ref, side=side):
                fill(left_ref, out_refs[side])


def outer(core, activated, attended, blocks):
    count, hidden = activated.shape
    rows, width = blocks[0].shape
    tile = attended.shape[1]
    steps = hidden // tile
    half = jax.ShapeDtypeStruct((hidden + tile, width // 2), BF16)
    return pl.pallas_call(
        outer_kernel,
        out_shape=(half, half),
        grid_spec=pltpu.PrefetchScalarGridSpec(
            num_scalar_prefetch=1,
            grid=(2, steps + 1),
            in_specs=[
                pl.BlockSpec((count, tile), lambda j, i, core_ref: (0, jnp.minimum(i, steps - 1))),
                pl.BlockSpec((count, tile), lambda j, i, core_ref: (0, 0)),
            ]
            + [
                pl.BlockSpec((rows, width // 2), lambda j, i, core_ref: (0, j ^ core_ref[0]))
                for _ in blocks
            ],
            out_specs=(
                pl.BlockSpec(
                    (tile, width // 2), lambda j, i, core_ref: (jnp.where(j == 0, i, steps), 0)
                ),
                pl.BlockSpec(
                    (tile, width // 2), lambda j, i, core_ref: (jnp.where(j == 0, 0, i), 0)
                ),
            ),
        ),
        compiler_params=pltpu.CompilerParams(vmem_limit_bytes=BIG_VMEM),
        cost_estimate=SMALL_COST,
    )(core[None].astype(jnp.int32), activated, attended, *blocks)


def split_shards(
    tokens,
    cotangent,
    seq_lengths,
    seq_order,
    ln1_gain,
    ln1_bias,
    ln2_gain,
    ln2_bias,
    w_qkv,
    b_qkv,
    w_dense,
    b_dense,
    w_up,
    b_up,
    w_down,
    b_down,
):
    me = lax.axis_index("shard")
    rep = lax.axis_index("rep")
    place = me // 2
    is_middle = (place == 1) | (place == 2)
    own = tokens[:, 0, :]
    own_grad = cotangent[:, 0, :]
    rows, width = own.shape
    group_tokens = rows * HEADS
    depth = w_up.shape[0]
    hidden = w_down.shape[0]
    wide = hidden + 3 * HEAD
    quarter = depth // 4

    up_rows = lax.dynamic_slice_in_dim(w_up, rep * quarter, quarter, 0)
    qkv_rows = lax.dynamic_slice_in_dim(w_qkv, rep * quarter, quarter, 0)

    def columns_for(target):
        pieces = [lax.dynamic_slice_in_dim(up_rows, target * hidden, hidden, 1)]
        for k in range(3):
            pieces.append(
                lax.dynamic_slice_in_dim(qkv_rows, k * width + target * HEAD, HEAD, 1)
            )
        return jnp.concatenate(pieces, axis=1)

    odd = jnp.stack([columns_for(me ^ (2 * z + 1)) for z in range(4)])
    odd_came = flip(odd, "shard", 1)
    x_near = flip(own, "shard", 2)
    x_across = send(own, MIDDLE)
    keep = [columns_for(me ^ (2 * z)) for z in range(4)]
    row_offsets, row_counts = stream_rows(seq_lengths[0], seq_order[0], HEADS)
    ends = (row_offsets + row_counts) * HEADS
    seq_scalars = jnp.concatenate([ends, me[None]]).astype(jnp.int32)
    row_range = jnp.arange(rows, dtype=jnp.int32)
    member = (row_range[:, None] >= row_offsets[None, :]) & (
        row_range[:, None] < (row_offsets + row_counts)[None, :]
    )
    in_seq = row_range - jnp.sum(jnp.where(member, row_offsets[None, :], 0), axis=1)
    block_range = jnp.arange(HEADS, dtype=jnp.int32)
    apart = block_range // 4 * 4 + block_range % 2 * 2 + block_range // 2 % 2
    positions = (
        in_seq.reshape(rows // TILE_ROWS, 1, TILE_ROWS) * HEADS + (apart ^ me)[None, :, None]
    )
    cosine, sine = rotary_tables(positions.reshape(-1).astype(F32))
    rest = 128 - ROT
    cosine = jnp.concatenate([cosine, cosine, jnp.ones((group_tokens, rest), F32)], axis=1)
    sine = jnp.concatenate([-sine, sine, jnp.zeros((group_tokens, rest), F32)], axis=1)
    tiled = (rows // TILE_ROWS, TILE_ROWS * HEADS, 128)
    cosine = cosine.reshape(tiled)
    sine = sine.reshape(tiled)


    gains = jnp.stack([ln1_gain, ln2_gain], axis=1)
    shifts = jnp.stack([ln1_bias, ln2_bias], axis=1)
    tall = [vector[:, None] for vector in (ln1_gain, ln1_bias, ln2_gain, ln2_bias)]
    b_in = jnp.concatenate(
        [lax.dynamic_slice_in_dim(b_up, me * hidden, hidden, 0)]
        + [lax.dynamic_slice_in_dim(b_qkv, k * width + me * HEAD, HEAD, 0) for k in range(3)]
    )
    own, own_grad, x_near, x_across, odd_came, gains, shifts, b_in, *both = hold(
        (own, own_grad, x_near, x_across, odd_came, gains, shifts, b_in, *keep, *tall),
        (cosine, sine),
    )
    keep, tall = both[:4], both[4:]
    pairs = [jnp.stack([keep[z], odd_came[z]]) for z in range(4)]
    got = [flip(pairs[z], "shard", 2 * z) for z in range(1, 4)]
    x_own_y = flip(own, "shard", 1)
    x_near_y = flip(x_near, "shard", 1)
    beside = [flip(pairs[0], "rep", 2)]
    x_near, x_across, own_grad, x_near_y, *got = hold(
        (x_near, x_across, own_grad, x_near_y, *got), (x_own_y, beside[0])
    )
    x_across_near = send(x_near, MIDDLE)
    x_two = send(x_across, OUTWARD)
    g_own_y = flip(own_grad, "shard", 1)
    beside = beside + [flip(jnp.stack(got), "rep", 2)]
    part = jnp.stack([pairs[0]] + got).reshape(HEADS, quarter, wide)
    normed = norm_blocks([own, x_near, x_own_y, x_near_y], (0, 1, 2, 3), None)
    x_across_near, x_two, own_grad, normed, *beside = hold(
        (x_across_near, x_two, own_grad, normed, *beside), (part, g_own_y)
    )
    two = jnp.where(is_middle, x_across_near, x_two)
    x_three = send(x_across_near, OUTWARD)
    g_across = send(own_grad, MIDDLE)
    x_two_y = flip(two, "shard", 1)
    beside = jnp.concatenate([beside[0][None], beside[1]]).reshape(HEADS, quarter, wide)
    part_c = flip(part, "rep", 1)
    beside_c = flip(beside, "rep", 1)
    normed = norm_blocks([two], (4,), normed)
    parts = (part, part_c, beside, beside_c)
    up_raw, qkv_raw, up_scaled, qkv_scaled, shifted = place_weights(
        me, rep, parts, gains, shifts, hidden
    )
    b_in = b_in[None, :] + shifted
    x_three, own_grad, g_across, x_two_y, normed, b_in = hold(
        (x_three, own_grad, g_across, x_two_y, normed, b_in), ()
    )
    three = jnp.where(is_middle, x_across, x_three)
    g_near = flip(own_grad, "shard", 2)
    x_three_y = flip(three, "shard", 1)
    normed = norm_blocks([three, x_two_y], (5, 6), normed)
    halfway = project(normed, up_scaled, qkv_scaled, b_in, 0, 3, [])
    g_near, x_three_y, *halfway = hold((g_near, x_three_y, *halfway), ())
    g_across_near = send(g_near, MIDDLE)
    g_two = send(g_across, OUTWARD)
    g_near_y = flip(g_near, "shard", 1)
    normed = norm_blocks([x_three_y], (7,), normed)
    activated, slope, qkv = project(normed, up_scaled, qkv_scaled, b_in, 3, 4, halfway)
    qkv = qkv.reshape(HEADS, rows, 3 * HEAD)
    attended, query, key = attend(seq_scalars, qkv, cosine, sine)
    attended = attended.reshape(group_tokens, HEAD)
    g_across_near, g_two, attended, g_near_y = hold((g_across_near, g_two, attended, g_near_y), ())
    g_two = jnp.where(is_middle, g_across_near, g_two)
    g_three = send(g_across_near, OUTWARD)
    g_two_y = flip(g_two, "shard", 1)
    far = combine(activated, attended, w_down, w_dense, rows, 1, 0)
    close = combine(activated, attended, w_down, w_dense, rows, 0, 0)
    g_three, g_near_y, g_two_y, *both = hold((g_three, g_near_y, g_two_y, *far, *close), ())
    far, close = both[:4], both[4:]
    g_three = jnp.where(is_middle, g_across, g_three)
    g_three_y = flip(g_three, "shard", 1)
    *grads, sums_one = pull([own_grad, g_near, g_own_y, g_near_y], w_down, w_dense, slope, 0, [])
    *grads, sums_two = pull([g_two, g_three], w_down, w_dense, slope, 2, grads)
    g_three_y, *both = hold((g_three_y, *far, *grads), ())
    far, grads = both[:4], both[4:]
    came_three = flip(far[3], "shard", 1)
    grad_pre, grad_attended, sums_three = pull(
        [g_two_y, g_three_y], w_down, w_dense, slope, 3, grads
    )
    pre_sums = sums_one + sums_two + sums_three
    my_core = rep % 2
    my_side = rep // 2
    my_row = me % 2

    def split(values, index):
        return (
            lax.dynamic_index_in_dim(values, index, 1, False),
            lax.dynamic_index_in_dim(values, 1 - index, 1, False),
        )

    def by_side(summed):
        return split(summed.reshape(HEADS, 2, quarter, summed.shape[-1]), my_side)

    def by_row(summed):
        return split(summed.reshape(4, 2, quarter, summed.shape[-1]), my_row)

    def joined(mine, came):
        return plus(mine, came).astype(BF16)

    def by_place(mine, came):
        both = jnp.stack([mine, came], axis=1)
        return [lax.dynamic_index_in_dim(both, place ^ z, 0, False) for z in range(4)]

    def far_places(pieces):
        return flip(jnp.stack(pieces[2:]), "shard", 4)

    def near_place(pieces, far):
        return flip(jnp.stack([pieces[1], far[1]]), "shard", 2)

    def sources(pieces, far, near):
        both = jnp.stack([pieces[0], near[0], far[0], near[1]])
        return both.reshape(HEADS, quarter, both.shape[-1])

    up_keep, up_give, up_sums = moments_of(
        my_core, normed, grad_pre, up_raw, tall[2], tall[3], pre_sums, quarter
    )
    three = joined(close[3], came_three)
    grad_attended, up_give, three, *far = hold((grad_attended, up_give, three, *far), ())
    came_two = flip(far[2], "shard", 1)
    from_corner = send(three, INWARD)
    up_came = flip(up_give, "rep", 1)
    grad_qkv, qkv_sums = attend_back(
        seq_scalars,
        qkv,
        grad_attended.reshape(HEADS, rows, HEAD),
        cosine,
        sine,
        query,
        key,
    )
    grad_qkv = grad_qkv.reshape(group_tokens, 3 * HEAD)
    qkv_keep, qkv_give, qkv_row_sums = moments_of(
        my_core, normed, grad_qkv, qkv_raw, tall[0], tall[1], qkv_sums, quarter
    )
    two = joined(close[2], came_two)
    up_keep, up_give = by_side(joined(up_keep, up_came))
    from_corner, up_give, qkv_give, grad_qkv, two, *far = hold(
        (from_corner, up_give, qkv_give, grad_qkv, two, *far), (up_keep,)
    )
    up_came = flip(up_give, "rep", 2)
    came_one = flip(far[1], "shard", 1)
    two = joined(two, from_corner)
    across_near = send(two, MIDDLE)
    across = send(two, INWARD)
    qkv_came = flip(qkv_give, "rep", 1)
    gy_far = combine(grad_pre, grad_qkv, up_scaled, qkv_scaled, rows, 1, 1)
    one = joined(close[1], came_one)
    up_keep, up_give = by_row(joined(up_keep, up_came))
    qkv_keep, qkv_give = by_side(joined(qkv_keep, qkv_came))
    up_give, across_near, across, qkv_give, own_grad, one, *both = hold(
        (up_give, across_near, across, qkv_give, own_grad, one, *far, *gy_far),
        (up_keep, qkv_keep),
    )
    far, gy_far = both[:4], both[4:]
    came_own = flip(far[0], "shard", 1)
    up_came = flip(up_give, "shard", 1)
    one = joined(one, across_near)
    three = plus(three, across).astype(BF16)
    one_near = flip(one, "shard", 2)
    three_across = send(three, MIDDLE)
    qkv_came = flip(qkv_give, "rep", 2)
    half_keep, half_give = outer(
        my_core,
        activated,
        attended,
        [own_grad, g_near, g_own_y, g_near_y, g_two, g_three, g_two_y, g_three_y],
    )
    out_sum = plus(close[0], came_own)
    up_pieces = by_place(up_keep, up_came)
    qkv_keep, qkv_give = by_row(joined(qkv_keep, qkv_came))
    (
        one_near,
        three_across,
        qkv_keep,
        qkv_give,
        half_give,
        up_sums,
        qkv_row_sums,
        out_sum,
        *both,
    ) = hold(
        (
            one_near,
            three_across,
            qkv_keep,
            qkv_give,
            half_give,
            up_sums,
            qkv_row_sums,
            out_sum,
            *up_pieces,
            *gy_far,
            grad_pre,
        ),
        (),
    )
    up_pieces, gy_far, grad_pre = both[:4], both[4:8], both[8]
    came_three = flip(gy_far[3], "shard", 1)
    qkv_came = flip(qkv_give, "shard", 1)
    up_far = far_places(up_pieces)
    half_came = flip(half_give, "rep", 1)
    small = jnp.concatenate(
        [
            qkv_row_sums.T.reshape(-1),
            up_sums.T.reshape(-1),
            jnp.sum(own_grad, axis=0, dtype=F32),
            jnp.where(
                block_range[:, None] == me, jnp.concatenate([pre_sums, qkv_sums], axis=1), 0.0
            ).reshape(-1),
        ]
    )
    small = small + flip(small, "rep", 2)
    out_sum = plus(out_sum, one_near, three_across)
    output = (own.astype(F32) + out_sum + (b_dense + b_down)).astype(BF16)
    gy_close = combine(grad_pre, grad_qkv, up_scaled, qkv_scaled, rows, 0, 1)
    qkv_pieces = by_place(qkv_keep, qkv_came)
    three = joined(gy_close[3], came_three)
    half = joined(half_keep, half_came)
    output, up_far, half, small, three, *both = hold(
        (output, up_far, half, small, three, *qkv_pieces, *gy_far, *gy_close), ()
    )
    qkv_pieces, gy_far, gy_close = both[:4], both[4:8], both[8:]
    came_two = flip(gy_far[2], "shard", 1)
    from_corner = send(three, INWARD)
    qkv_far = far_places(qkv_pieces)
    half_far = flip(half, "rep", 2)
    small = small + flip(small, "rep", 1)
    two = joined(gy_close[2], came_two)
    from_corner, qkv_far, small, two, *gy_far = hold(
        (from_corner, qkv_far, small, two, *gy_far), ()
    )
    came_one = flip(gy_far[1], "shard", 1)
    two = joined(two, from_corner)
    across_near = send(two, MIDDLE)
    across = send(two, INWARD)
    up_near = near_place(up_pieces, up_far)
    one = joined(gy_close[1], came_one)
    up_part = sources(up_pieces, up_far, up_near)
    across_near, across, up_part, half_far, one, *gy_far = hold(
        (across_near, across, up_part, half_far, one, *gy_far), ()
    )
    came_own = flip(gy_far[0], "shard", 1)
    one = joined(one, across_near)
    three = plus(three, across).astype(BF16)
    one_near = flip(one, "shard", 2)
    three_across = send(three, MIDDLE)
    up_beside = flip(up_part, "rep", 2)
    qkv_near = near_place(qkv_pieces, qkv_far)
    half = joined(half, half_far)
    gy = plus(gy_close[0], came_own)
    qkv_part = sources(qkv_pieces, qkv_far, qkv_near)
    one_near, three_across, qkv_part, up_beside, half, small, gy = hold(
        (one_near, three_across, qkv_part, up_beside, half, small, gy), ()
    )
    qkv_beside = flip(qkv_part, "rep", 2)
    up_c = flip(jnp.stack([up_part, up_beside]), "rep", 1)
    other = flip(half, "rep", 1)
    small = small + flip(small, "shard", 1)
    gy = plus(gy, one_near, three_across)
    own_normed, own_rstd = normalize(own)
    input_grad = own_grad.astype(F32) + own_rstd * (
        gy
        - jnp.mean(gy, axis=-1, keepdims=True)
        - own_normed * jnp.mean(gy * own_normed, axis=-1, keepdims=True)
    )
    input_grad = input_grad[:, None, :]
    up_grad = place_grads(me, rep, (up_part, up_c[0], up_beside, up_c[1]), 1)
    down_grad, dense_grad = place_halves(my_core, half, other, hidden)
    qkv_c = flip(qkv_part, "rep", 1)
    input_grad, up_grad, down_grad, qkv_beside, qkv_c, small = hold(
        (input_grad, up_grad, down_grad, qkv_beside, qkv_c, small), ()
    )
    qkv_beside_c = flip(qkv_beside, "rep", 1)
    one, two, three = [flip(small, "shard", bit) for bit in (2, 4, 6)]
    qkv_grad = place_grads(me, rep, (qkv_part, qkv_c, qkv_beside, qkv_beside_c), 3)
    small, one, two, three = hold((small, one, two, three), (qkv_grad,))
    small = (small + one) + (two + three)
    vectors = small[: 5 * width].reshape(5, width)
    slots = small[5 * width :].reshape(HEADS, wide)
    b_up_grad = slots[:, :hidden].reshape(-1)
    b_qkv_grad = slots[:, hidden:].reshape(HEADS, 3, HEAD).transpose(1, 0, 2).reshape(-1)
    return (
        output[:, None, :],
        input_grad,
        vectors[0],
        vectors[1],
        vectors[2],
        vectors[3],
        qkv_grad,
        b_qkv_grad,
        dense_grad,
        vectors[4],
        up_grad,
        b_up_grad,
        down_grad,
        vectors[4],
    )


def solution(mesh):
    in_specs = (
        P("rep", "shard", None),
        P("rep", "shard", None),
        P("rep", None),
        P("rep", None),
        P(),
        P(),
        P(),
        P(),
        P("shard", None),
        P(),
        P("shard", None),
        P(),
        P("shard", None),
        P(),
        P("shard", None),
        P(),
    )
    out_specs = (
        P("rep", "shard", None),
        P("rep", "shard", None),
        P(),
        P(),
        P(),
        P(),
        P("shard", None),
        P(),
        P("shard", None),
        P(),
        P("shard", None),
        P(),
        P("shard", None),
        P(),
    )
    body = split_shards if mesh.shape["shard"] == HEADS else shards
    return jax.shard_map(
        body, mesh=mesh, in_specs=in_specs, out_specs=out_specs, check_vma=False
    )
```

```python
import functools
import math

import jax
import jax.numpy as jnp
from jax import lax
from jax.experimental import pallas as pl
from jax.experimental.pallas import tpu as pltpu
from jax.sharding import PartitionSpec as P

HEADS = 8
HEAD = 256
ROT = 64


EPSILON = 1e-05
MASKED = -1e30


def layer_norm(vector, gain_vec, shift_vec):
    mean_val = jnp.mean(vector, axis=-1, keepdims=True)
    centered = vector - mean_val
    variance = jnp.mean(centered * centered, axis=-1, keepdims=True)
    return centered * lax.rsqrt(variance + EPSILON) * gain_vec + shift_vec


def gelu_exact(vector):
    return jax.nn.gelu(vector, approximate=False)


def rotary_tables(positions):
    half_rot = ROT // 2
    freq_index = jnp.arange(half_rot, dtype=jnp.float32)
    inverse_freq = jnp.exp(freq_index * (-2.0 * math.log(10000.0) / ROT))
    angles = positions[:, None] * inverse_freq[None, :]
    return (jnp.cos(angles), jnp.sin(angles))


def rotate(heads_in, cosine_table, sine_table):
    half_rot = ROT // 2
    first_half = heads_in[..., :half_rot]
    second_half = heads_in[..., half_rot:ROT]
    cos_wide = cosine_table[:, None, :]
    sin_wide = sine_table[:, None, :]
    return jnp.concatenate(
        [
            first_half * cos_wide - second_half * sin_wide,
            second_half * cos_wide + first_half * sin_wide,
            heads_in[..., ROT:],
        ],
        axis=-1,
    )


def stream_rows(lengths, seq_perm, shard_count):
    seq_range = jnp.arange(lengths.shape[0], dtype=jnp.int32)
    ranking = jnp.sum(
        jnp.where(seq_perm[:, None] == seq_range[None, :], seq_range[:, None], 0), axis=0
    )
    offsets = jnp.sum(jnp.where(ranking[None, :] < ranking[:, None], lengths[None, :], 0), axis=1)
    return (offsets // shard_count, lengths // shard_count)


def row_product(left, right):
    return jnp.dot(left.T, right, preferred_element_type=jnp.float32)


def block_mask(seq_flag, positions, live):
    return (
        live[:, None]
        & live[None, :]
        & (seq_flag[:, None] == seq_flag[None, :])
        & (positions[None, :] <= positions[:, None])
    )


def shards(
    tokens,
    cotangent,
    seq_lengths,
    seq_order,
    ln1_gain,
    ln1_bias,
    ln2_gain,
    ln2_bias,
    w_qkv,
    b_qkv,
    w_dense,
    b_dense,
    w_up,
    b_up,
    w_down,
    b_down,
):
    shard_count = lax.axis_size("shard")
    my_index = lax.axis_index("shard")
    inputs = tokens[:, 0, :].astype(jnp.float32)
    grad_out = cotangent[:, 0, :]
    local_rows, width = inputs.shape
    slot_rows = 2 * (local_rows // shard_count) - 4
    buffer_rows = slot_rows * shard_count
    row_offsets, row_counts = stream_rows(seq_lengths[0], seq_order[0], shard_count)
    first_count = row_counts[0::2]
    second_count = row_counts[1::2]
    first_start = row_offsets[0::2]
    second_start = row_offsets[1::2]
    slot_range = jnp.arange(slot_rows, dtype=jnp.int32)[None, :]
    in_first = slot_range < first_count[:, None]
    slot_live = slot_range < (first_count + second_count)[:, None]
    source_rows = jnp.where(
        in_first,
        first_start[:, None] + slot_range,
        second_start[:, None] + slot_range - first_count[:, None],
    )
    source_rows = jnp.where(slot_live, source_rows, 0)
    seq_range = jnp.arange(row_counts.shape[0], dtype=jnp.int32)
    parity = seq_range % 2
    slot_base = seq_range // 2 * slot_rows + parity * row_counts[seq_range - parity] - row_offsets
    token_range = jnp.arange(local_rows, dtype=jnp.int32)[:, None]
    member = (token_range >= row_offsets[None, :]) & (
        token_range < (row_offsets + row_counts)[None, :]
    )
    return_rows = token_range[:, 0] + jnp.sum(jnp.where(member, slot_base[None, :], 0), axis=1)
    own_first = first_count[my_index]
    own_second = second_count[my_index]
    buffer_range = jnp.arange(buffer_rows, dtype=jnp.int32)
    slot_index = buffer_range % slot_rows
    source_index = buffer_range // slot_rows
    seq_flag = (slot_index >= own_first).astype(jnp.int32)
    positions = (slot_index - seq_flag * own_first) * shard_count + source_index
    live = slot_index < own_first + own_second
    attn_full, dense_full = (
        lax.all_gather(w_qkv, "shard", axis=0, tiled=True),
        lax.all_gather(w_dense, "shard", axis=0, tiled=True),
    )
    up_full, down_full = (
        lax.all_gather(w_up, "shard", axis=0, tiled=True),
        lax.all_gather(w_down, "shard", axis=0, tiled=True),
    )
    normed_one_wide, pull_one = jax.vjp(layer_norm, inputs, ln1_gain, ln1_bias)
    normed_two_wide, pull_two = jax.vjp(layer_norm, inputs, ln2_gain, ln2_bias)
    normed_one = normed_one_wide.astype(jnp.bfloat16)
    normed_two = normed_two_wide.astype(jnp.bfloat16)
    qkv = (jnp.dot(normed_one, attn_full, preferred_element_type=jnp.float32) + b_qkv).astype(
        jnp.bfloat16
    )
    arrived = lax.all_to_all(
        jnp.take(qkv, source_rows, axis=0), "shard", split_axis=0, concat_axis=0, tiled=True
    )
    arrived = arrived.reshape(buffer_rows, 3 * width)
    heads_shape = (buffer_rows, HEADS, HEAD)
    cosine_table, sine_table = rotary_tables(positions.astype(jnp.float32))

    def rotate_here(heads_in):
        return rotate(heads_in, cosine_table, sine_table)

    query_wide, pull_query = jax.vjp(
        rotate_here, arrived[:, :width].astype(jnp.float32).reshape(heads_shape)
    )
    key_wide, pull_key = jax.vjp(
        rotate_here, arrived[:, width : 2 * width].astype(jnp.float32).reshape(heads_shape)
    )
    rotated_queries = query_wide.astype(jnp.bfloat16)
    rotated_keys = key_wide.astype(jnp.bfloat16)
    value_heads = arrived[:, 2 * width :].reshape(heads_shape)
    sources_per = shard_count
    while sources_per > 1 and sources_per * slot_rows > 1024:
        sources_per = sources_per // 2
    block_rows = sources_per * slot_rows
    block_total = buffer_rows // block_rows
    score_scale = HEAD ** (-0.5)

    def forward_block(block_index):
        allowed = block_mask(seq_flag, positions, live)
        scores = (
            jnp.einsum(
                "qhe,khe->hqk", rotated_queries, rotated_keys, preferred_element_type=jnp.float32
            )
            * score_scale
        )
        scores = jnp.where(allowed[None], scores, MASKED)
        row_max = jnp.max(scores, axis=-1, keepdims=True)
        exp_scores = jnp.exp(scores - row_max)
        exp_total = jnp.sum(exp_scores, axis=-1, keepdims=True)
        attn_probs = jnp.where(allowed[None], exp_scores / exp_total, 0.0)
        attended_blk = jnp.einsum(
            "hqk,khe->qhe",
            attn_probs.astype(jnp.bfloat16),
            value_heads,
            preferred_element_type=jnp.float32,
        )
        return (attended_blk.astype(jnp.bfloat16), row_max[..., 0] + jnp.log(exp_total[..., 0]))

    attended_blocks, log_totals = lax.map(forward_block, jnp.arange(block_total, dtype=jnp.int32))
    attended_slots = attended_blocks.reshape(shard_count, slot_rows, width)
    attn_back = lax.all_to_all(
        attended_slots, "shard", split_axis=0, concat_axis=0, tiled=True
    ).reshape(buffer_rows, width)
    attn_in = jnp.take(attn_back, return_rows, axis=0)
    attn_out = jnp.dot(attn_in, dense_full, preferred_element_type=jnp.float32) + b_dense
    pre_up = jnp.dot(normed_two, up_full, preferred_element_type=jnp.float32) + b_up
    activated_wide, pull_gelu = jax.vjp(gelu_exact, pre_up)
    activated = activated_wide.astype(jnp.bfloat16)
    mlp_out = jnp.dot(activated, down_full, preferred_element_type=jnp.float32) + b_down
    output = (inputs + attn_out + mlp_out).astype(jnp.bfloat16)
    attn_second, dense_second = (
        lax.all_gather(w_qkv, "shard", axis=0, tiled=True),
        lax.all_gather(w_dense, "shard", axis=0, tiled=True),
    )
    up_second, down_second = (
        lax.all_gather(w_up, "shard", axis=0, tiled=True),
        lax.all_gather(w_down, "shard", axis=0, tiled=True),
    )
    grad_attended = jnp.dot(grad_out, dense_second.T, preferred_element_type=jnp.float32).astype(
        jnp.bfloat16
    )
    grad_slots = jnp.where(
        slot_live[:, :, None],
        jnp.take(grad_attended, source_rows, axis=0),
        jnp.zeros((), jnp.bfloat16),
    )
    grad_heads = lax.all_to_all(
        grad_slots, "shard", split_axis=0, concat_axis=0, tiled=True
    ).reshape(heads_shape)

    def backward_block(carried, block_index):
        grad_keys, grad_values = carried
        allowed = block_mask(seq_flag, positions, live)
        scores = (
            jnp.einsum(
                "qhe,khe->hqk", rotated_queries, rotated_keys, preferred_element_type=jnp.float32
            )
            * score_scale
        )
        attn_probs = jnp.where(
            allowed[None], jnp.exp(scores - log_totals[block_index][..., None]), 0.0
        )
        grad_probs = jnp.einsum(
            "qhe,khe->hqk", grad_heads, value_heads, preferred_element_type=jnp.float32
        )
        row_delta = jnp.sum(attn_probs * grad_probs, axis=-1, keepdims=True)
        grad_scores = (attn_probs * (grad_probs - row_delta)).astype(jnp.bfloat16)
        grad_query = (
            jnp.einsum(
                "hqk,khe->qhe", grad_scores, rotated_keys, preferred_element_type=jnp.float32
            )
            * score_scale
        )
        grad_keys = (
            grad_keys
            + jnp.einsum(
                "hqk,qhe->khe", grad_scores, rotated_queries, preferred_element_type=jnp.float32
            )
            * score_scale
        )
        grad_values = grad_values + jnp.einsum(
            "hqk,qhe->khe",
            attn_probs.astype(jnp.bfloat16),
            grad_heads,
            preferred_element_type=jnp.float32,
        )
        return ((grad_keys, grad_values), grad_query)

    zero_heads = jnp.zeros(heads_shape, jnp.float32)
    (grad_keys, grad_values), grad_query_blocks = lax.scan(
        backward_block, (zero_heads, zero_heads), jnp.arange(block_total, dtype=jnp.int32)
    )
    grad_q_pre = pull_query(grad_query_blocks.reshape(heads_shape))[0]
    grad_k_pre = pull_key(grad_keys)[0]
    grad_qkv_slots = jnp.concatenate(
        [
            grad_q_pre.reshape(buffer_rows, width),
            grad_k_pre.reshape(buffer_rows, width),
            grad_values.reshape(buffer_rows, width),
        ],
        axis=1,
    ).astype(jnp.bfloat16)
    grad_qkv_slots = grad_qkv_slots.reshape(shard_count, slot_rows, 3 * width)
    grad_qkv_back = lax.all_to_all(grad_qkv_slots, "shard", split_axis=0, concat_axis=0, tiled=True)
    grad_qkv = jnp.take(grad_qkv_back.reshape(buffer_rows, 3 * width), return_rows, axis=0)
    grad_activated = jnp.dot(grad_out, down_second.T, preferred_element_type=jnp.float32)
    grad_pre = pull_gelu(grad_activated)[0].astype(jnp.bfloat16)
    grad_normed_one = jnp.dot(grad_qkv, attn_second.T, preferred_element_type=jnp.float32)
    grad_normed_two = jnp.dot(grad_pre, up_second.T, preferred_element_type=jnp.float32)
    grad_in_one, grad_gain_one, grad_bias_one = pull_one(grad_normed_one)
    grad_in_two, grad_gain_two, grad_bias_two = pull_two(grad_normed_two)
    input_grad = grad_out.astype(jnp.float32) + grad_in_one + grad_in_two
    qkv_rows = lax.psum_scatter(
        row_product(normed_one, grad_qkv).astype(jnp.bfloat16),
        "shard",
        scatter_dimension=0,
        tiled=True,
    ).astype(jnp.float32)
    dense_rows = lax.psum_scatter(
        row_product(attn_in, grad_out).astype(jnp.bfloat16),
        "shard",
        scatter_dimension=0,
        tiled=True,
    ).astype(jnp.float32)
    up_rows = lax.psum_scatter(
        row_product(normed_two, grad_pre).astype(jnp.bfloat16),
        "shard",
        scatter_dimension=0,
        tiled=True,
    ).astype(jnp.float32)
    down_rows = lax.psum_scatter(
        row_product(activated, grad_out).astype(jnp.bfloat16),
        "shard",
        scatter_dimension=0,
        tiled=True,
    ).astype(jnp.float32)
    qkv_rows, dense_rows, up_rows, down_rows = (
        lax.psum(qkv_rows.astype(jnp.bfloat16), "rep").astype(jnp.float32),
        lax.psum(dense_rows.astype(jnp.bfloat16), "rep").astype(jnp.float32),
        lax.psum(up_rows.astype(jnp.bfloat16), "rep").astype(jnp.float32),
        lax.psum(down_rows.astype(jnp.bfloat16), "rep").astype(jnp.float32),
    )
    out_column_sum = jnp.sum(grad_out, axis=0, dtype=jnp.float32)
    small_totals = lax.psum(
        (
            grad_gain_one,
            grad_bias_one,
            grad_gain_two,
            grad_bias_two,
            jnp.sum(grad_qkv, axis=0, dtype=jnp.float32),
            out_column_sum,
            jnp.sum(grad_pre, axis=0, dtype=jnp.float32),
        ),
        ("rep", "shard"),
    )
    return (
        output[:, None, :],
        input_grad[:, None, :],
        small_totals[0],
        small_totals[1],
        small_totals[2],
        small_totals[3],
        qkv_rows,
        small_totals[4],
        dense_rows,
        small_totals[5],
        up_rows,
        small_totals[6],
        down_rows,
        small_totals[5],
    )


TILE_ROWS = 32
BIG_VMEM = 60 << 20
SMALL_COST = pl.CostEstimate(flops=1 << 20, bytes_accessed=1 << 20, transcendentals=0)
F32 = jnp.float32
BF16 = jnp.bfloat16


def flip(value, axis, bit):
    size = lax.axis_size(axis)
    return lax.ppermute(value, axis, [(i, i ^ bit) for i in range(size)])


def send(value, pairs):
    return lax.ppermute(value, "shard", [(2 * a + y, 2 * b + y) for a, b in pairs for y in (0, 1)])


MIDDLE = ((1, 2), (2, 1))
OUTWARD = ((1, 0), (2, 3))
INWARD = ((0, 1), (3, 2))


def plus(*terms):
    total = terms[0].astype(F32)
    for term in terms[1:]:
        total = total + term.astype(F32)
    return total


def hold(values, gates):
    return lax.optimization_barrier(tuple(values) + tuple(gates))[: len(values)]


def turn(heads_in, cosine, sine):
    left = heads_in[:, :128]
    lane = lax.broadcasted_iota(jnp.int32, left.shape, 1)
    half = ROT // 2
    partner = jnp.where(lane < half, pltpu.roll(left, 128 - half, 1), pltpu.roll(left, half, 1))
    return jnp.concatenate([left * cosine + partner * sine, heads_in[:, 128:]], axis=1)


def token_labels(my_index, shape, dim):
    inner = lax.broadcasted_iota(jnp.int32, shape, dim)
    block = inner // TILE_ROWS
    apart = block // 4 * 4 + block % 2 * 2 + block // 2 % 2
    return (inner % TILE_ROWS) * HEADS + jnp.bitwise_xor(apart, my_index)


def tile_weights(tile, seq_ref, query, key_tiles, count):
    tile_tokens = TILE_ROWS * HEADS
    my_index = seq_ref[count]
    query_label = token_labels(my_index, (tile_tokens, 1), 0) + tile * tile_tokens
    key_label = token_labels(my_index, (1, tile_tokens), 1)
    scores = []
    for place, key in key_tiles:
        label = key_label + place * tile_tokens
        last = jnp.full(label.shape, 1 << 30, jnp.int32)
        for k in range(count):
            last = jnp.minimum(last, jnp.where(label < seq_ref[k], seq_ref[k], 1 << 30))
        allowed = query_label < last
        if place == tile:
            allowed = allowed & (label <= query_label)
        product = lax.dot_general(query, key, (((1,), (1,)), ((), ())), preferred_element_type=F32)
        scores.append(jnp.where(allowed, product * HEAD ** (-0.5), MASKED))
    scores = jnp.concatenate(scores, axis=1)
    exp_scores = jnp.exp(scores - jnp.max(scores, axis=1, keepdims=True))
    return exp_scores * (1.0 / jnp.sum(exp_scores, axis=1, keepdims=True))


def attend_kernel(seq_ref, qkv_ref, cos_ref, sin_ref, out_ref, query_ref, key_ref):
    tiles = query_ref.shape[0]
    tile_tokens = TILE_ROWS * HEADS

    def part(tile, lane):
        rows = qkv_ref[:, tile * TILE_ROWS : (tile + 1) * TILE_ROWS, lane : lane + HEAD]
        return rows.reshape(tile_tokens, HEAD)

    for tile in range(tiles):
        cosine, sine = cos_ref[tile], sin_ref[tile]
        query = turn(part(tile, 0).astype(F32), cosine, sine).astype(BF16)
        query_ref[tile] = query
        key_ref[tile] = turn(part(tile, HEAD).astype(F32), cosine, sine).astype(BF16)
        near = list(range(max(tile - 2, 0), tile + 1))
        probs = tile_weights(
            tile, seq_ref, query, [(k, key_ref[k]) for k in near], seq_ref.shape[0] - 1
        ).astype(BF16)
        total = jnp.zeros((tile_tokens, HEAD), F32)
        for at, k in enumerate(near):
            total = total + jnp.dot(
                probs[:, at * tile_tokens : (at + 1) * tile_tokens],
                part(k, 2 * HEAD),
                preferred_element_type=F32,
            )
        out_ref[:, tile * TILE_ROWS : (tile + 1) * TILE_ROWS, :] = total.astype(BF16).reshape(
            HEADS, TILE_ROWS, HEAD
        )


def attend_back_kernel(
    seq_ref, qkv_ref, grad_ref, cos_ref, sin_ref, query_ref, key_ref, out_ref, sum_ref, gk_ref, gv_ref
):
    tiles = query_ref.shape[0]
    tile_tokens = TILE_ROWS * HEADS
    scale = HEAD ** (-0.5)
    over_rows = (((0,), (0,)), ((), ()))
    over_lanes = (((1,), (1,)), ((), ()))

    def rows_of(tile):
        return slice(tile * TILE_ROWS, (tile + 1) * TILE_ROWS)

    def put(tile, lane, value):
        low = value.astype(BF16)
        out_ref[:, rows_of(tile), lane : lane + HEAD] = low.reshape(HEADS, TILE_ROWS, HEAD)
        columns = jnp.sum(low.astype(F32), axis=0, keepdims=True)
        if tile == 0:
            sum_ref[:, lane : lane + HEAD] = columns
        else:
            sum_ref[:, lane : lane + HEAD] += columns

    def finish(tile):
        put(tile, HEAD, turn(gk_ref[tile] * scale, cos_ref[tile], -sin_ref[tile]))
        put(tile, 2 * HEAD, gv_ref[tile])

    for tile in range(tiles):
        query = query_ref[tile]
        near = list(range(max(tile - 2, 0), tile + 1))
        grad = grad_ref[:, rows_of(tile), :].reshape(tile_tokens, HEAD)
        probs = tile_weights(
            tile, seq_ref, query, [(k, key_ref[k]) for k in near], seq_ref.shape[0] - 1
        )
        grad_probs = jnp.concatenate(
            [
                lax.dot_general(
                    grad,
                    qkv_ref[:, rows_of(k), 2 * HEAD :].reshape(tile_tokens, HEAD),
                    over_lanes,
                    preferred_element_type=F32,
                )
                for k in near
            ],
            axis=1,
        )
        delta = jnp.sum(probs * grad_probs, axis=1, keepdims=True)
        grad_scores = (probs * (grad_probs - delta)).astype(BF16)
        probs = probs.astype(BF16)
        grad_query = jnp.zeros((tile_tokens, HEAD), F32)
        for at, k in enumerate(near):
            span = slice(at * tile_tokens, (at + 1) * tile_tokens)
            grad_query = grad_query + jnp.dot(
                grad_scores[:, span], key_ref[k], preferred_element_type=F32
            )
            to_key = lax.dot_general(
                grad_scores[:, span], query, over_rows, preferred_element_type=F32
            )
            to_value = lax.dot_general(probs[:, span], grad, over_rows, preferred_element_type=F32)
            if k == tile:
                gk_ref[k] = to_key
                gv_ref[k] = to_value
            else:
                gk_ref[k] += to_key
                gv_ref[k] += to_value
        put(tile, 0, turn(grad_query * scale, cos_ref[tile], -sin_ref[tile]))
        if tile >= 2:
            finish(tile - 2)
    for tile in range(max(tiles - 2, 0), tiles):
        finish(tile)


def one_spec(shape):
    return pl.BlockSpec(shape, lambda i: (0,) * len(shape), pipeline_mode=pl.Buffered(1))


SMEM_SPEC = pl.BlockSpec(memory_space=pltpu.SMEM)


def attend(seq_scalars, qkv, cosine, sine):
    blocks, rows, _ = qkv.shape
    tiled = (rows // TILE_ROWS, blocks * TILE_ROWS, HEAD)
    return pl.pallas_call(
        attend_kernel,
        out_shape=(
            jax.ShapeDtypeStruct((blocks, rows, HEAD), BF16),
            jax.ShapeDtypeStruct(tiled, BF16),
            jax.ShapeDtypeStruct(tiled, BF16),
        ),
        grid=(1,),
        in_specs=[SMEM_SPEC] + [one_spec(array.shape) for array in (qkv, cosine, sine)],
        out_specs=(one_spec((blocks, rows, HEAD)), one_spec(tiled), one_spec(tiled)),
        compiler_params=pltpu.CompilerParams(vmem_limit_bytes=BIG_VMEM),
        cost_estimate=SMALL_COST,
    )(seq_scalars, qkv, cosine, sine)


def attend_back(seq_scalars, qkv, grad, cosine, sine, query, key):
    blocks, rows, wide = qkv.shape
    return pl.pallas_call(
        attend_back_kernel,
        out_shape=(
            jax.ShapeDtypeStruct((blocks, rows, wide), BF16),
            jax.ShapeDtypeStruct((1, wide), F32),
        ),
        grid=(1,),
        in_specs=[SMEM_SPEC]
        + [one_spec(array.shape) for array in (qkv, grad, cosine, sine, query, key)],
        out_specs=(one_spec((blocks, rows, wide)), one_spec((1, wide))),
        scratch_shapes=[pltpu.VMEM(query.shape, F32), pltpu.VMEM(query.shape, F32)],
        compiler_params=pltpu.CompilerParams(vmem_limit_bytes=BIG_VMEM),
        cost_estimate=SMALL_COST,
    )(seq_scalars, qkv, grad, cosine, sine, query, key)


def copy_kernel(in_ref, out_ref):
    out_ref[...] = in_ref[...]


def settled(values):
    return pl.pallas_call(
        copy_kernel,
        out_shape=jax.ShapeDtypeStruct(values.shape, values.dtype),
        grid=(1,),
        in_specs=[pl.BlockSpec(values.shape, lambda i: (0, 0))],
        out_specs=pl.BlockSpec(values.shape, lambda i: (0, 0)),
        cost_estimate=SMALL_COST,
    )(values)


def pack_kernel(at_ref, up_ref, qkv_ref, odd_ref, even_ref):
    third = qkv_ref.shape[1] // 3
    hidden = up_ref.shape[1] // HEADS
    for k in range(HEADS):
        out_ref = even_ref if k % 2 == 0 else odd_ref
        target = at_ref[0] ^ k
        start = pl.multiple_of(target * hidden, hidden)
        out_ref[k // 2, :, :hidden] = up_ref[:, pl.ds(start, hidden)]
        for j in range(3):
            start = pl.multiple_of(j * third + target * HEAD, HEAD)
            out_ref[k // 2, :, hidden + j * HEAD : hidden + (j + 1) * HEAD] = qkv_ref[
                :, pl.ds(start, HEAD)
            ]


def pack(me, rep, w_up, w_qkv, hidden):
    quarter = w_up.shape[0] // 4
    shape = (HEADS // 2, quarter, hidden + 3 * HEAD)
    packed = jax.ShapeDtypeStruct(shape, BF16)
    return pl.pallas_call(
        pack_kernel,
        out_shape=(packed, packed),
        grid_spec=pltpu.PrefetchScalarGridSpec(
            num_scalar_prefetch=1,
            grid=(1,),
            in_specs=[
                pl.BlockSpec((quarter, weight.shape[1]), lambda i, at_ref: (at_ref[1], 0))
                for weight in (w_up, w_qkv)
            ],
            out_specs=tuple(pl.BlockSpec(shape, lambda i, at_ref: (0, 0, 0)) for _ in range(2)),
        ),
        compiler_params=pltpu.CompilerParams(vmem_limit_bytes=24 << 20),
        cost_estimate=SMALL_COST,
    )(jnp.stack([me, rep]).astype(jnp.int32), w_up, w_qkv)


def place_weights_kernel(
    at_ref, p0_ref, p1_ref, p2_ref, p3_ref, norms_ref, *out_refs, hidden
):
    raw_refs, scaled_refs, sum_ref = out_refs[:2], out_refs[2:4], out_refs[4]
    quarter, wide = p0_ref.shape[1:]

    @pl.when(pl.program_id(0) == 0)
    def _():
        sum_ref[...] = jnp.zeros_like(sum_ref)

    for k, part_ref in enumerate((p0_ref, p1_ref, p2_ref, p3_ref)):
        rows = pl.ds(pl.multiple_of((at_ref[1] ^ k) * quarter, quarter), quarter)
        for norm, columns in ((1, slice(0, hidden)), (0, slice(hidden, wide))):
            raw = part_ref[0, :, columns]
            raw_refs[1 - norm][rows, :] = raw
            weight = raw.astype(F32)
            gain = norms_ref[rows, 2 * norm : 2 * norm + 1]
            shift = norms_ref[rows, 2 * norm + 1 : 2 * norm + 2]
            scaled_refs[1 - norm][rows, :] = (weight * gain).astype(BF16)
            sum_ref[:, columns] += jnp.sum(weight * shift, axis=0, keepdims=True)


def place_weights(me, rep, parts, norms, hidden):
    count, rows, wide = parts[0].shape
    widths = (hidden, wide - hidden) * 2
    four = pl.BlockSpec((4 * rows, 4), lambda i, at_ref: (i ^ at_ref[0], 0))
    part = pl.BlockSpec((1, rows, wide), lambda i, at_ref: (i, 0, 0))
    return pl.pallas_call(
        functools.partial(place_weights_kernel, hidden=hidden),
        out_shape=tuple(jax.ShapeDtypeStruct((count * 4 * rows, n), BF16) for n in widths)
        + (jax.ShapeDtypeStruct((1, wide), F32),),
        grid_spec=pltpu.PrefetchScalarGridSpec(
            num_scalar_prefetch=1,
            grid=(count,),
            in_specs=[part] * 4 + [four],
            out_specs=tuple(
                pl.BlockSpec((4 * rows, n), lambda i, at_ref: (i ^ at_ref[0], 0)) for n in widths
            )
            + (pl.BlockSpec((1, wide), lambda i, at_ref: (0, 0)),),
        ),
        compiler_params=pltpu.CompilerParams(vmem_limit_bytes=BIG_VMEM),
        cost_estimate=SMALL_COST,
    )(jnp.stack([me, rep]).astype(jnp.int32), *parts, norms)


def place_grads_kernel(at_ref, p0_ref, p1_ref, p2_ref, p3_ref, out_ref, *, pieces):
    quarter, wide = p0_ref.shape[1:]
    source = pl.program_id(0) ^ at_ref[0]
    size = wide // pieces
    for k, part_ref in enumerate((p0_ref, p1_ref, p2_ref, p3_ref)):
        rows = pl.ds(pl.multiple_of((at_ref[1] ^ k) * quarter, quarter), quarter)
        values = part_ref[0].astype(F32)
        if pieces == 1:
            out_ref[rows, :] = values
        else:
            for j in range(pieces):
                start = pl.multiple_of((j * HEADS + source) * size, size)
                out_ref[rows, pl.ds(start, size)] = values[:, j * size : (j + 1) * size]


def place_grads(me, rep, parts, pieces):
    count, rows, wide = parts[0].shape
    part = pl.BlockSpec((1, rows, wide), lambda i, at_ref: (i, 0, 0))
    if pieces == 1:
        out = pl.BlockSpec((4 * rows, wide), lambda i, at_ref: (0, i ^ at_ref[0]))
    else:
        out = pl.BlockSpec((4 * rows, count * wide), lambda i, at_ref: (0, 0))
    return pl.pallas_call(
        functools.partial(place_grads_kernel, pieces=pieces),
        out_shape=jax.ShapeDtypeStruct((4 * rows, count * wide), F32),
        grid_spec=pltpu.PrefetchScalarGridSpec(
            num_scalar_prefetch=1, grid=(count,), in_specs=[part] * 4, out_specs=out
        ),
        compiler_params=pltpu.CompilerParams(vmem_limit_bytes=40 << 20),
        cost_estimate=SMALL_COST,
    )(jnp.stack([me, rep]).astype(jnp.int32), *parts)


def place_halves_kernel(core_ref, mine_ref, other_ref, down_ref, dense_ref, *, cut):
    half = mine_ref.shape[1]

    def fill(out_ref):
        for part_ref, core in ((mine_ref, core_ref[0]), (other_ref, 1 - core_ref[0])):
            start = pl.multiple_of(core * half, half)
            out_ref[:, pl.ds(start, half)] = part_ref[...].astype(F32)

    @pl.when(pl.program_id(0) < cut)
    def _():
        fill(down_ref)

    @pl.when(pl.program_id(0) >= cut)
    def _():
        fill(dense_ref)


def place_halves(core, mine, other, hidden):
    rows, half = mine.shape
    tile = 256
    cut = hidden // tile
    part = pl.BlockSpec((tile, half), lambda i, core_ref: (i, 0))
    return pl.pallas_call(
        functools.partial(place_halves_kernel, cut=cut),
        out_shape=(
            jax.ShapeDtypeStruct((hidden, 2 * half), F32),
            jax.ShapeDtypeStruct((rows - hidden, 2 * half), F32),
        ),
        grid_spec=pltpu.PrefetchScalarGridSpec(
            num_scalar_prefetch=1,
            grid=(rows // tile,),
            in_specs=[part, part],
            out_specs=(
                pl.BlockSpec((tile, 2 * half), lambda i, core_ref: (jnp.minimum(i, cut - 1), 0)),
                pl.BlockSpec((tile, 2 * half), lambda i, core_ref: (jnp.maximum(i - cut, 0), 0)),
            ),
        ),
        compiler_params=pltpu.CompilerParams(vmem_limit_bytes=32 << 20),
        cost_estimate=SMALL_COST,
    )(core[None].astype(jnp.int32), mine, other)


def normalize(values):
    values = values.astype(F32)
    centered = values - jnp.mean(values, axis=-1, keepdims=True)
    rstd = lax.rsqrt(jnp.mean(centered * centered, axis=-1, keepdims=True) + EPSILON)
    return centered * rstd, rstd


def norm_kernel(*refs, count, steps):
    blocks, out_ref = refs[:count], refs[-1]
    for k in range(count):

        @pl.when(pl.program_id(0) // steps == k)
        def _(block_ref=blocks[k]):
            out_ref[...] = normalize(block_ref[...])[0].astype(BF16)


def norm_blocks(blocks, places, buffer):
    rows, width = blocks[0].shape
    steps = 2
    tile = rows // steps
    count = len(blocks)

    def spec(k):
        return pl.BlockSpec((tile, width), lambda i: (jnp.clip(i - steps * k, 0, steps - 1), 0))

    def put(i):
        place = places[0]
        for k in range(1, count):
            place = jnp.where(i // steps >= k, places[k], place)
        return place * steps + i % steps, 0

    extra = [] if buffer is None else [buffer]
    return pl.pallas_call(
        functools.partial(norm_kernel, count=count, steps=steps),
        out_shape=jax.ShapeDtypeStruct((HEADS * rows, width), BF16),
        grid=(count * steps,),
        in_specs=[spec(k) for k in range(count)] + [pl.BlockSpec(memory_space=pl.ANY)] * len(extra),
        out_specs=pl.BlockSpec((tile, width), put),
        input_output_aliases={count: 0} if extra else {},
        cost_estimate=SMALL_COST,
    )(*blocks, *extra)


def dot32(left, right, left_dim=1, right_dim=0):
    return lax.dot_general(
        left, right, (((left_dim,), (right_dim,)), ((), ())), preferred_element_type=F32
    )


def tokens_spec(tile, width, first):
    return pl.BlockSpec((tile, width), lambda i: (first + i, 0))


def whole_spec(shape):
    return pl.BlockSpec(shape, lambda i: (0, 0), pipeline_mode=pl.Buffered(1))


def block_specs(count, tile, width):
    return [pl.BlockSpec((tile, width), lambda i: (0, 0)) for _ in range(count)]


def project_kernel(normed_ref, up_ref, qkv_w_ref, shift_ref, *refs):
    act_ref, slope_ref, qkv_ref = refs[-3:]
    hidden = act_ref.shape[1]
    lanes = 256
    for start in range(0, hidden, lanes):
        columns = slice(start, start + lanes)
        value = dot32(normed_ref[...], up_ref[:, columns]) + shift_ref[:, columns]
        normal = 0.5 + 0.5 * lax.erf(value * (0.5**0.5))
        bell = jnp.exp(value * value * -0.5) * ((2.0 * math.pi) ** -0.5)
        act_ref[:, columns] = (value * normal).astype(BF16)
        slope_ref[:, columns] = (normal + value * bell).astype(BF16)
    for start in range(0, qkv_ref.shape[1], lanes):
        columns = slice(start, start + lanes)
        value = dot32(normed_ref[...], qkv_w_ref[:, columns])
        value = value + shift_ref[:, hidden + start : hidden + start + lanes]
        qkv_ref[:, columns] = value.astype(BF16)


def project(normed, w_up, w_qkv, shift, first, last, buffers):
    count, width = normed.shape
    tile = 2 * count // HEADS
    widths = (w_up.shape[1], w_up.shape[1], w_qkv.shape[1])
    return pl.pallas_call(
        project_kernel,
        out_shape=tuple(jax.ShapeDtypeStruct((count, n), BF16) for n in widths),
        grid=(last - first,),
        in_specs=[
            tokens_spec(tile, width, first),
            whole_spec(w_up.shape),
            whole_spec(w_qkv.shape),
            whole_spec(shift.shape),
        ]
        + [pl.BlockSpec(memory_space=pl.ANY)] * len(buffers),
        out_specs=tuple(tokens_spec(tile, n, first) for n in widths),
        input_output_aliases={4 + k: k for k in range(len(buffers))},
        compiler_params=pltpu.CompilerParams(vmem_limit_bytes=BIG_VMEM),
        cost_estimate=SMALL_COST,
    )(normed, w_up, w_qkv, shift, *buffers)


def combine_kernel(one_a_ref, one_b_ref, two_a_ref, two_b_ref, w_one_ref, w_two_ref, *out_refs, right_dim):
    rows = out_refs[0].shape[0]
    for pair, (one_ref, two_ref) in enumerate(((one_a_ref, two_a_ref), (one_b_ref, two_b_ref))):
        value = dot32(one_ref[...], w_one_ref[...], 1, right_dim)
        value = value + dot32(two_ref[...], w_two_ref[...], 1, right_dim)
        out_refs[2 * pair][...] = value[:rows].astype(BF16)
        out_refs[2 * pair + 1][...] = value[rows:].astype(BF16)


def combine(one, two, w_one, w_two, rows, side, right_dim):
    width = w_one.shape[1 - right_dim]
    lanes = 256

    def weight_spec(weight):
        if right_dim:
            return pl.BlockSpec((lanes, weight.shape[1]), lambda i: (i, 0))
        return pl.BlockSpec((weight.shape[0], lanes), lambda i: (0, i))

    def left_spec(left, pair):
        return pl.BlockSpec(
            (2 * rows, left.shape[1]),
            lambda i: (2 * pair + side, 0),
            pipeline_mode=pl.Buffered(1),
        )

    return pl.pallas_call(
        functools.partial(combine_kernel, right_dim=right_dim),
        out_shape=tuple(jax.ShapeDtypeStruct((rows, width), BF16) for _ in range(4)),
        grid=(width // lanes,),
        in_specs=[left_spec(left, pair) for left in (one, two) for pair in (0, 1)]
        + [weight_spec(w_one), weight_spec(w_two)],
        out_specs=tuple(pl.BlockSpec((rows, lanes), lambda i: (0, i)) for _ in range(4)),
        compiler_params=pltpu.CompilerParams(vmem_limit_bytes=BIG_VMEM),
        cost_estimate=SMALL_COST,
    )(one, one, two, two, w_one, w_two)


def pull_kernel(*refs, count):
    blocks, (w_one_ref, w_two_ref, slope_ref) = refs[:count], refs[count : count + 3]
    pre_ref, att_ref, sum_ref, left_ref, sems = refs[-5:]
    rows = blocks[0].shape[0]
    last = pl.num_programs(0) - 1

    @pl.when(pl.program_id(0) == 0)
    def _():
        copies = [
            pltpu.make_async_copy(block, left_ref.at[pl.ds(k * rows, rows)], sems.at[k])
            for k, block in enumerate(blocks)
        ]
        for copy in copies:
            copy.start()
        for copy in copies:
            copy.wait()

    @pl.when(pl.program_id(0) < last)
    def _():
        value = dot32(left_ref[...], w_one_ref[...], 1, 1)
        value = (value * slope_ref[...].astype(F32)).astype(BF16)
        pre_ref[...] = value
        sum_ref[...] = jnp.sum(value.astype(F32), axis=0, keepdims=True)

    @pl.when(pl.program_id(0) == last)
    def _():
        att_ref[...] = dot32(left_ref[...], w_two_ref[...], 1, 1).astype(BF16)


def pull(blocks, w_down, w_dense, slope, part, buffers):
    rows, width = blocks[0].shape
    hidden, head = w_down.shape[0], w_dense.shape[0]
    tokens = HEADS * rows
    count = len(blocks)
    lanes = 256
    steps = hidden // lanes

    def at(i):
        return jnp.minimum(i, steps - 1)

    anywhere = pl.BlockSpec(memory_space=pl.ANY)
    return pl.pallas_call(
        functools.partial(pull_kernel, count=count),
        out_shape=(
            jax.ShapeDtypeStruct((tokens, hidden), BF16),
            jax.ShapeDtypeStruct((tokens, head), BF16),
            jax.ShapeDtypeStruct((1, hidden), F32),
        ),
        grid=(steps + 1,),
        in_specs=[anywhere] * count
        + [
            pl.BlockSpec((lanes, width), lambda i: (at(i), 0)),
            whole_spec(w_dense.shape),
            pl.BlockSpec((count * rows, lanes), lambda i: (part, at(i))),
        ]
        + [anywhere] * len(buffers),
        out_specs=(
            pl.BlockSpec((count * rows, lanes), lambda i: (part, at(i))),
            pl.BlockSpec((count * rows, head), lambda i: (part, 0)),
            pl.BlockSpec((1, lanes), lambda i: (0, at(i))),
        ),
        scratch_shapes=[pltpu.VMEM((count * rows, width), BF16), pltpu.SemaphoreType.DMA((count,))],
        input_output_aliases={count + 3 + k: k for k in range(len(buffers))},
        compiler_params=pltpu.CompilerParams(vmem_limit_bytes=BIG_VMEM),
        cost_estimate=SMALL_COST,
    )(*blocks, w_down, w_dense, slope, *buffers)


def moments_kernel(
    core_ref,
    normed_ref,
    right_ref,
    weight_ref,
    norms_ref,
    columns_ref,
    keep_ref,
    give_ref,
    gain_sum_ref,
    bias_sum_ref,
    low_ref,
    *,
    quarter,
    norm,
):
    lanes = 256
    turned = normed_ref[...].T
    gain = norms_ref[:, 2 * norm : 2 * norm + 1]
    shift = norms_ref[:, 2 * norm + 1 : 2 * norm + 2]
    gain_terms, bias_terms = None, None
    for start in range(0, low_ref.shape[1], lanes):
        columns = slice(start, start + lanes)
        moment = dot32(turned, right_ref[:, columns])
        weight = weight_ref[:, columns].astype(F32)
        total = columns_ref[:, columns]
        low_ref[:, columns] = (moment * gain + shift * total).astype(BF16)
        one, two = moment * weight, weight * total
        gain_terms = one if gain_terms is None else gain_terms + one
        bias_terms = two if bias_terms is None else bias_terms + two
    for terms, sum_ref in ((gain_terms, gain_sum_ref), (bias_terms, bias_sum_ref)):
        sum_ref[...] = jnp.sum(terms.T, axis=0, keepdims=True)
    for core in (0, 1):

        @pl.when(core_ref[0] == core)
        def _(core=core):
            for k in range(low_ref.shape[0] // quarter):
                target = keep_ref if k % 2 == core else give_ref
                target[k // 2 * quarter : (k // 2 + 1) * quarter, :] = low_ref[
                    k * quarter : (k + 1) * quarter, :
                ]


def moments_of(core, normed, right, weight, norms, norm, columns, quarter):
    count, width = normed.shape
    wide = weight.shape[1]
    tile = 8 * quarter
    return pl.pallas_call(
        functools.partial(moments_kernel, quarter=quarter, norm=norm),
        out_shape=(
            jax.ShapeDtypeStruct((width // 2, wide), BF16),
            jax.ShapeDtypeStruct((width // 2, wide), BF16),
            jax.ShapeDtypeStruct((1, width), F32),
            jax.ShapeDtypeStruct((1, width), F32),
        ),
        grid=(width // tile,),
        in_specs=[
            SMEM_SPEC,
            pl.BlockSpec((count, tile), lambda i: (0, i)),
            whole_spec(right.shape),
            tokens_spec(tile, wide, 0),
            tokens_spec(tile, 4, 0),
            whole_spec(columns.shape),
        ],
        out_specs=(
            tokens_spec(tile // 2, wide, 0),
            tokens_spec(tile // 2, wide, 0),
            pl.BlockSpec((1, tile), lambda i: (0, i)),
            pl.BlockSpec((1, tile), lambda i: (0, i)),
        ),
        scratch_shapes=[pltpu.VMEM((tile, wide), BF16)],
        compiler_params=pltpu.CompilerParams(vmem_limit_bytes=BIG_VMEM),
        cost_estimate=SMALL_COST,
    )(core[None].astype(jnp.int32), normed, right, weight, norms, columns)


def outer_kernel(core_ref, act_ref, att_ref, *refs):
    blocks, out_refs = refs[:HEADS], refs[HEADS:]
    rows = blocks[0].shape[0]
    lanes = 512
    last = pl.num_programs(1) - 1

    def fill(left_ref, out_ref):
        turned = left_ref[...].T
        for start in range(0, out_ref.shape[1], lanes):
            columns = slice(start, start + lanes)
            total = None
            for k, block_ref in enumerate(blocks):
                term = dot32(turned[:, k * rows : (k + 1) * rows], block_ref[:, columns])
                total = term if total is None else total + term
            out_ref[:, columns] = total.astype(BF16)

    for side in (0, 1):
        for left_ref, chosen in (
            (act_ref, pl.program_id(1) < last),
            (att_ref, pl.program_id(1) == last),
        ):

            @pl.when((pl.program_id(0) == side) & chosen)
            def _(left_ref=left_ref, side=side):
                fill(left_ref, out_refs[side])


def outer(core, activated, attended, blocks):
    count, hidden = activated.shape
    rows, width = blocks[0].shape
    tile = attended.shape[1]
    steps = hidden // tile
    half = jax.ShapeDtypeStruct((hidden + tile, width // 2), BF16)
    return pl.pallas_call(
        outer_kernel,
        out_shape=(half, half),
        grid_spec=pltpu.PrefetchScalarGridSpec(
            num_scalar_prefetch=1,
            grid=(2, steps + 1),
            in_specs=[
                pl.BlockSpec((count, tile), lambda j, i, core_ref: (0, jnp.minimum(i, steps - 1))),
                pl.BlockSpec((count, tile), lambda j, i, core_ref: (0, 0)),
            ]
            + [
                pl.BlockSpec((rows, width // 2), lambda j, i, core_ref: (0, j ^ core_ref[0]))
                for _ in blocks
            ],
            out_specs=(
                pl.BlockSpec(
                    (tile, width // 2), lambda j, i, core_ref: (jnp.where(j == 0, i, steps), 0)
                ),
                pl.BlockSpec(
                    (tile, width // 2), lambda j, i, core_ref: (jnp.where(j == 0, 0, i), 0)
                ),
            ),
        ),
        compiler_params=pltpu.CompilerParams(vmem_limit_bytes=BIG_VMEM),
        cost_estimate=SMALL_COST,
    )(core[None].astype(jnp.int32), activated, attended, *blocks)


def split_shards(
    tokens,
    cotangent,
    seq_lengths,
    seq_order,
    ln1_gain,
    ln1_bias,
    ln2_gain,
    ln2_bias,
    w_qkv,
    b_qkv,
    w_dense,
    b_dense,
    w_up,
    b_up,
    w_down,
    b_down,
):
    me = lax.axis_index("shard")
    rep = lax.axis_index("rep")
    place = me // 2
    is_middle = (place == 1) | (place == 2)
    own = tokens[:, 0, :]
    own_grad = cotangent[:, 0, :]
    rows, width = own.shape
    group_tokens = rows * HEADS
    depth = w_up.shape[0]
    hidden = w_down.shape[0]
    wide = hidden + 3 * HEAD
    quarter = depth // 4

    odd, keep = pack(me, rep, w_up, w_qkv, hidden)
    odd_came = flip(odd, "shard", 1)
    x_near = flip(own, "shard", 2)
    x_across = send(own, MIDDLE)
    row_offsets, row_counts = stream_rows(seq_lengths[0], seq_order[0], HEADS)
    ends = (row_offsets + row_counts) * HEADS
    seq_scalars = jnp.concatenate([ends, me[None]]).astype(jnp.int32)
    row_range = jnp.arange(rows, dtype=jnp.int32)
    member = (row_range[:, None] >= row_offsets[None, :]) & (
        row_range[:, None] < (row_offsets + row_counts)[None, :]
    )
    in_seq = row_range - jnp.sum(jnp.where(member, row_offsets[None, :], 0), axis=1)
    block_range = jnp.arange(HEADS, dtype=jnp.int32)
    apart = block_range // 4 * 4 + block_range % 2 * 2 + block_range // 2 % 2
    positions = (
        in_seq.reshape(rows // TILE_ROWS, 1, TILE_ROWS) * HEADS + (apart ^ me)[None, :, None]
    )
    cosine, sine = rotary_tables(positions.reshape(-1).astype(F32))
    rest = 128 - ROT
    cosine = jnp.concatenate([cosine, cosine, jnp.ones((group_tokens, rest), F32)], axis=1)
    sine = jnp.concatenate([-sine, sine, jnp.zeros((group_tokens, rest), F32)], axis=1)
    tiled = (rows // TILE_ROWS, TILE_ROWS * HEADS, 128)
    cosine = cosine.reshape(tiled)
    sine = sine.reshape(tiled)


    norms = settled(jnp.stack([ln1_gain, ln1_bias, ln2_gain, ln2_bias], axis=1))
    out_columns = jnp.sum(own_grad, axis=0, dtype=F32)
    b_in = jnp.concatenate(
        [lax.dynamic_slice_in_dim(b_up, me * hidden, hidden, 0)]
        + [lax.dynamic_slice_in_dim(b_qkv, k * width + me * HEAD, HEAD, 0) for k in range(3)]
    )
    pairs = jnp.stack([keep, odd_came], axis=1)
    own, own_grad, x_near, x_across, norms, b_in, out_columns, *pairs = hold(
        (own, own_grad, x_near, x_across, norms, b_in, out_columns, *[pairs[z] for z in range(4)]),
        (cosine, sine),
    )
    got = [flip(pairs[z], "shard", 2 * z) for z in range(1, 4)]
    x_own_y = flip(own, "shard", 1)
    x_near_y = flip(x_near, "shard", 1)
    beside = [flip(pairs[0], "rep", 2)]
    got = jnp.stack(got)
    x_near, x_across, own_grad, x_near_y, got = hold(
        (x_near, x_across, own_grad, x_near_y, got), (x_own_y, beside[0])
    )
    x_across_near = send(x_near, MIDDLE)
    x_two = send(x_across, OUTWARD)
    g_own_y = flip(own_grad, "shard", 1)
    beside = beside + [flip(got, "rep", 2)]
    part = jnp.concatenate([pairs[0][None], got]).reshape(HEADS, quarter, wide)
    normed = norm_blocks([own, x_near, x_own_y, x_near_y], (0, 1, 2, 3), None)
    x_across_near, x_two, own_grad, normed, *beside = hold(
        (x_across_near, x_two, own_grad, normed, *beside), (part, g_own_y)
    )
    two = jnp.where(is_middle, x_across_near, x_two)
    x_three = send(x_across_near, OUTWARD)
    g_across = send(own_grad, MIDDLE)
    x_two_y = flip(two, "shard", 1)
    beside = jnp.concatenate([beside[0][None], beside[1]]).reshape(HEADS, quarter, wide)
    part_c = flip(part, "rep", 1)
    beside_c = flip(beside, "rep", 1)
    normed = norm_blocks([two], (4,), normed)
    parts = (part, part_c, beside, beside_c)
    up_raw, qkv_raw, up_scaled, qkv_scaled, shifted = place_weights(
        me, rep, parts, norms, hidden
    )
    b_in = b_in[None, :] + shifted
    (x_two_y,) = hold((x_two_y,), (b_in,))
    normed = norm_blocks([x_two_y], (6,), normed)
    x_three, own_grad, g_across, normed, b_in = hold(
        (x_three, own_grad, g_across, normed, b_in), ()
    )
    three = jnp.where(is_middle, x_across, x_three)
    g_near = flip(own_grad, "shard", 2)
    x_three_y = flip(three, "shard", 1)
    normed = norm_blocks([three], (5,), normed)
    halfway = project(normed, up_scaled, qkv_scaled, b_in, 0, 3, [])
    g_near, x_three_y, *halfway = hold((g_near, x_three_y, *halfway), ())
    g_across_near = send(g_near, MIDDLE)
    g_two = send(g_across, OUTWARD)
    g_near_y = flip(g_near, "shard", 1)
    normed = norm_blocks([x_three_y], (7,), normed)
    activated, slope, qkv = project(normed, up_scaled, qkv_scaled, b_in, 3, 4, halfway)
    qkv = qkv.reshape(HEADS, rows, 3 * HEAD)
    attended, query, key = attend(seq_scalars, qkv, cosine, sine)
    attended = attended.reshape(group_tokens, HEAD)
    g_across_near, g_two, attended, g_near_y = hold((g_across_near, g_two, attended, g_near_y), ())
    g_two = jnp.where(is_middle, g_across_near, g_two)
    g_three = send(g_across_near, OUTWARD)
    g_two_y = flip(g_two, "shard", 1)
    far = combine(activated, attended, w_down, w_dense, rows, 1, 0)
    close = combine(activated, attended, w_down, w_dense, rows, 0, 0)
    g_three, g_near_y, g_two_y, *both = hold((g_three, g_near_y, g_two_y, *far, *close), ())
    far, close = both[:4], both[4:]
    g_three = jnp.where(is_middle, g_across, g_three)
    g_three_y = flip(g_three, "shard", 1)
    *grads, sums_one = pull([own_grad, g_near, g_own_y, g_near_y], w_down, w_dense, slope, 0, [])
    *grads, sums_two = pull([g_two, g_three], w_down, w_dense, slope, 2, grads)
    g_three_y, *both = hold((g_three_y, *far, *grads), ())
    far, grads = both[:4], both[4:]
    came_three = flip(far[3], "shard", 1)
    grad_pre, grad_attended, sums_three = pull(
        [g_two_y, g_three_y], w_down, w_dense, slope, 3, grads
    )
    pre_sums = sums_one + sums_two + sums_three
    my_core = rep % 2
    my_side = rep // 2
    my_row = me % 2

    def split(values, index):
        return (
            lax.dynamic_index_in_dim(values, index, 1, False),
            lax.dynamic_index_in_dim(values, 1 - index, 1, False),
        )

    def by_side(summed):
        return split(summed.reshape(HEADS, 2, quarter, summed.shape[-1]), my_side)

    def by_row(summed):
        return split(summed.reshape(4, 2, quarter, summed.shape[-1]), my_row)

    def joined(mine, came):
        return plus(mine, came).astype(BF16)

    def by_place(mine, came):
        both = jnp.stack([mine, came], axis=1)
        return [lax.dynamic_index_in_dim(both, place ^ z, 0, False) for z in range(4)]

    def far_places(pieces):
        return flip(jnp.stack(pieces[2:]), "shard", 4)

    def near_place(pieces, far):
        return flip(jnp.stack([pieces[1], far[1]]), "shard", 2)

    def sources(pieces, far, near):
        both = jnp.stack([pieces[0], near[0], far[0], near[1]])
        return both.reshape(HEADS, quarter, both.shape[-1])

    up_keep, up_give, *up_sums = moments_of(
        my_core, normed, grad_pre, up_raw, norms, 1, pre_sums, quarter
    )
    three = joined(close[3], came_three)
    grad_attended, up_give, three, *far = hold((grad_attended, up_give, three, *far), ())
    came_two = flip(far[2], "shard", 1)
    from_corner = send(three, INWARD)
    up_came = flip(up_give, "rep", 1)
    grad_qkv, qkv_sums = attend_back(
        seq_scalars,
        qkv,
        grad_attended.reshape(HEADS, rows, HEAD),
        cosine,
        sine,
        query,
        key,
    )
    grad_qkv = grad_qkv.reshape(group_tokens, 3 * HEAD)
    qkv_keep, qkv_give, *qkv_row_sums = moments_of(
        my_core, normed, grad_qkv, qkv_raw, norms, 0, qkv_sums, quarter
    )
    two = joined(close[2], came_two)
    up_keep, up_give = by_side(joined(up_keep, up_came))
    from_corner, up_give, qkv_give, grad_qkv, two, *far = hold(
        (from_corner, up_give, qkv_give, grad_qkv, two, *far), (up_keep,)
    )
    up_came = flip(up_give, "rep", 2)
    came_one = flip(far[1], "shard", 1)
    two = joined(two, from_corner)
    across_near = send(two, MIDDLE)
    across = send(two, INWARD)
    qkv_came = flip(qkv_give, "rep", 1)
    gy_far = combine(grad_pre, grad_qkv, up_scaled, qkv_scaled, rows, 1, 1)
    one = joined(close[1], came_one)
    up_keep, up_give = by_row(joined(up_keep, up_came))
    qkv_keep, qkv_give = by_side(joined(qkv_keep, qkv_came))
    small = jnp.concatenate(
        [vector[0] for vector in (*qkv_row_sums, *up_sums)]
        + [
            out_columns,
            jnp.where(
                block_range[:, None] == me, jnp.concatenate([pre_sums, qkv_sums], axis=1), 0.0
            ).reshape(-1),
        ]
    )
    up_give, across_near, across, qkv_give, own_grad, one, small, *both = hold(
        (up_give, across_near, across, qkv_give, own_grad, one, small, *far, *gy_far),
        (up_keep, qkv_keep),
    )
    far, gy_far = both[:4], both[4:]
    came_own = flip(far[0], "shard", 1)
    up_came = flip(up_give, "shard", 1)
    one = joined(one, across_near)
    three = plus(three, across).astype(BF16)
    one_near = flip(one, "shard", 2)
    three_across = send(three, MIDDLE)
    qkv_came = flip(qkv_give, "rep", 2)
    half_keep, half_give = outer(
        my_core,
        activated,
        attended,
        [own_grad, g_near, g_own_y, g_near_y, g_two, g_three, g_two_y, g_three_y],
    )
    out_sum = plus(close[0], came_own)
    up_pieces = by_place(up_keep, up_came)
    qkv_keep, qkv_give = by_row(joined(qkv_keep, qkv_came))
    (
        one_near,
        three_across,
        qkv_keep,
        qkv_give,
        half_give,
        out_sum,
        *both,
    ) = hold(
        (
            one_near,
            three_across,
            qkv_keep,
            qkv_give,
            half_give,
            out_sum,
            *up_pieces,
            *gy_far,
            grad_pre,
        ),
        (),
    )
    up_pieces, gy_far, grad_pre = both[:4], both[4:8], both[8]
    came_three = flip(gy_far[3], "shard", 1)
    qkv_came = flip(qkv_give, "shard", 1)
    up_far = far_places(up_pieces)
    half_came = flip(half_give, "rep", 1)
    small_side = flip(small, "rep", 2)
    out_sum = plus(out_sum, one_near, three_across)
    output = (own.astype(F32) + out_sum + (b_dense + b_down)).astype(BF16)
    gy_close = combine(grad_pre, grad_qkv, up_scaled, qkv_scaled, rows, 0, 1)
    qkv_pieces = by_place(qkv_keep, qkv_came)
    three = joined(gy_close[3], came_three)
    output, up_far, half_came, small, small_side, three, *both = hold(
        (output, up_far, half_came, small, small_side, three, *qkv_pieces, *gy_far, *gy_close), ()
    )
    qkv_pieces, gy_far, gy_close = both[:4], both[4:8], both[8:]
    came_two = flip(gy_far[2], "shard", 1)
    from_corner = send(three, INWARD)
    qkv_far = far_places(qkv_pieces)
    half = joined(half_keep, half_came)
    half_far = flip(half, "rep", 2)
    small = small + small_side
    small_side = flip(small, "rep", 1)
    two = joined(gy_close[2], came_two)
    from_corner, qkv_far, small, small_side, two, *gy_far = hold(
        (from_corner, qkv_far, small, small_side, two, *gy_far), ()
    )
    came_one = flip(gy_far[1], "shard", 1)
    two = joined(two, from_corner)
    across_near = send(two, MIDDLE)
    across = send(two, INWARD)
    up_near = near_place(up_pieces, up_far)
    one = joined(gy_close[1], came_one)
    up_part = sources(up_pieces, up_far, up_near)
    across_near, across, up_part, half_far, one, qkv_far, *gy_far = hold(
        (across_near, across, up_part, half_far, one, qkv_far, *gy_far), ()
    )
    came_own = flip(gy_far[0], "shard", 1)
    one = joined(one, across_near)
    three = plus(three, across).astype(BF16)
    one_near = flip(one, "shard", 2)
    three_across = send(three, MIDDLE)
    up_beside = flip(up_part, "rep", 2)
    qkv_near = near_place(qkv_pieces, qkv_far)
    half = joined(half, half_far)
    gy = plus(gy_close[0], came_own)
    qkv_part = sources(qkv_pieces, qkv_far, qkv_near)
    one_near, three_across, qkv_part, up_beside, half, small, gy = hold(
        (one_near, three_across, qkv_part, up_beside, half, small, gy), ()
    )
    qkv_beside = flip(qkv_part, "rep", 2)
    up_c = flip(jnp.stack([up_part, up_beside]), "rep", 1)
    other = flip(half, "rep", 1)
    small = small + small_side
    small = small + flip(small, "shard", 1)
    gy = plus(gy, one_near, three_across)
    own_normed, own_rstd = normalize(own)
    input_grad = own_grad.astype(F32) + own_rstd * (
        gy
        - jnp.mean(gy, axis=-1, keepdims=True)
        - own_normed * jnp.mean(gy * own_normed, axis=-1, keepdims=True)
    )
    input_grad = input_grad[:, None, :]
    up_grad = place_grads(me, rep, (up_part, up_c[0], up_beside, up_c[1]), 1)
    down_grad, dense_grad = place_halves(my_core, half, other, hidden)
    qkv_c = flip(qkv_part, "rep", 1)
    input_grad, up_grad, down_grad, qkv_beside, qkv_c, small = hold(
        (input_grad, up_grad, down_grad, qkv_beside, qkv_c, small), ()
    )
    qkv_beside_c = flip(qkv_beside, "rep", 1)
    one, two, three = [flip(small, "shard", bit) for bit in (2, 4, 6)]
    qkv_grad = place_grads(me, rep, (qkv_part, qkv_c, qkv_beside, qkv_beside_c), 3)
    small, one, two, three = hold((small, one, two, three), (qkv_grad,))
    small = (small + one) + (two + three)
    vectors = small[: 5 * width].reshape(5, width)
    slots = small[5 * width :].reshape(HEADS, wide)
    b_up_grad = slots[:, :hidden].reshape(-1)
    b_qkv_grad = slots[:, hidden:].reshape(HEADS, 3, HEAD).transpose(1, 0, 2).reshape(-1)
    return (
        output[:, None, :],
        input_grad,
        vectors[0],
        vectors[1],
        vectors[2],
        vectors[3],
        qkv_grad,
        b_qkv_grad,
        dense_grad,
        vectors[4],
        up_grad,
        b_up_grad,
        down_grad,
        vectors[4],
    )


def solution(mesh):
    in_specs = (
        P("rep", "shard", None),
        P("rep", "shard", None),
        P("rep", None),
        P("rep", None),
        P(),
        P(),
        P(),
        P(),
        P("shard", None),
        P(),
        P("shard", None),
        P(),
        P("shard", None),
        P(),
        P("shard", None),
        P(),
    )
    out_specs = (
        P("rep", "shard", None),
        P("rep", "shard", None),
        P(),
        P(),
        P(),
        P(),
        P("shard", None),
        P(),
        P("shard", None),
        P(),
        P("shard", None),
        P(),
        P("shard", None),
        P(),
    )
    body = split_shards if mesh.shape["shard"] == HEADS else shards
    return jax.shard_map(
        body, mesh=mesh, in_specs=in_specs, out_specs=out_specs, check_vma=False
    )
```

```python
import functools
import math

import jax
import jax.numpy as jnp
from jax import lax
from jax.experimental import pallas as pl
from jax.experimental.pallas import tpu as pltpu
from jax.sharding import PartitionSpec as P

HEADS = 8
HEAD = 256
ROT = 64


EPSILON = 1e-05
MASKED = -1e30


def layer_norm(vector, gain_vec, shift_vec):
    mean_val = jnp.mean(vector, axis=-1, keepdims=True)
    centered = vector - mean_val
    variance = jnp.mean(centered * centered, axis=-1, keepdims=True)
    return centered * lax.rsqrt(variance + EPSILON) * gain_vec + shift_vec


def gelu_exact(vector):
    return jax.nn.gelu(vector, approximate=False)


def rotary_tables(positions):
    half_rot = ROT // 2
    freq_index = jnp.arange(half_rot, dtype=jnp.float32)
    inverse_freq = jnp.exp(freq_index * (-2.0 * math.log(10000.0) / ROT))
    angles = positions[:, None] * inverse_freq[None, :]
    return (jnp.cos(angles), jnp.sin(angles))


def rotate(heads_in, cosine_table, sine_table):
    half_rot = ROT // 2
    first_half = heads_in[..., :half_rot]
    second_half = heads_in[..., half_rot:ROT]
    cos_wide = cosine_table[:, None, :]
    sin_wide = sine_table[:, None, :]
    return jnp.concatenate(
        [
            first_half * cos_wide - second_half * sin_wide,
            second_half * cos_wide + first_half * sin_wide,
            heads_in[..., ROT:],
        ],
        axis=-1,
    )


def stream_rows(lengths, seq_perm, shard_count):
    seq_range = jnp.arange(lengths.shape[0], dtype=jnp.int32)
    ranking = jnp.sum(
        jnp.where(seq_perm[:, None] == seq_range[None, :], seq_range[:, None], 0), axis=0
    )
    offsets = jnp.sum(jnp.where(ranking[None, :] < ranking[:, None], lengths[None, :], 0), axis=1)
    return (offsets // shard_count, lengths // shard_count)


def row_product(left, right):
    return jnp.dot(left.T, right, preferred_element_type=jnp.float32)


def block_mask(seq_flag, positions, live):
    return (
        live[:, None]
        & live[None, :]
        & (seq_flag[:, None] == seq_flag[None, :])
        & (positions[None, :] <= positions[:, None])
    )


def shards(
    tokens,
    cotangent,
    seq_lengths,
    seq_order,
    ln1_gain,
    ln1_bias,
    ln2_gain,
    ln2_bias,
    w_qkv,
    b_qkv,
    w_dense,
    b_dense,
    w_up,
    b_up,
    w_down,
    b_down,
):
    shard_count = lax.axis_size("shard")
    my_index = lax.axis_index("shard")
    inputs = tokens[:, 0, :].astype(jnp.float32)
    grad_out = cotangent[:, 0, :]
    local_rows, width = inputs.shape
    slot_rows = 2 * (local_rows // shard_count) - 4
    buffer_rows = slot_rows * shard_count
    row_offsets, row_counts = stream_rows(seq_lengths[0], seq_order[0], shard_count)
    first_count = row_counts[0::2]
    second_count = row_counts[1::2]
    first_start = row_offsets[0::2]
    second_start = row_offsets[1::2]
    slot_range = jnp.arange(slot_rows, dtype=jnp.int32)[None, :]
    in_first = slot_range < first_count[:, None]
    slot_live = slot_range < (first_count + second_count)[:, None]
    source_rows = jnp.where(
        in_first,
        first_start[:, None] + slot_range,
        second_start[:, None] + slot_range - first_count[:, None],
    )
    source_rows = jnp.where(slot_live, source_rows, 0)
    seq_range = jnp.arange(row_counts.shape[0], dtype=jnp.int32)
    parity = seq_range % 2
    slot_base = seq_range // 2 * slot_rows + parity * row_counts[seq_range - parity] - row_offsets
    token_range = jnp.arange(local_rows, dtype=jnp.int32)[:, None]
    member = (token_range >= row_offsets[None, :]) & (
        token_range < (row_offsets + row_counts)[None, :]
    )
    return_rows = token_range[:, 0] + jnp.sum(jnp.where(member, slot_base[None, :], 0), axis=1)
    own_first = first_count[my_index]
    own_second = second_count[my_index]
    buffer_range = jnp.arange(buffer_rows, dtype=jnp.int32)
    slot_index = buffer_range % slot_rows
    source_index = buffer_range // slot_rows
    seq_flag = (slot_index >= own_first).astype(jnp.int32)
    positions = (slot_index - seq_flag * own_first) * shard_count + source_index
    live = slot_index < own_first + own_second
    attn_full, dense_full = (
        lax.all_gather(w_qkv, "shard", axis=0, tiled=True),
        lax.all_gather(w_dense, "shard", axis=0, tiled=True),
    )
    up_full, down_full = (
        lax.all_gather(w_up, "shard", axis=0, tiled=True),
        lax.all_gather(w_down, "shard", axis=0, tiled=True),
    )
    normed_one_wide, pull_one = jax.vjp(layer_norm, inputs, ln1_gain, ln1_bias)
    normed_two_wide, pull_two = jax.vjp(layer_norm, inputs, ln2_gain, ln2_bias)
    normed_one = normed_one_wide.astype(jnp.bfloat16)
    normed_two = normed_two_wide.astype(jnp.bfloat16)
    qkv = (jnp.dot(normed_one, attn_full, preferred_element_type=jnp.float32) + b_qkv).astype(
        jnp.bfloat16
    )
    arrived = lax.all_to_all(
        jnp.take(qkv, source_rows, axis=0), "shard", split_axis=0, concat_axis=0, tiled=True
    )
    arrived = arrived.reshape(buffer_rows, 3 * width)
    heads_shape = (buffer_rows, HEADS, HEAD)
    cosine_table, sine_table = rotary_tables(positions.astype(jnp.float32))

    def rotate_here(heads_in):
        return rotate(heads_in, cosine_table, sine_table)

    query_wide, pull_query = jax.vjp(
        rotate_here, arrived[:, :width].astype(jnp.float32).reshape(heads_shape)
    )
    key_wide, pull_key = jax.vjp(
        rotate_here, arrived[:, width : 2 * width].astype(jnp.float32).reshape(heads_shape)
    )
    rotated_queries = query_wide.astype(jnp.bfloat16)
    rotated_keys = key_wide.astype(jnp.bfloat16)
    value_heads = arrived[:, 2 * width :].reshape(heads_shape)
    sources_per = shard_count
    while sources_per > 1 and sources_per * slot_rows > 1024:
        sources_per = sources_per // 2
    block_rows = sources_per * slot_rows
    block_total = buffer_rows // block_rows
    score_scale = HEAD ** (-0.5)

    def forward_block(block_index):
        allowed = block_mask(seq_flag, positions, live)
        scores = (
            jnp.einsum(
                "qhe,khe->hqk", rotated_queries, rotated_keys, preferred_element_type=jnp.float32
            )
            * score_scale
        )
        scores = jnp.where(allowed[None], scores, MASKED)
        row_max = jnp.max(scores, axis=-1, keepdims=True)
        exp_scores = jnp.exp(scores - row_max)
        exp_total = jnp.sum(exp_scores, axis=-1, keepdims=True)
        attn_probs = jnp.where(allowed[None], exp_scores / exp_total, 0.0)
        attended_blk = jnp.einsum(
            "hqk,khe->qhe",
            attn_probs.astype(jnp.bfloat16),
            value_heads,
            preferred_element_type=jnp.float32,
        )
        return (attended_blk.astype(jnp.bfloat16), row_max[..., 0] + jnp.log(exp_total[..., 0]))

    attended_blocks, log_totals = lax.map(forward_block, jnp.arange(block_total, dtype=jnp.int32))
    attended_slots = attended_blocks.reshape(shard_count, slot_rows, width)
    attn_back = lax.all_to_all(
        attended_slots, "shard", split_axis=0, concat_axis=0, tiled=True
    ).reshape(buffer_rows, width)
    attn_in = jnp.take(attn_back, return_rows, axis=0)
    attn_out = jnp.dot(attn_in, dense_full, preferred_element_type=jnp.float32) + b_dense
    pre_up = jnp.dot(normed_two, up_full, preferred_element_type=jnp.float32) + b_up
    activated_wide, pull_gelu = jax.vjp(gelu_exact, pre_up)
    activated = activated_wide.astype(jnp.bfloat16)
    mlp_out = jnp.dot(activated, down_full, preferred_element_type=jnp.float32) + b_down
    output = (inputs + attn_out + mlp_out).astype(jnp.bfloat16)
    attn_second, dense_second = (
        lax.all_gather(w_qkv, "shard", axis=0, tiled=True),
        lax.all_gather(w_dense, "shard", axis=0, tiled=True),
    )
    up_second, down_second = (
        lax.all_gather(w_up, "shard", axis=0, tiled=True),
        lax.all_gather(w_down, "shard", axis=0, tiled=True),
    )
    grad_attended = jnp.dot(grad_out, dense_second.T, preferred_element_type=jnp.float32).astype(
        jnp.bfloat16
    )
    grad_slots = jnp.where(
        slot_live[:, :, None],
        jnp.take(grad_attended, source_rows, axis=0),
        jnp.zeros((), jnp.bfloat16),
    )
    grad_heads = lax.all_to_all(
        grad_slots, "shard", split_axis=0, concat_axis=0, tiled=True
    ).reshape(heads_shape)

    def backward_block(carried, block_index):
        grad_keys, grad_values = carried
        allowed = block_mask(seq_flag, positions, live)
        scores = (
            jnp.einsum(
                "qhe,khe->hqk", rotated_queries, rotated_keys, preferred_element_type=jnp.float32
            )
            * score_scale
        )
        attn_probs = jnp.where(
            allowed[None], jnp.exp(scores - log_totals[block_index][..., None]), 0.0
        )
        grad_probs = jnp.einsum(
            "qhe,khe->hqk", grad_heads, value_heads, preferred_element_type=jnp.float32
        )
        row_delta = jnp.sum(attn_probs * grad_probs, axis=-1, keepdims=True)
        grad_scores = (attn_probs * (grad_probs - row_delta)).astype(jnp.bfloat16)
        grad_query = (
            jnp.einsum(
                "hqk,khe->qhe", grad_scores, rotated_keys, preferred_element_type=jnp.float32
            )
            * score_scale
        )
        grad_keys = (
            grad_keys
            + jnp.einsum(
                "hqk,qhe->khe", grad_scores, rotated_queries, preferred_element_type=jnp.float32
            )
            * score_scale
        )
        grad_values = grad_values + jnp.einsum(
            "hqk,qhe->khe",
            attn_probs.astype(jnp.bfloat16),
            grad_heads,
            preferred_element_type=jnp.float32,
        )
        return ((grad_keys, grad_values), grad_query)

    zero_heads = jnp.zeros(heads_shape, jnp.float32)
    (grad_keys, grad_values), grad_query_blocks = lax.scan(
        backward_block, (zero_heads, zero_heads), jnp.arange(block_total, dtype=jnp.int32)
    )
    grad_q_pre = pull_query(grad_query_blocks.reshape(heads_shape))[0]
    grad_k_pre = pull_key(grad_keys)[0]
    grad_qkv_slots = jnp.concatenate(
        [
            grad_q_pre.reshape(buffer_rows, width),
            grad_k_pre.reshape(buffer_rows, width),
            grad_values.reshape(buffer_rows, width),
        ],
        axis=1,
    ).astype(jnp.bfloat16)
    grad_qkv_slots = grad_qkv_slots.reshape(shard_count, slot_rows, 3 * width)
    grad_qkv_back = lax.all_to_all(grad_qkv_slots, "shard", split_axis=0, concat_axis=0, tiled=True)
    grad_qkv = jnp.take(grad_qkv_back.reshape(buffer_rows, 3 * width), return_rows, axis=0)
    grad_activated = jnp.dot(grad_out, down_second.T, preferred_element_type=jnp.float32)
    grad_pre = pull_gelu(grad_activated)[0].astype(jnp.bfloat16)
    grad_normed_one = jnp.dot(grad_qkv, attn_second.T, preferred_element_type=jnp.float32)
    grad_normed_two = jnp.dot(grad_pre, up_second.T, preferred_element_type=jnp.float32)
    grad_in_one, grad_gain_one, grad_bias_one = pull_one(grad_normed_one)
    grad_in_two, grad_gain_two, grad_bias_two = pull_two(grad_normed_two)
    input_grad = grad_out.astype(jnp.float32) + grad_in_one + grad_in_two
    qkv_rows = lax.psum_scatter(
        row_product(normed_one, grad_qkv).astype(jnp.bfloat16),
        "shard",
        scatter_dimension=0,
        tiled=True,
    ).astype(jnp.float32)
    dense_rows = lax.psum_scatter(
        row_product(attn_in, grad_out).astype(jnp.bfloat16),
        "shard",
        scatter_dimension=0,
        tiled=True,
    ).astype(jnp.float32)
    up_rows = lax.psum_scatter(
        row_product(normed_two, grad_pre).astype(jnp.bfloat16),
        "shard",
        scatter_dimension=0,
        tiled=True,
    ).astype(jnp.float32)
    down_rows = lax.psum_scatter(
        row_product(activated, grad_out).astype(jnp.bfloat16),
        "shard",
        scatter_dimension=0,
        tiled=True,
    ).astype(jnp.float32)
    qkv_rows, dense_rows, up_rows, down_rows = (
        lax.psum(qkv_rows.astype(jnp.bfloat16), "rep").astype(jnp.float32),
        lax.psum(dense_rows.astype(jnp.bfloat16), "rep").astype(jnp.float32),
        lax.psum(up_rows.astype(jnp.bfloat16), "rep").astype(jnp.float32),
        lax.psum(down_rows.astype(jnp.bfloat16), "rep").astype(jnp.float32),
    )
    out_column_sum = jnp.sum(grad_out, axis=0, dtype=jnp.float32)
    small_totals = lax.psum(
        (
            grad_gain_one,
            grad_bias_one,
            grad_gain_two,
            grad_bias_two,
            jnp.sum(grad_qkv, axis=0, dtype=jnp.float32),
            out_column_sum,
            jnp.sum(grad_pre, axis=0, dtype=jnp.float32),
        ),
        ("rep", "shard"),
    )
    return (
        output[:, None, :],
        input_grad[:, None, :],
        small_totals[0],
        small_totals[1],
        small_totals[2],
        small_totals[3],
        qkv_rows,
        small_totals[4],
        dense_rows,
        small_totals[5],
        up_rows,
        small_totals[6],
        down_rows,
        small_totals[5],
    )


TILE_ROWS = 32
BIG_VMEM = 60 << 20
SMALL_COST = pl.CostEstimate(flops=1 << 20, bytes_accessed=1 << 20, transcendentals=0)
F32 = jnp.float32
BF16 = jnp.bfloat16


def flip(value, axis, bit):
    size = lax.axis_size(axis)
    return lax.ppermute(value, axis, [(i, i ^ bit) for i in range(size)])


def send(value, pairs):
    return lax.ppermute(value, "shard", [(2 * a + y, 2 * b + y) for a, b in pairs for y in (0, 1)])


MIDDLE = ((1, 2), (2, 1))
OUTWARD = ((1, 0), (2, 3))
INWARD = ((0, 1), (3, 2))


def plus(*terms):
    total = terms[0].astype(F32)
    for term in terms[1:]:
        total = total + term.astype(F32)
    return total


def hold(values, gates):
    return lax.optimization_barrier(tuple(values) + tuple(gates))[: len(values)]


def turn(heads_in, cosine, sine):
    left = heads_in[:, :128]
    lane = lax.broadcasted_iota(jnp.int32, left.shape, 1)
    half = ROT // 2
    partner = jnp.where(lane < half, pltpu.roll(left, 128 - half, 1), pltpu.roll(left, half, 1))
    return jnp.concatenate([left * cosine + partner * sine, heads_in[:, 128:]], axis=1)


def token_labels(my_index, shape, dim):
    inner = lax.broadcasted_iota(jnp.int32, shape, dim)
    block = inner // TILE_ROWS
    apart = block // 4 * 4 + block % 2 * 2 + block // 2 % 2
    return (inner % TILE_ROWS) * HEADS + jnp.bitwise_xor(apart, my_index)


def tile_weights(tile, seq_ref, query, key_tiles, count):
    tile_tokens = TILE_ROWS * HEADS
    my_index = seq_ref[count]
    query_label = token_labels(my_index, (tile_tokens, 1), 0) + tile * tile_tokens
    key_label = token_labels(my_index, (1, tile_tokens), 1)
    scores = []
    for place, key in key_tiles:
        label = key_label + place * tile_tokens
        last = jnp.full(label.shape, 1 << 30, jnp.int32)
        for k in range(count):
            last = jnp.minimum(last, jnp.where(label < seq_ref[k], seq_ref[k], 1 << 30))
        allowed = query_label < last
        if place == tile:
            allowed = allowed & (label <= query_label)
        product = lax.dot_general(query, key, (((1,), (1,)), ((), ())), preferred_element_type=F32)
        scores.append(jnp.where(allowed, product * HEAD ** (-0.5), MASKED))
    scores = jnp.concatenate(scores, axis=1)
    exp_scores = jnp.exp(scores - jnp.max(scores, axis=1, keepdims=True))
    return exp_scores * (1.0 / jnp.sum(exp_scores, axis=1, keepdims=True))


def attend_kernel(seq_ref, qkv_ref, cos_ref, sin_ref, out_ref, query_ref, key_ref):
    tiles = query_ref.shape[0]
    tile_tokens = TILE_ROWS * HEADS

    def part(tile, lane):
        rows = qkv_ref[:, tile * TILE_ROWS : (tile + 1) * TILE_ROWS, lane : lane + HEAD]
        return rows.reshape(tile_tokens, HEAD)

    for tile in range(tiles):
        cosine, sine = cos_ref[tile], sin_ref[tile]
        query = turn(part(tile, 0).astype(F32), cosine, sine).astype(BF16)
        query_ref[tile] = query
        key_ref[tile] = turn(part(tile, HEAD).astype(F32), cosine, sine).astype(BF16)
        near = list(range(max(tile - 2, 0), tile + 1))
        probs = tile_weights(
            tile, seq_ref, query, [(k, key_ref[k]) for k in near], seq_ref.shape[0] - 1
        ).astype(BF16)
        total = jnp.zeros((tile_tokens, HEAD), F32)
        for at, k in enumerate(near):
            total = total + jnp.dot(
                probs[:, at * tile_tokens : (at + 1) * tile_tokens],
                part(k, 2 * HEAD),
                preferred_element_type=F32,
            )
        out_ref[:, tile * TILE_ROWS : (tile + 1) * TILE_ROWS, :] = total.astype(BF16).reshape(
            HEADS, TILE_ROWS, HEAD
        )


def attend_back_kernel(
    seq_ref, qkv_ref, grad_ref, cos_ref, sin_ref, query_ref, key_ref, out_ref, sum_ref, gk_ref, gv_ref
):
    tiles = query_ref.shape[0]
    tile_tokens = TILE_ROWS * HEADS
    scale = HEAD ** (-0.5)
    over_rows = (((0,), (0,)), ((), ()))
    over_lanes = (((1,), (1,)), ((), ()))

    def rows_of(tile):
        return slice(tile * TILE_ROWS, (tile + 1) * TILE_ROWS)

    def put(tile, lane, value):
        low = value.astype(BF16)
        out_ref[:, rows_of(tile), lane : lane + HEAD] = low.reshape(HEADS, TILE_ROWS, HEAD)
        columns = jnp.sum(low.astype(F32), axis=0, keepdims=True)
        if tile == 0:
            sum_ref[:, lane : lane + HEAD] = columns
        else:
            sum_ref[:, lane : lane + HEAD] += columns

    def finish(tile):
        put(tile, HEAD, turn(gk_ref[tile] * scale, cos_ref[tile], -sin_ref[tile]))
        put(tile, 2 * HEAD, gv_ref[tile])

    for tile in range(tiles):
        query = query_ref[tile]
        near = list(range(max(tile - 2, 0), tile + 1))
        grad = grad_ref[:, rows_of(tile), :].reshape(tile_tokens, HEAD)
        probs = tile_weights(
            tile, seq_ref, query, [(k, key_ref[k]) for k in near], seq_ref.shape[0] - 1
        )
        grad_probs = jnp.concatenate(
            [
                lax.dot_general(
                    grad,
                    qkv_ref[:, rows_of(k), 2 * HEAD :].reshape(tile_tokens, HEAD),
                    over_lanes,
                    preferred_element_type=F32,
                )
                for k in near
            ],
            axis=1,
        )
        delta = jnp.sum(probs * grad_probs, axis=1, keepdims=True)
        grad_scores = (probs * (grad_probs - delta)).astype(BF16)
        probs = probs.astype(BF16)
        grad_query = jnp.zeros((tile_tokens, HEAD), F32)
        for at, k in enumerate(near):
            span = slice(at * tile_tokens, (at + 1) * tile_tokens)
            grad_query = grad_query + jnp.dot(
                grad_scores[:, span], key_ref[k], preferred_element_type=F32
            )
            to_key = lax.dot_general(
                grad_scores[:, span], query, over_rows, preferred_element_type=F32
            )
            to_value = lax.dot_general(probs[:, span], grad, over_rows, preferred_element_type=F32)
            if k == tile:
                gk_ref[k] = to_key
                gv_ref[k] = to_value
            else:
                gk_ref[k] += to_key
                gv_ref[k] += to_value
        put(tile, 0, turn(grad_query * scale, cos_ref[tile], -sin_ref[tile]))
        if tile >= 2:
            finish(tile - 2)
    for tile in range(max(tiles - 2, 0), tiles):
        finish(tile)


def one_spec(shape):
    return pl.BlockSpec(shape, lambda i: (0,) * len(shape), pipeline_mode=pl.Buffered(1))


SMEM_SPEC = pl.BlockSpec(memory_space=pltpu.SMEM)


def attend(seq_scalars, qkv, cosine, sine):
    blocks, rows, _ = qkv.shape
    tiled = (rows // TILE_ROWS, blocks * TILE_ROWS, HEAD)
    return pl.pallas_call(
        attend_kernel,
        out_shape=(
            jax.ShapeDtypeStruct((blocks, rows, HEAD), BF16),
            jax.ShapeDtypeStruct(tiled, BF16),
            jax.ShapeDtypeStruct(tiled, BF16),
        ),
        grid=(1,),
        in_specs=[SMEM_SPEC] + [one_spec(array.shape) for array in (qkv, cosine, sine)],
        out_specs=(one_spec((blocks, rows, HEAD)), one_spec(tiled), one_spec(tiled)),
        compiler_params=pltpu.CompilerParams(vmem_limit_bytes=BIG_VMEM),
        cost_estimate=SMALL_COST,
    )(seq_scalars, qkv, cosine, sine)


def attend_back(seq_scalars, qkv, grad, cosine, sine, query, key):
    blocks, rows, wide = qkv.shape
    return pl.pallas_call(
        attend_back_kernel,
        out_shape=(
            jax.ShapeDtypeStruct((blocks, rows, wide), BF16),
            jax.ShapeDtypeStruct((1, wide), F32),
        ),
        grid=(1,),
        in_specs=[SMEM_SPEC]
        + [one_spec(array.shape) for array in (qkv, grad, cosine, sine, query, key)],
        out_specs=(one_spec((blocks, rows, wide)), one_spec((1, wide))),
        scratch_shapes=[pltpu.VMEM(query.shape, F32), pltpu.VMEM(query.shape, F32)],
        compiler_params=pltpu.CompilerParams(vmem_limit_bytes=BIG_VMEM),
        cost_estimate=SMALL_COST,
    )(seq_scalars, qkv, grad, cosine, sine, query, key)


def copy_kernel(in_ref, out_ref):
    out_ref[...] = in_ref[...]


def settled(values):
    return pl.pallas_call(
        copy_kernel,
        out_shape=jax.ShapeDtypeStruct(values.shape, values.dtype),
        grid=(1,),
        in_specs=[pl.BlockSpec(values.shape, lambda i: (0, 0))],
        out_specs=pl.BlockSpec(values.shape, lambda i: (0, 0)),
        cost_estimate=SMALL_COST,
    )(values)


def pack_kernel(at_ref, up_ref, qkv_ref, odd_ref, even_ref):
    third = qkv_ref.shape[1] // 3
    hidden = up_ref.shape[1] // HEADS
    for k in range(HEADS):
        out_ref = even_ref if k % 2 == 0 else odd_ref
        target = at_ref[0] ^ k
        start = pl.multiple_of(target * hidden, hidden)
        out_ref[k // 2, :, :hidden] = up_ref[:, pl.ds(start, hidden)]
        for j in range(3):
            start = pl.multiple_of(j * third + target * HEAD, HEAD)
            out_ref[k // 2, :, hidden + j * HEAD : hidden + (j + 1) * HEAD] = qkv_ref[
                :, pl.ds(start, HEAD)
            ]


def pack(me, rep, w_up, w_qkv, hidden):
    quarter = w_up.shape[0] // 4
    shape = (HEADS // 2, quarter, hidden + 3 * HEAD)
    packed = jax.ShapeDtypeStruct(shape, BF16)
    return pl.pallas_call(
        pack_kernel,
        out_shape=(packed, packed),
        grid_spec=pltpu.PrefetchScalarGridSpec(
            num_scalar_prefetch=1,
            grid=(1,),
            in_specs=[
                pl.BlockSpec((quarter, weight.shape[1]), lambda i, at_ref: (at_ref[1], 0))
                for weight in (w_up, w_qkv)
            ],
            out_specs=tuple(pl.BlockSpec(shape, lambda i, at_ref: (0, 0, 0)) for _ in range(2)),
        ),
        compiler_params=pltpu.CompilerParams(vmem_limit_bytes=24 << 20),
        cost_estimate=SMALL_COST,
    )(jnp.stack([me, rep]).astype(jnp.int32), w_up, w_qkv)


def place_weights_kernel(
    at_ref, p0_ref, p1_ref, p2_ref, p3_ref, norms_ref, *out_refs, hidden
):
    raw_refs, scaled_refs, sum_ref = out_refs[:2], out_refs[2:4], out_refs[4]
    quarter, wide = p0_ref.shape[1:]

    @pl.when(pl.program_id(0) == 0)
    def _():
        sum_ref[...] = jnp.zeros_like(sum_ref)

    for k, part_ref in enumerate((p0_ref, p1_ref, p2_ref, p3_ref)):
        rows = pl.ds(pl.multiple_of((at_ref[1] ^ k) * quarter, quarter), quarter)
        for norm, columns in ((1, slice(0, hidden)), (0, slice(hidden, wide))):
            raw = part_ref[0, :, columns]
            raw_refs[1 - norm][rows, :] = raw
            weight = raw.astype(F32)
            gain = norms_ref[rows, 2 * norm : 2 * norm + 1]
            shift = norms_ref[rows, 2 * norm + 1 : 2 * norm + 2]
            scaled_refs[1 - norm][rows, :] = (weight * gain).astype(BF16)
            sum_ref[:, columns] += jnp.sum(weight * shift, axis=0, keepdims=True)


def place_weights(me, rep, parts, norms, hidden):
    count, rows, wide = parts[0].shape
    widths = (hidden, wide - hidden) * 2
    four = pl.BlockSpec((4 * rows, 4), lambda i, at_ref: (i ^ at_ref[0], 0))
    part = pl.BlockSpec((1, rows, wide), lambda i, at_ref: (i, 0, 0))
    return pl.pallas_call(
        functools.partial(place_weights_kernel, hidden=hidden),
        out_shape=tuple(jax.ShapeDtypeStruct((count * 4 * rows, n), BF16) for n in widths)
        + (jax.ShapeDtypeStruct((1, wide), F32),),
        grid_spec=pltpu.PrefetchScalarGridSpec(
            num_scalar_prefetch=1,
            grid=(count,),
            in_specs=[part] * 4 + [four],
            out_specs=tuple(
                pl.BlockSpec((4 * rows, n), lambda i, at_ref: (i ^ at_ref[0], 0)) for n in widths
            )
            + (pl.BlockSpec((1, wide), lambda i, at_ref: (0, 0)),),
        ),
        compiler_params=pltpu.CompilerParams(vmem_limit_bytes=BIG_VMEM),
        cost_estimate=SMALL_COST,
    )(jnp.stack([me, rep]).astype(jnp.int32), *parts, norms)


def place_grads_kernel(at_ref, p0_ref, p1_ref, p2_ref, p3_ref, out_ref, *, pieces):
    quarter, wide = p0_ref.shape[1:]
    source = pl.program_id(0) ^ at_ref[0]
    size = wide // pieces
    for k, part_ref in enumerate((p0_ref, p1_ref, p2_ref, p3_ref)):
        rows = pl.ds(pl.multiple_of((at_ref[1] ^ k) * quarter, quarter), quarter)
        values = part_ref[0].astype(F32)
        if pieces == 1:
            out_ref[rows, :] = values
        else:
            for j in range(pieces):
                start = pl.multiple_of((j * HEADS + source) * size, size)
                out_ref[rows, pl.ds(start, size)] = values[:, j * size : (j + 1) * size]


def place_grads(me, rep, parts, pieces):
    count, rows, wide = parts[0].shape
    part = pl.BlockSpec((1, rows, wide), lambda i, at_ref: (i, 0, 0))
    if pieces == 1:
        out = pl.BlockSpec((4 * rows, wide), lambda i, at_ref: (0, i ^ at_ref[0]))
    else:
        out = pl.BlockSpec((4 * rows, count * wide), lambda i, at_ref: (0, 0))
    return pl.pallas_call(
        functools.partial(place_grads_kernel, pieces=pieces),
        out_shape=jax.ShapeDtypeStruct((4 * rows, count * wide), F32),
        grid_spec=pltpu.PrefetchScalarGridSpec(
            num_scalar_prefetch=1, grid=(count,), in_specs=[part] * 4, out_specs=out
        ),
        compiler_params=pltpu.CompilerParams(vmem_limit_bytes=40 << 20),
        cost_estimate=SMALL_COST,
    )(jnp.stack([me, rep]).astype(jnp.int32), *parts)


def place_halves_kernel(core_ref, mine_ref, other_ref, down_ref, dense_ref, *, cut):
    half = mine_ref.shape[1]

    def fill(out_ref):
        for part_ref, core in ((mine_ref, core_ref[0]), (other_ref, 1 - core_ref[0])):
            start = pl.multiple_of(core * half, half)
            out_ref[:, pl.ds(start, half)] = part_ref[...].astype(F32)

    @pl.when(pl.program_id(0) < cut)
    def _():
        fill(down_ref)

    @pl.when(pl.program_id(0) >= cut)
    def _():
        fill(dense_ref)


def place_halves(core, mine, other, hidden):
    rows, half = mine.shape
    tile = 256
    cut = hidden // tile
    part = pl.BlockSpec((tile, half), lambda i, core_ref: (i, 0))
    return pl.pallas_call(
        functools.partial(place_halves_kernel, cut=cut),
        out_shape=(
            jax.ShapeDtypeStruct((hidden, 2 * half), F32),
            jax.ShapeDtypeStruct((rows - hidden, 2 * half), F32),
        ),
        grid_spec=pltpu.PrefetchScalarGridSpec(
            num_scalar_prefetch=1,
            grid=(rows // tile,),
            in_specs=[part, part],
            out_specs=(
                pl.BlockSpec((tile, 2 * half), lambda i, core_ref: (jnp.minimum(i, cut - 1), 0)),
                pl.BlockSpec((tile, 2 * half), lambda i, core_ref: (jnp.maximum(i - cut, 0), 0)),
            ),
        ),
        compiler_params=pltpu.CompilerParams(vmem_limit_bytes=32 << 20),
        cost_estimate=SMALL_COST,
    )(core[None].astype(jnp.int32), mine, other)


def normalize(values):
    values = values.astype(F32)
    centered = values - jnp.mean(values, axis=-1, keepdims=True)
    rstd = lax.rsqrt(jnp.mean(centered * centered, axis=-1, keepdims=True) + EPSILON)
    return centered * rstd, rstd


def norm_kernel(*refs, count, steps):
    blocks, out_ref = refs[:count], refs[-1]
    for k in range(count):

        @pl.when(pl.program_id(0) // steps == k)
        def _(block_ref=blocks[k]):
            out_ref[...] = normalize(block_ref[...])[0].astype(BF16)


def norm_blocks(blocks, places, buffer):
    rows, width = blocks[0].shape
    steps = 2
    tile = rows // steps
    count = len(blocks)

    def spec(k):
        return pl.BlockSpec((tile, width), lambda i: (jnp.clip(i - steps * k, 0, steps - 1), 0))

    def put(i):
        place = places[0]
        for k in range(1, count):
            place = jnp.where(i // steps >= k, places[k], place)
        return place * steps + i % steps, 0

    extra = [] if buffer is None else [buffer]
    return pl.pallas_call(
        functools.partial(norm_kernel, count=count, steps=steps),
        out_shape=jax.ShapeDtypeStruct((HEADS * rows, width), BF16),
        grid=(count * steps,),
        in_specs=[spec(k) for k in range(count)] + [pl.BlockSpec(memory_space=pl.ANY)] * len(extra),
        out_specs=pl.BlockSpec((tile, width), put),
        input_output_aliases={count: 0} if extra else {},
        cost_estimate=SMALL_COST,
    )(*blocks, *extra)


def dot32(left, right, left_dim=1, right_dim=0):
    return lax.dot_general(
        left, right, (((left_dim,), (right_dim,)), ((), ())), preferred_element_type=F32
    )


def tokens_spec(tile, width, first):
    return pl.BlockSpec((tile, width), lambda i: (first + i, 0))


def whole_spec(shape):
    return pl.BlockSpec(shape, lambda i: (0, 0), pipeline_mode=pl.Buffered(1))


def block_specs(count, tile, width):
    return [pl.BlockSpec((tile, width), lambda i: (0, 0)) for _ in range(count)]


def project_kernel(normed_ref, up_ref, qkv_w_ref, shift_ref, *refs):
    act_ref, slope_ref, qkv_ref = refs[-3:]
    hidden = act_ref.shape[1]
    lanes = 256
    for start in range(0, hidden, lanes):
        columns = slice(start, start + lanes)
        value = dot32(normed_ref[...], up_ref[:, columns]) + shift_ref[:, columns]
        normal = 0.5 + 0.5 * lax.erf(value * (0.5**0.5))
        bell = jnp.exp(value * value * -0.5) * ((2.0 * math.pi) ** -0.5)
        act_ref[:, columns] = (value * normal).astype(BF16)
        slope_ref[:, columns] = (normal + value * bell).astype(BF16)
    for start in range(0, qkv_ref.shape[1], lanes):
        columns = slice(start, start + lanes)
        value = dot32(normed_ref[...], qkv_w_ref[:, columns])
        value = value + shift_ref[:, hidden + start : hidden + start + lanes]
        qkv_ref[:, columns] = value.astype(BF16)


def project(normed, w_up, w_qkv, shift, first, last, buffers):
    count, width = normed.shape
    tile = 2 * count // HEADS
    widths = (w_up.shape[1], w_up.shape[1], w_qkv.shape[1])
    return pl.pallas_call(
        project_kernel,
        out_shape=tuple(jax.ShapeDtypeStruct((count, n), BF16) for n in widths),
        grid=(last - first,),
        in_specs=[
            tokens_spec(tile, width, first),
            whole_spec(w_up.shape),
            whole_spec(w_qkv.shape),
            whole_spec(shift.shape),
        ]
        + [pl.BlockSpec(memory_space=pl.ANY)] * len(buffers),
        out_specs=tuple(tokens_spec(tile, n, first) for n in widths),
        input_output_aliases={4 + k: k for k in range(len(buffers))},
        compiler_params=pltpu.CompilerParams(vmem_limit_bytes=BIG_VMEM),
        cost_estimate=SMALL_COST,
    )(normed, w_up, w_qkv, shift, *buffers)


def combine_kernel(one_a_ref, one_b_ref, two_a_ref, two_b_ref, w_one_ref, w_two_ref, *out_refs, right_dim):
    rows = out_refs[0].shape[0]
    for pair, (one_ref, two_ref) in enumerate(((one_a_ref, two_a_ref), (one_b_ref, two_b_ref))):
        value = dot32(one_ref[...], w_one_ref[...], 1, right_dim)
        value = value + dot32(two_ref[...], w_two_ref[...], 1, right_dim)
        out_refs[2 * pair][...] = value[:rows].astype(BF16)
        out_refs[2 * pair + 1][...] = value[rows:].astype(BF16)


def combine(one, two, w_one, w_two, rows, side, right_dim):
    width = w_one.shape[1 - right_dim]
    lanes = 512

    def weight_spec(weight):
        if right_dim:
            return pl.BlockSpec((lanes, weight.shape[1]), lambda i: (i, 0))
        return pl.BlockSpec((weight.shape[0], lanes), lambda i: (0, i))

    def left_spec(left, pair):
        return pl.BlockSpec(
            (2 * rows, left.shape[1]),
            lambda i: (2 * pair + side, 0),
            pipeline_mode=pl.Buffered(1),
        )

    return pl.pallas_call(
        functools.partial(combine_kernel, right_dim=right_dim),
        out_shape=tuple(jax.ShapeDtypeStruct((rows, width), BF16) for _ in range(4)),
        grid=(width // lanes,),
        in_specs=[left_spec(left, pair) for left in (one, two) for pair in (0, 1)]
        + [weight_spec(w_one), weight_spec(w_two)],
        out_specs=tuple(pl.BlockSpec((rows, lanes), lambda i: (0, i)) for _ in range(4)),
        compiler_params=pltpu.CompilerParams(vmem_limit_bytes=BIG_VMEM),
        cost_estimate=SMALL_COST,
    )(one, one, two, two, w_one, w_two)


def pull_kernel(*refs, count):
    blocks, (w_one_ref, w_two_ref, slope_ref) = refs[:count], refs[count : count + 3]
    pre_ref, att_ref, sum_ref, left_ref, sems = refs[-5:]
    rows = blocks[0].shape[0]
    last = pl.num_programs(0) - 1

    @pl.when(pl.program_id(0) == 0)
    def _():
        copies = [
            pltpu.make_async_copy(block, left_ref.at[pl.ds(k * rows, rows)], sems.at[k])
            for k, block in enumerate(blocks)
        ]
        for copy in copies:
            copy.start()
        for copy in copies:
            copy.wait()

    @pl.when(pl.program_id(0) < last)
    def _():
        value = dot32(left_ref[...], w_one_ref[...], 1, 1)
        value = (value * slope_ref[...].astype(F32)).astype(BF16)
        pre_ref[...] = value
        sum_ref[...] = jnp.sum(value.astype(F32), axis=0, keepdims=True)

    @pl.when(pl.program_id(0) == last)
    def _():
        att_ref[...] = dot32(left_ref[...], w_two_ref[...], 1, 1).astype(BF16)


def pull(blocks, w_down, w_dense, slope, part, buffers):
    rows, width = blocks[0].shape
    hidden, head = w_down.shape[0], w_dense.shape[0]
    tokens = HEADS * rows
    count = len(blocks)
    lanes = 256
    steps = hidden // lanes

    def at(i):
        return jnp.minimum(i, steps - 1)

    anywhere = pl.BlockSpec(memory_space=pl.ANY)
    return pl.pallas_call(
        functools.partial(pull_kernel, count=count),
        out_shape=(
            jax.ShapeDtypeStruct((tokens, hidden), BF16),
            jax.ShapeDtypeStruct((tokens, head), BF16),
            jax.ShapeDtypeStruct((1, hidden), F32),
        ),
        grid=(steps + 1,),
        in_specs=[anywhere] * count
        + [
            pl.BlockSpec((lanes, width), lambda i: (at(i), 0)),
            whole_spec(w_dense.shape),
            pl.BlockSpec((count * rows, lanes), lambda i: (part, at(i))),
        ]
        + [anywhere] * len(buffers),
        out_specs=(
            pl.BlockSpec((count * rows, lanes), lambda i: (part, at(i))),
            pl.BlockSpec((count * rows, head), lambda i: (part, 0)),
            pl.BlockSpec((1, lanes), lambda i: (0, at(i))),
        ),
        scratch_shapes=[pltpu.VMEM((count * rows, width), BF16), pltpu.SemaphoreType.DMA((count,))],
        input_output_aliases={count + 3 + k: k for k in range(len(buffers))},
        compiler_params=pltpu.CompilerParams(vmem_limit_bytes=BIG_VMEM),
        cost_estimate=SMALL_COST,
    )(*blocks, w_down, w_dense, slope, *buffers)


def moments_kernel(
    core_ref,
    normed_ref,
    right_ref,
    weight_ref,
    norms_ref,
    columns_ref,
    keep_ref,
    give_ref,
    gain_sum_ref,
    bias_sum_ref,
    low_ref,
    *,
    quarter,
    norm,
):
    lanes = 256
    turned = normed_ref[...].T
    gain = norms_ref[:, 2 * norm : 2 * norm + 1]
    shift = norms_ref[:, 2 * norm + 1 : 2 * norm + 2]
    gain_terms, bias_terms = None, None
    for start in range(0, low_ref.shape[1], lanes):
        columns = slice(start, start + lanes)
        moment = dot32(turned, right_ref[:, columns])
        weight = weight_ref[:, columns].astype(F32)
        total = columns_ref[:, columns]
        low_ref[:, columns] = (moment * gain + shift * total).astype(BF16)
        one, two = moment * weight, weight * total
        gain_terms = one if gain_terms is None else gain_terms + one
        bias_terms = two if bias_terms is None else bias_terms + two
    for terms, sum_ref in ((gain_terms, gain_sum_ref), (bias_terms, bias_sum_ref)):
        sum_ref[...] = jnp.sum(terms.T, axis=0, keepdims=True)
    for core in (0, 1):

        @pl.when(core_ref[0] == core)
        def _(core=core):
            for k in range(low_ref.shape[0] // quarter):
                target = keep_ref if k % 2 == core else give_ref
                target[k // 2 * quarter : (k // 2 + 1) * quarter, :] = low_ref[
                    k * quarter : (k + 1) * quarter, :
                ]


def moments_of(core, normed, right, weight, norms, norm, columns, quarter):
    count, width = normed.shape
    wide = weight.shape[1]
    tile = 8 * quarter
    return pl.pallas_call(
        functools.partial(moments_kernel, quarter=quarter, norm=norm),
        out_shape=(
            jax.ShapeDtypeStruct((width // 2, wide), BF16),
            jax.ShapeDtypeStruct((width // 2, wide), BF16),
            jax.ShapeDtypeStruct((1, width), F32),
            jax.ShapeDtypeStruct((1, width), F32),
        ),
        grid=(width // tile,),
        in_specs=[
            SMEM_SPEC,
            pl.BlockSpec((count, tile), lambda i: (0, i)),
            whole_spec(right.shape),
            tokens_spec(tile, wide, 0),
            tokens_spec(tile, 4, 0),
            whole_spec(columns.shape),
        ],
        out_specs=(
            tokens_spec(tile // 2, wide, 0),
            tokens_spec(tile // 2, wide, 0),
            pl.BlockSpec((1, tile), lambda i: (0, i)),
            pl.BlockSpec((1, tile), lambda i: (0, i)),
        ),
        scratch_shapes=[pltpu.VMEM((tile, wide), BF16)],
        compiler_params=pltpu.CompilerParams(vmem_limit_bytes=BIG_VMEM),
        cost_estimate=SMALL_COST,
    )(core[None].astype(jnp.int32), normed, right, weight, norms, columns)


def outer_kernel(core_ref, act_ref, att_ref, *refs):
    blocks, out_refs = refs[:HEADS], refs[HEADS:]
    rows = blocks[0].shape[0]
    lanes = 512
    last = pl.num_programs(1) - 1

    def fill(left_ref, out_ref):
        turned = left_ref[...].T
        for start in range(0, out_ref.shape[1], lanes):
            columns = slice(start, start + lanes)
            total = None
            for k, block_ref in enumerate(blocks):
                term = dot32(turned[:, k * rows : (k + 1) * rows], block_ref[:, columns])
                total = term if total is None else total + term
            out_ref[:, columns] = total.astype(BF16)

    for side in (0, 1):
        for left_ref, chosen in (
            (act_ref, pl.program_id(1) < last),
            (att_ref, pl.program_id(1) == last),
        ):

            @pl.when((pl.program_id(0) == side) & chosen)
            def _(left_ref=left_ref, side=side):
                fill(left_ref, out_refs[side])


def outer(core, activated, attended, blocks):
    count, hidden = activated.shape
    rows, width = blocks[0].shape
    tile = attended.shape[1]
    steps = hidden // tile
    half = jax.ShapeDtypeStruct((hidden + tile, width // 2), BF16)
    return pl.pallas_call(
        outer_kernel,
        out_shape=(half, half),
        grid_spec=pltpu.PrefetchScalarGridSpec(
            num_scalar_prefetch=1,
            grid=(2, steps + 1),
            in_specs=[
                pl.BlockSpec((count, tile), lambda j, i, core_ref: (0, jnp.minimum(i, steps - 1))),
                pl.BlockSpec((count, tile), lambda j, i, core_ref: (0, 0)),
            ]
            + [
                pl.BlockSpec((rows, width // 2), lambda j, i, core_ref: (0, j ^ core_ref[0]))
                for _ in blocks
            ],
            out_specs=(
                pl.BlockSpec(
                    (tile, width // 2), lambda j, i, core_ref: (jnp.where(j == 0, i, steps), 0)
                ),
                pl.BlockSpec(
                    (tile, width // 2), lambda j, i, core_ref: (jnp.where(j == 0, 0, i), 0)
                ),
            ),
        ),
        compiler_params=pltpu.CompilerParams(vmem_limit_bytes=BIG_VMEM),
        cost_estimate=SMALL_COST,
    )(core[None].astype(jnp.int32), activated, attended, *blocks)


def split_shards(
    tokens,
    cotangent,
    seq_lengths,
    seq_order,
    ln1_gain,
    ln1_bias,
    ln2_gain,
    ln2_bias,
    w_qkv,
    b_qkv,
    w_dense,
    b_dense,
    w_up,
    b_up,
    w_down,
    b_down,
):
    me = lax.axis_index("shard")
    rep = lax.axis_index("rep")
    place = me // 2
    is_middle = (place == 1) | (place == 2)
    own = tokens[:, 0, :]
    own_grad = cotangent[:, 0, :]
    rows, width = own.shape
    group_tokens = rows * HEADS
    depth = w_up.shape[0]
    hidden = w_down.shape[0]
    wide = hidden + 3 * HEAD
    quarter = depth // 4

    odd, keep = pack(me, rep, w_up, w_qkv, hidden)
    odd_came = flip(odd, "shard", 1)
    x_near = flip(own, "shard", 2)
    x_across = send(own, MIDDLE)
    row_offsets, row_counts = stream_rows(seq_lengths[0], seq_order[0], HEADS)
    ends = (row_offsets + row_counts) * HEADS
    seq_scalars = jnp.concatenate([ends, me[None]]).astype(jnp.int32)
    row_range = jnp.arange(rows, dtype=jnp.int32)
    member = (row_range[:, None] >= row_offsets[None, :]) & (
        row_range[:, None] < (row_offsets + row_counts)[None, :]
    )
    in_seq = row_range - jnp.sum(jnp.where(member, row_offsets[None, :], 0), axis=1)
    block_range = jnp.arange(HEADS, dtype=jnp.int32)
    apart = block_range // 4 * 4 + block_range % 2 * 2 + block_range // 2 % 2
    positions = (
        in_seq.reshape(rows // TILE_ROWS, 1, TILE_ROWS) * HEADS + (apart ^ me)[None, :, None]
    )
    cosine, sine = rotary_tables(positions.reshape(-1).astype(F32))
    rest = 128 - ROT
    cosine = jnp.concatenate([cosine, cosine, jnp.ones((group_tokens, rest), F32)], axis=1)
    sine = jnp.concatenate([-sine, sine, jnp.zeros((group_tokens, rest), F32)], axis=1)
    tiled = (rows // TILE_ROWS, TILE_ROWS * HEADS, 128)
    cosine = cosine.reshape(tiled)
    sine = sine.reshape(tiled)


    norms = settled(jnp.stack([ln1_gain, ln1_bias, ln2_gain, ln2_bias], axis=1))
    out_columns = jnp.sum(own_grad, axis=0, dtype=F32)
    b_in = jnp.concatenate(
        [lax.dynamic_slice_in_dim(b_up, me * hidden, hidden, 0)]
        + [lax.dynamic_slice_in_dim(b_qkv, k * width + me * HEAD, HEAD, 0) for k in range(3)]
    )
    pairs = jnp.stack([keep, odd_came], axis=1)
    own, own_grad, x_near, x_across, norms, b_in, out_columns, *pairs = hold(
        (own, own_grad, x_near, x_across, norms, b_in, out_columns, *[pairs[z] for z in range(4)]),
        (cosine, sine),
    )
    got = [flip(pairs[z], "shard", 2 * z) for z in range(1, 4)]
    x_own_y = flip(own, "shard", 1)
    x_near_y = flip(x_near, "shard", 1)
    beside = [flip(pairs[0], "rep", 2)]
    got = jnp.stack(got)
    x_near, x_across, own_grad, x_near_y, got = hold(
        (x_near, x_across, own_grad, x_near_y, got), (x_own_y, beside[0])
    )
    x_across_near = send(x_near, MIDDLE)
    x_two = send(x_across, OUTWARD)
    g_own_y = flip(own_grad, "shard", 1)
    beside = beside + [flip(got, "rep", 2)]
    part = jnp.concatenate([pairs[0][None], got]).reshape(HEADS, quarter, wide)
    normed = norm_blocks([own, x_near, x_own_y, x_near_y], (0, 1, 2, 3), None)
    x_across_near, x_two, own_grad, normed, *beside = hold(
        (x_across_near, x_two, own_grad, normed, *beside), (part, g_own_y)
    )
    two = jnp.where(is_middle, x_across_near, x_two)
    x_three = send(x_across_near, OUTWARD)
    g_across = send(own_grad, MIDDLE)
    x_two_y = flip(two, "shard", 1)
    beside = jnp.concatenate([beside[0][None], beside[1]]).reshape(HEADS, quarter, wide)
    part_c = flip(part, "rep", 1)
    beside_c = flip(beside, "rep", 1)
    normed = norm_blocks([two], (4,), normed)
    parts = (part, part_c, beside, beside_c)
    up_raw, qkv_raw, up_scaled, qkv_scaled, shifted = place_weights(
        me, rep, parts, norms, hidden
    )
    b_in = b_in[None, :] + shifted
    (x_two_y,) = hold((x_two_y,), (b_in,))
    normed = norm_blocks([x_two_y], (6,), normed)
    x_three, own_grad, g_across, normed, b_in = hold(
        (x_three, own_grad, g_across, normed, b_in), ()
    )
    three = jnp.where(is_middle, x_across, x_three)
    g_near = flip(own_grad, "shard", 2)
    x_three_y = flip(three, "shard", 1)
    normed = norm_blocks([three], (5,), normed)
    halfway = project(normed, up_scaled, qkv_scaled, b_in, 0, 3, [])
    g_near, x_three_y, *halfway = hold((g_near, x_three_y, *halfway), ())
    g_across_near = send(g_near, MIDDLE)
    g_two = send(g_across, OUTWARD)
    g_near_y = flip(g_near, "shard", 1)
    normed = norm_blocks([x_three_y], (7,), normed)
    activated, slope, qkv = project(normed, up_scaled, qkv_scaled, b_in, 3, 4, halfway)
    qkv = qkv.reshape(HEADS, rows, 3 * HEAD)
    attended, query, key = attend(seq_scalars, qkv, cosine, sine)
    attended = attended.reshape(group_tokens, HEAD)
    g_across_near, g_two, attended, g_near_y = hold((g_across_near, g_two, attended, g_near_y), ())
    g_two = jnp.where(is_middle, g_across_near, g_two)
    g_three = send(g_across_near, OUTWARD)
    g_two_y = flip(g_two, "shard", 1)
    far = combine(activated, attended, w_down, w_dense, rows, 1, 0)
    close = combine(activated, attended, w_down, w_dense, rows, 0, 0)
    g_three, g_near_y, g_two_y, *both = hold((g_three, g_near_y, g_two_y, *far, *close), ())
    far, close = both[:4], both[4:]
    g_three = jnp.where(is_middle, g_across, g_three)
    g_three_y = flip(g_three, "shard", 1)
    *grads, sums_one = pull([own_grad, g_near, g_own_y, g_near_y], w_down, w_dense, slope, 0, [])
    *grads, sums_two = pull([g_two, g_three], w_down, w_dense, slope, 2, grads)
    g_three_y, *both = hold((g_three_y, *far, *grads), ())
    far, grads = both[:4], both[4:]
    came_three = flip(far[3], "shard", 1)
    grad_pre, grad_attended, sums_three = pull(
        [g_two_y, g_three_y], w_down, w_dense, slope, 3, grads
    )
    pre_sums = sums_one + sums_two + sums_three
    my_core = rep % 2
    my_side = rep // 2
    my_row = me % 2

    def split(values, index):
        return (
            lax.dynamic_index_in_dim(values, index, 1, False),
            lax.dynamic_index_in_dim(values, 1 - index, 1, False),
        )

    def by_side(summed):
        return split(summed.reshape(HEADS, 2, quarter, summed.shape[-1]), my_side)

    def by_row(summed):
        return split(summed.reshape(4, 2, quarter, summed.shape[-1]), my_row)

    def joined(mine, came):
        return plus(mine, came).astype(BF16)

    def by_place(mine, came):
        both = jnp.stack([mine, came], axis=1)
        return [lax.dynamic_index_in_dim(both, place ^ z, 0, False) for z in range(4)]

    def far_places(pieces):
        return flip(jnp.stack(pieces[2:]), "shard", 4)

    def near_place(pieces, far):
        return flip(jnp.stack([pieces[1], far[1]]), "shard", 2)

    def sources(pieces, far, near):
        both = jnp.stack([pieces[0], near[0], far[0], near[1]])
        return both.reshape(HEADS, quarter, both.shape[-1])

    up_keep, up_give, *up_sums = moments_of(
        my_core, normed, grad_pre, up_raw, norms, 1, pre_sums, quarter
    )
    three = joined(close[3], came_three)
    grad_attended, up_give, three, *far = hold((grad_attended, up_give, three, *far), ())
    came_two = flip(far[2], "shard", 1)
    from_corner = send(three, INWARD)
    up_came = flip(up_give, "rep", 1)
    grad_qkv, qkv_sums = attend_back(
        seq_scalars,
        qkv,
        grad_attended.reshape(HEADS, rows, HEAD),
        cosine,
        sine,
        query,
        key,
    )
    grad_qkv = grad_qkv.reshape(group_tokens, 3 * HEAD)
    qkv_keep, qkv_give, *qkv_row_sums = moments_of(
        my_core, normed, grad_qkv, qkv_raw, norms, 0, qkv_sums, quarter
    )
    two = joined(close[2], came_two)
    up_keep, up_give = by_side(joined(up_keep, up_came))
    from_corner, up_give, qkv_give, grad_qkv, two, *far = hold(
        (from_corner, up_give, qkv_give, grad_qkv, two, *far), (up_keep,)
    )
    up_came = flip(up_give, "rep", 2)
    came_one = flip(far[1], "shard", 1)
    two = joined(two, from_corner)
    across_near = send(two, MIDDLE)
    across = send(two, INWARD)
    qkv_came = flip(qkv_give, "rep", 1)
    gy_far = combine(grad_pre, grad_qkv, up_scaled, qkv_scaled, rows, 1, 1)
    one = joined(close[1], came_one)
    up_keep, up_give = by_row(joined(up_keep, up_came))
    qkv_keep, qkv_give = by_side(joined(qkv_keep, qkv_came))
    small = jnp.concatenate(
        [vector[0] for vector in (*qkv_row_sums, *up_sums)]
        + [
            out_columns,
            jnp.where(
                block_range[:, None] == me, jnp.concatenate([pre_sums, qkv_sums], axis=1), 0.0
            ).reshape(-1),
        ]
    )
    up_give, across_near, across, qkv_give, own_grad, one, small, *both = hold(
        (up_give, across_near, across, qkv_give, own_grad, one, small, *far, *gy_far),
        (up_keep, qkv_keep),
    )
    far, gy_far = both[:4], both[4:]
    came_own = flip(far[0], "shard", 1)
    up_came = flip(up_give, "shard", 1)
    one = joined(one, across_near)
    three = plus(three, across).astype(BF16)
    one_near = flip(one, "shard", 2)
    three_across = send(three, MIDDLE)
    qkv_came = flip(qkv_give, "rep", 2)
    half_keep, half_give = outer(
        my_core,
        activated,
        attended,
        [own_grad, g_near, g_own_y, g_near_y, g_two, g_three, g_two_y, g_three_y],
    )
    out_sum = plus(close[0], came_own)
    up_pieces = by_place(up_keep, up_came)
    qkv_keep, qkv_give = by_row(joined(qkv_keep, qkv_came))
    (
        one_near,
        three_across,
        qkv_keep,
        qkv_give,
        half_give,
        out_sum,
        *both,
    ) = hold(
        (
            one_near,
            three_across,
            qkv_keep,
            qkv_give,
            half_give,
            out_sum,
            *up_pieces,
            *gy_far,
            grad_pre,
        ),
        (),
    )
    up_pieces, gy_far, grad_pre = both[:4], both[4:8], both[8]
    came_three = flip(gy_far[3], "shard", 1)
    qkv_came = flip(qkv_give, "shard", 1)
    up_far = far_places(up_pieces)
    half_came = flip(half_give, "rep", 1)
    small_side = flip(small, "rep", 2)
    out_sum = plus(out_sum, one_near, three_across)
    output = (own.astype(F32) + out_sum + (b_dense + b_down)).astype(BF16)
    gy_close = combine(grad_pre, grad_qkv, up_scaled, qkv_scaled, rows, 0, 1)
    qkv_pieces = by_place(qkv_keep, qkv_came)
    three = joined(gy_close[3], came_three)
    output, up_far, half_came, small, small_side, three, *both = hold(
        (output, up_far, half_came, small, small_side, three, *qkv_pieces, *gy_far, *gy_close), ()
    )
    qkv_pieces, gy_far, gy_close = both[:4], both[4:8], both[8:]
    came_two = flip(gy_far[2], "shard", 1)
    from_corner = send(three, INWARD)
    qkv_far = far_places(qkv_pieces)
    half = joined(half_keep, half_came)
    half_far = flip(half, "rep", 2)
    small = small + small_side
    small_side = flip(small, "rep", 1)
    two = joined(gy_close[2], came_two)
    from_corner, qkv_far, small, small_side, two, *gy_far = hold(
        (from_corner, qkv_far, small, small_side, two, *gy_far), ()
    )
    came_one = flip(gy_far[1], "shard", 1)
    two = joined(two, from_corner)
    across_near = send(two, MIDDLE)
    across = send(two, INWARD)
    up_near = near_place(up_pieces, up_far)
    one = joined(gy_close[1], came_one)
    up_part = sources(up_pieces, up_far, up_near)
    across_near, across, up_part, half_far, one, qkv_far, *gy_far = hold(
        (across_near, across, up_part, half_far, one, qkv_far, *gy_far), ()
    )
    came_own = flip(gy_far[0], "shard", 1)
    one = joined(one, across_near)
    three = plus(three, across).astype(BF16)
    one_near = flip(one, "shard", 2)
    three_across = send(three, MIDDLE)
    up_beside = flip(up_part, "rep", 2)
    qkv_near = near_place(qkv_pieces, qkv_far)
    half = joined(half, half_far)
    gy = plus(gy_close[0], came_own)
    qkv_part = sources(qkv_pieces, qkv_far, qkv_near)
    one_near, three_across, qkv_part, up_beside, half, small, gy = hold(
        (one_near, three_across, qkv_part, up_beside, half, small, gy), ()
    )
    qkv_beside = flip(qkv_part, "rep", 2)
    up_c = flip(jnp.stack([up_part, up_beside]), "rep", 1)
    other = flip(half, "rep", 1)
    small = small + small_side
    small = small + flip(small, "shard", 1)
    gy = plus(gy, one_near, three_across)
    own_normed, own_rstd = normalize(own)
    input_grad = own_grad.astype(F32) + own_rstd * (
        gy
        - jnp.mean(gy, axis=-1, keepdims=True)
        - own_normed * jnp.mean(gy * own_normed, axis=-1, keepdims=True)
    )
    input_grad = input_grad[:, None, :]
    up_grad = place_grads(me, rep, (up_part, up_c[0], up_beside, up_c[1]), 1)
    down_grad, dense_grad = place_halves(my_core, half, other, hidden)
    qkv_c = flip(qkv_part, "rep", 1)
    input_grad, up_grad, down_grad, qkv_beside, qkv_c, small = hold(
        (input_grad, up_grad, down_grad, qkv_beside, qkv_c, small), ()
    )
    qkv_beside_c = flip(qkv_beside, "rep", 1)
    one, two, three = [flip(small, "shard", bit) for bit in (2, 4, 6)]
    qkv_grad = place_grads(me, rep, (qkv_part, qkv_c, qkv_beside, qkv_beside_c), 3)
    small, one, two, three = hold((small, one, two, three), (qkv_grad,))
    small = (small + one) + (two + three)
    vectors = small[: 5 * width].reshape(5, width)
    slots = small[5 * width :].reshape(HEADS, wide)
    b_up_grad = slots[:, :hidden].reshape(-1)
    b_qkv_grad = slots[:, hidden:].reshape(HEADS, 3, HEAD).transpose(1, 0, 2).reshape(-1)
    return (
        output[:, None, :],
        input_grad,
        vectors[0],
        vectors[1],
        vectors[2],
        vectors[3],
        qkv_grad,
        b_qkv_grad,
        dense_grad,
        vectors[4],
        up_grad,
        b_up_grad,
        down_grad,
        vectors[4],
    )


def solution(mesh):
    in_specs = (
        P("rep", "shard", None),
        P("rep", "shard", None),
        P("rep", None),
        P("rep", None),
        P(),
        P(),
        P(),
        P(),
        P("shard", None),
        P(),
        P("shard", None),
        P(),
        P("shard", None),
        P(),
        P("shard", None),
        P(),
    )
    out_specs = (
        P("rep", "shard", None),
        P("rep", "shard", None),
        P(),
        P(),
        P(),
        P(),
        P("shard", None),
        P(),
        P("shard", None),
        P(),
        P("shard", None),
        P(),
        P("shard", None),
        P(),
    )
    body = split_shards if mesh.shape["shard"] == HEADS else shards
    return jax.shard_map(
        body, mesh=mesh, in_specs=in_specs, out_specs=out_specs, check_vma=False
    )
```

```python
import functools
import math

import jax
import jax.numpy as jnp
from jax import lax
from jax.experimental import pallas as pl
from jax.experimental.pallas import tpu as pltpu
from jax.sharding import PartitionSpec as P

HEADS = 8
HEAD = 256
ROT = 64


EPSILON = 1e-05
MASKED = -1e30


def layer_norm(vector, gain_vec, shift_vec):
    mean_val = jnp.mean(vector, axis=-1, keepdims=True)
    centered = vector - mean_val
    variance = jnp.mean(centered * centered, axis=-1, keepdims=True)
    return centered * lax.rsqrt(variance + EPSILON) * gain_vec + shift_vec


def gelu_exact(vector):
    return jax.nn.gelu(vector, approximate=False)


def rotary_tables(positions):
    half_rot = ROT // 2
    freq_index = jnp.arange(half_rot, dtype=jnp.float32)
    inverse_freq = jnp.exp(freq_index * (-2.0 * math.log(10000.0) / ROT))
    angles = positions[:, None] * inverse_freq[None, :]
    return (jnp.cos(angles), jnp.sin(angles))


def rotate(heads_in, cosine_table, sine_table):
    half_rot = ROT // 2
    first_half = heads_in[..., :half_rot]
    second_half = heads_in[..., half_rot:ROT]
    cos_wide = cosine_table[:, None, :]
    sin_wide = sine_table[:, None, :]
    return jnp.concatenate(
        [
            first_half * cos_wide - second_half * sin_wide,
            second_half * cos_wide + first_half * sin_wide,
            heads_in[..., ROT:],
        ],
        axis=-1,
    )


def stream_rows(lengths, seq_perm, shard_count):
    seq_range = jnp.arange(lengths.shape[0], dtype=jnp.int32)
    ranking = jnp.sum(
        jnp.where(seq_perm[:, None] == seq_range[None, :], seq_range[:, None], 0), axis=0
    )
    offsets = jnp.sum(jnp.where(ranking[None, :] < ranking[:, None], lengths[None, :], 0), axis=1)
    return (offsets // shard_count, lengths // shard_count)


def row_product(left, right):
    return jnp.dot(left.T, right, preferred_element_type=jnp.float32)


def block_mask(seq_flag, positions, live):
    return (
        live[:, None]
        & live[None, :]
        & (seq_flag[:, None] == seq_flag[None, :])
        & (positions[None, :] <= positions[:, None])
    )


def shards(
    tokens,
    cotangent,
    seq_lengths,
    seq_order,
    ln1_gain,
    ln1_bias,
    ln2_gain,
    ln2_bias,
    w_qkv,
    b_qkv,
    w_dense,
    b_dense,
    w_up,
    b_up,
    w_down,
    b_down,
):
    shard_count = lax.axis_size("shard")
    my_index = lax.axis_index("shard")
    inputs = tokens[:, 0, :].astype(jnp.float32)
    grad_out = cotangent[:, 0, :]
    local_rows, width = inputs.shape
    slot_rows = 2 * (local_rows // shard_count) - 4
    buffer_rows = slot_rows * shard_count
    row_offsets, row_counts = stream_rows(seq_lengths[0], seq_order[0], shard_count)
    first_count = row_counts[0::2]
    second_count = row_counts[1::2]
    first_start = row_offsets[0::2]
    second_start = row_offsets[1::2]
    slot_range = jnp.arange(slot_rows, dtype=jnp.int32)[None, :]
    in_first = slot_range < first_count[:, None]
    slot_live = slot_range < (first_count + second_count)[:, None]
    source_rows = jnp.where(
        in_first,
        first_start[:, None] + slot_range,
        second_start[:, None] + slot_range - first_count[:, None],
    )
    source_rows = jnp.where(slot_live, source_rows, 0)
    seq_range = jnp.arange(row_counts.shape[0], dtype=jnp.int32)
    parity = seq_range % 2
    slot_base = seq_range // 2 * slot_rows + parity * row_counts[seq_range - parity] - row_offsets
    token_range = jnp.arange(local_rows, dtype=jnp.int32)[:, None]
    member = (token_range >= row_offsets[None, :]) & (
        token_range < (row_offsets + row_counts)[None, :]
    )
    return_rows = token_range[:, 0] + jnp.sum(jnp.where(member, slot_base[None, :], 0), axis=1)
    own_first = first_count[my_index]
    own_second = second_count[my_index]
    buffer_range = jnp.arange(buffer_rows, dtype=jnp.int32)
    slot_index = buffer_range % slot_rows
    source_index = buffer_range // slot_rows
    seq_flag = (slot_index >= own_first).astype(jnp.int32)
    positions = (slot_index - seq_flag * own_first) * shard_count + source_index
    live = slot_index < own_first + own_second
    attn_full, dense_full = (
        lax.all_gather(w_qkv, "shard", axis=0, tiled=True),
        lax.all_gather(w_dense, "shard", axis=0, tiled=True),
    )
    up_full, down_full = (
        lax.all_gather(w_up, "shard", axis=0, tiled=True),
        lax.all_gather(w_down, "shard", axis=0, tiled=True),
    )
    normed_one_wide, pull_one = jax.vjp(layer_norm, inputs, ln1_gain, ln1_bias)
    normed_two_wide, pull_two = jax.vjp(layer_norm, inputs, ln2_gain, ln2_bias)
    normed_one = normed_one_wide.astype(jnp.bfloat16)
    normed_two = normed_two_wide.astype(jnp.bfloat16)
    qkv = (jnp.dot(normed_one, attn_full, preferred_element_type=jnp.float32) + b_qkv).astype(
        jnp.bfloat16
    )
    arrived = lax.all_to_all(
        jnp.take(qkv, source_rows, axis=0), "shard", split_axis=0, concat_axis=0, tiled=True
    )
    arrived = arrived.reshape(buffer_rows, 3 * width)
    heads_shape = (buffer_rows, HEADS, HEAD)
    cosine_table, sine_table = rotary_tables(positions.astype(jnp.float32))

    def rotate_here(heads_in):
        return rotate(heads_in, cosine_table, sine_table)

    query_wide, pull_query = jax.vjp(
        rotate_here, arrived[:, :width].astype(jnp.float32).reshape(heads_shape)
    )
    key_wide, pull_key = jax.vjp(
        rotate_here, arrived[:, width : 2 * width].astype(jnp.float32).reshape(heads_shape)
    )
    rotated_queries = query_wide.astype(jnp.bfloat16)
    rotated_keys = key_wide.astype(jnp.bfloat16)
    value_heads = arrived[:, 2 * width :].reshape(heads_shape)
    sources_per = shard_count
    while sources_per > 1 and sources_per * slot_rows > 1024:
        sources_per = sources_per // 2
    block_rows = sources_per * slot_rows
    block_total = buffer_rows // block_rows
    score_scale = HEAD ** (-0.5)

    def forward_block(block_index):
        allowed = block_mask(seq_flag, positions, live)
        scores = (
            jnp.einsum(
                "qhe,khe->hqk", rotated_queries, rotated_keys, preferred_element_type=jnp.float32
            )
            * score_scale
        )
        scores = jnp.where(allowed[None], scores, MASKED)
        row_max = jnp.max(scores, axis=-1, keepdims=True)
        exp_scores = jnp.exp(scores - row_max)
        exp_total = jnp.sum(exp_scores, axis=-1, keepdims=True)
        attn_probs = jnp.where(allowed[None], exp_scores / exp_total, 0.0)
        attended_blk = jnp.einsum(
            "hqk,khe->qhe",
            attn_probs.astype(jnp.bfloat16),
            value_heads,
            preferred_element_type=jnp.float32,
        )
        return (attended_blk.astype(jnp.bfloat16), row_max[..., 0] + jnp.log(exp_total[..., 0]))

    attended_blocks, log_totals = lax.map(forward_block, jnp.arange(block_total, dtype=jnp.int32))
    attended_slots = attended_blocks.reshape(shard_count, slot_rows, width)
    attn_back = lax.all_to_all(
        attended_slots, "shard", split_axis=0, concat_axis=0, tiled=True
    ).reshape(buffer_rows, width)
    attn_in = jnp.take(attn_back, return_rows, axis=0)
    attn_out = jnp.dot(attn_in, dense_full, preferred_element_type=jnp.float32) + b_dense
    pre_up = jnp.dot(normed_two, up_full, preferred_element_type=jnp.float32) + b_up
    activated_wide, pull_gelu = jax.vjp(gelu_exact, pre_up)
    activated = activated_wide.astype(jnp.bfloat16)
    mlp_out = jnp.dot(activated, down_full, preferred_element_type=jnp.float32) + b_down
    output = (inputs + attn_out + mlp_out).astype(jnp.bfloat16)
    attn_second, dense_second = (
        lax.all_gather(w_qkv, "shard", axis=0, tiled=True),
        lax.all_gather(w_dense, "shard", axis=0, tiled=True),
    )
    up_second, down_second = (
        lax.all_gather(w_up, "shard", axis=0, tiled=True),
        lax.all_gather(w_down, "shard", axis=0, tiled=True),
    )
    grad_attended = jnp.dot(grad_out, dense_second.T, preferred_element_type=jnp.float32).astype(
        jnp.bfloat16
    )
    grad_slots = jnp.where(
        slot_live[:, :, None],
        jnp.take(grad_attended, source_rows, axis=0),
        jnp.zeros((), jnp.bfloat16),
    )
    grad_heads = lax.all_to_all(
        grad_slots, "shard", split_axis=0, concat_axis=0, tiled=True
    ).reshape(heads_shape)

    def backward_block(carried, block_index):
        grad_keys, grad_values = carried
        allowed = block_mask(seq_flag, positions, live)
        scores = (
            jnp.einsum(
                "qhe,khe->hqk", rotated_queries, rotated_keys, preferred_element_type=jnp.float32
            )
            * score_scale
        )
        attn_probs = jnp.where(
            allowed[None], jnp.exp(scores - log_totals[block_index][..., None]), 0.0
        )
        grad_probs = jnp.einsum(
            "qhe,khe->hqk", grad_heads, value_heads, preferred_element_type=jnp.float32
        )
        row_delta = jnp.sum(attn_probs * grad_probs, axis=-1, keepdims=True)
        grad_scores = (attn_probs * (grad_probs - row_delta)).astype(jnp.bfloat16)
        grad_query = (
            jnp.einsum(
                "hqk,khe->qhe", grad_scores, rotated_keys, preferred_element_type=jnp.float32
            )
            * score_scale
        )
        grad_keys = (
            grad_keys
            + jnp.einsum(
                "hqk,qhe->khe", grad_scores, rotated_queries, preferred_element_type=jnp.float32
            )
            * score_scale
        )
        grad_values = grad_values + jnp.einsum(
            "hqk,qhe->khe",
            attn_probs.astype(jnp.bfloat16),
            grad_heads,
            preferred_element_type=jnp.float32,
        )
        return ((grad_keys, grad_values), grad_query)

    zero_heads = jnp.zeros(heads_shape, jnp.float32)
    (grad_keys, grad_values), grad_query_blocks = lax.scan(
        backward_block, (zero_heads, zero_heads), jnp.arange(block_total, dtype=jnp.int32)
    )
    grad_q_pre = pull_query(grad_query_blocks.reshape(heads_shape))[0]
    grad_k_pre = pull_key(grad_keys)[0]
    grad_qkv_slots = jnp.concatenate(
        [
            grad_q_pre.reshape(buffer_rows, width),
            grad_k_pre.reshape(buffer_rows, width),
            grad_values.reshape(buffer_rows, width),
        ],
        axis=1,
    ).astype(jnp.bfloat16)
    grad_qkv_slots = grad_qkv_slots.reshape(shard_count, slot_rows, 3 * width)
    grad_qkv_back = lax.all_to_all(grad_qkv_slots, "shard", split_axis=0, concat_axis=0, tiled=True)
    grad_qkv = jnp.take(grad_qkv_back.reshape(buffer_rows, 3 * width), return_rows, axis=0)
    grad_activated = jnp.dot(grad_out, down_second.T, preferred_element_type=jnp.float32)
    grad_pre = pull_gelu(grad_activated)[0].astype(jnp.bfloat16)
    grad_normed_one = jnp.dot(grad_qkv, attn_second.T, preferred_element_type=jnp.float32)
    grad_normed_two = jnp.dot(grad_pre, up_second.T, preferred_element_type=jnp.float32)
    grad_in_one, grad_gain_one, grad_bias_one = pull_one(grad_normed_one)
    grad_in_two, grad_gain_two, grad_bias_two = pull_two(grad_normed_two)
    input_grad = grad_out.astype(jnp.float32) + grad_in_one + grad_in_two
    qkv_rows = lax.psum_scatter(
        row_product(normed_one, grad_qkv).astype(jnp.bfloat16),
        "shard",
        scatter_dimension=0,
        tiled=True,
    ).astype(jnp.float32)
    dense_rows = lax.psum_scatter(
        row_product(attn_in, grad_out).astype(jnp.bfloat16),
        "shard",
        scatter_dimension=0,
        tiled=True,
    ).astype(jnp.float32)
    up_rows = lax.psum_scatter(
        row_product(normed_two, grad_pre).astype(jnp.bfloat16),
        "shard",
        scatter_dimension=0,
        tiled=True,
    ).astype(jnp.float32)
    down_rows = lax.psum_scatter(
        row_product(activated, grad_out).astype(jnp.bfloat16),
        "shard",
        scatter_dimension=0,
        tiled=True,
    ).astype(jnp.float32)
    qkv_rows, dense_rows, up_rows, down_rows = (
        lax.psum(qkv_rows.astype(jnp.bfloat16), "rep").astype(jnp.float32),
        lax.psum(dense_rows.astype(jnp.bfloat16), "rep").astype(jnp.float32),
        lax.psum(up_rows.astype(jnp.bfloat16), "rep").astype(jnp.float32),
        lax.psum(down_rows.astype(jnp.bfloat16), "rep").astype(jnp.float32),
    )
    out_column_sum = jnp.sum(grad_out, axis=0, dtype=jnp.float32)
    small_totals = lax.psum(
        (
            grad_gain_one,
            grad_bias_one,
            grad_gain_two,
            grad_bias_two,
            jnp.sum(grad_qkv, axis=0, dtype=jnp.float32),
            out_column_sum,
            jnp.sum(grad_pre, axis=0, dtype=jnp.float32),
        ),
        ("rep", "shard"),
    )
    return (
        output[:, None, :],
        input_grad[:, None, :],
        small_totals[0],
        small_totals[1],
        small_totals[2],
        small_totals[3],
        qkv_rows,
        small_totals[4],
        dense_rows,
        small_totals[5],
        up_rows,
        small_totals[6],
        down_rows,
        small_totals[5],
    )


TILE_ROWS = 32
BIG_VMEM = 60 << 20
SMALL_COST = pl.CostEstimate(flops=1 << 20, bytes_accessed=1 << 20, transcendentals=0)
F32 = jnp.float32
BF16 = jnp.bfloat16


def flip(value, axis, bit):
    size = lax.axis_size(axis)
    return lax.ppermute(value, axis, [(i, i ^ bit) for i in range(size)])


def send(value, pairs):
    return lax.ppermute(value, "shard", [(2 * a + y, 2 * b + y) for a, b in pairs for y in (0, 1)])


MIDDLE = ((1, 2), (2, 1))
OUTWARD = ((1, 0), (2, 3))
INWARD = ((0, 1), (3, 2))


def plus(*terms):
    total = terms[0].astype(F32)
    for term in terms[1:]:
        total = total + term.astype(F32)
    return total


def hold(values, gates):
    return lax.optimization_barrier(tuple(values) + tuple(gates))[: len(values)]


def turn(heads_in, cosine, sine):
    left = heads_in[:, :128]
    lane = lax.broadcasted_iota(jnp.int32, left.shape, 1)
    half = ROT // 2
    partner = jnp.where(lane < half, pltpu.roll(left, 128 - half, 1), pltpu.roll(left, half, 1))
    return jnp.concatenate([left * cosine + partner * sine, heads_in[:, 128:]], axis=1)


def token_labels(my_index, shape, dim):
    inner = lax.broadcasted_iota(jnp.int32, shape, dim)
    block = inner // TILE_ROWS
    apart = block // 4 * 4 + block % 2 * 2 + block // 2 % 2
    return (inner % TILE_ROWS) * HEADS + jnp.bitwise_xor(apart, my_index)


def tile_weights(tile, seq_ref, query, key_tiles, count):
    tile_tokens = TILE_ROWS * HEADS
    my_index = seq_ref[count]
    query_label = token_labels(my_index, (tile_tokens, 1), 0) + tile * tile_tokens
    key_label = token_labels(my_index, (1, tile_tokens), 1)
    scores = []
    for place, key in key_tiles:
        label = key_label + place * tile_tokens
        last = jnp.full(label.shape, 1 << 30, jnp.int32)
        for k in range(count):
            last = jnp.minimum(last, jnp.where(label < seq_ref[k], seq_ref[k], 1 << 30))
        allowed = query_label < last
        if place == tile:
            allowed = allowed & (label <= query_label)
        product = lax.dot_general(query, key, (((1,), (1,)), ((), ())), preferred_element_type=F32)
        scores.append(jnp.where(allowed, product * HEAD ** (-0.5), MASKED))
    scores = jnp.concatenate(scores, axis=1)
    exp_scores = jnp.exp(scores - jnp.max(scores, axis=1, keepdims=True))
    return exp_scores * (1.0 / jnp.sum(exp_scores, axis=1, keepdims=True))


def attend_kernel(seq_ref, qkv_ref, cos_ref, sin_ref, out_ref, query_ref, key_ref):
    tiles = query_ref.shape[0]
    tile_tokens = TILE_ROWS * HEADS

    def part(tile, lane):
        rows = qkv_ref[:, tile * TILE_ROWS : (tile + 1) * TILE_ROWS, lane : lane + HEAD]
        return rows.reshape(tile_tokens, HEAD)

    for tile in range(tiles):
        cosine, sine = cos_ref[tile], sin_ref[tile]
        query = turn(part(tile, 0).astype(F32), cosine, sine).astype(BF16)
        query_ref[tile] = query
        key_ref[tile] = turn(part(tile, HEAD).astype(F32), cosine, sine).astype(BF16)
        near = list(range(max(tile - 2, 0), tile + 1))
        probs = tile_weights(
            tile, seq_ref, query, [(k, key_ref[k]) for k in near], seq_ref.shape[0] - 1
        ).astype(BF16)
        total = jnp.zeros((tile_tokens, HEAD), F32)
        for at, k in enumerate(near):
            total = total + jnp.dot(
                probs[:, at * tile_tokens : (at + 1) * tile_tokens],
                part(k, 2 * HEAD),
                preferred_element_type=F32,
            )
        out_ref[:, tile * TILE_ROWS : (tile + 1) * TILE_ROWS, :] = total.astype(BF16).reshape(
            HEADS, TILE_ROWS, HEAD
        )


def attend_back_kernel(
    seq_ref, qkv_ref, grad_ref, cos_ref, sin_ref, query_ref, key_ref, out_ref, sum_ref, gk_ref, gv_ref
):
    tiles = query_ref.shape[0]
    tile_tokens = TILE_ROWS * HEADS
    scale = HEAD ** (-0.5)
    over_rows = (((0,), (0,)), ((), ()))
    over_lanes = (((1,), (1,)), ((), ()))

    def rows_of(tile):
        return slice(tile * TILE_ROWS, (tile + 1) * TILE_ROWS)

    def put(tile, lane, value):
        low = value.astype(BF16)
        out_ref[:, rows_of(tile), lane : lane + HEAD] = low.reshape(HEADS, TILE_ROWS, HEAD)
        columns = jnp.sum(low.astype(F32), axis=0, keepdims=True)
        if tile == 0:
            sum_ref[:, lane : lane + HEAD] = columns
        else:
            sum_ref[:, lane : lane + HEAD] += columns

    def finish(tile):
        put(tile, HEAD, turn(gk_ref[tile] * scale, cos_ref[tile], -sin_ref[tile]))
        put(tile, 2 * HEAD, gv_ref[tile])

    for tile in range(tiles):
        query = query_ref[tile]
        near = list(range(max(tile - 2, 0), tile + 1))
        grad = grad_ref[:, rows_of(tile), :].reshape(tile_tokens, HEAD)
        probs = tile_weights(
            tile, seq_ref, query, [(k, key_ref[k]) for k in near], seq_ref.shape[0] - 1
        )
        grad_probs = jnp.concatenate(
            [
                lax.dot_general(
                    grad,
                    qkv_ref[:, rows_of(k), 2 * HEAD :].reshape(tile_tokens, HEAD),
                    over_lanes,
                    preferred_element_type=F32,
                )
                for k in near
            ],
            axis=1,
        )
        delta = jnp.sum(probs * grad_probs, axis=1, keepdims=True)
        grad_scores = (probs * (grad_probs - delta)).astype(BF16)
        probs = probs.astype(BF16)
        grad_query = jnp.zeros((tile_tokens, HEAD), F32)
        for at, k in enumerate(near):
            span = slice(at * tile_tokens, (at + 1) * tile_tokens)
            grad_query = grad_query + jnp.dot(
                grad_scores[:, span], key_ref[k], preferred_element_type=F32
            )
            to_key = lax.dot_general(
                grad_scores[:, span], query, over_rows, preferred_element_type=F32
            )
            to_value = lax.dot_general(probs[:, span], grad, over_rows, preferred_element_type=F32)
            if k == tile:
                gk_ref[k] = to_key
                gv_ref[k] = to_value
            else:
                gk_ref[k] += to_key
                gv_ref[k] += to_value
        put(tile, 0, turn(grad_query * scale, cos_ref[tile], -sin_ref[tile]))
        if tile >= 2:
            finish(tile - 2)
    for tile in range(max(tiles - 2, 0), tiles):
        finish(tile)


def one_spec(shape):
    return pl.BlockSpec(shape, lambda i: (0,) * len(shape), pipeline_mode=pl.Buffered(1))


SMEM_SPEC = pl.BlockSpec(memory_space=pltpu.SMEM)


def attend(seq_scalars, qkv, cosine, sine):
    blocks, rows, _ = qkv.shape
    tiled = (rows // TILE_ROWS, blocks * TILE_ROWS, HEAD)
    return pl.pallas_call(
        attend_kernel,
        out_shape=(
            jax.ShapeDtypeStruct((blocks, rows, HEAD), BF16),
            jax.ShapeDtypeStruct(tiled, BF16),
            jax.ShapeDtypeStruct(tiled, BF16),
        ),
        grid=(1,),
        in_specs=[SMEM_SPEC] + [one_spec(array.shape) for array in (qkv, cosine, sine)],
        out_specs=(one_spec((blocks, rows, HEAD)), one_spec(tiled), one_spec(tiled)),
        compiler_params=pltpu.CompilerParams(vmem_limit_bytes=BIG_VMEM),
        cost_estimate=SMALL_COST,
    )(seq_scalars, qkv, cosine, sine)


def attend_back(seq_scalars, qkv, grad, cosine, sine, query, key):
    blocks, rows, wide = qkv.shape
    return pl.pallas_call(
        attend_back_kernel,
        out_shape=(
            jax.ShapeDtypeStruct((blocks, rows, wide), BF16),
            jax.ShapeDtypeStruct((1, wide), F32),
        ),
        grid=(1,),
        in_specs=[SMEM_SPEC]
        + [one_spec(array.shape) for array in (qkv, grad, cosine, sine, query, key)],
        out_specs=(one_spec((blocks, rows, wide)), one_spec((1, wide))),
        scratch_shapes=[pltpu.VMEM(query.shape, F32), pltpu.VMEM(query.shape, F32)],
        compiler_params=pltpu.CompilerParams(vmem_limit_bytes=BIG_VMEM),
        cost_estimate=SMALL_COST,
    )(seq_scalars, qkv, grad, cosine, sine, query, key)


def copy_kernel(in_ref, out_ref):
    out_ref[...] = in_ref[...]


def settled(values):
    return pl.pallas_call(
        copy_kernel,
        out_shape=jax.ShapeDtypeStruct(values.shape, values.dtype),
        grid=(1,),
        in_specs=[pl.BlockSpec(values.shape, lambda i: (0, 0))],
        out_specs=pl.BlockSpec(values.shape, lambda i: (0, 0)),
        cost_estimate=SMALL_COST,
    )(values)


def pack_kernel(at_ref, up_ref, qkv_ref, odd_ref, even_ref):
    third = qkv_ref.shape[1] // 3
    hidden = up_ref.shape[1] // HEADS
    for k in range(HEADS):
        out_ref = even_ref if k % 2 == 0 else odd_ref
        target = at_ref[0] ^ k
        start = pl.multiple_of(target * hidden, hidden)
        out_ref[k // 2, :, :hidden] = up_ref[:, pl.ds(start, hidden)]
        for j in range(3):
            start = pl.multiple_of(j * third + target * HEAD, HEAD)
            out_ref[k // 2, :, hidden + j * HEAD : hidden + (j + 1) * HEAD] = qkv_ref[
                :, pl.ds(start, HEAD)
            ]


def pack(me, rep, w_up, w_qkv, hidden):
    quarter = w_up.shape[0] // 4
    shape = (HEADS // 2, quarter, hidden + 3 * HEAD)
    packed = jax.ShapeDtypeStruct(shape, BF16)
    return pl.pallas_call(
        pack_kernel,
        out_shape=(packed, packed),
        grid_spec=pltpu.PrefetchScalarGridSpec(
            num_scalar_prefetch=1,
            grid=(1,),
            in_specs=[
                pl.BlockSpec((quarter, weight.shape[1]), lambda i, at_ref: (at_ref[1], 0))
                for weight in (w_up, w_qkv)
            ],
            out_specs=tuple(pl.BlockSpec(shape, lambda i, at_ref: (0, 0, 0)) for _ in range(2)),
        ),
        compiler_params=pltpu.CompilerParams(vmem_limit_bytes=24 << 20),
        cost_estimate=SMALL_COST,
    )(jnp.stack([me, rep]).astype(jnp.int32), w_up, w_qkv)


def place_weights_kernel(
    at_ref, p0_ref, p1_ref, p2_ref, p3_ref, norms_ref, *out_refs, hidden
):
    raw_refs, scaled_refs, sum_ref = out_refs[:2], out_refs[2:4], out_refs[4]
    quarter, wide = p0_ref.shape[1:]

    @pl.when(pl.program_id(0) == 0)
    def _():
        sum_ref[...] = jnp.zeros_like(sum_ref)

    for k, part_ref in enumerate((p0_ref, p1_ref, p2_ref, p3_ref)):
        rows = pl.ds(pl.multiple_of((at_ref[1] ^ k) * quarter, quarter), quarter)
        for norm, columns in ((1, slice(0, hidden)), (0, slice(hidden, wide))):
            raw = part_ref[0, :, columns]
            raw_refs[1 - norm][rows, :] = raw
            weight = raw.astype(F32)
            gain = norms_ref[rows, 2 * norm : 2 * norm + 1]
            shift = norms_ref[rows, 2 * norm + 1 : 2 * norm + 2]
            scaled_refs[1 - norm][rows, :] = (weight * gain).astype(BF16)
            sum_ref[:, columns] += jnp.sum(weight * shift, axis=0, keepdims=True)


def place_weights(me, rep, parts, norms, hidden):
    count, rows, wide = parts[0].shape
    widths = (hidden, wide - hidden) * 2
    four = pl.BlockSpec((4 * rows, 4), lambda i, at_ref: (i ^ at_ref[0], 0))
    part = pl.BlockSpec((1, rows, wide), lambda i, at_ref: (i, 0, 0))
    return pl.pallas_call(
        functools.partial(place_weights_kernel, hidden=hidden),
        out_shape=tuple(jax.ShapeDtypeStruct((count * 4 * rows, n), BF16) for n in widths)
        + (jax.ShapeDtypeStruct((1, wide), F32),),
        grid_spec=pltpu.PrefetchScalarGridSpec(
            num_scalar_prefetch=1,
            grid=(count,),
            in_specs=[part] * 4 + [four],
            out_specs=tuple(
                pl.BlockSpec((4 * rows, n), lambda i, at_ref: (i ^ at_ref[0], 0)) for n in widths
            )
            + (pl.BlockSpec((1, wide), lambda i, at_ref: (0, 0)),),
        ),
        compiler_params=pltpu.CompilerParams(vmem_limit_bytes=BIG_VMEM),
        cost_estimate=SMALL_COST,
    )(jnp.stack([me, rep]).astype(jnp.int32), *parts, norms)


def place_grads_kernel(at_ref, p0_ref, p1_ref, p2_ref, p3_ref, out_ref, *, pieces):
    quarter, wide = p0_ref.shape[1:]
    source = pl.program_id(0) ^ at_ref[0]
    size = wide // pieces
    for k, part_ref in enumerate((p0_ref, p1_ref, p2_ref, p3_ref)):
        rows = pl.ds(pl.multiple_of((at_ref[1] ^ k) * quarter, quarter), quarter)
        values = part_ref[0].astype(F32)
        if pieces == 1:
            out_ref[rows, :] = values
        else:
            for j in range(pieces):
                start = pl.multiple_of((j * HEADS + source) * size, size)
                out_ref[rows, pl.ds(start, size)] = values[:, j * size : (j + 1) * size]


def place_grads(me, rep, parts, pieces):
    count, rows, wide = parts[0].shape
    part = pl.BlockSpec((1, rows, wide), lambda i, at_ref: (i, 0, 0))
    if pieces == 1:
        out = pl.BlockSpec((4 * rows, wide), lambda i, at_ref: (0, i ^ at_ref[0]))
    else:
        out = pl.BlockSpec((4 * rows, count * wide), lambda i, at_ref: (0, 0))
    return pl.pallas_call(
        functools.partial(place_grads_kernel, pieces=pieces),
        out_shape=jax.ShapeDtypeStruct((4 * rows, count * wide), F32),
        grid_spec=pltpu.PrefetchScalarGridSpec(
            num_scalar_prefetch=1, grid=(count,), in_specs=[part] * 4, out_specs=out
        ),
        compiler_params=pltpu.CompilerParams(vmem_limit_bytes=40 << 20),
        cost_estimate=SMALL_COST,
    )(jnp.stack([me, rep]).astype(jnp.int32), *parts)


def place_halves_kernel(core_ref, mine_ref, other_ref, down_ref, dense_ref, *, cut):
    half = mine_ref.shape[1]

    def fill(out_ref):
        for part_ref, core in ((mine_ref, core_ref[0]), (other_ref, 1 - core_ref[0])):
            start = pl.multiple_of(core * half, half)
            out_ref[:, pl.ds(start, half)] = part_ref[...].astype(F32)

    @pl.when(pl.program_id(0) < cut)
    def _():
        fill(down_ref)

    @pl.when(pl.program_id(0) >= cut)
    def _():
        fill(dense_ref)


def place_halves(core, mine, other, hidden):
    rows, half = mine.shape
    tile = 256
    cut = hidden // tile
    part = pl.BlockSpec((tile, half), lambda i, core_ref: (i, 0))
    return pl.pallas_call(
        functools.partial(place_halves_kernel, cut=cut),
        out_shape=(
            jax.ShapeDtypeStruct((hidden, 2 * half), F32),
            jax.ShapeDtypeStruct((rows - hidden, 2 * half), F32),
        ),
        grid_spec=pltpu.PrefetchScalarGridSpec(
            num_scalar_prefetch=1,
            grid=(rows // tile,),
            in_specs=[part, part],
            out_specs=(
                pl.BlockSpec((tile, 2 * half), lambda i, core_ref: (jnp.minimum(i, cut - 1), 0)),
                pl.BlockSpec((tile, 2 * half), lambda i, core_ref: (jnp.maximum(i - cut, 0), 0)),
            ),
        ),
        compiler_params=pltpu.CompilerParams(vmem_limit_bytes=32 << 20),
        cost_estimate=SMALL_COST,
    )(core[None].astype(jnp.int32), mine, other)


def normalize(values):
    values = values.astype(F32)
    centered = values - jnp.mean(values, axis=-1, keepdims=True)
    rstd = lax.rsqrt(jnp.mean(centered * centered, axis=-1, keepdims=True) + EPSILON)
    return centered * rstd, rstd


def norm_kernel(*refs, count, steps):
    blocks, out_ref = refs[:count], refs[-1]
    for k in range(count):

        @pl.when(pl.program_id(0) // steps == k)
        def _(block_ref=blocks[k]):
            out_ref[...] = normalize(block_ref[...])[0].astype(BF16)


def norm_blocks(blocks, places, buffer):
    rows, width = blocks[0].shape
    steps = 2
    tile = rows // steps
    count = len(blocks)

    def spec(k):
        return pl.BlockSpec((tile, width), lambda i: (jnp.clip(i - steps * k, 0, steps - 1), 0))

    def put(i):
        place = places[0]
        for k in range(1, count):
            place = jnp.where(i // steps >= k, places[k], place)
        return place * steps + i % steps, 0

    extra = [] if buffer is None else [buffer]
    return pl.pallas_call(
        functools.partial(norm_kernel, count=count, steps=steps),
        out_shape=jax.ShapeDtypeStruct((HEADS * rows, width), BF16),
        grid=(count * steps,),
        in_specs=[spec(k) for k in range(count)] + [pl.BlockSpec(memory_space=pl.ANY)] * len(extra),
        out_specs=pl.BlockSpec((tile, width), put),
        input_output_aliases={count: 0} if extra else {},
        cost_estimate=SMALL_COST,
    )(*blocks, *extra)


def dot32(left, right, left_dim=1, right_dim=0):
    return lax.dot_general(
        left, right, (((left_dim,), (right_dim,)), ((), ())), preferred_element_type=F32
    )


def tokens_spec(tile, width, first):
    return pl.BlockSpec((tile, width), lambda i: (first + i, 0))


def whole_spec(shape):
    return pl.BlockSpec(shape, lambda i: (0, 0), pipeline_mode=pl.Buffered(1))


def block_specs(count, tile, width):
    return [pl.BlockSpec((tile, width), lambda i: (0, 0)) for _ in range(count)]


def project_kernel(normed_ref, up_ref, qkv_w_ref, shift_ref, *refs):
    act_ref, slope_ref, qkv_ref = refs[-3:]
    hidden = act_ref.shape[1]
    lanes = 256
    for start in range(0, hidden, lanes):
        columns = slice(start, start + lanes)
        value = dot32(normed_ref[...], up_ref[:, columns]) + shift_ref[:, columns]
        normal = 0.5 + 0.5 * lax.erf(value * (0.5**0.5))
        bell = jnp.exp(value * value * -0.5) * ((2.0 * math.pi) ** -0.5)
        act_ref[:, columns] = (value * normal).astype(BF16)
        slope_ref[:, columns] = (normal + value * bell).astype(BF16)
    for start in range(0, qkv_ref.shape[1], lanes):
        columns = slice(start, start + lanes)
        value = dot32(normed_ref[...], qkv_w_ref[:, columns])
        value = value + shift_ref[:, hidden + start : hidden + start + lanes]
        qkv_ref[:, columns] = value.astype(BF16)


def project(normed, w_up, w_qkv, shift, first, last, buffers):
    count, width = normed.shape
    tile = 2 * count // HEADS
    widths = (w_up.shape[1], w_up.shape[1], w_qkv.shape[1])
    return pl.pallas_call(
        project_kernel,
        out_shape=tuple(jax.ShapeDtypeStruct((count, n), BF16) for n in widths),
        grid=(last - first,),
        in_specs=[
            tokens_spec(tile, width, first),
            whole_spec(w_up.shape),
            whole_spec(w_qkv.shape),
            whole_spec(shift.shape),
        ]
        + [pl.BlockSpec(memory_space=pl.ANY)] * len(buffers),
        out_specs=tuple(tokens_spec(tile, n, first) for n in widths),
        input_output_aliases={4 + k: k for k in range(len(buffers))},
        compiler_params=pltpu.CompilerParams(vmem_limit_bytes=BIG_VMEM),
        cost_estimate=SMALL_COST,
    )(normed, w_up, w_qkv, shift, *buffers)


def combine_kernel(one_a_ref, one_b_ref, two_a_ref, two_b_ref, w_one_ref, w_two_ref, *out_refs, right_dim):
    rows = out_refs[0].shape[0]
    for pair, (one_ref, two_ref) in enumerate(((one_a_ref, two_a_ref), (one_b_ref, two_b_ref))):
        value = dot32(one_ref[...], w_one_ref[...], 1, right_dim)
        value = value + dot32(two_ref[...], w_two_ref[...], 1, right_dim)
        out_refs[2 * pair][...] = value[:rows].astype(BF16)
        out_refs[2 * pair + 1][...] = value[rows:].astype(BF16)


def combine(one, two, w_one, w_two, rows, side, right_dim):
    width = w_one.shape[1 - right_dim]
    lanes = 512

    def weight_spec(weight):
        if right_dim:
            return pl.BlockSpec((lanes, weight.shape[1]), lambda i: (i, 0))
        return pl.BlockSpec((weight.shape[0], lanes), lambda i: (0, i))

    def left_spec(left, pair):
        return pl.BlockSpec(
            (2 * rows, left.shape[1]),
            lambda i: (2 * pair + side, 0),
            pipeline_mode=pl.Buffered(1),
        )

    return pl.pallas_call(
        functools.partial(combine_kernel, right_dim=right_dim),
        out_shape=tuple(jax.ShapeDtypeStruct((rows, width), BF16) for _ in range(4)),
        grid=(width // lanes,),
        in_specs=[left_spec(left, pair) for left in (one, two) for pair in (0, 1)]
        + [weight_spec(w_one), weight_spec(w_two)],
        out_specs=tuple(pl.BlockSpec((rows, lanes), lambda i: (0, i)) for _ in range(4)),
        compiler_params=pltpu.CompilerParams(vmem_limit_bytes=BIG_VMEM),
        cost_estimate=SMALL_COST,
    )(one, one, two, two, w_one, w_two)


def pull_kernel(*refs, count):
    blocks, (w_one_ref, w_two_ref, slope_ref) = refs[:count], refs[count : count + 3]
    pre_ref, att_ref, sum_ref, left_ref, sems = refs[-5:]
    rows = blocks[0].shape[0]
    last = pl.num_programs(0) - 1

    @pl.when(pl.program_id(0) == 0)
    def _():
        copies = [
            pltpu.make_async_copy(block, left_ref.at[pl.ds(k * rows, rows)], sems.at[k])
            for k, block in enumerate(blocks)
        ]
        for copy in copies:
            copy.start()
        for copy in copies:
            copy.wait()

    @pl.when(pl.program_id(0) < last)
    def _():
        value = dot32(left_ref[...], w_one_ref[...], 1, 1)
        value = (value * slope_ref[...].astype(F32)).astype(BF16)
        pre_ref[...] = value
        sum_ref[...] = jnp.sum(value.astype(F32), axis=0, keepdims=True)

    @pl.when(pl.program_id(0) == last)
    def _():
        att_ref[...] = dot32(left_ref[...], w_two_ref[...], 1, 1).astype(BF16)


def pull(blocks, w_down, w_dense, slope, part, buffers):
    rows, width = blocks[0].shape
    hidden, head = w_down.shape[0], w_dense.shape[0]
    tokens = HEADS * rows
    count = len(blocks)
    lanes = 256
    steps = hidden // lanes

    def at(i):
        return jnp.minimum(i, steps - 1)

    anywhere = pl.BlockSpec(memory_space=pl.ANY)
    return pl.pallas_call(
        functools.partial(pull_kernel, count=count),
        out_shape=(
            jax.ShapeDtypeStruct((tokens, hidden), BF16),
            jax.ShapeDtypeStruct((tokens, head), BF16),
            jax.ShapeDtypeStruct((1, hidden), F32),
        ),
        grid=(steps + 1,),
        in_specs=[anywhere] * count
        + [
            pl.BlockSpec((lanes, width), lambda i: (at(i), 0)),
            whole_spec(w_dense.shape),
            pl.BlockSpec((count * rows, lanes), lambda i: (part, at(i))),
        ]
        + [anywhere] * len(buffers),
        out_specs=(
            pl.BlockSpec((count * rows, lanes), lambda i: (part, at(i))),
            pl.BlockSpec((count * rows, head), lambda i: (part, 0)),
            pl.BlockSpec((1, lanes), lambda i: (0, at(i))),
        ),
        scratch_shapes=[pltpu.VMEM((count * rows, width), BF16), pltpu.SemaphoreType.DMA((count,))],
        input_output_aliases={count + 3 + k: k for k in range(len(buffers))},
        compiler_params=pltpu.CompilerParams(vmem_limit_bytes=BIG_VMEM),
        cost_estimate=SMALL_COST,
    )(*blocks, w_down, w_dense, slope, *buffers)


def moments_kernel(
    core_ref,
    normed_ref,
    right_ref,
    weight_ref,
    norms_ref,
    columns_ref,
    keep_ref,
    give_ref,
    gain_sum_ref,
    bias_sum_ref,
    low_ref,
    *,
    quarter,
    norm,
):
    lanes = 256
    turned = normed_ref[...].T
    gain = norms_ref[:, 2 * norm : 2 * norm + 1]
    shift = norms_ref[:, 2 * norm + 1 : 2 * norm + 2]
    gain_terms, bias_terms = None, None
    for start in range(0, low_ref.shape[1], lanes):
        columns = slice(start, start + lanes)
        moment = dot32(turned, right_ref[:, columns])
        weight = weight_ref[:, columns].astype(F32)
        total = columns_ref[:, columns]
        low_ref[:, columns] = (moment * gain + shift * total).astype(BF16)
        one, two = moment * weight, weight * total
        gain_terms = one if gain_terms is None else gain_terms + one
        bias_terms = two if bias_terms is None else bias_terms + two
    for terms, sum_ref in ((gain_terms, gain_sum_ref), (bias_terms, bias_sum_ref)):
        sum_ref[...] = jnp.sum(terms.T, axis=0, keepdims=True)
    for core in (0, 1):

        @pl.when(core_ref[0] == core)
        def _(core=core):
            for k in range(low_ref.shape[0] // quarter):
                target = keep_ref if k % 2 == core else give_ref
                target[k // 2 * quarter : (k // 2 + 1) * quarter, :] = low_ref[
                    k * quarter : (k + 1) * quarter, :
                ]


def moments_of(core, normed, right, weight, norms, norm, columns, quarter):
    count, width = normed.shape
    wide = weight.shape[1]
    tile = 8 * quarter
    return pl.pallas_call(
        functools.partial(moments_kernel, quarter=quarter, norm=norm),
        out_shape=(
            jax.ShapeDtypeStruct((width // 2, wide), BF16),
            jax.ShapeDtypeStruct((width // 2, wide), BF16),
            jax.ShapeDtypeStruct((1, width), F32),
            jax.ShapeDtypeStruct((1, width), F32),
        ),
        grid=(width // tile,),
        in_specs=[
            SMEM_SPEC,
            pl.BlockSpec((count, tile), lambda i: (0, i)),
            whole_spec(right.shape),
            tokens_spec(tile, wide, 0),
            tokens_spec(tile, 4, 0),
            whole_spec(columns.shape),
        ],
        out_specs=(
            tokens_spec(tile // 2, wide, 0),
            tokens_spec(tile // 2, wide, 0),
            pl.BlockSpec((1, tile), lambda i: (0, i)),
            pl.BlockSpec((1, tile), lambda i: (0, i)),
        ),
        scratch_shapes=[pltpu.VMEM((tile, wide), BF16)],
        compiler_params=pltpu.CompilerParams(vmem_limit_bytes=BIG_VMEM),
        cost_estimate=SMALL_COST,
    )(core[None].astype(jnp.int32), normed, right, weight, norms, columns)


def outer_kernel(core_ref, act_ref, att_ref, *refs):
    blocks, out_refs = refs[:HEADS], refs[HEADS:]
    rows = blocks[0].shape[0]
    lanes = 512
    last = pl.num_programs(1) - 1

    def fill(left_ref, out_ref):
        turned = left_ref[...].T
        for start in range(0, out_ref.shape[1], lanes):
            columns = slice(start, start + lanes)
            total = None
            for k, block_ref in enumerate(blocks):
                term = dot32(turned[:, k * rows : (k + 1) * rows], block_ref[:, columns])
                total = term if total is None else total + term
            out_ref[:, columns] = total.astype(BF16)

    for side in (0, 1):
        for left_ref, chosen in (
            (act_ref, pl.program_id(1) < last),
            (att_ref, pl.program_id(1) == last),
        ):

            @pl.when((pl.program_id(0) == side) & chosen)
            def _(left_ref=left_ref, side=side):
                fill(left_ref, out_refs[side])


def outer(core, activated, attended, blocks):
    count, hidden = activated.shape
    rows, width = blocks[0].shape
    tile = attended.shape[1]
    steps = hidden // tile
    half = jax.ShapeDtypeStruct((hidden + tile, width // 2), BF16)
    return pl.pallas_call(
        outer_kernel,
        out_shape=(half, half),
        grid_spec=pltpu.PrefetchScalarGridSpec(
            num_scalar_prefetch=1,
            grid=(2, steps + 1),
            in_specs=[
                pl.BlockSpec((count, tile), lambda j, i, core_ref: (0, jnp.minimum(i, steps - 1))),
                pl.BlockSpec((count, tile), lambda j, i, core_ref: (0, 0)),
            ]
            + [
                pl.BlockSpec((rows, width // 2), lambda j, i, core_ref: (0, j ^ core_ref[0]))
                for _ in blocks
            ],
            out_specs=(
                pl.BlockSpec(
                    (tile, width // 2), lambda j, i, core_ref: (jnp.where(j == 0, i, steps), 0)
                ),
                pl.BlockSpec(
                    (tile, width // 2), lambda j, i, core_ref: (jnp.where(j == 0, 0, i), 0)
                ),
            ),
        ),
        compiler_params=pltpu.CompilerParams(vmem_limit_bytes=BIG_VMEM),
        cost_estimate=SMALL_COST,
    )(core[None].astype(jnp.int32), activated, attended, *blocks)


def split_shards(
    tokens,
    cotangent,
    seq_lengths,
    seq_order,
    ln1_gain,
    ln1_bias,
    ln2_gain,
    ln2_bias,
    w_qkv,
    b_qkv,
    w_dense,
    b_dense,
    w_up,
    b_up,
    w_down,
    b_down,
):
    me = lax.axis_index("shard")
    rep = lax.axis_index("rep")
    place = me // 2
    is_middle = (place == 1) | (place == 2)
    own = tokens[:, 0, :]
    own_grad = cotangent[:, 0, :]
    rows, width = own.shape
    group_tokens = rows * HEADS
    depth = w_up.shape[0]
    hidden = w_down.shape[0]
    wide = hidden + 3 * HEAD
    quarter = depth // 4

    odd, keep = pack(me, rep, w_up, w_qkv, hidden)
    odd_came = flip(odd, "shard", 1)
    x_near = flip(own, "shard", 2)
    x_across = send(own, MIDDLE)
    row_offsets, row_counts = stream_rows(seq_lengths[0], seq_order[0], HEADS)
    ends = (row_offsets + row_counts) * HEADS
    seq_scalars = jnp.concatenate([ends, me[None]]).astype(jnp.int32)
    row_range = jnp.arange(rows, dtype=jnp.int32)
    member = (row_range[:, None] >= row_offsets[None, :]) & (
        row_range[:, None] < (row_offsets + row_counts)[None, :]
    )
    in_seq = row_range - jnp.sum(jnp.where(member, row_offsets[None, :], 0), axis=1)
    block_range = jnp.arange(HEADS, dtype=jnp.int32)
    apart = block_range // 4 * 4 + block_range % 2 * 2 + block_range // 2 % 2
    positions = (
        in_seq.reshape(rows // TILE_ROWS, 1, TILE_ROWS) * HEADS + (apart ^ me)[None, :, None]
    )
    cosine, sine = rotary_tables(positions.reshape(-1).astype(F32))
    rest = 128 - ROT
    cosine = jnp.concatenate([cosine, cosine, jnp.ones((group_tokens, rest), F32)], axis=1)
    sine = jnp.concatenate([-sine, sine, jnp.zeros((group_tokens, rest), F32)], axis=1)
    tiled = (rows // TILE_ROWS, TILE_ROWS * HEADS, 128)
    cosine = cosine.reshape(tiled)
    sine = sine.reshape(tiled)


    norms = settled(jnp.stack([ln1_gain, ln1_bias, ln2_gain, ln2_bias], axis=1))
    out_columns = jnp.sum(own_grad, axis=0, dtype=F32)
    b_in = jnp.concatenate(
        [lax.dynamic_slice_in_dim(b_up, me * hidden, hidden, 0)]
        + [lax.dynamic_slice_in_dim(b_qkv, k * width + me * HEAD, HEAD, 0) for k in range(3)]
    )
    pairs = jnp.stack([keep, odd_came], axis=1)
    own, own_grad, x_near, x_across, norms, b_in, out_columns, *pairs = hold(
        (own, own_grad, x_near, x_across, norms, b_in, out_columns, *[pairs[z] for z in range(4)]),
        (cosine, sine),
    )
    got = [flip(pairs[z], "shard", 2 * z) for z in range(1, 4)]
    x_own_y = flip(own, "shard", 1)
    x_near_y = flip(x_near, "shard", 1)
    beside = [flip(pairs[0], "rep", 2)]
    got = jnp.stack(got)
    x_near, x_across, own_grad, x_near_y, got = hold(
        (x_near, x_across, own_grad, x_near_y, got), (x_own_y, beside[0])
    )
    x_across_near = send(x_near, MIDDLE)
    x_two = send(x_across, OUTWARD)
    g_own_y = flip(own_grad, "shard", 1)
    beside = beside + [flip(got, "rep", 2)]
    part = jnp.concatenate([pairs[0][None], got]).reshape(HEADS, quarter, wide)
    normed = norm_blocks([own, x_near, x_own_y, x_near_y], (0, 1, 2, 3), None)
    x_across_near, x_two, own_grad, normed, *beside = hold(
        (x_across_near, x_two, own_grad, normed, *beside), (part, g_own_y)
    )
    two = jnp.where(is_middle, x_across_near, x_two)
    x_three = send(x_across_near, OUTWARD)
    g_across = send(own_grad, MIDDLE)
    x_two_y = flip(two, "shard", 1)
    beside = jnp.concatenate([beside[0][None], beside[1]]).reshape(HEADS, quarter, wide)
    part_c = flip(part, "rep", 1)
    beside_c = flip(beside, "rep", 1)
    normed = norm_blocks([two], (4,), normed)
    parts = (part, part_c, beside, beside_c)
    up_raw, qkv_raw, up_scaled, qkv_scaled, shifted = place_weights(
        me, rep, parts, norms, hidden
    )
    b_in = b_in[None, :] + shifted
    (x_two_y,) = hold((x_two_y,), (b_in,))
    normed = norm_blocks([x_two_y], (6,), normed)
    x_three, own_grad, g_across, normed, b_in = hold(
        (x_three, own_grad, g_across, normed, b_in), ()
    )
    three = jnp.where(is_middle, x_across, x_three)
    g_near = flip(own_grad, "shard", 2)
    x_three_y = flip(three, "shard", 1)
    normed = norm_blocks([three], (5,), normed)
    halfway = project(normed, up_scaled, qkv_scaled, b_in, 0, 3, [])
    g_near, x_three_y, *halfway = hold((g_near, x_three_y, *halfway), ())
    g_across_near = send(g_near, MIDDLE)
    g_two = send(g_across, OUTWARD)
    g_near_y = flip(g_near, "shard", 1)
    normed = norm_blocks([x_three_y], (7,), normed)
    activated, slope, qkv = project(normed, up_scaled, qkv_scaled, b_in, 3, 4, halfway)
    qkv = qkv.reshape(HEADS, rows, 3 * HEAD)
    attended, query, key = attend(seq_scalars, qkv, cosine, sine)
    attended = attended.reshape(group_tokens, HEAD)
    g_across_near, g_two, attended, g_near_y = hold((g_across_near, g_two, attended, g_near_y), ())
    g_two = jnp.where(is_middle, g_across_near, g_two)
    g_three = send(g_across_near, OUTWARD)
    g_two_y = flip(g_two, "shard", 1)
    far = combine(activated, attended, w_down, w_dense, rows, 1, 0)
    close = combine(activated, attended, w_down, w_dense, rows, 0, 0)
    g_three, g_near_y, g_two_y, *both = hold((g_three, g_near_y, g_two_y, *far, *close), ())
    far, close = both[:4], both[4:]
    g_three = jnp.where(is_middle, g_across, g_three)
    g_three_y = flip(g_three, "shard", 1)
    *grads, sums_one = pull([own_grad, g_near, g_own_y, g_near_y], w_down, w_dense, slope, 0, [])
    *grads, sums_two = pull([g_two, g_three], w_down, w_dense, slope, 2, grads)
    g_three_y, *both = hold((g_three_y, *far, *grads), ())
    far, grads = both[:4], both[4:]
    came_three = flip(far[3], "shard", 1)
    grad_pre, grad_attended, sums_three = pull(
        [g_two_y, g_three_y], w_down, w_dense, slope, 3, grads
    )
    pre_sums = sums_one + sums_two + sums_three
    my_core = rep % 2
    my_side = rep // 2
    my_row = me % 2

    def split(values, index):
        return (
            lax.dynamic_index_in_dim(values, index, 1, False),
            lax.dynamic_index_in_dim(values, 1 - index, 1, False),
        )

    def by_side(summed):
        return split(summed.reshape(HEADS, 2, quarter, summed.shape[-1]), my_side)

    def by_row(summed):
        return split(summed.reshape(4, 2, quarter, summed.shape[-1]), my_row)

    def joined(mine, came):
        return plus(mine, came).astype(BF16)

    def by_place(mine, came):
        both = jnp.stack([mine, came], axis=1)
        return [lax.dynamic_index_in_dim(both, place ^ z, 0, False) for z in range(4)]

    def far_places(pieces):
        return flip(jnp.stack(pieces[2:]), "shard", 4)

    def near_place(pieces, far):
        return flip(jnp.stack([pieces[1], far[1]]), "shard", 2)

    def sources(pieces, far, near):
        both = jnp.stack([pieces[0], near[0], far[0], near[1]])
        return both.reshape(HEADS, quarter, both.shape[-1])

    up_keep, up_give, *up_sums = moments_of(
        my_core, normed, grad_pre, up_raw, norms, 1, pre_sums, quarter
    )
    three = joined(close[3], came_three)
    grad_attended, up_give, three, *far = hold((grad_attended, up_give, three, *far), ())
    came_two = flip(far[2], "shard", 1)
    from_corner = send(three, INWARD)
    up_came = flip(up_give, "rep", 1)
    grad_qkv, qkv_sums = attend_back(
        seq_scalars,
        qkv,
        grad_attended.reshape(HEADS, rows, HEAD),
        cosine,
        sine,
        query,
        key,
    )
    grad_qkv = grad_qkv.reshape(group_tokens, 3 * HEAD)
    qkv_keep, qkv_give, *qkv_row_sums = moments_of(
        my_core, normed, grad_qkv, qkv_raw, norms, 0, qkv_sums, quarter
    )
    two = joined(close[2], came_two)
    up_keep, up_give = by_side(joined(up_keep, up_came))
    from_corner, up_give, qkv_give, grad_qkv, two, *far = hold(
        (from_corner, up_give, qkv_give, grad_qkv, two, *far), (up_keep,)
    )
    up_came = flip(up_give, "rep", 2)
    came_one = flip(far[1], "shard", 1)
    two = joined(two, from_corner)
    across_near = send(two, MIDDLE)
    across = send(two, INWARD)
    qkv_came = flip(qkv_give, "rep", 1)
    gy_far = combine(grad_pre, grad_qkv, up_scaled, qkv_scaled, rows, 1, 1)
    one = joined(close[1], came_one)
    up_keep, up_give = by_row(joined(up_keep, up_came))
    qkv_keep, qkv_give = by_side(joined(qkv_keep, qkv_came))
    small = jnp.concatenate(
        [vector[0] for vector in (*qkv_row_sums, *up_sums)]
        + [
            out_columns,
            jnp.where(
                block_range[:, None] == me, jnp.concatenate([pre_sums, qkv_sums], axis=1), 0.0
            ).reshape(-1),
        ]
    )
    up_give, across_near, across, qkv_give, own_grad, one, small, *both = hold(
        (up_give, across_near, across, qkv_give, own_grad, one, small, *far, *gy_far),
        (up_keep, qkv_keep),
    )
    far, gy_far = both[:4], both[4:]
    came_own = flip(far[0], "shard", 1)
    up_came = flip(up_give, "shard", 1)
    one = joined(one, across_near)
    three = plus(three, across).astype(BF16)
    one_near = flip(one, "shard", 2)
    three_across = send(three, MIDDLE)
    qkv_came = flip(qkv_give, "rep", 2)
    half_keep, half_give = outer(
        my_core,
        activated,
        attended,
        [own_grad, g_near, g_own_y, g_near_y, g_two, g_three, g_two_y, g_three_y],
    )
    out_sum = plus(close[0], came_own)
    up_pieces = by_place(up_keep, up_came)
    qkv_keep, qkv_give = by_row(joined(qkv_keep, qkv_came))
    (
        one_near,
        three_across,
        qkv_keep,
        qkv_give,
        half_give,
        out_sum,
        *both,
    ) = hold(
        (
            one_near,
            three_across,
            qkv_keep,
            qkv_give,
            half_give,
            out_sum,
            *up_pieces,
            *gy_far,
            grad_pre,
        ),
        (),
    )
    up_pieces, gy_far, grad_pre = both[:4], both[4:8], both[8]
    came_three = flip(gy_far[3], "shard", 1)
    qkv_came = flip(qkv_give, "shard", 1)
    up_far = far_places(up_pieces)
    half_came = flip(half_give, "rep", 1)
    small_side = flip(small, "rep", 2)
    out_sum = plus(out_sum, one_near, three_across)
    output = (own.astype(F32) + out_sum + (b_dense + b_down)).astype(BF16)
    gy_close = combine(grad_pre, grad_qkv, up_scaled, qkv_scaled, rows, 0, 1)
    qkv_pieces = by_place(qkv_keep, qkv_came)
    three = joined(gy_close[3], came_three)
    output, up_far, half_came, small, small_side, three, *both = hold(
        (output, up_far, half_came, small, small_side, three, *qkv_pieces, *gy_far, *gy_close), ()
    )
    qkv_pieces, gy_far, gy_close = both[:4], both[4:8], both[8:]
    came_two = flip(gy_far[2], "shard", 1)
    from_corner = send(three, INWARD)
    qkv_far = far_places(qkv_pieces)
    half = joined(half_keep, half_came)
    half_far = flip(half, "rep", 2)
    small = small + small_side
    small_side = flip(small, "rep", 1)
    two = joined(gy_close[2], came_two)
    from_corner, qkv_far, small, small_side, two, *gy_far = hold(
        (from_corner, qkv_far, small, small_side, two, *gy_far), ()
    )
    came_one = flip(gy_far[1], "shard", 1)
    two = joined(two, from_corner)
    across_near = send(two, MIDDLE)
    across = send(two, INWARD)
    up_near = near_place(up_pieces, up_far)
    one = joined(gy_close[1], came_one)
    up_part = sources(up_pieces, up_far, up_near)
    across_near, across, up_part, half_far, one, qkv_far, *gy_far = hold(
        (across_near, across, up_part, half_far, one, qkv_far, *gy_far), ()
    )
    came_own = flip(gy_far[0], "shard", 1)
    one = joined(one, across_near)
    three = plus(three, across).astype(BF16)
    one_near = flip(one, "shard", 2)
    three_across = send(three, MIDDLE)
    up_beside = flip(up_part, "rep", 2)
    qkv_near = near_place(qkv_pieces, qkv_far)
    half = joined(half, half_far)
    gy = plus(gy_close[0], came_own)
    qkv_part = sources(qkv_pieces, qkv_far, qkv_near)
    one_near, three_across, qkv_part, up_beside, half, small, gy = hold(
        (one_near, three_across, qkv_part, up_beside, half, small, gy), ()
    )
    qkv_beside = flip(qkv_part, "rep", 2)
    up_c = flip(jnp.stack([up_part, up_beside]), "rep", 1)
    other = flip(half, "rep", 1)
    small = small + small_side
    small = small + flip(small, "shard", 1)
    gy = plus(gy, one_near, three_across)
    own_normed, own_rstd = normalize(own)
    input_grad = own_grad.astype(F32) + own_rstd * (
        gy
        - jnp.mean(gy, axis=-1, keepdims=True)
        - own_normed * jnp.mean(gy * own_normed, axis=-1, keepdims=True)
    )
    input_grad = input_grad[:, None, :]
    up_grad = place_grads(me, rep, (up_part, up_c[0], up_beside, up_c[1]), 1)
    down_grad, dense_grad = place_halves(my_core, half, other, hidden)
    qkv_c = flip(qkv_part, "rep", 1)
    (small,) = hold((small,), (up_c, qkv_c, other))
    one, two, three = [flip(small, "shard", bit) for bit in (2, 4, 6)]
    small = (small + one) + (two + three)
    input_grad, up_grad, down_grad, qkv_beside, qkv_c, small = hold(
        (input_grad, up_grad, down_grad, qkv_beside, qkv_c, small), ()
    )
    qkv_beside_c = flip(qkv_beside, "rep", 1)
    qkv_grad = place_grads(me, rep, (qkv_part, qkv_c, qkv_beside, qkv_beside_c), 3)
    vectors = small[: 5 * width].reshape(5, width)
    slots = small[5 * width :].reshape(HEADS, wide)
    b_up_grad = slots[:, :hidden].reshape(-1)
    b_qkv_grad = slots[:, hidden:].reshape(HEADS, 3, HEAD).transpose(1, 0, 2).reshape(-1)
    return (
        output[:, None, :],
        input_grad,
        vectors[0],
        vectors[1],
        vectors[2],
        vectors[3],
        qkv_grad,
        b_qkv_grad,
        dense_grad,
        vectors[4],
        up_grad,
        b_up_grad,
        down_grad,
        vectors[4],
    )


def solution(mesh):
    in_specs = (
        P("rep", "shard", None),
        P("rep", "shard", None),
        P("rep", None),
        P("rep", None),
        P(),
        P(),
        P(),
        P(),
        P("shard", None),
        P(),
        P("shard", None),
        P(),
        P("shard", None),
        P(),
        P("shard", None),
        P(),
    )
    out_specs = (
        P("rep", "shard", None),
        P("rep", "shard", None),
        P(),
        P(),
        P(),
        P(),
        P("shard", None),
        P(),
        P("shard", None),
        P(),
        P("shard", None),
        P(),
        P("shard", None),
        P(),
    )
    body = split_shards if mesh.shape["shard"] == HEADS else shards
    return jax.shard_map(
        body, mesh=mesh, in_specs=in_specs, out_specs=out_specs, check_vma=False
    )
```

```python
import functools
import math

import jax
import jax.numpy as jnp
from jax import lax
from jax.experimental import pallas as pl
from jax.experimental.pallas import tpu as pltpu
from jax.sharding import PartitionSpec as P

HEADS = 8
HEAD = 256
ROT = 64


EPSILON = 1e-05
MASKED = -1e30


def layer_norm(vector, gain_vec, shift_vec):
    mean_val = jnp.mean(vector, axis=-1, keepdims=True)
    centered = vector - mean_val
    variance = jnp.mean(centered * centered, axis=-1, keepdims=True)
    return centered * lax.rsqrt(variance + EPSILON) * gain_vec + shift_vec


def gelu_exact(vector):
    return jax.nn.gelu(vector, approximate=False)


def rotary_tables(positions):
    half_rot = ROT // 2
    freq_index = jnp.arange(half_rot, dtype=jnp.float32)
    inverse_freq = jnp.exp(freq_index * (-2.0 * math.log(10000.0) / ROT))
    angles = positions[:, None] * inverse_freq[None, :]
    return (jnp.cos(angles), jnp.sin(angles))


def rotate(heads_in, cosine_table, sine_table):
    half_rot = ROT // 2
    first_half = heads_in[..., :half_rot]
    second_half = heads_in[..., half_rot:ROT]
    cos_wide = cosine_table[:, None, :]
    sin_wide = sine_table[:, None, :]
    return jnp.concatenate(
        [
            first_half * cos_wide - second_half * sin_wide,
            second_half * cos_wide + first_half * sin_wide,
            heads_in[..., ROT:],
        ],
        axis=-1,
    )


def stream_rows(lengths, seq_perm, shard_count):
    seq_range = jnp.arange(lengths.shape[0], dtype=jnp.int32)
    ranking = jnp.sum(
        jnp.where(seq_perm[:, None] == seq_range[None, :], seq_range[:, None], 0), axis=0
    )
    offsets = jnp.sum(jnp.where(ranking[None, :] < ranking[:, None], lengths[None, :], 0), axis=1)
    return (offsets // shard_count, lengths // shard_count)


def row_product(left, right):
    return jnp.dot(left.T, right, preferred_element_type=jnp.float32)


def block_mask(seq_flag, positions, live):
    return (
        live[:, None]
        & live[None, :]
        & (seq_flag[:, None] == seq_flag[None, :])
        & (positions[None, :] <= positions[:, None])
    )


def shards(
    tokens,
    cotangent,
    seq_lengths,
    seq_order,
    ln1_gain,
    ln1_bias,
    ln2_gain,
    ln2_bias,
    w_qkv,
    b_qkv,
    w_dense,
    b_dense,
    w_up,
    b_up,
    w_down,
    b_down,
):
    shard_count = lax.axis_size("shard")
    my_index = lax.axis_index("shard")
    inputs = tokens[:, 0, :].astype(jnp.float32)
    grad_out = cotangent[:, 0, :]
    local_rows, width = inputs.shape
    slot_rows = 2 * (local_rows // shard_count) - 4
    buffer_rows = slot_rows * shard_count
    row_offsets, row_counts = stream_rows(seq_lengths[0], seq_order[0], shard_count)
    first_count = row_counts[0::2]
    second_count = row_counts[1::2]
    first_start = row_offsets[0::2]
    second_start = row_offsets[1::2]
    slot_range = jnp.arange(slot_rows, dtype=jnp.int32)[None, :]
    in_first = slot_range < first_count[:, None]
    slot_live = slot_range < (first_count + second_count)[:, None]
    source_rows = jnp.where(
        in_first,
        first_start[:, None] + slot_range,
        second_start[:, None] + slot_range - first_count[:, None],
    )
    source_rows = jnp.where(slot_live, source_rows, 0)
    seq_range = jnp.arange(row_counts.shape[0], dtype=jnp.int32)
    parity = seq_range % 2
    slot_base = seq_range // 2 * slot_rows + parity * row_counts[seq_range - parity] - row_offsets
    token_range = jnp.arange(local_rows, dtype=jnp.int32)[:, None]
    member = (token_range >= row_offsets[None, :]) & (
        token_range < (row_offsets + row_counts)[None, :]
    )
    return_rows = token_range[:, 0] + jnp.sum(jnp.where(member, slot_base[None, :], 0), axis=1)
    own_first = first_count[my_index]
    own_second = second_count[my_index]
    buffer_range = jnp.arange(buffer_rows, dtype=jnp.int32)
    slot_index = buffer_range % slot_rows
    source_index = buffer_range // slot_rows
    seq_flag = (slot_index >= own_first).astype(jnp.int32)
    positions = (slot_index - seq_flag * own_first) * shard_count + source_index
    live = slot_index < own_first + own_second
    attn_full, dense_full = (
        lax.all_gather(w_qkv, "shard", axis=0, tiled=True),
        lax.all_gather(w_dense, "shard", axis=0, tiled=True),
    )
    up_full, down_full = (
        lax.all_gather(w_up, "shard", axis=0, tiled=True),
        lax.all_gather(w_down, "shard", axis=0, tiled=True),
    )
    normed_one_wide, pull_one = jax.vjp(layer_norm, inputs, ln1_gain, ln1_bias)
    normed_two_wide, pull_two = jax.vjp(layer_norm, inputs, ln2_gain, ln2_bias)
    normed_one = normed_one_wide.astype(jnp.bfloat16)
    normed_two = normed_two_wide.astype(jnp.bfloat16)
    qkv = (jnp.dot(normed_one, attn_full, preferred_element_type=jnp.float32) + b_qkv).astype(
        jnp.bfloat16
    )
    arrived = lax.all_to_all(
        jnp.take(qkv, source_rows, axis=0), "shard", split_axis=0, concat_axis=0, tiled=True
    )
    arrived = arrived.reshape(buffer_rows, 3 * width)
    heads_shape = (buffer_rows, HEADS, HEAD)
    cosine_table, sine_table = rotary_tables(positions.astype(jnp.float32))

    def rotate_here(heads_in):
        return rotate(heads_in, cosine_table, sine_table)

    query_wide, pull_query = jax.vjp(
        rotate_here, arrived[:, :width].astype(jnp.float32).reshape(heads_shape)
    )
    key_wide, pull_key = jax.vjp(
        rotate_here, arrived[:, width : 2 * width].astype(jnp.float32).reshape(heads_shape)
    )
    rotated_queries = query_wide.astype(jnp.bfloat16)
    rotated_keys = key_wide.astype(jnp.bfloat16)
    value_heads = arrived[:, 2 * width :].reshape(heads_shape)
    sources_per = shard_count
    while sources_per > 1 and sources_per * slot_rows > 1024:
        sources_per = sources_per // 2
    block_rows = sources_per * slot_rows
    block_total = buffer_rows // block_rows
    score_scale = HEAD ** (-0.5)

    def forward_block(block_index):
        allowed = block_mask(seq_flag, positions, live)
        scores = (
            jnp.einsum(
                "qhe,khe->hqk", rotated_queries, rotated_keys, preferred_element_type=jnp.float32
            )
            * score_scale
        )
        scores = jnp.where(allowed[None], scores, MASKED)
        row_max = jnp.max(scores, axis=-1, keepdims=True)
        exp_scores = jnp.exp(scores - row_max)
        exp_total = jnp.sum(exp_scores, axis=-1, keepdims=True)
        attn_probs = jnp.where(allowed[None], exp_scores / exp_total, 0.0)
        attended_blk = jnp.einsum(
            "hqk,khe->qhe",
            attn_probs.astype(jnp.bfloat16),
            value_heads,
            preferred_element_type=jnp.float32,
        )
        return (attended_blk.astype(jnp.bfloat16), row_max[..., 0] + jnp.log(exp_total[..., 0]))

    attended_blocks, log_totals = lax.map(forward_block, jnp.arange(block_total, dtype=jnp.int32))
    attended_slots = attended_blocks.reshape(shard_count, slot_rows, width)
    attn_back = lax.all_to_all(
        attended_slots, "shard", split_axis=0, concat_axis=0, tiled=True
    ).reshape(buffer_rows, width)
    attn_in = jnp.take(attn_back, return_rows, axis=0)
    attn_out = jnp.dot(attn_in, dense_full, preferred_element_type=jnp.float32) + b_dense
    pre_up = jnp.dot(normed_two, up_full, preferred_element_type=jnp.float32) + b_up
    activated_wide, pull_gelu = jax.vjp(gelu_exact, pre_up)
    activated = activated_wide.astype(jnp.bfloat16)
    mlp_out = jnp.dot(activated, down_full, preferred_element_type=jnp.float32) + b_down
    output = (inputs + attn_out + mlp_out).astype(jnp.bfloat16)
    attn_second, dense_second = (
        lax.all_gather(w_qkv, "shard", axis=0, tiled=True),
        lax.all_gather(w_dense, "shard", axis=0, tiled=True),
    )
    up_second, down_second = (
        lax.all_gather(w_up, "shard", axis=0, tiled=True),
        lax.all_gather(w_down, "shard", axis=0, tiled=True),
    )
    grad_attended = jnp.dot(grad_out, dense_second.T, preferred_element_type=jnp.float32).astype(
        jnp.bfloat16
    )
    grad_slots = jnp.where(
        slot_live[:, :, None],
        jnp.take(grad_attended, source_rows, axis=0),
        jnp.zeros((), jnp.bfloat16),
    )
    grad_heads = lax.all_to_all(
        grad_slots, "shard", split_axis=0, concat_axis=0, tiled=True
    ).reshape(heads_shape)

    def backward_block(carried, block_index):
        grad_keys, grad_values = carried
        allowed = block_mask(seq_flag, positions, live)
        scores = (
            jnp.einsum(
                "qhe,khe->hqk", rotated_queries, rotated_keys, preferred_element_type=jnp.float32
            )
            * score_scale
        )
        attn_probs = jnp.where(
            allowed[None], jnp.exp(scores - log_totals[block_index][..., None]), 0.0
        )
        grad_probs = jnp.einsum(
            "qhe,khe->hqk", grad_heads, value_heads, preferred_element_type=jnp.float32
        )
        row_delta = jnp.sum(attn_probs * grad_probs, axis=-1, keepdims=True)
        grad_scores = (attn_probs * (grad_probs - row_delta)).astype(jnp.bfloat16)
        grad_query = (
            jnp.einsum(
                "hqk,khe->qhe", grad_scores, rotated_keys, preferred_element_type=jnp.float32
            )
            * score_scale
        )
        grad_keys = (
            grad_keys
            + jnp.einsum(
                "hqk,qhe->khe", grad_scores, rotated_queries, preferred_element_type=jnp.float32
            )
            * score_scale
        )
        grad_values = grad_values + jnp.einsum(
            "hqk,qhe->khe",
            attn_probs.astype(jnp.bfloat16),
            grad_heads,
            preferred_element_type=jnp.float32,
        )
        return ((grad_keys, grad_values), grad_query)

    zero_heads = jnp.zeros(heads_shape, jnp.float32)
    (grad_keys, grad_values), grad_query_blocks = lax.scan(
        backward_block, (zero_heads, zero_heads), jnp.arange(block_total, dtype=jnp.int32)
    )
    grad_q_pre = pull_query(grad_query_blocks.reshape(heads_shape))[0]
    grad_k_pre = pull_key(grad_keys)[0]
    grad_qkv_slots = jnp.concatenate(
        [
            grad_q_pre.reshape(buffer_rows, width),
            grad_k_pre.reshape(buffer_rows, width),
            grad_values.reshape(buffer_rows, width),
        ],
        axis=1,
    ).astype(jnp.bfloat16)
    grad_qkv_slots = grad_qkv_slots.reshape(shard_count, slot_rows, 3 * width)
    grad_qkv_back = lax.all_to_all(grad_qkv_slots, "shard", split_axis=0, concat_axis=0, tiled=True)
    grad_qkv = jnp.take(grad_qkv_back.reshape(buffer_rows, 3 * width), return_rows, axis=0)
    grad_activated = jnp.dot(grad_out, down_second.T, preferred_element_type=jnp.float32)
    grad_pre = pull_gelu(grad_activated)[0].astype(jnp.bfloat16)
    grad_normed_one = jnp.dot(grad_qkv, attn_second.T, preferred_element_type=jnp.float32)
    grad_normed_two = jnp.dot(grad_pre, up_second.T, preferred_element_type=jnp.float32)
    grad_in_one, grad_gain_one, grad_bias_one = pull_one(grad_normed_one)
    grad_in_two, grad_gain_two, grad_bias_two = pull_two(grad_normed_two)
    input_grad = grad_out.astype(jnp.float32) + grad_in_one + grad_in_two
    qkv_rows = lax.psum_scatter(
        row_product(normed_one, grad_qkv).astype(jnp.bfloat16),
        "shard",
        scatter_dimension=0,
        tiled=True,
    ).astype(jnp.float32)
    dense_rows = lax.psum_scatter(
        row_product(attn_in, grad_out).astype(jnp.bfloat16),
        "shard",
        scatter_dimension=0,
        tiled=True,
    ).astype(jnp.float32)
    up_rows = lax.psum_scatter(
        row_product(normed_two, grad_pre).astype(jnp.bfloat16),
        "shard",
        scatter_dimension=0,
        tiled=True,
    ).astype(jnp.float32)
    down_rows = lax.psum_scatter(
        row_product(activated, grad_out).astype(jnp.bfloat16),
        "shard",
        scatter_dimension=0,
        tiled=True,
    ).astype(jnp.float32)
    qkv_rows, dense_rows, up_rows, down_rows = (
        lax.psum(qkv_rows.astype(jnp.bfloat16), "rep").astype(jnp.float32),
        lax.psum(dense_rows.astype(jnp.bfloat16), "rep").astype(jnp.float32),
        lax.psum(up_rows.astype(jnp.bfloat16), "rep").astype(jnp.float32),
        lax.psum(down_rows.astype(jnp.bfloat16), "rep").astype(jnp.float32),
    )
    out_column_sum = jnp.sum(grad_out, axis=0, dtype=jnp.float32)
    small_totals = lax.psum(
        (
            grad_gain_one,
            grad_bias_one,
            grad_gain_two,
            grad_bias_two,
            jnp.sum(grad_qkv, axis=0, dtype=jnp.float32),
            out_column_sum,
            jnp.sum(grad_pre, axis=0, dtype=jnp.float32),
        ),
        ("rep", "shard"),
    )
    return (
        output[:, None, :],
        input_grad[:, None, :],
        small_totals[0],
        small_totals[1],
        small_totals[2],
        small_totals[3],
        qkv_rows,
        small_totals[4],
        dense_rows,
        small_totals[5],
        up_rows,
        small_totals[6],
        down_rows,
        small_totals[5],
    )


TILE_ROWS = 32
BIG_VMEM = 60 << 20
SMALL_COST = pl.CostEstimate(flops=1 << 20, bytes_accessed=1 << 20, transcendentals=0)
F32 = jnp.float32
BF16 = jnp.bfloat16


def flip(value, axis, bit):
    size = lax.axis_size(axis)
    return lax.ppermute(value, axis, [(i, i ^ bit) for i in range(size)])


def send(value, pairs):
    return lax.ppermute(value, "shard", [(2 * a + y, 2 * b + y) for a, b in pairs for y in (0, 1)])


MIDDLE = ((1, 2), (2, 1))
OUTWARD = ((1, 0), (2, 3))
INWARD = ((0, 1), (3, 2))


def plus(*terms):
    total = terms[0].astype(F32)
    for term in terms[1:]:
        total = total + term.astype(F32)
    return total


def hold(values, gates):
    return lax.optimization_barrier(tuple(values) + tuple(gates))[: len(values)]


def turn(heads_in, cosine, sine):
    left = heads_in[:, :128]
    lane = lax.broadcasted_iota(jnp.int32, left.shape, 1)
    half = ROT // 2
    partner = jnp.where(lane < half, pltpu.roll(left, 128 - half, 1), pltpu.roll(left, half, 1))
    return jnp.concatenate([left * cosine + partner * sine, heads_in[:, 128:]], axis=1)


def token_labels(my_index, shape, dim):
    inner = lax.broadcasted_iota(jnp.int32, shape, dim)
    block = inner // TILE_ROWS
    apart = block // 4 * 4 + block % 2 * 2 + block // 2 % 2
    return (inner % TILE_ROWS) * HEADS + jnp.bitwise_xor(apart, my_index)


def tile_weights(tile, seq_ref, query, key_tiles, count):
    tile_tokens = TILE_ROWS * HEADS
    my_index = seq_ref[count]
    query_label = token_labels(my_index, (tile_tokens, 1), 0) + tile * tile_tokens
    key_label = token_labels(my_index, (1, tile_tokens), 1)
    scores = []
    for place, key in key_tiles:
        label = key_label + place * tile_tokens
        last = jnp.full(label.shape, 1 << 30, jnp.int32)
        for k in range(count):
            last = jnp.minimum(last, jnp.where(label < seq_ref[k], seq_ref[k], 1 << 30))
        allowed = query_label < last
        if place == tile:
            allowed = allowed & (label <= query_label)
        product = lax.dot_general(query, key, (((1,), (1,)), ((), ())), preferred_element_type=F32)
        scores.append(jnp.where(allowed, product * HEAD ** (-0.5), MASKED))
    scores = jnp.concatenate(scores, axis=1)
    exp_scores = jnp.exp(scores - jnp.max(scores, axis=1, keepdims=True))
    return exp_scores * (1.0 / jnp.sum(exp_scores, axis=1, keepdims=True))


def attend_kernel(seq_ref, qkv_ref, cos_ref, sin_ref, out_ref, query_ref, key_ref):
    tiles = query_ref.shape[0]
    tile_tokens = TILE_ROWS * HEADS

    def part(tile, lane):
        rows = qkv_ref[:, tile * TILE_ROWS : (tile + 1) * TILE_ROWS, lane : lane + HEAD]
        return rows.reshape(tile_tokens, HEAD)

    for tile in range(tiles):
        cosine, sine = cos_ref[tile], sin_ref[tile]
        query = turn(part(tile, 0).astype(F32), cosine, sine).astype(BF16)
        query_ref[tile] = query
        key_ref[tile] = turn(part(tile, HEAD).astype(F32), cosine, sine).astype(BF16)
        near = list(range(max(tile - 2, 0), tile + 1))
        probs = tile_weights(
            tile, seq_ref, query, [(k, key_ref[k]) for k in near], seq_ref.shape[0] - 1
        ).astype(BF16)
        total = jnp.zeros((tile_tokens, HEAD), F32)
        for at, k in enumerate(near):
            total = total + jnp.dot(
                probs[:, at * tile_tokens : (at + 1) * tile_tokens],
                part(k, 2 * HEAD),
                preferred_element_type=F32,
            )
        out_ref[:, tile * TILE_ROWS : (tile + 1) * TILE_ROWS, :] = total.astype(BF16).reshape(
            HEADS, TILE_ROWS, HEAD
        )


def attend_back_kernel(
    seq_ref, qkv_ref, grad_ref, cos_ref, sin_ref, query_ref, key_ref, out_ref, sum_ref, gk_ref, gv_ref
):
    tiles = query_ref.shape[0]
    tile_tokens = TILE_ROWS * HEADS
    scale = HEAD ** (-0.5)
    over_rows = (((0,), (0,)), ((), ()))
    over_lanes = (((1,), (1,)), ((), ()))

    def rows_of(tile):
        return slice(tile * TILE_ROWS, (tile + 1) * TILE_ROWS)

    def put(tile, lane, value):
        low = value.astype(BF16)
        out_ref[:, rows_of(tile), lane : lane + HEAD] = low.reshape(HEADS, TILE_ROWS, HEAD)
        columns = jnp.sum(low.astype(F32), axis=0, keepdims=True)
        if tile == 0:
            sum_ref[:, lane : lane + HEAD] = columns
        else:
            sum_ref[:, lane : lane + HEAD] += columns

    def finish(tile):
        put(tile, HEAD, turn(gk_ref[tile] * scale, cos_ref[tile], -sin_ref[tile]))
        put(tile, 2 * HEAD, gv_ref[tile])

    for tile in range(tiles):
        query = query_ref[tile]
        near = list(range(max(tile - 2, 0), tile + 1))
        grad = grad_ref[:, rows_of(tile), :].reshape(tile_tokens, HEAD)
        probs = tile_weights(
            tile, seq_ref, query, [(k, key_ref[k]) for k in near], seq_ref.shape[0] - 1
        )
        grad_probs = jnp.concatenate(
            [
                lax.dot_general(
                    grad,
                    qkv_ref[:, rows_of(k), 2 * HEAD :].reshape(tile_tokens, HEAD),
                    over_lanes,
                    preferred_element_type=F32,
                )
                for k in near
            ],
            axis=1,
        )
        delta = jnp.sum(probs * grad_probs, axis=1, keepdims=True)
        grad_scores = (probs * (grad_probs - delta)).astype(BF16)
        probs = probs.astype(BF16)
        grad_query = jnp.zeros((tile_tokens, HEAD), F32)
        for at, k in enumerate(near):
            span = slice(at * tile_tokens, (at + 1) * tile_tokens)
            grad_query = grad_query + jnp.dot(
                grad_scores[:, span], key_ref[k], preferred_element_type=F32
            )
            to_key = lax.dot_general(
                grad_scores[:, span], query, over_rows, preferred_element_type=F32
            )
            to_value = lax.dot_general(probs[:, span], grad, over_rows, preferred_element_type=F32)
            if k == tile:
                gk_ref[k] = to_key
                gv_ref[k] = to_value
            else:
                gk_ref[k] += to_key
                gv_ref[k] += to_value
        put(tile, 0, turn(grad_query * scale, cos_ref[tile], -sin_ref[tile]))
        if tile >= 2:
            finish(tile - 2)
    for tile in range(max(tiles - 2, 0), tiles):
        finish(tile)


def one_spec(shape):
    return pl.BlockSpec(shape, lambda i: (0,) * len(shape), pipeline_mode=pl.Buffered(1))


SMEM_SPEC = pl.BlockSpec(memory_space=pltpu.SMEM)


def attend(seq_scalars, qkv, cosine, sine):
    blocks, rows, _ = qkv.shape
    tiled = (rows // TILE_ROWS, blocks * TILE_ROWS, HEAD)
    return pl.pallas_call(
        attend_kernel,
        out_shape=(
            jax.ShapeDtypeStruct((blocks, rows, HEAD), BF16),
            jax.ShapeDtypeStruct(tiled, BF16),
            jax.ShapeDtypeStruct(tiled, BF16),
        ),
        grid=(1,),
        in_specs=[SMEM_SPEC] + [one_spec(array.shape) for array in (qkv, cosine, sine)],
        out_specs=(one_spec((blocks, rows, HEAD)), one_spec(tiled), one_spec(tiled)),
        compiler_params=pltpu.CompilerParams(vmem_limit_bytes=BIG_VMEM),
        cost_estimate=SMALL_COST,
    )(seq_scalars, qkv, cosine, sine)


def attend_back(seq_scalars, qkv, grad, cosine, sine, query, key):
    blocks, rows, wide = qkv.shape
    return pl.pallas_call(
        attend_back_kernel,
        out_shape=(
            jax.ShapeDtypeStruct((blocks, rows, wide), BF16),
            jax.ShapeDtypeStruct((1, wide), F32),
        ),
        grid=(1,),
        in_specs=[SMEM_SPEC]
        + [one_spec(array.shape) for array in (qkv, grad, cosine, sine, query, key)],
        out_specs=(one_spec((blocks, rows, wide)), one_spec((1, wide))),
        scratch_shapes=[pltpu.VMEM(query.shape, F32), pltpu.VMEM(query.shape, F32)],
        compiler_params=pltpu.CompilerParams(vmem_limit_bytes=BIG_VMEM),
        cost_estimate=SMALL_COST,
    )(seq_scalars, qkv, grad, cosine, sine, query, key)


def copy_kernel(in_ref, out_ref):
    out_ref[...] = in_ref[...]


def settled(values):
    return pl.pallas_call(
        copy_kernel,
        out_shape=jax.ShapeDtypeStruct(values.shape, values.dtype),
        grid=(1,),
        in_specs=[pl.BlockSpec(values.shape, lambda i: (0, 0))],
        out_specs=pl.BlockSpec(values.shape, lambda i: (0, 0)),
        cost_estimate=SMALL_COST,
    )(values)


def pack_kernel(at_ref, up_ref, qkv_ref, odd_ref, even_ref):
    third = qkv_ref.shape[1] // 3
    hidden = up_ref.shape[1] // HEADS
    for k in range(HEADS):
        out_ref = even_ref if k % 2 == 0 else odd_ref
        target = at_ref[0] ^ k
        start = pl.multiple_of(target * hidden, hidden)
        out_ref[k // 2, :, :hidden] = up_ref[:, pl.ds(start, hidden)]
        for j in range(3):
            start = pl.multiple_of(j * third + target * HEAD, HEAD)
            out_ref[k // 2, :, hidden + j * HEAD : hidden + (j + 1) * HEAD] = qkv_ref[
                :, pl.ds(start, HEAD)
            ]


def pack(me, rep, w_up, w_qkv, hidden):
    quarter = w_up.shape[0] // 4
    shape = (HEADS // 2, quarter, hidden + 3 * HEAD)
    packed = jax.ShapeDtypeStruct(shape, BF16)
    return pl.pallas_call(
        pack_kernel,
        out_shape=(packed, packed),
        grid_spec=pltpu.PrefetchScalarGridSpec(
            num_scalar_prefetch=1,
            grid=(1,),
            in_specs=[
                pl.BlockSpec((quarter, weight.shape[1]), lambda i, at_ref: (at_ref[1], 0))
                for weight in (w_up, w_qkv)
            ],
            out_specs=tuple(pl.BlockSpec(shape, lambda i, at_ref: (0, 0, 0)) for _ in range(2)),
        ),
        compiler_params=pltpu.CompilerParams(vmem_limit_bytes=24 << 20),
        cost_estimate=SMALL_COST,
    )(jnp.stack([me, rep]).astype(jnp.int32), w_up, w_qkv)


def place_weights_kernel(
    at_ref, p0_ref, p1_ref, p2_ref, p3_ref, norms_ref, *out_refs, hidden
):
    raw_refs, scaled_refs, sum_ref = out_refs[:2], out_refs[2:4], out_refs[4]
    quarter, wide = p0_ref.shape[1:]

    @pl.when(pl.program_id(0) == 0)
    def _():
        sum_ref[...] = jnp.zeros_like(sum_ref)

    for k, part_ref in enumerate((p0_ref, p1_ref, p2_ref, p3_ref)):
        rows = pl.ds(pl.multiple_of((at_ref[1] ^ k) * quarter, quarter), quarter)
        for norm, columns in ((1, slice(0, hidden)), (0, slice(hidden, wide))):
            raw = part_ref[0, :, columns]
            raw_refs[1 - norm][rows, :] = raw
            weight = raw.astype(F32)
            gain = norms_ref[rows, 2 * norm : 2 * norm + 1]
            shift = norms_ref[rows, 2 * norm + 1 : 2 * norm + 2]
            scaled_refs[1 - norm][rows, :] = (weight * gain).astype(BF16)
            sum_ref[:, columns] += jnp.sum(weight * shift, axis=0, keepdims=True)


def place_weights(me, rep, parts, norms, hidden):
    count, rows, wide = parts[0].shape
    widths = (hidden, wide - hidden) * 2
    four = pl.BlockSpec((4 * rows, 4), lambda i, at_ref: (i ^ at_ref[0], 0))
    part = pl.BlockSpec((1, rows, wide), lambda i, at_ref: (i, 0, 0))
    return pl.pallas_call(
        functools.partial(place_weights_kernel, hidden=hidden),
        out_shape=tuple(jax.ShapeDtypeStruct((count * 4 * rows, n), BF16) for n in widths)
        + (jax.ShapeDtypeStruct((1, wide), F32),),
        grid_spec=pltpu.PrefetchScalarGridSpec(
            num_scalar_prefetch=1,
            grid=(count,),
            in_specs=[part] * 4 + [four],
            out_specs=tuple(
                pl.BlockSpec((4 * rows, n), lambda i, at_ref: (i ^ at_ref[0], 0)) for n in widths
            )
            + (pl.BlockSpec((1, wide), lambda i, at_ref: (0, 0)),),
        ),
        compiler_params=pltpu.CompilerParams(vmem_limit_bytes=BIG_VMEM),
        cost_estimate=SMALL_COST,
    )(jnp.stack([me, rep]).astype(jnp.int32), *parts, norms)


def place_grads_kernel(at_ref, p0_ref, p1_ref, p2_ref, p3_ref, out_ref, *, pieces):
    quarter, wide = p0_ref.shape[1:]
    source = pl.program_id(0) ^ at_ref[0]
    size = wide // pieces
    for k, part_ref in enumerate((p0_ref, p1_ref, p2_ref, p3_ref)):
        rows = pl.ds(pl.multiple_of((at_ref[1] ^ k) * quarter, quarter), quarter)
        values = part_ref[0].astype(F32)
        if pieces == 1:
            out_ref[rows, :] = values
        else:
            for j in range(pieces):
                start = pl.multiple_of((j * HEADS + source) * size, size)
                out_ref[rows, pl.ds(start, size)] = values[:, j * size : (j + 1) * size]


def place_grads(me, rep, parts, pieces):
    count, rows, wide = parts[0].shape
    part = pl.BlockSpec((1, rows, wide), lambda i, at_ref: (i, 0, 0))
    if pieces == 1:
        out = pl.BlockSpec((4 * rows, wide), lambda i, at_ref: (0, i ^ at_ref[0]))
    else:
        out = pl.BlockSpec((4 * rows, count * wide), lambda i, at_ref: (0, 0))
    return pl.pallas_call(
        functools.partial(place_grads_kernel, pieces=pieces),
        out_shape=jax.ShapeDtypeStruct((4 * rows, count * wide), F32),
        grid_spec=pltpu.PrefetchScalarGridSpec(
            num_scalar_prefetch=1, grid=(count,), in_specs=[part] * 4, out_specs=out
        ),
        compiler_params=pltpu.CompilerParams(vmem_limit_bytes=40 << 20),
        cost_estimate=SMALL_COST,
    )(jnp.stack([me, rep]).astype(jnp.int32), *parts)


def place_halves_kernel(core_ref, mine_ref, other_ref, down_ref, dense_ref, *, cut):
    half = mine_ref.shape[1]

    def fill(out_ref):
        for part_ref, core in ((mine_ref, core_ref[0]), (other_ref, 1 - core_ref[0])):
            start = pl.multiple_of(core * half, half)
            out_ref[:, pl.ds(start, half)] = part_ref[...].astype(F32)

    @pl.when(pl.program_id(0) < cut)
    def _():
        fill(down_ref)

    @pl.when(pl.program_id(0) >= cut)
    def _():
        fill(dense_ref)


def place_halves(core, mine, other, hidden):
    rows, half = mine.shape
    tile = 256
    cut = hidden // tile
    part = pl.BlockSpec((tile, half), lambda i, core_ref: (i, 0))
    return pl.pallas_call(
        functools.partial(place_halves_kernel, cut=cut),
        out_shape=(
            jax.ShapeDtypeStruct((hidden, 2 * half), F32),
            jax.ShapeDtypeStruct((rows - hidden, 2 * half), F32),
        ),
        grid_spec=pltpu.PrefetchScalarGridSpec(
            num_scalar_prefetch=1,
            grid=(rows // tile,),
            in_specs=[part, part],
            out_specs=(
                pl.BlockSpec((tile, 2 * half), lambda i, core_ref: (jnp.minimum(i, cut - 1), 0)),
                pl.BlockSpec((tile, 2 * half), lambda i, core_ref: (jnp.maximum(i - cut, 0), 0)),
            ),
        ),
        compiler_params=pltpu.CompilerParams(vmem_limit_bytes=32 << 20),
        cost_estimate=SMALL_COST,
    )(core[None].astype(jnp.int32), mine, other)


def normalize(values):
    values = values.astype(F32)
    centered = values - jnp.mean(values, axis=-1, keepdims=True)
    rstd = lax.rsqrt(jnp.mean(centered * centered, axis=-1, keepdims=True) + EPSILON)
    return centered * rstd, rstd


def norm_kernel(*refs, count, steps):
    blocks, out_ref = refs[:count], refs[-1]
    for k in range(count):

        @pl.when(pl.program_id(0) // steps == k)
        def _(block_ref=blocks[k]):
            out_ref[...] = normalize(block_ref[...])[0].astype(BF16)


def norm_blocks(blocks, places, buffer):
    rows, width = blocks[0].shape
    steps = 2
    tile = rows // steps
    count = len(blocks)

    def spec(k):
        return pl.BlockSpec((tile, width), lambda i: (jnp.clip(i - steps * k, 0, steps - 1), 0))

    def put(i):
        place = places[0]
        for k in range(1, count):
            place = jnp.where(i // steps >= k, places[k], place)
        return place * steps + i % steps, 0

    extra = [] if buffer is None else [buffer]
    return pl.pallas_call(
        functools.partial(norm_kernel, count=count, steps=steps),
        out_shape=jax.ShapeDtypeStruct((HEADS * rows, width), BF16),
        grid=(count * steps,),
        in_specs=[spec(k) for k in range(count)] + [pl.BlockSpec(memory_space=pl.ANY)] * len(extra),
        out_specs=pl.BlockSpec((tile, width), put),
        input_output_aliases={count: 0} if extra else {},
        cost_estimate=SMALL_COST,
    )(*blocks, *extra)


def dot32(left, right, left_dim=1, right_dim=0):
    return lax.dot_general(
        left, right, (((left_dim,), (right_dim,)), ((), ())), preferred_element_type=F32
    )


def tokens_spec(tile, width, first):
    return pl.BlockSpec((tile, width), lambda i: (first + i, 0))


def whole_spec(shape):
    return pl.BlockSpec(shape, lambda i: (0, 0), pipeline_mode=pl.Buffered(1))


def block_specs(count, tile, width):
    return [pl.BlockSpec((tile, width), lambda i: (0, 0)) for _ in range(count)]


def project_kernel(normed_ref, up_ref, qkv_w_ref, shift_ref, *refs):
    act_ref, slope_ref, qkv_ref = refs[-3:]
    hidden = act_ref.shape[1]
    lanes = 256
    for start in range(0, hidden, lanes):
        columns = slice(start, start + lanes)
        value = dot32(normed_ref[...], up_ref[:, columns]) + shift_ref[:, columns]
        normal = 0.5 + 0.5 * lax.erf(value * (0.5**0.5))
        bell = jnp.exp(value * value * -0.5) * ((2.0 * math.pi) ** -0.5)
        act_ref[:, columns] = (value * normal).astype(BF16)
        slope_ref[:, columns] = (normal + value * bell).astype(BF16)
    for start in range(0, qkv_ref.shape[1], lanes):
        columns = slice(start, start + lanes)
        value = dot32(normed_ref[...], qkv_w_ref[:, columns])
        value = value + shift_ref[:, hidden + start : hidden + start + lanes]
        qkv_ref[:, columns] = value.astype(BF16)


def project(normed, w_up, w_qkv, shift, first, last, buffers):
    count, width = normed.shape
    tile = 2 * count // HEADS
    widths = (w_up.shape[1], w_up.shape[1], w_qkv.shape[1])
    return pl.pallas_call(
        project_kernel,
        out_shape=tuple(jax.ShapeDtypeStruct((count, n), BF16) for n in widths),
        grid=(last - first,),
        in_specs=[
            tokens_spec(tile, width, first),
            whole_spec(w_up.shape),
            whole_spec(w_qkv.shape),
            whole_spec(shift.shape),
        ]
        + [pl.BlockSpec(memory_space=pl.ANY)] * len(buffers),
        out_specs=tuple(tokens_spec(tile, n, first) for n in widths),
        input_output_aliases={4 + k: k for k in range(len(buffers))},
        compiler_params=pltpu.CompilerParams(vmem_limit_bytes=BIG_VMEM),
        cost_estimate=SMALL_COST,
    )(normed, w_up, w_qkv, shift, *buffers)


def combine_kernel(one_a_ref, one_b_ref, two_a_ref, two_b_ref, w_one_ref, w_two_ref, *out_refs, right_dim):
    rows = out_refs[0].shape[0]
    for pair, (one_ref, two_ref) in enumerate(((one_a_ref, two_a_ref), (one_b_ref, two_b_ref))):
        value = dot32(one_ref[...], w_one_ref[...], 1, right_dim)
        value = value + dot32(two_ref[...], w_two_ref[...], 1, right_dim)
        out_refs[2 * pair][...] = value[:rows].astype(BF16)
        out_refs[2 * pair + 1][...] = value[rows:].astype(BF16)


def combine(one, two, w_one, w_two, rows, side, right_dim):
    width = w_one.shape[1 - right_dim]
    lanes = 512

    def weight_spec(weight):
        if right_dim:
            return pl.BlockSpec((lanes, weight.shape[1]), lambda i: (i, 0))
        return pl.BlockSpec((weight.shape[0], lanes), lambda i: (0, i))

    def left_spec(left, pair):
        return pl.BlockSpec(
            (2 * rows, left.shape[1]),
            lambda i: (2 * pair + side, 0),
            pipeline_mode=pl.Buffered(1),
        )

    return pl.pallas_call(
        functools.partial(combine_kernel, right_dim=right_dim),
        out_shape=tuple(jax.ShapeDtypeStruct((rows, width), BF16) for _ in range(4)),
        grid=(width // lanes,),
        in_specs=[left_spec(left, pair) for left in (one, two) for pair in (0, 1)]
        + [weight_spec(w_one), weight_spec(w_two)],
        out_specs=tuple(pl.BlockSpec((rows, lanes), lambda i: (0, i)) for _ in range(4)),
        compiler_params=pltpu.CompilerParams(vmem_limit_bytes=BIG_VMEM),
        cost_estimate=SMALL_COST,
    )(one, one, two, two, w_one, w_two)


def pull_kernel(*refs, count):
    blocks, (w_one_ref, w_two_ref, slope_ref) = refs[:count], refs[count : count + 3]
    pre_ref, att_ref, sum_ref, left_ref, sems = refs[-5:]
    rows = blocks[0].shape[0]
    last = pl.num_programs(0) - 1

    @pl.when(pl.program_id(0) == 0)
    def _():
        copies = [
            pltpu.make_async_copy(block, left_ref.at[pl.ds(k * rows, rows)], sems.at[k])
            for k, block in enumerate(blocks)
        ]
        for copy in copies:
            copy.start()
        for copy in copies:
            copy.wait()

    @pl.when(pl.program_id(0) < last)
    def _():
        value = dot32(left_ref[...], w_one_ref[...], 1, 1)
        value = (value * slope_ref[...].astype(F32)).astype(BF16)
        pre_ref[...] = value
        sum_ref[...] = jnp.sum(value.astype(F32), axis=0, keepdims=True)

    @pl.when(pl.program_id(0) == last)
    def _():
        att_ref[...] = dot32(left_ref[...], w_two_ref[...], 1, 1).astype(BF16)


def pull(blocks, w_down, w_dense, slope, part, buffers):
    rows, width = blocks[0].shape
    hidden, head = w_down.shape[0], w_dense.shape[0]
    tokens = HEADS * rows
    count = len(blocks)
    lanes = 512
    steps = hidden // lanes

    def at(i):
        return jnp.minimum(i, steps - 1)

    anywhere = pl.BlockSpec(memory_space=pl.ANY)
    return pl.pallas_call(
        functools.partial(pull_kernel, count=count),
        out_shape=(
            jax.ShapeDtypeStruct((tokens, hidden), BF16),
            jax.ShapeDtypeStruct((tokens, head), BF16),
            jax.ShapeDtypeStruct((1, hidden), F32),
        ),
        grid=(steps + 1,),
        in_specs=[anywhere] * count
        + [
            pl.BlockSpec((lanes, width), lambda i: (at(i), 0)),
            whole_spec(w_dense.shape),
            pl.BlockSpec((count * rows, lanes), lambda i: (part, at(i))),
        ]
        + [anywhere] * len(buffers),
        out_specs=(
            pl.BlockSpec((count * rows, lanes), lambda i: (part, at(i))),
            pl.BlockSpec((count * rows, head), lambda i: (part, 0)),
            pl.BlockSpec((1, lanes), lambda i: (0, at(i))),
        ),
        scratch_shapes=[pltpu.VMEM((count * rows, width), BF16), pltpu.SemaphoreType.DMA((count,))],
        input_output_aliases={count + 3 + k: k for k in range(len(buffers))},
        compiler_params=pltpu.CompilerParams(vmem_limit_bytes=BIG_VMEM),
        cost_estimate=SMALL_COST,
    )(*blocks, w_down, w_dense, slope, *buffers)


def moments_kernel(
    core_ref,
    normed_ref,
    right_ref,
    weight_ref,
    norms_ref,
    columns_ref,
    keep_ref,
    give_ref,
    gain_sum_ref,
    bias_sum_ref,
    low_ref,
    *,
    quarter,
    norm,
):
    lanes = 256
    turned = normed_ref[...].T
    gain = norms_ref[:, 2 * norm : 2 * norm + 1]
    shift = norms_ref[:, 2 * norm + 1 : 2 * norm + 2]
    gain_terms, bias_terms = None, None
    for start in range(0, low_ref.shape[1], lanes):
        columns = slice(start, start + lanes)
        moment = dot32(turned, right_ref[:, columns])
        weight = weight_ref[:, columns].astype(F32)
        total = columns_ref[:, columns]
        low_ref[:, columns] = (moment * gain + shift * total).astype(BF16)
        one, two = moment * weight, weight * total
        gain_terms = one if gain_terms is None else gain_terms + one
        bias_terms = two if bias_terms is None else bias_terms + two
    for terms, sum_ref in ((gain_terms, gain_sum_ref), (bias_terms, bias_sum_ref)):
        sum_ref[...] = jnp.sum(terms.T, axis=0, keepdims=True)
    for core in (0, 1):

        @pl.when(core_ref[0] == core)
        def _(core=core):
            for k in range(low_ref.shape[0] // quarter):
                target = keep_ref if k % 2 == core else give_ref
                target[k // 2 * quarter : (k // 2 + 1) * quarter, :] = low_ref[
                    k * quarter : (k + 1) * quarter, :
                ]


def moments_of(core, normed, right, weight, norms, norm, columns, quarter):
    count, width = normed.shape
    wide = weight.shape[1]
    tile = 8 * quarter
    return pl.pallas_call(
        functools.partial(moments_kernel, quarter=quarter, norm=norm),
        out_shape=(
            jax.ShapeDtypeStruct((width // 2, wide), BF16),
            jax.ShapeDtypeStruct((width // 2, wide), BF16),
            jax.ShapeDtypeStruct((1, width), F32),
            jax.ShapeDtypeStruct((1, width), F32),
        ),
        grid=(width // tile,),
        in_specs=[
            SMEM_SPEC,
            pl.BlockSpec((count, tile), lambda i: (0, i)),
            whole_spec(right.shape),
            tokens_spec(tile, wide, 0),
            tokens_spec(tile, 4, 0),
            whole_spec(columns.shape),
        ],
        out_specs=(
            tokens_spec(tile // 2, wide, 0),
            tokens_spec(tile // 2, wide, 0),
            pl.BlockSpec((1, tile), lambda i: (0, i)),
            pl.BlockSpec((1, tile), lambda i: (0, i)),
        ),
        scratch_shapes=[pltpu.VMEM((tile, wide), BF16)],
        compiler_params=pltpu.CompilerParams(vmem_limit_bytes=BIG_VMEM),
        cost_estimate=SMALL_COST,
    )(core[None].astype(jnp.int32), normed, right, weight, norms, columns)


def outer_kernel(core_ref, act_ref, att_ref, *refs):
    blocks, out_refs = refs[:HEADS], refs[HEADS:]
    rows = blocks[0].shape[0]
    lanes = 512
    last = pl.num_programs(1) - 1

    def fill(left_ref, out_ref):
        turned = left_ref[...].T
        for start in range(0, out_ref.shape[1], lanes):
            columns = slice(start, start + lanes)
            total = None
            for k, block_ref in enumerate(blocks):
                term = dot32(turned[:, k * rows : (k + 1) * rows], block_ref[:, columns])
                total = term if total is None else total + term
            out_ref[:, columns] = total.astype(BF16)

    for side in (0, 1):
        for left_ref, chosen in (
            (act_ref, pl.program_id(1) < last),
            (att_ref, pl.program_id(1) == last),
        ):

            @pl.when((pl.program_id(0) == side) & chosen)
            def _(left_ref=left_ref, side=side):
                fill(left_ref, out_refs[side])


def outer(core, activated, attended, blocks):
    count, hidden = activated.shape
    rows, width = blocks[0].shape
    tile = attended.shape[1]
    steps = hidden // tile
    half = jax.ShapeDtypeStruct((hidden + tile, width // 2), BF16)
    return pl.pallas_call(
        outer_kernel,
        out_shape=(half, half),
        grid_spec=pltpu.PrefetchScalarGridSpec(
            num_scalar_prefetch=1,
            grid=(2, steps + 1),
            in_specs=[
                pl.BlockSpec((count, tile), lambda j, i, core_ref: (0, jnp.minimum(i, steps - 1))),
                pl.BlockSpec((count, tile), lambda j, i, core_ref: (0, 0)),
            ]
            + [
                pl.BlockSpec((rows, width // 2), lambda j, i, core_ref: (0, j ^ core_ref[0]))
                for _ in blocks
            ],
            out_specs=(
                pl.BlockSpec(
                    (tile, width // 2), lambda j, i, core_ref: (jnp.where(j == 0, i, steps), 0)
                ),
                pl.BlockSpec(
                    (tile, width // 2), lambda j, i, core_ref: (jnp.where(j == 0, 0, i), 0)
                ),
            ),
        ),
        compiler_params=pltpu.CompilerParams(vmem_limit_bytes=BIG_VMEM),
        cost_estimate=SMALL_COST,
    )(core[None].astype(jnp.int32), activated, attended, *blocks)


def split_shards(
    tokens,
    cotangent,
    seq_lengths,
    seq_order,
    ln1_gain,
    ln1_bias,
    ln2_gain,
    ln2_bias,
    w_qkv,
    b_qkv,
    w_dense,
    b_dense,
    w_up,
    b_up,
    w_down,
    b_down,
):
    me = lax.axis_index("shard")
    rep = lax.axis_index("rep")
    place = me // 2
    is_middle = (place == 1) | (place == 2)
    own = tokens[:, 0, :]
    own_grad = cotangent[:, 0, :]
    rows, width = own.shape
    group_tokens = rows * HEADS
    depth = w_up.shape[0]
    hidden = w_down.shape[0]
    wide = hidden + 3 * HEAD
    quarter = depth // 4

    odd, keep = pack(me, rep, w_up, w_qkv, hidden)
    odd_came = flip(odd, "shard", 1)
    x_near = flip(own, "shard", 2)
    x_across = send(own, MIDDLE)
    row_offsets, row_counts = stream_rows(seq_lengths[0], seq_order[0], HEADS)
    ends = (row_offsets + row_counts) * HEADS
    seq_scalars = jnp.concatenate([ends, me[None]]).astype(jnp.int32)
    row_range = jnp.arange(rows, dtype=jnp.int32)
    member = (row_range[:, None] >= row_offsets[None, :]) & (
        row_range[:, None] < (row_offsets + row_counts)[None, :]
    )
    in_seq = row_range - jnp.sum(jnp.where(member, row_offsets[None, :], 0), axis=1)
    block_range = jnp.arange(HEADS, dtype=jnp.int32)
    apart = block_range // 4 * 4 + block_range % 2 * 2 + block_range // 2 % 2
    positions = (
        in_seq.reshape(rows // TILE_ROWS, 1, TILE_ROWS) * HEADS + (apart ^ me)[None, :, None]
    )
    cosine, sine = rotary_tables(positions.reshape(-1).astype(F32))
    rest = 128 - ROT
    cosine = jnp.concatenate([cosine, cosine, jnp.ones((group_tokens, rest), F32)], axis=1)
    sine = jnp.concatenate([-sine, sine, jnp.zeros((group_tokens, rest), F32)], axis=1)
    tiled = (rows // TILE_ROWS, TILE_ROWS * HEADS, 128)
    cosine = cosine.reshape(tiled)
    sine = sine.reshape(tiled)


    norms = settled(jnp.stack([ln1_gain, ln1_bias, ln2_gain, ln2_bias], axis=1))
    out_columns = jnp.sum(own_grad, axis=0, dtype=F32)
    b_in = jnp.concatenate(
        [lax.dynamic_slice_in_dim(b_up, me * hidden, hidden, 0)]
        + [lax.dynamic_slice_in_dim(b_qkv, k * width + me * HEAD, HEAD, 0) for k in range(3)]
    )
    pairs = jnp.stack([keep, odd_came], axis=1)
    own, own_grad, x_near, x_across, norms, b_in, out_columns, *pairs = hold(
        (own, own_grad, x_near, x_across, norms, b_in, out_columns, *[pairs[z] for z in range(4)]),
        (cosine, sine),
    )
    got = [flip(pairs[z], "shard", 2 * z) for z in range(1, 4)]
    x_own_y = flip(own, "shard", 1)
    x_near_y = flip(x_near, "shard", 1)
    beside = [flip(pairs[0], "rep", 2)]
    got = jnp.stack(got)
    x_near, x_across, own_grad, x_near_y, got = hold(
        (x_near, x_across, own_grad, x_near_y, got), (x_own_y, beside[0])
    )
    x_across_near = send(x_near, MIDDLE)
    x_two = send(x_across, OUTWARD)
    g_own_y = flip(own_grad, "shard", 1)
    beside = beside + [flip(got, "rep", 2)]
    part = jnp.concatenate([pairs[0][None], got]).reshape(HEADS, quarter, wide)
    normed = norm_blocks([own, x_near, x_own_y, x_near_y], (0, 1, 2, 3), None)
    x_across_near, x_two, own_grad, normed, *beside = hold(
        (x_across_near, x_two, own_grad, normed, *beside), (part, g_own_y)
    )
    two = jnp.where(is_middle, x_across_near, x_two)
    x_three = send(x_across_near, OUTWARD)
    g_across = send(own_grad, MIDDLE)
    x_two_y = flip(two, "shard", 1)
    beside = jnp.concatenate([beside[0][None], beside[1]]).reshape(HEADS, quarter, wide)
    part_c = flip(part, "rep", 1)
    beside_c = flip(beside, "rep", 1)
    normed = norm_blocks([two], (4,), normed)
    parts = (part, part_c, beside, beside_c)
    up_raw, qkv_raw, up_scaled, qkv_scaled, shifted = place_weights(
        me, rep, parts, norms, hidden
    )
    b_in = b_in[None, :] + shifted
    (x_two_y,) = hold((x_two_y,), (b_in,))
    normed = norm_blocks([x_two_y], (6,), normed)
    x_three, own_grad, g_across, normed, b_in = hold(
        (x_three, own_grad, g_across, normed, b_in), ()
    )
    three = jnp.where(is_middle, x_across, x_three)
    g_near = flip(own_grad, "shard", 2)
    x_three_y = flip(three, "shard", 1)
    normed = norm_blocks([three], (5,), normed)
    halfway = project(normed, up_scaled, qkv_scaled, b_in, 0, 3, [])
    g_near, x_three_y, *halfway = hold((g_near, x_three_y, *halfway), ())
    g_across_near = send(g_near, MIDDLE)
    g_two = send(g_across, OUTWARD)
    g_near_y = flip(g_near, "shard", 1)
    normed = norm_blocks([x_three_y], (7,), normed)
    activated, slope, qkv = project(normed, up_scaled, qkv_scaled, b_in, 3, 4, halfway)
    qkv = qkv.reshape(HEADS, rows, 3 * HEAD)
    attended, query, key = attend(seq_scalars, qkv, cosine, sine)
    attended = attended.reshape(group_tokens, HEAD)
    g_across_near, g_two, attended, g_near_y = hold((g_across_near, g_two, attended, g_near_y), ())
    g_two = jnp.where(is_middle, g_across_near, g_two)
    g_three = send(g_across_near, OUTWARD)
    g_two_y = flip(g_two, "shard", 1)
    far = combine(activated, attended, w_down, w_dense, rows, 1, 0)
    close = combine(activated, attended, w_down, w_dense, rows, 0, 0)
    g_three, g_near_y, g_two_y, *both = hold((g_three, g_near_y, g_two_y, *far, *close), ())
    far, close = both[:4], both[4:]
    g_three = jnp.where(is_middle, g_across, g_three)
    g_three_y = flip(g_three, "shard", 1)
    *grads, sums_one = pull([own_grad, g_near, g_own_y, g_near_y], w_down, w_dense, slope, 0, [])
    *grads, sums_two = pull([g_two, g_three], w_down, w_dense, slope, 2, grads)
    g_three_y, *both = hold((g_three_y, *far, *grads), ())
    far, grads = both[:4], both[4:]
    came_three = flip(far[3], "shard", 1)
    grad_pre, grad_attended, sums_three = pull(
        [g_two_y, g_three_y], w_down, w_dense, slope, 3, grads
    )
    pre_sums = sums_one + sums_two + sums_three
    my_core = rep % 2
    my_side = rep // 2
    my_row = me % 2

    def split(values, index):
        return (
            lax.dynamic_index_in_dim(values, index, 1, False),
            lax.dynamic_index_in_dim(values, 1 - index, 1, False),
        )

    def by_side(summed):
        return split(summed.reshape(HEADS, 2, quarter, summed.shape[-1]), my_side)

    def by_row(summed):
        return split(summed.reshape(4, 2, quarter, summed.shape[-1]), my_row)

    def joined(mine, came):
        return plus(mine, came).astype(BF16)

    def by_place(mine, came):
        both = jnp.stack([mine, came], axis=1)
        return [lax.dynamic_index_in_dim(both, place ^ z, 0, False) for z in range(4)]

    def far_places(pieces):
        return flip(jnp.stack(pieces[2:]), "shard", 4)

    def near_place(pieces, far):
        return flip(jnp.stack([pieces[1], far[1]]), "shard", 2)

    def sources(pieces, far, near):
        both = jnp.stack([pieces[0], near[0], far[0], near[1]])
        return both.reshape(HEADS, quarter, both.shape[-1])

    up_keep, up_give, *up_sums = moments_of(
        my_core, normed, grad_pre, up_raw, norms, 1, pre_sums, quarter
    )
    three = joined(close[3], came_three)
    grad_attended, up_give, three, *far = hold((grad_attended, up_give, three, *far), ())
    came_two = flip(far[2], "shard", 1)
    from_corner = send(three, INWARD)
    up_came = flip(up_give, "rep", 1)
    grad_qkv, qkv_sums = attend_back(
        seq_scalars,
        qkv,
        grad_attended.reshape(HEADS, rows, HEAD),
        cosine,
        sine,
        query,
        key,
    )
    grad_qkv = grad_qkv.reshape(group_tokens, 3 * HEAD)
    qkv_keep, qkv_give, *qkv_row_sums = moments_of(
        my_core, normed, grad_qkv, qkv_raw, norms, 0, qkv_sums, quarter
    )
    two = joined(close[2], came_two)
    up_keep, up_give = by_side(joined(up_keep, up_came))
    from_corner, up_give, qkv_give, grad_qkv, two, *far = hold(
        (from_corner, up_give, qkv_give, grad_qkv, two, *far), (up_keep,)
    )
    up_came = flip(up_give, "rep", 2)
    came_one = flip(far[1], "shard", 1)
    two = joined(two, from_corner)
    across_near = send(two, MIDDLE)
    across = send(two, INWARD)
    qkv_came = flip(qkv_give, "rep", 1)
    gy_far = combine(grad_pre, grad_qkv, up_scaled, qkv_scaled, rows, 1, 1)
    one = joined(close[1], came_one)
    up_keep, up_give = by_row(joined(up_keep, up_came))
    qkv_keep, qkv_give = by_side(joined(qkv_keep, qkv_came))
    small = jnp.concatenate(
        [vector[0] for vector in (*qkv_row_sums, *up_sums)]
        + [
            out_columns,
            jnp.where(
                block_range[:, None] == me, jnp.concatenate([pre_sums, qkv_sums], axis=1), 0.0
            ).reshape(-1),
        ]
    )
    up_give, across_near, across, qkv_give, own_grad, one, small, *both = hold(
        (up_give, across_near, across, qkv_give, own_grad, one, small, *far, *gy_far),
        (up_keep, qkv_keep),
    )
    far, gy_far = both[:4], both[4:]
    came_own = flip(far[0], "shard", 1)
    up_came = flip(up_give, "shard", 1)
    one = joined(one, across_near)
    three = plus(three, across).astype(BF16)
    one_near = flip(one, "shard", 2)
    three_across = send(three, MIDDLE)
    qkv_came = flip(qkv_give, "rep", 2)
    half_keep, half_give = outer(
        my_core,
        activated,
        attended,
        [own_grad, g_near, g_own_y, g_near_y, g_two, g_three, g_two_y, g_three_y],
    )
    out_sum = plus(close[0], came_own)
    up_pieces = by_place(up_keep, up_came)
    qkv_keep, qkv_give = by_row(joined(qkv_keep, qkv_came))
    (
        one_near,
        three_across,
        qkv_keep,
        qkv_give,
        half_give,
        out_sum,
        *both,
    ) = hold(
        (
            one_near,
            three_across,
            qkv_keep,
            qkv_give,
            half_give,
            out_sum,
            *up_pieces,
            *gy_far,
            grad_pre,
        ),
        (),
    )
    up_pieces, gy_far, grad_pre = both[:4], both[4:8], both[8]
    came_three = flip(gy_far[3], "shard", 1)
    qkv_came = flip(qkv_give, "shard", 1)
    up_far = far_places(up_pieces)
    half_came = flip(half_give, "rep", 1)
    small_side = flip(small, "rep", 2)
    out_sum = plus(out_sum, one_near, three_across)
    output = (own.astype(F32) + out_sum + (b_dense + b_down)).astype(BF16)
    gy_close = combine(grad_pre, grad_qkv, up_scaled, qkv_scaled, rows, 0, 1)
    qkv_pieces = by_place(qkv_keep, qkv_came)
    three = joined(gy_close[3], came_three)
    output, up_far, half_came, small, small_side, three, *both = hold(
        (output, up_far, half_came, small, small_side, three, *qkv_pieces, *gy_far, *gy_close), ()
    )
    qkv_pieces, gy_far, gy_close = both[:4], both[4:8], both[8:]
    came_two = flip(gy_far[2], "shard", 1)
    from_corner = send(three, INWARD)
    qkv_far = far_places(qkv_pieces)
    half = joined(half_keep, half_came)
    half_far = flip(half, "rep", 2)
    small = small + small_side
    small_side = flip(small, "rep", 1)
    two = joined(gy_close[2], came_two)
    from_corner, qkv_far, small, small_side, two, *gy_far = hold(
        (from_corner, qkv_far, small, small_side, two, *gy_far), ()
    )
    came_one = flip(gy_far[1], "shard", 1)
    two = joined(two, from_corner)
    across_near = send(two, MIDDLE)
    across = send(two, INWARD)
    up_near = near_place(up_pieces, up_far)
    one = joined(gy_close[1], came_one)
    up_part = sources(up_pieces, up_far, up_near)
    across_near, across, up_part, half_far, one, qkv_far, *gy_far = hold(
        (across_near, across, up_part, half_far, one, qkv_far, *gy_far), ()
    )
    came_own = flip(gy_far[0], "shard", 1)
    one = joined(one, across_near)
    three = plus(three, across).astype(BF16)
    one_near = flip(one, "shard", 2)
    three_across = send(three, MIDDLE)
    up_beside = flip(up_part, "rep", 2)
    qkv_near = near_place(qkv_pieces, qkv_far)
    half = joined(half, half_far)
    gy = plus(gy_close[0], came_own)
    qkv_part = sources(qkv_pieces, qkv_far, qkv_near)
    one_near, three_across, qkv_part, up_beside, half, small, gy = hold(
        (one_near, three_across, qkv_part, up_beside, half, small, gy), ()
    )
    qkv_beside = flip(qkv_part, "rep", 2)
    up_c = flip(jnp.stack([up_part, up_beside]), "rep", 1)
    other = flip(half, "rep", 1)
    small = small + small_side
    small = small + flip(small, "shard", 1)
    gy = plus(gy, one_near, three_across)
    own_normed, own_rstd = normalize(own)
    input_grad = own_grad.astype(F32) + own_rstd * (
        gy
        - jnp.mean(gy, axis=-1, keepdims=True)
        - own_normed * jnp.mean(gy * own_normed, axis=-1, keepdims=True)
    )
    input_grad = input_grad[:, None, :]
    up_grad = place_grads(me, rep, (up_part, up_c[0], up_beside, up_c[1]), 1)
    down_grad, dense_grad = place_halves(my_core, half, other, hidden)
    qkv_c = flip(qkv_part, "rep", 1)
    (small,) = hold((small,), (up_c, qkv_c, other))
    one, two, three = [flip(small, "shard", bit) for bit in (2, 4, 6)]
    small = (small + one) + (two + three)
    input_grad, up_grad, down_grad, qkv_beside, qkv_c, small = hold(
        (input_grad, up_grad, down_grad, qkv_beside, qkv_c, small), ()
    )
    qkv_beside_c = flip(qkv_beside, "rep", 1)
    qkv_grad = place_grads(me, rep, (qkv_part, qkv_c, qkv_beside, qkv_beside_c), 3)
    vectors = small[: 5 * width].reshape(5, width)
    slots = small[5 * width :].reshape(HEADS, wide)
    b_up_grad = slots[:, :hidden].reshape(-1)
    b_qkv_grad = slots[:, hidden:].reshape(HEADS, 3, HEAD).transpose(1, 0, 2).reshape(-1)
    return (
        output[:, None, :],
        input_grad,
        vectors[0],
        vectors[1],
        vectors[2],
        vectors[3],
        qkv_grad,
        b_qkv_grad,
        dense_grad,
        vectors[4],
        up_grad,
        b_up_grad,
        down_grad,
        vectors[4],
    )


def solution(mesh):
    in_specs = (
        P("rep", "shard", None),
        P("rep", "shard", None),
        P("rep", None),
        P("rep", None),
        P(),
        P(),
        P(),
        P(),
        P("shard", None),
        P(),
        P("shard", None),
        P(),
        P("shard", None),
        P(),
        P("shard", None),
        P(),
    )
    out_specs = (
        P("rep", "shard", None),
        P("rep", "shard", None),
        P(),
        P(),
        P(),
        P(),
        P("shard", None),
        P(),
        P("shard", None),
        P(),
        P("shard", None),
        P(),
        P("shard", None),
        P(),
    )
    body = split_shards if mesh.shape["shard"] == HEADS else shards
    return jax.shard_map(
        body, mesh=mesh, in_specs=in_specs, out_specs=out_specs, check_vma=False
    )
```
